32 devices in a mesh: wide: 8 (over y, x, core), narrow: 4 (over z).
Axes of the slice: x: 2, y: 2, z: 4, core: 2. Of those that a mesh axis runs over, the one named last changes fastest.
Arguments:
- tokens: bfloat16 [100352, 384], P(('wide', 'narrow')), may hold values from -6 to 6
- grid_sizes: int32 [128], P('wide'), may hold values from 14 to 24, as said below
- cotangent: bfloat16 [100352, 384], P(('wide', 'narrow')), may hold values from -6 to 6
- attn_weight: float32 [384, 1536], replicated
- attn_first: float32 [384, 1536], replicated, may hold values from -512 to 512
- attn_second: float32 [384, 1536], replicated, may hold values from 9031.68 to 36126.72
- rel_table: float32 [169, 12], replicated, may hold values from -4 to 4
- table_first: float32 [169, 12], replicated, may hold values from -96 to 96
- table_second: float32 [169, 12], replicated, may hold values from 250.88 to 1003.52
- vectors: float32 [8, 384], replicated
- vector_first: float32 [8, 384], replicated, may hold values from -2048 to 2048
- vector_second: float32 [8, 384], replicated, may hold values from 100352 to 401408
- mlp_weight: float32 [2, 1536, 384], P(None, 'narrow')
- mlp_first: float32 [2, 1536, 384], P(None, 'narrow'), may hold values from -512 to 512
- mlp_second: float32 [2, 1536, 384], P(None, 'narrow'), may hold values from 6272 to 25088
- mlp_bias: float32 [1536], P('narrow'), may hold values from -1.5 to 1.5
- bias_first: float32 [1536], P('narrow'), may hold values from -512 to 512
- bias_second: float32 [1536], P('narrow'), may hold values from 6272 to 25088
Outputs:
- outputs: bfloat16 [100352, 384], P(('wide', 'narrow'))
- input_grad: float32 [100352, 384], P(('wide', 'narrow'))
- rms_values: float32 [3], replicated
- attn_new: float32 [384, 1536], replicated
- attn_low: bfloat16 [384, 1536], replicated
- attn_first_new: float32 [384, 1536], replicated
- attn_second_new: float32 [384, 1536], replicated
- table_new: float32 [169, 12], replicated
- table_first_new: float32 [169, 12], replicated
- table_second_new: float32 [169, 12], replicated
- vector_new: float32 [8, 384], replicated
- vector_first_new: float32 [8, 384], replicated
- vector_second_new: float32 [8, 384], replicated
- mlp_new: float32 [2, 1536, 384], P(None, 'narrow')
- mlp_low: bfloat16 [2, 1536, 384], P(None, 'narrow')
- mlp_first_new: float32 [2, 1536, 384], P(None, 'narrow')
- mlp_second_new: float32 [2, 1536, 384], P(None, 'narrow')
- bias_new: float32 [1536], P('narrow')
- bias_first_new: float32 [1536], P('narrow')
- bias_second_new: float32 [1536], P('narrow')
The draws below stay inside these ranges and needn't reach their ends.
Inputs may be any that keep to these rules, and one draw needn't show every extreme that they name: `grid_sizes`: each entry is 14 or 24; the first image has 14, and the last image of each group of 16 has 24.
All inputs are finite; a program needn't handle non-finite values.
Results may differ from the reference program's by a relative error of at most 0.0055.
The reference program's roundings to bfloat16 on the way count: a program that leaves them out, or rounds other values in their place, can miss the bound.
Values may be sent and summed in bfloat16 or wider, within the bound.
A program may use at most 256 MiB of HBM per device.

```python
import math
import jax
import jax.numpy as jnp
from jax import lax

D = 384
HEADS = 12
HEAD_DIM = 32
FF = 1536
WIN = 7
PAD_GRID = 28
STEP = 5
BLOCK_IMG = 4
IMG_W = 16
WTOK = 49
TABLE = 169
WPI = 16
IMG = 128
WINDOWS = 2048
TOKENS = 100352


def draw_grid_sizes(key, part):
    key = jax.random.fold_in(key, 11)
    rolled = jax.random.randint(key, (IMG,), 0, 100)
    position = jnp.arange(IMG)
    limit = 20 + 75 * position // max(IMG - 1, 1)
    larger = ((rolled < limit) | (position % IMG_W == IMG_W - 1)) & (position != 0)
    return jnp.where(larger, 24, 14).astype(jnp.int32)


def draw_attn_weight(key, part):
    key = jax.random.fold_in(key, 5)
    base = jnp.clip(jax.random.normal(key, (D, 4 * D), jnp.float32), -6.0, 6.0)
    column = jnp.arange(4 * D)[None, :]
    return base * jnp.where(column >= 3 * D, (8.0 / D) ** 0.5, D ** (-0.5))


def draw_vectors(key, part):
    key = jax.random.fold_in(key, 7)
    base = jnp.clip(jax.random.normal(key, (8, D), jnp.float32), -5.0, 5.0)
    row_index = jnp.arange(8)[:, None]
    is_gain = (row_index == 0) | (row_index == 5)
    return jnp.where(is_gain, jnp.exp(0.3 * base), 0.3 * base)


def draw_mlp_weight(key, part):
    key = jax.random.fold_in(key, 9)
    base = jnp.clip(jax.random.normal(key, (2, FF, D), jnp.float32), -6.0, 6.0)
    layer_index = jnp.arange(2)[:, None, None]
    return base * jnp.where(layer_index == 0, D ** (-0.5), FF ** (-0.5))


def block_levels(own_key, shape, cuts, least, top_value):
    def one(dim, shards_of):
        draws = jax.random.uniform(jax.random.fold_in(jax.random.fold_in(own_key, 6), dim), (shards_of,), jnp.float32, least / len(cuts), top_value / len(cuts))
        return jnp.repeat(jnp.exp(draws), shape[dim] // shards_of).reshape((-1,) + (1,) * (len(shape) - dim - 1))

    factor_of = one(*cuts[0])
    for cut in cuts[1:]:
        factor_of = factor_of * one(*cut)
    return factor_of


def normal_values(rng, shape, deviation, most, cuts=(), kind=jnp.bfloat16):
    loudness = block_levels(rng, shape, cuts, -0.22, 0.18) if cuts else 1.0
    entries = jax.random.normal(rng, shape, jnp.float32) * deviation * loudness
    return jnp.minimum(jnp.maximum(entries, -most), most).astype(kind)


def setup_inputs(seed: int = 0) -> dict:
    streams_of = jax.random.split(jax.random.key(seed), 19)
    return {
        "tokens": normal_values(streams_of[0], (TOKENS, D), 1.0, 6.0, ((0, 32),)),
        "grid_sizes": draw_grid_sizes(jax.random.fold_in(streams_of[18], 71), 0),
        "cotangent": normal_values(streams_of[2], (TOKENS, D), 1.0, 6.0, ((0, 32),)),
        "attn_weight": draw_attn_weight(jax.random.fold_in(streams_of[18], 71), 0),
        "attn_first": normal_values(streams_of[4], (D, 4 * D), (0.3 * TOKENS ** 0.5), 512.0, (), jnp.float32),
        "attn_second": jnp.clip(jnp.exp(jax.random.uniform(streams_of[5], (D, 4 * D), jnp.float32, math.log(9031.68), math.log(36126.72))), 9031.68, 36126.72),
        "rel_table": normal_values(streams_of[6], (TABLE, HEADS), 1.0, 4.0, (), jnp.float32),
        "table_first": normal_values(streams_of[7], (TABLE, HEADS), (0.05 * TOKENS ** 0.5), 96.0, (), jnp.float32),
        "table_second": jnp.clip(jnp.exp(jax.random.uniform(streams_of[8], (TABLE, HEADS), jnp.float32, math.log(250.88), math.log(1003.52))), 250.88, 1003.52),
        "vectors": draw_vectors(jax.random.fold_in(streams_of[18], 71), 0),
        "vector_first": normal_values(streams_of[10], (8, D), (TOKENS ** 0.5), 2048.0, (), jnp.float32),
        "vector_second": jnp.clip(jnp.exp(jax.random.uniform(streams_of[11], (8, D), jnp.float32, math.log(100352.0), math.log(401408.0))), 100352.0, 401408.0),
        "mlp_weight": draw_mlp_weight(jax.random.fold_in(streams_of[18], 71), 0),
        "mlp_first": normal_values(streams_of[13], (2, FF, D), (0.25 * TOKENS ** 0.5), 512.0, ((1, 4),), jnp.float32),
        "mlp_second": jnp.clip(jnp.exp(math.log(25088.0) - 1.3862944 * jax.random.uniform(streams_of[14], (2, FF, D), jnp.float32) ** block_levels(streams_of[14], (2, FF, D), ((1, 4),), -0.2, 0.2)), 6272.0, 25088.0),
        "mlp_bias": normal_values(streams_of[15], (FF,), 0.3, 1.5, ((0, 4),), jnp.float32),
        "bias_first": normal_values(streams_of[16], (FF,), (0.25 * TOKENS ** 0.5), 512.0, ((0, 4),), jnp.float32),
        "bias_second": jnp.clip(jnp.exp(math.log(25088.0) - 1.3862944 * jax.random.uniform(streams_of[17], (FF,), jnp.float32) ** block_levels(streams_of[17], (FF,), ((0, 4),), -0.2, 0.2)), 6272.0, 25088.0),
    }


@jax.custom_vjp
def low(v):
    return lax.optimization_barrier(v.astype(jnp.bfloat16)).astype(jnp.float32)

@jax.custom_vjp
def low_back(v):
    return v

def low_keep(v):
    return (low(v), None)

def low_pass(kept, grad):
    return (grad,)

def back_keep(v):
    return (v, None)

def back_low(kept, grad):
    return (low(grad),)
low.defvjp(low_keep, low_pass)
low_back.defvjp(back_keep, back_low)
norm_eps = 1e-05
mask_fill = -10000.0
beta_one = 0.5
beta_two = 0.5
adam_eps = 1e-08
highest = lax.Precision.HIGHEST

def layer_norm(tensor, gain_row, shift_row):
    centred = tensor - lax.optimization_barrier(jnp.mean(tensor, -1, keepdims=True))
    spread = lax.optimization_barrier(jnp.mean(centred * centred, -1, keepdims=True))
    return centred * lax.rsqrt(spread + norm_eps) * gain_row + shift_row

def relative_index():
    position = jnp.arange(WTOK)
    cell_row = position // WIN
    cell_col = position % WIN
    offset = (cell_row[:, None] - cell_row[None, :] + WIN - 1) * (2 * WIN - 1)
    return (offset + cell_col[:, None] - cell_col[None, :] + WIN - 1).astype(jnp.int32)

def window_mask(grid_sizes, first_win, win_total):
    group_windows = IMG_W * WPI
    windows = first_win + jnp.arange(win_total)
    local_win = windows % group_windows
    image_idx = windows // group_windows * IMG_W + local_win % IMG_W
    inner_win = WPI - 1 - local_win // IMG_W
    pick_table = (image_idx[:, None] == jnp.arange(grid_sizes.shape[0])[None, :]).astype(jnp.int32)
    grid_side = lax.optimization_barrier(jnp.sum(pick_table * grid_sizes[None, :], 1))
    across = PAD_GRID // WIN
    position = jnp.arange(WTOK)
    cell_row = (inner_win // across)[:, None] * WIN + (position // WIN)[None, :]
    cell_col = (inner_win % across)[:, None] * WIN + (position % WIN)[None, :]
    inside = (cell_row < grid_side[:, None]) & (cell_col < grid_side[:, None])
    return inside.astype(jnp.float32).reshape(-1)

def forward(attn_weight, rel_table, vectors, mlp_weight, mlp_bias, inputs, validity):
    model_width = inputs.shape[1]
    win_count = inputs.shape[0] // WTOK
    token_keep = validity[:, None]
    shaped = (win_count, WTOK, HEADS, HEAD_DIM)
    first_low = low(layer_norm(inputs, vectors[0], vectors[1]))
    weight_low = low(attn_weight)
    project = jnp.dot(first_low, weight_low[:, :3 * model_width], precision=highest)
    queries = low(low_back(project[:, :model_width] + vectors[2])).reshape(shaped)
    key_rows = low(low_back(project[:, model_width:2 * model_width])).reshape(shaped)
    values = low(low_back(project[:, 2 * model_width:3 * model_width] + vectors[3])).reshape(shaped)
    rel_bias = jnp.transpose(rel_table[relative_index()], (2, 0, 1))
    key_fill = ((1.0 - validity) * mask_fill).reshape(win_count, WTOK)
    raw_scores = jnp.einsum('wqhd,wkhd->whqk', queries, key_rows, precision=highest)
    scores = low_back(raw_scores) * HEAD_DIM ** (-0.5) + rel_bias[None] + key_fill[:, None, None, :]
    probs_low = low(jax.nn.softmax(scores, axis=-1))
    mixed_heads = jnp.einsum('whqk,wkhd->wqhd', probs_low, values, precision=highest).reshape(-1, model_width)
    mixed_heads = low(low_back(mixed_heads))
    attn_out = low_back(jnp.dot(mixed_heads, weight_low[:, 3 * model_width:], precision=highest)) + vectors[4]
    attn_branch = attn_out * token_keep
    stream = inputs + attn_branch
    second_low = low(layer_norm(stream, vectors[5], vectors[6]))
    hidden_low = low(mlp_weight)
    pre_act = low_back(jnp.dot(second_low, hidden_low[0].T, precision=highest) + mlp_bias)
    active = low(jax.nn.gelu(pre_act, approximate=True))
    mlp_out = jnp.dot(active, hidden_low[1], precision=highest) + vectors[7]
    mlp_branch = mlp_out * token_keep
    return (stream + mlp_branch, (attn_branch, mlp_branch))

def adam_step(weight, gradient, first_old, second_old, rate_value, decay_value):
    first_new = beta_one * first_old + (1.0 - beta_one) * gradient
    second_new = beta_two * second_old + (1.0 - beta_two) * gradient * gradient
    fix_one = 1.0 - beta_one ** STEP
    fix_two = 1.0 - beta_two ** STEP
    update = rate_value * (first_new / fix_one) / (jnp.sqrt(second_new / fix_two) + adam_eps)
    return (weight - update - rate_value * decay_value * weight, first_new, second_new)

def reference(tokens, grid_sizes, cotangent, attn_weight, attn_first, attn_second, rel_table, table_first, table_second, vectors, vector_first, vector_second, mlp_weight, mlp_first, mlp_second, mlp_bias, bias_first, bias_second):
    model_width = tokens.shape[1]
    validity = window_mask(grid_sizes, 0, WINDOWS)
    blocks = IMG // BLOCK_IMG
    block_rows = BLOCK_IMG * WPI * WTOK
    inputs = tokens.astype(jnp.float32).reshape(blocks, block_rows, model_width)
    grads_in = cotangent.astype(jnp.float32).reshape(blocks, block_rows, model_width)
    masks = validity.reshape(blocks, block_rows)
    params = (attn_weight, rel_table, vectors, mlp_weight, mlp_bias)

    def one_block(running, block_item):
        block_in, block_grad, block_mask = block_item

        def wrapped(attn_p, table_p, vector_p, weight_p, bias_p, tensor):
            return forward(attn_p, table_p, vector_p, weight_p, bias_p, tensor, block_mask)
        block_out, pull_back, branches = jax.vjp(wrapped, *params, block_in, has_aux=True)
        gradients = pull_back(block_grad)
        running = tuple((old + new for old, new in zip(running, gradients[:5])))
        token_keep = block_mask[:, None]
        partial_sums = jnp.stack([jnp.sum(block_in * block_in * token_keep), jnp.sum(branches[0] * branches[0]), jnp.sum(branches[1] * branches[1]), jnp.sum(block_mask)])
        return (running, (block_out.astype(jnp.bfloat16), gradients[5], partial_sums))
    zero_grads = tuple((jnp.zeros_like(param) for param in params))
    totals, (outputs, input_grad, partial_sums) = lax.scan(one_block, zero_grads, (inputs, grads_in, masks))
    stat_totals = lax.optimization_barrier(jnp.sum(partial_sums, 0))
    rms_values = jnp.sqrt(stat_totals[:3] / (stat_totals[3] * model_width))
    attn_new, attn_first_new, attn_second_new = adam_step(attn_weight, totals[0], attn_first, attn_second, 0.02, 0.05)
    table_new, table_first_new, table_second_new = adam_step(rel_table, totals[1], table_first, table_second, 0.3, 0.0)
    vector_new, vector_first_new, vector_second_new = adam_step(vectors, totals[2], vector_first, vector_second, 0.3, 0.0)
    mlp_new, mlp_first_new, mlp_second_new = adam_step(mlp_weight, totals[3], mlp_first, mlp_second, 0.02, 0.05)
    bias_new, bias_first_new, bias_second_new = adam_step(mlp_bias, totals[4], bias_first, bias_second, 0.1, 0.0)
    return (outputs.reshape(TOKENS, model_width), input_grad.reshape(TOKENS, model_width), rms_values, attn_new, attn_new.astype(jnp.bfloat16), attn_first_new, attn_second_new, table_new, table_first_new, table_second_new, vector_new, vector_first_new, vector_second_new, mlp_new, mlp_new.astype(jnp.bfloat16), mlp_first_new, mlp_second_new, bias_new, bias_first_new, bias_second_new)
```

```python
import jax
import jax.numpy as jnp
import numpy as np
from jax import lax
from jax.sharding import PartitionSpec as P
from jax.experimental import pallas as pl
from jax.experimental.pallas import tpu as pltpu

WIN = 7
WTOK = 49
WPI = 16
IMG_W = 16
STEP = 5
CW = 5
CR = 256
SLOT = 64
KR = 56
HG = 4
LOG2E = 1.4426950408889634

norm_eps = 1e-05
beta_one = 0.5
beta_two = 0.5
adam_eps = 1e-08
highest = lax.Precision.HIGHEST
f32 = jnp.float32
bf16 = jnp.bfloat16


def nn(a, b):
    return lax.dot_general(a, b, (((1,), (0,)), ((), ())), preferred_element_type=f32)


def nt(a, b):
    return lax.dot_general(a, b, (((1,), (1,)), ((), ())), preferred_element_type=f32)


def tn(a, b):
    return lax.dot_general(a, b, (((0,), (0,)), ((), ())), preferred_element_type=f32)


def row_info():
    r = np.arange(CR)
    win = r // WTOK
    p = r % WTOK
    info = np.stack([win, p // WIN, p % WIN]).astype(np.float32)
    info[1, win >= CW] = 1000.0
    return np.ascontiguousarray(np.broadcast_to(info[:, :, None], (3, CR, 128)))


def key_info():
    p = np.arange(KR)
    info = np.stack([p // WIN, p % WIN]).astype(np.float32)
    return np.ascontiguousarray(np.broadcast_to(info[:, :, None], (2, KR, 128)))


def head_mask(head_size):
    row = np.arange(HG * SLOT)
    lane = np.arange(HG * head_size)
    return (((row // SLOT)[:, None] == (lane // head_size)[None, :]) & ((row % SLOT) < WTOK)[:, None]).astype(np.float32)


def fold_rows(t):
    return jnp.sum(t.reshape(t.shape[0] // 8, 8, t.shape[1]), 0)


def rep(v, n):
    return jnp.concatenate([v] * n, 1)


def list_windows(sides, narrow, wins, slots, idx, lim_r, lim_c):
    def one(w, n):
        place = narrow * wins + w
        u = WPI - 1 - place // IMG_W
        side = sides[lax.rem(place, IMG_W)]
        r = side - WIN * (u // 4)
        c = side - WIN * lax.rem(u, 4)
        idx[n] = w
        lim_r[n] = r.astype(f32)
        lim_c[n] = c.astype(f32)
        return jnp.where((r > 0) & (c > 0), n + 1, n)

    n = lax.fori_loop(0, wins, one, 0)

    def blank(s, carry):
        @pl.when(s >= n)
        def _():
            idx[s] = wins
            lim_r[s] = 0.0
            lim_c[s] = 0.0
        return carry

    lax.fori_loop(0, slots, blank, 0)
    return n


def chunk_valid(info, lim_r, lim_c, first):
    win = info[0]
    r = jnp.full_like(win, 0.0)
    c = jnp.full_like(win, 0.0)
    for i in range(CW):
        here = win == float(i)
        r = jnp.where(here, lim_r[first + i], r)
        c = jnp.where(here, lim_c[first + i], c)
    return jnp.where((info[1] < r) & (info[2] < c), 1.0, 0.0)


def norm_stats(x):
    mean = jnp.mean(x, -1, keepdims=True)
    centred = x - mean
    inverse = lax.rsqrt(jnp.mean(centred * centred, -1, keepdims=True) + norm_eps)
    return centred * inverse, inverse


def norm_grad(g, xhat, inverse, gain):
    scaled = g * gain
    m1 = jnp.mean(scaled, -1, keepdims=True)
    m2 = jnp.mean(scaled * xhat, -1, keepdims=True)
    return inverse * (scaled - m1 - xhat * m2)


def spread(src, stage, slots):
    wins = src.shape[0] // WTOK
    part = IMG_W * WTOK
    slots[...] = jnp.zeros_like(slots)

    def one(b, carry):
        stage[...] = src[pl.ds(pl.multiple_of(b * part, part), part), :].astype(f32)
        for i in range(IMG_W):
            slots[b * IMG_W + i, :WTOK, :] = stage[WTOK * i : WTOK * i + WTOK, :]
        return carry

    lax.fori_loop(0, wins // IMG_W, one, 0)


def gather_back(slots, stage, dst):
    wins = dst.shape[0] // WTOK
    part = IMG_W * WTOK

    def one(b, carry):
        for i in range(IMG_W):
            stage[WTOK * i : WTOK * i + WTOK, :] = slots[b * IMG_W + i, :WTOK, :]
        dst[pl.ds(pl.multiple_of(b * part, part), part), :] = stage[...].astype(dst.dtype)
        return carry

    lax.fori_loop(0, wins // IMG_W, one, 0)


def attn_forward(narrow_ref, sides, tok, wq, vec, bias, rinfo, kinfo, hmask,
                 x_out, qkv_out, prob_out, mixed_out, stream_out, stat_out,
                 tok32, stage, xs, pj, mx, idx, lim_r, lim_c, count):
    step = pl.program_id(0)
    wins = tok.shape[0] // WTOK
    width = tok.shape[1]
    groups = width // 128

    @pl.when(step == 0)
    def _():
        count[0] = list_windows(sides, narrow_ref[0], wins, idx.shape[0], idx, lim_r, lim_c)
        spread(tok, stage, tok32)
        xs[...] = jnp.zeros_like(xs)
        pj[...] = jnp.zeros_like(pj)
        mx[...] = jnp.zeros_like(mx)
        stat_out[...] = jnp.zeros_like(stat_out)

    @pl.when(step * CW < count[0])
    def _():
        first = step * CW
        for i in range(CW):
            xs[WTOK * i : WTOK * i + KR, :] = tok32[idx[first + i]]
        x = xs[:CR, :]
        x_out[0] = x.astype(bf16)
        valid = chunk_valid(rinfo, lim_r, lim_c, first)
        keep = rep(valid, groups)
        xhat, _ = norm_stats(x)
        low = (xhat * vec[0:1] + vec[1:2]).astype(bf16)
        pj[:CR, :width] = nn(low, wq[:, :width]) + vec[2:3]
        pj[:CR, width : 2 * width] = nn(low, wq[:, width : 2 * width])
        pj[:CR, 2 * width :] = nn(low, wq[:, 2 * width : 3 * width]) + vec[3:4]
        for i in range(CW):
            rows = slice(WTOK * i, WTOK * i + SLOT)
            qkv = pj[rows, :].astype(bf16)
            qkv_out[0, i] = qkv
            fill = jnp.where((kinfo[0] < lim_r[first + i]) & (kinfo[1] < lim_c[first + i]), 0.0, -10000.0 * LOG2E)
            fill = rep(fill, 2)
            for g in range(groups):
                q = qkv[:, 128 * g : 128 * g + 128]
                k = qkv[:KR, width + 128 * g : width + 128 * g + 128]
                v = qkv[:KR, 2 * width + 128 * g : 2 * width + 128 * g + 128]
                q_bd = jnp.concatenate([q] * HG, 0) * hmask[...]
                s = nt(k, q_bd) * (32 ** (-0.5) * LOG2E) + bias[g] + fill
                e = jnp.exp2(s - jnp.max(s, 0, keepdims=True))
                prob = e / jnp.sum(e, 0, keepdims=True)
                prob_out[0, i, g] = prob
                wide_mix = tn(prob.astype(bf16), v)
                hm = hmask[...].astype(f32)
                o = wide_mix * hm
                o = o[:SLOT] + o[SLOT : 2 * SLOT] + o[2 * SLOT : 3 * SLOT] + o[3 * SLOT :]
                mx[WTOK * i : WTOK * i + KR, 128 * g : 128 * g + 128] = o[:KR]
        mixed = mx[:CR, :].astype(bf16)
        mixed_out[0] = mixed
        branch = (nn(mixed, wq[:, 3 * width :]) + vec[4:5]) * keep
        stream_out[0] = x + branch
        stat_out[0] += fold_rows(x * x * keep)
        stat_out[1] += fold_rows(branch * branch)
        stat_out[2, :, :128] += fold_rows(valid)


def mlp_both(narrow_ref, sides, tok, cot, w1, w2, wo, vec, hidden_bias, rinfo, mixed_in, stream_in,
             out_ref, grad_stream_out, grad_mixed_out, dw1, dw2, dwo, dbias, dvec, stat_out,
             out32, cot32, stage, cs, gm, idx, lim_r, lim_c, count):
    step = pl.program_id(0)
    wins = tok.shape[0] // WTOK
    width = tok.shape[1]
    groups = width // 128
    hidden = w1.shape[0]
    tile = 384

    @pl.when(step == 0)
    def _():
        count[0] = list_windows(sides, narrow_ref[0], wins, idx.shape[0], idx, lim_r, lim_c)
        spread(tok, stage, out32)
        spread(cot, stage, cot32)
        cs[...] = jnp.zeros_like(cs)
        gm[...] = jnp.zeros_like(gm)
        for ref in (dw1, dw2, dwo, dbias, dvec, stat_out):
            ref[...] = jnp.zeros_like(ref)

    @pl.when(step * CW < count[0])
    def _():
        first = step * CW
        for i in range(CW):
            cs[WTOK * i : WTOK * i + KR, :] = cot32[idx[first + i]]
        cotan = cs[:CR, :]
        keep = rep(chunk_valid(rinfo, lim_r, lim_c, first), groups)
        stream = stream_in[0]
        xhat, inverse = norm_stats(stream)
        second = (xhat * vec[5:6] + vec[6:7]).astype(bf16)
        kept_cot = cotan * keep
        grad_low = kept_cot.astype(bf16)
        mlp_out = jnp.zeros((CR, width), f32)
        grad_second = jnp.zeros((CR, width), f32)
        for t in range(hidden // tile):
            cols = slice(tile * t, tile * t + tile)
            pre = nt(second, w1[cols, :]) + hidden_bias[0:1, cols]
            inner = 0.7978845608028654 * (pre + 0.044715 * (pre * pre * pre))
            th = jnp.tanh(inner)
            active = (0.5 * pre * (1.0 + th)).astype(bf16)
            slope = 0.5 * (1.0 + th) + (0.5 * pre) * (1.0 - th * th) * (
                0.7978845608028654 * (1.0 + 3 * 0.044715 * (pre * pre)))
            grad_pre32 = nt(grad_low, w2[cols, :]) * slope
            grad_pre = grad_pre32.astype(bf16)
            mlp_out += nn(active, w2[cols, :])
            grad_second += nn(grad_pre, w1[cols, :])
            dw1[:, cols] += tn(second, grad_pre)
            dw2[:, cols] += tn(grad_low, active)
            dbias[:, cols] += fold_rows(grad_pre.astype(f32))
        branch = (mlp_out + vec[7:8]) * keep
        result = stream + branch
        stat_out[...] += fold_rows(branch * branch)
        grad_stream = cotan + norm_grad(grad_second, xhat, inverse, vec[5:6])
        grad_stream_out[0] = grad_stream
        dvec[0] += fold_rows(grad_second * xhat)
        dvec[1] += fold_rows(grad_second)
        dvec[2] += fold_rows(kept_cot)
        grad_attn = grad_stream * keep
        dvec[3] += fold_rows(grad_attn)
        grad_attn_low = grad_attn.astype(bf16)
        dwo[...] += tn(mixed_in[0], grad_attn_low)
        gm[:CR, :] = nt(grad_attn_low, wo[...])
        cs[:CR, :] = result
        for i in range(CW):
            rows = slice(WTOK * i, WTOK * i + SLOT)
            grad_mixed_out[0, i] = gm[rows, :].astype(bf16)

            @pl.when(first + i < count[0])
            def _():
                out32[idx[first + i], :WTOK, :] = cs[WTOK * i : WTOK * i + WTOK, :]

    @pl.when(step == pl.num_programs(0) - 1)
    def _():
        gather_back(out32, stage, out_ref)


def attn_backward(narrow_ref, sides, cot, wq, vec, rinfo, hmask, x_in, qkv_in, prob_in, grad_mixed_in, grad_stream_in,
                  input_grad, dwq, dbias, dvec, dtable,
                  ig32, stage, dp, gs, idx, lim_r, lim_c, count):
    step = pl.program_id(0)
    wins = cot.shape[0] // WTOK
    width = cot.shape[1]
    groups = width // 128

    @pl.when(step == 0)
    def _():
        count[0] = list_windows(sides, narrow_ref[0], wins, idx.shape[0], idx, lim_r, lim_c)
        spread(cot, stage, ig32)
        dp[...] = jnp.zeros_like(dp)
        for ref in (dwq, dbias, dvec, dtable):
            ref[...] = jnp.zeros_like(ref)

    @pl.when(step * CW < count[0])
    def _():
        first = step * CW
        for i in range(CW):
            rows = slice(WTOK * i, WTOK * i + KR)
            for g in range(groups):
                q = qkv_in[0, i, :, 128 * g : 128 * g + 128]
                k = qkv_in[0, i, :KR, width + 128 * g : width + 128 * g + 128]
                v = qkv_in[0, i, :KR, 2 * width + 128 * g : 2 * width + 128 * g + 128]
                do = grad_mixed_in[0, i, :, 128 * g : 128 * g + 128]
                q_bd = jnp.concatenate([q] * HG, 0) * hmask[...]
                do_bd = jnp.concatenate([do] * HG, 0) * hmask[...]
                prob = prob_in[0, i, g]
                gp = nt(v, do_bd)
                ds = prob * (gp - jnp.sum(gp * prob, 0, keepdims=True))
                dtable[g] += ds
                raw = (ds * 32 ** (-0.5)).astype(bf16)
                hm = hmask[...].astype(f32)
                o = tn(raw, k) * hm
                dq = o[:SLOT] + o[SLOT : 2 * SLOT] + o[2 * SLOT : 3 * SLOT] + o[3 * SLOT :]
                dp[rows, 128 * g : 128 * g + 128] = dq[:KR]
                dp[rows, width + 128 * g : width + 128 * g + 128] = nn(raw, q_bd)
                dp[rows, 2 * width + 128 * g : 2 * width + 128 * g + 128] = nn(prob.astype(bf16), do_bd)
        dproj = dp[:CR, :].astype(bf16)
        x = x_in[0].astype(f32)
        xhat, inverse = norm_stats(x)
        low = (xhat * vec[0:1] + vec[1:2]).astype(bf16)
        for j in range(3):
            cols = slice(width * j, width * j + width)
            dwq[:, cols] += tn(low, dproj[:, cols])
        dbias[0] += fold_rows(dproj[:, :width].astype(f32))
        dbias[1] += fold_rows(dproj[:, 2 * width :].astype(f32))
        grad_normed = nt(dproj, wq[:, : 3 * width])
        dvec[0] += fold_rows(grad_normed * xhat)
        dvec[1] += fold_rows(grad_normed)
        gs[:CR, :] = grad_stream_in[0] + norm_grad(grad_normed, xhat, inverse, vec[0:1])
        for i in range(CW):
            @pl.when(first + i < count[0])
            def _():
                ig32[idx[first + i], :WTOK, :] = gs[WTOK * i : WTOK * i + WTOK, :]

    @pl.when(step == pl.num_programs(0) - 1)
    def _():
        gather_back(ig32, stage, input_grad)


def whole(a):
    nd = len(a.shape)
    return pl.BlockSpec(a.shape, lambda *_: (0,) * nd)


def per_chunk(shape):
    nd = len(shape)
    return pl.BlockSpec((1,) + tuple(shape[1:]), lambda c, *_: (c,) + (0,) * (nd - 1))


def sds(shape, dt):
    return jax.ShapeDtypeStruct(shape, dt)


def call(body, scalars, wholes, chunked, out_wholes, out_chunked, order_out, scratch, steps, cost):
    in_specs = [whole(a) for a in wholes] + [per_chunk(a.shape) for a in chunked]
    outs = [sds(s, d) for _, s, d in order_out]
    out_specs = [whole(sds(s, d)) if kind == "w" else per_chunk(s) for kind, s, d in order_out]
    slots = steps * CW
    return pl.pallas_call(
        body,
        grid_spec=pltpu.PrefetchScalarGridSpec(
            num_scalar_prefetch=len(scalars),
            grid=(steps,),
            in_specs=in_specs,
            out_specs=out_specs,
            scratch_shapes=list(scratch) + [
                pltpu.SMEM((slots + 1,), jnp.int32),
                pltpu.SMEM((slots + 1,), f32),
                pltpu.SMEM((slots + 1,), f32),
                pltpu.SMEM((1,), jnp.int32),
            ],
        ),
        out_shape=outs,
        compiler_params=pltpu.CompilerParams(vmem_limit_bytes=60 * 1024 * 1024, dimension_semantics=("arbitrary",)),
        cost_estimate=pl.CostEstimate(flops=cost, bytes_accessed=20000000, transcendentals=0),
    )(*scalars, *wholes, *chunked)


def bias_layout(rel_table):
    pos = np.arange(WTOK)
    row, col = pos // WIN, pos % WIN
    off = (row[:, None] - row[None, :] + WIN - 1) * (2 * WIN - 1) + col[:, None] - col[None, :] + WIN - 1
    full = np.full((KR, SLOT), -1, np.int32)
    full[:WTOK, :WTOK] = off.T
    return full


def expand_bias(rel_table):
    full = bias_layout(rel_table)
    heads = rel_table.shape[1]
    hot = (jnp.asarray(full)[:, :, None] == jnp.arange(rel_table.shape[0])).astype(f32)
    b = jnp.einsum("kqt,th->khq", hot, rel_table * LOG2E, precision=highest)
    b = b.reshape(KR, heads // HG, HG * SLOT).transpose(1, 0, 2)
    dead = (np.arange(KR) >= WTOK)[None, :, None]
    return jnp.where(dead, -1e30, b), hot


def block(tokens, grid_sizes, cotangent, attn_weight, rel_table, vectors, w1, w2, mlp_bias, narrow):
    rows, width = tokens.shape
    wins = rows // WTOK
    heads = rel_table.shape[1]
    groups = heads // HG
    steps = -(-wins // CW)
    weight_low = attn_weight.astype(bf16)
    bias, hot = expand_bias(rel_table)
    rinfo = jnp.asarray(row_info())
    kinfo = jnp.asarray(key_info())
    hmask = jnp.asarray(head_mask(width // heads), bf16)
    slots32 = pltpu.VMEM((wins + 1, KR, width), f32)
    stage = pltpu.VMEM((IMG_W * WTOK, width), f32)
    scal = (narrow.reshape(1).astype(jnp.int32), grid_sizes)
    x, qkv, prob, mixed, stream, stat0 = call(
        attn_forward, scal, (tokens, weight_low, vectors, bias, rinfo, kinfo, hmask), (), None, None,
        [("c", (steps, CR, width), bf16), ("c", (steps, CW, SLOT, 3 * width), bf16),
         ("c", (steps, CW, groups, KR, HG * SLOT), f32), ("c", (steps, CR, width), bf16),
         ("c", (steps, CR, width), f32), ("w", (3, 8, width), f32)],
        [slots32, stage, pltpu.VMEM((CR + 16, width), f32),
         pltpu.VMEM((CR + 16, 3 * width), f32), pltpu.VMEM((CR + 16, width), f32)],
        steps, 8 * rows * width * width)
    outputs, grad_stream, grad_mixed, dw1, dw2, dwo, dhid, dvec2, stat1 = call(
        mlp_both, scal, (tokens, cotangent, w1, w2, weight_low[:, 3 * width :], vectors, mlp_bias.reshape(1, -1), rinfo),
        (mixed, stream), None, None,
        [("w", (rows, width), bf16), ("c", (steps, CR, width), f32), ("c", (steps, CW, SLOT, width), bf16),
         ("w", (width, w1.shape[0]), f32), ("w", (width, w1.shape[0]), f32), ("w", (width, width), f32),
         ("w", (8, w1.shape[0]), f32), ("w", (4, 8, width), f32), ("w", (8, width), f32)],
        [slots32, slots32, stage,
         pltpu.VMEM((CR + 16, width), f32), pltpu.VMEM((CR + 16, width), f32)],
        steps, 52 * rows * width * width)
    input_grad, dwq, dqv, dvec1, dtab = call(
        attn_backward, scal, (cotangent, weight_low, vectors, rinfo, hmask),
        (x, qkv, prob, grad_mixed, grad_stream), None, None,
        [("w", (rows, width), f32), ("w", (width, 3 * width), f32), ("w", (2, 8, width), f32), ("w", (2, 8, width), f32),
         ("w", (groups, KR, HG * SLOT), f32)],
        [slots32, stage, pltpu.VMEM((CR + 16, 3 * width), f32), pltpu.VMEM((CR + 16, width), f32)],
        steps, 16 * rows * width * width)
    dt = dtab.transpose(1, 0, 2).reshape(KR, heads, SLOT)
    table_grad = jnp.einsum("kqt,khq->th", hot, dt, precision=highest)
    dqv = jnp.sum(dqv, 1)
    dvec1 = jnp.sum(dvec1, 1)
    dvec2 = jnp.sum(dvec2, 1)
    vector_grad = jnp.stack([dvec1[0], dvec1[1], dqv[0], dqv[1], dvec2[3], dvec2[0], dvec2[1], dvec2[2]])
    stats = jnp.stack([jnp.sum(stat0[0]), jnp.sum(stat0[1]), jnp.sum(stat1), jnp.sum(stat0[2, :, 0])])
    attn_grad = jnp.concatenate([dwq, dwo], 1)
    return outputs, input_grad, stats, attn_grad, table_grad, vector_grad, dw1, dw2, jnp.sum(dhid, 0)


def adam_step(weight, gradient, first_old, second_old, rate_value, decay_value):
    first_new = beta_one * first_old + (1.0 - beta_one) * gradient
    second_new = beta_two * second_old + (1.0 - beta_two) * gradient * gradient
    fix_one = 1.0 - beta_one**STEP
    fix_two = 1.0 - beta_two**STEP
    update = rate_value * (first_new / fix_one) / (jnp.sqrt(second_new / fix_two) + adam_eps)
    return (weight - update - rate_value * decay_value * weight, first_new, second_new)


def shards(tokens, grid_sizes, cotangent, attn_weight, attn_first, attn_second, rel_table, table_first, table_second,
           vectors, vector_first, vector_second, mlp_weight, mlp_first, mlp_second, mlp_bias, bias_first, bias_second):
    width = tokens.shape[1]
    hidden_low = lax.all_gather(mlp_weight.astype(bf16), "narrow", axis=1, tiled=True)
    hidden_bias = lax.all_gather(mlp_bias, "narrow", axis=0, tiled=True)
    outputs, input_grad, stats, attn_grad, table_grad, vector_grad, dw1, dw2, dhid = block(
        tokens, grid_sizes, cotangent, attn_weight, rel_table, vectors, hidden_low[0], hidden_low[1], hidden_bias,
        lax.axis_index("narrow"))
    both = ("wide", "narrow")
    stat_totals = lax.psum(stats, both)
    weight_grad = lax.psum(lax.psum_scatter(jnp.stack([dw1, dw2]), "narrow", scatter_dimension=2, tiled=True), "wide")
    weight_grad = weight_grad.transpose(0, 2, 1)
    hidden_bias_grad = lax.psum(lax.psum_scatter(dhid, "narrow", scatter_dimension=0, tiled=True), "wide")
    attn_grad, table_grad, vector_grad = lax.psum((attn_grad, table_grad, vector_grad), both)
    rms_values = jnp.sqrt(stat_totals[:3] / (stat_totals[3] * width))
    attn_new, attn_first_new, attn_second_new = adam_step(attn_weight, attn_grad, attn_first, attn_second, 0.02, 0.05)
    table_new, table_first_new, table_second_new = adam_step(rel_table, table_grad, table_first, table_second, 0.3, 0.0)
    vector_new, vector_first_new, vector_second_new = adam_step(vectors, vector_grad, vector_first, vector_second, 0.3, 0.0)
    mlp_new, mlp_first_new, mlp_second_new = adam_step(mlp_weight, weight_grad, mlp_first, mlp_second, 0.02, 0.05)
    bias_new, bias_first_new, bias_second_new = adam_step(mlp_bias, hidden_bias_grad, bias_first, bias_second, 0.1, 0.0)
    return (outputs, input_grad, rms_values, attn_new, attn_new.astype(bf16), attn_first_new, attn_second_new,
            table_new, table_first_new, table_second_new, vector_new, vector_first_new, vector_second_new,
            mlp_new, mlp_new.astype(bf16), mlp_first_new, mlp_second_new, bias_new, bias_first_new, bias_second_new)


def solution(mesh):
    rows = P(("wide", "narrow"), None)
    split = P(None, "narrow", None)
    return jax.shard_map(
        shards, mesh=mesh,
        in_specs=(rows, P("wide"), rows) + (P(),) * 9 + (split,) * 3 + (P("narrow"),) * 3,
        out_specs=(rows, rows) + (P(),) * 11 + (split,) * 4 + (P("narrow"),) * 3,
        check_vma=False)
```

```python
import functools

import jax
import jax.numpy as jnp
import numpy as np
from jax import lax
from jax.sharding import PartitionSpec as P
from jax.experimental import pallas as pl
from jax.experimental.pallas import tpu as pltpu

WIN = 7
WTOK = 49
WPI = 16
IMG_W = 16
STEP = 5
CW = 5
CR = 256
SLOT = 64
KR = 56
HG = 4
LOG2E = 1.4426950408889634

norm_eps = 1e-05
beta_one = 0.5
beta_two = 0.5
adam_eps = 1e-08
highest = lax.Precision.HIGHEST
f32 = jnp.float32
bf16 = jnp.bfloat16


def nn(a, b):
    return lax.dot_general(a, b, (((1,), (0,)), ((), ())), preferred_element_type=f32)


def nt(a, b):
    return lax.dot_general(a, b, (((1,), (1,)), ((), ())), preferred_element_type=f32)


def tn(a, b):
    return lax.dot_general(a, b, (((0,), (0,)), ((), ())), preferred_element_type=f32)


def row_info():
    r = np.arange(CR)
    win = r // WTOK
    p = r % WTOK
    info = np.stack([win, p // WIN, p % WIN]).astype(np.float32)
    info[1, win >= CW] = 1000.0
    return np.ascontiguousarray(np.broadcast_to(info[:, :, None], (3, CR, 128)))


def key_info():
    p = np.arange(KR)
    info = np.stack([p // WIN, p % WIN]).astype(np.float32)
    return np.ascontiguousarray(np.broadcast_to(info[:, :, None], (2, KR, 128)))


def head_mask(head_size):
    row = np.arange(HG * SLOT)
    lane = np.arange(HG * head_size)
    return (((row // SLOT)[:, None] == (lane // head_size)[None, :]) & ((row % SLOT) < WTOK)[:, None]).astype(np.float32)


def fold_rows(t):
    return jnp.sum(t.reshape(t.shape[0] // 8, 8, t.shape[1]), 0)


def rep(v, n):
    return jnp.concatenate([v] * n, 1)


def list_windows(sides, narrow, wins, slots, idx, lim_r, lim_c):
    def one(w, n):
        place = narrow * wins + w
        u = WPI - 1 - place // IMG_W
        side = sides[lax.rem(place, IMG_W)]
        r = side - WIN * (u // 4)
        c = side - WIN * lax.rem(u, 4)
        idx[n] = w
        lim_r[n] = r.astype(f32)
        lim_c[n] = c.astype(f32)
        return jnp.where((r > 0) & (c > 0), n + 1, n)

    n = lax.fori_loop(0, wins, one, 0)

    def blank(s, carry):
        @pl.when(s >= n)
        def _():
            idx[s] = wins
            lim_r[s] = 0.0
            lim_c[s] = 0.0
        return carry

    lax.fori_loop(0, slots, blank, 0)
    return n


def chunk_valid(info, lim_r, lim_c, first):
    win = info[0]
    r = jnp.full_like(win, 0.0)
    c = jnp.full_like(win, 0.0)
    for i in range(CW):
        here = win == float(i)
        r = jnp.where(here, lim_r[first + i], r)
        c = jnp.where(here, lim_c[first + i], c)
    return jnp.where((info[1] < r) & (info[2] < c), 1.0, 0.0)


def norm_stats(x):
    mean = jnp.mean(x, -1, keepdims=True)
    centred = x - mean
    inverse = lax.rsqrt(jnp.mean(centred * centred, -1, keepdims=True) + norm_eps)
    return centred * inverse, inverse


def norm_grad(g, xhat, inverse, gain):
    scaled = g * gain
    m1 = jnp.mean(scaled, -1, keepdims=True)
    m2 = jnp.mean(scaled * xhat, -1, keepdims=True)
    return inverse * (scaled - m1 - xhat * m2)


def spread(src, stage, slots):
    wins = src.shape[0] // WTOK
    part = IMG_W * WTOK
    slots[...] = jnp.zeros_like(slots)

    def one(b, carry):
        stage[...] = src[pl.ds(pl.multiple_of(b * part, part), part), :].astype(f32)
        for i in range(IMG_W):
            slots[b * IMG_W + i, :WTOK, :] = stage[WTOK * i : WTOK * i + WTOK, :]
        return carry

    lax.fori_loop(0, wins // IMG_W, one, 0)


def gather_back(slots, stage, dst):
    wins = dst.shape[0] // WTOK
    part = IMG_W * WTOK

    def one(b, carry):
        for i in range(IMG_W):
            stage[WTOK * i : WTOK * i + WTOK, :] = slots[b * IMG_W + i, :WTOK, :]
        dst[pl.ds(pl.multiple_of(b * part, part), part), :] = stage[...].astype(dst.dtype)
        return carry

    lax.fori_loop(0, wins // IMG_W, one, 0)


def attn_forward(narrow_ref, sides, tok, wq, vec, bias, rinfo, kinfo, hmask,
                 x_out, qkv_out, prob_out, mixed_out, stream_out, stat_out,
                 tok32, stage, xs, pj, mx, idx, lim_r, lim_c, count):
    step = pl.program_id(0)
    wins = tok.shape[0] // WTOK
    width = tok.shape[1]
    groups = width // 128

    @pl.when(step == 0)
    def _():
        count[0] = list_windows(sides, narrow_ref[0], wins, idx.shape[0], idx, lim_r, lim_c)
        spread(tok, stage, tok32)
        xs[...] = jnp.zeros_like(xs)
        pj[...] = jnp.zeros_like(pj)
        mx[...] = jnp.zeros_like(mx)
        stat_out[...] = jnp.zeros_like(stat_out)

    @pl.when(step * CW < count[0])
    def _():
        first = step * CW
        for i in range(CW):
            xs[WTOK * i : WTOK * i + KR, :] = tok32[idx[first + i]]
        x = xs[:CR, :]
        x_out[0] = x.astype(bf16)
        valid = chunk_valid(rinfo, lim_r, lim_c, first)
        keep = rep(valid, groups)
        xhat, _ = norm_stats(x)
        low = (xhat * vec[0:1] + vec[1:2]).astype(bf16)
        pj[:CR, :width] = nn(low, wq[:, :width]) + vec[2:3]
        pj[:CR, width : 2 * width] = nn(low, wq[:, width : 2 * width])
        pj[:CR, 2 * width :] = nn(low, wq[:, 2 * width : 3 * width]) + vec[3:4]
        for i in range(CW):
            rows = slice(WTOK * i, WTOK * i + SLOT)
            qkv = pj[rows, :].astype(bf16)
            qkv_out[0, i] = qkv
            fill = jnp.where((kinfo[0] < lim_r[first + i]) & (kinfo[1] < lim_c[first + i]), 0.0, -10000.0 * LOG2E)
            fill = rep(fill, 2)
            for g in range(groups):
                q = qkv[:, 128 * g : 128 * g + 128]
                k = qkv[:KR, width + 128 * g : width + 128 * g + 128]
                v = qkv[:KR, 2 * width + 128 * g : 2 * width + 128 * g + 128]
                q_bd = jnp.concatenate([q] * HG, 0) * hmask[...]
                s = nt(k, q_bd) * (32 ** (-0.5) * LOG2E) + bias[g] + fill
                e = jnp.exp2(s - jnp.max(s, 0, keepdims=True))
                prob = e / jnp.sum(e, 0, keepdims=True)
                prob_out[0, i, g] = prob
                wide_mix = tn(prob.astype(bf16), v)
                hm = hmask[...].astype(f32)
                o = wide_mix * hm
                o = o[:SLOT] + o[SLOT : 2 * SLOT] + o[2 * SLOT : 3 * SLOT] + o[3 * SLOT :]
                mx[WTOK * i : WTOK * i + KR, 128 * g : 128 * g + 128] = o[:KR]
        mixed = mx[:CR, :].astype(bf16)
        mixed_out[0] = mixed
        branch = (nn(mixed, wq[:, 3 * width :]) + vec[4:5]) * keep
        stream_out[0] = x + branch
        stat_out[0] += fold_rows(x * x * keep)
        stat_out[1] += fold_rows(branch * branch)
        stat_out[2, :, :128] += fold_rows(valid)


def mlp_both(narrow_ref, sides, tok, cot, w1, w2, wo, vec, hidden_bias, rinfo, mixed_in, stream_in,
             out_ref, grad_stream_out, grad_mixed_out, dmlp, dwo, dbias, dvec, stat_out,
             dw1, dw2, out32, cot32, stage, cs, gm, idx, lim_r, lim_c, count):
    step = pl.program_id(0)
    wins = tok.shape[0] // WTOK
    width = tok.shape[1]
    groups = width // 128
    hidden = w1.shape[0]
    tile = 384

    @pl.when(step == 0)
    def _():
        count[0] = list_windows(sides, narrow_ref[0], wins, idx.shape[0], idx, lim_r, lim_c)
        spread(tok, stage, out32)
        spread(cot, stage, cot32)
        cs[...] = jnp.zeros_like(cs)
        gm[...] = jnp.zeros_like(gm)
        for ref in (dw1, dw2, dwo, dbias, dvec, stat_out):
            ref[...] = jnp.zeros_like(ref)

    @pl.when(step * CW < count[0])
    def _():
        first = step * CW
        for i in range(CW):
            cs[WTOK * i : WTOK * i + KR, :] = cot32[idx[first + i]]
        cotan = cs[:CR, :]
        keep = rep(chunk_valid(rinfo, lim_r, lim_c, first), groups)
        stream = stream_in[0]
        xhat, inverse = norm_stats(stream)
        second = (xhat * vec[5:6] + vec[6:7]).astype(bf16)
        kept_cot = cotan * keep
        grad_low = kept_cot.astype(bf16)
        mlp_out = jnp.zeros((CR, width), f32)
        grad_second = jnp.zeros((CR, width), f32)
        for t in range(hidden // tile):
            cols = slice(tile * t, tile * t + tile)
            pre = nt(second, w1[cols, :]) + hidden_bias[0:1, cols]
            inner = 0.7978845608028654 * (pre + 0.044715 * (pre * pre * pre))
            th = jnp.tanh(inner)
            active = (0.5 * pre * (1.0 + th)).astype(bf16)
            slope = 0.5 * (1.0 + th) + (0.5 * pre) * (1.0 - th * th) * (
                0.7978845608028654 * (1.0 + 3 * 0.044715 * (pre * pre)))
            grad_pre32 = nt(grad_low, w2[cols, :]) * slope
            grad_pre = grad_pre32.astype(bf16)
            mlp_out += nn(active, w2[cols, :])
            grad_second += nn(grad_pre, w1[cols, :])
            dw1[:, cols] += tn(second, grad_pre)
            dw2[:, cols] += tn(grad_low, active)
            dbias[:, cols] += fold_rows(grad_pre.astype(f32))
        branch = (mlp_out + vec[7:8]) * keep
        result = stream + branch
        stat_out[...] += fold_rows(branch * branch)
        grad_stream = cotan + norm_grad(grad_second, xhat, inverse, vec[5:6])
        grad_stream_out[0] = grad_stream
        dvec[0] += fold_rows(grad_second * xhat)
        dvec[1] += fold_rows(grad_second)
        dvec[2] += fold_rows(kept_cot)
        grad_attn = grad_stream * keep
        dvec[3] += fold_rows(grad_attn)
        grad_attn_low = grad_attn.astype(bf16)
        dwo[...] += tn(mixed_in[0], grad_attn_low)
        gm[:CR, :] = nt(grad_attn_low, wo[...])
        cs[:CR, :] = result
        for i in range(CW):
            rows = slice(WTOK * i, WTOK * i + SLOT)
            grad_mixed_out[0, i] = gm[rows, :].astype(bf16)

            @pl.when(first + i < count[0])
            def _():
                out32[idx[first + i], :WTOK, :] = cs[WTOK * i : WTOK * i + WTOK, :]

    @pl.when(step == pl.num_programs(0) - 1)
    def _():
        gather_back(out32, stage, out_ref)
        parts, twice, _ = dmlp.shape
        share = twice // 2
        for j, ref in enumerate((dw1, dw2)):
            for t in range(hidden // tile):
                turned = ref[:, tile * t : tile * t + tile].T
                for piece in range(tile // share):
                    n = (tile * t) // share + piece
                    dmlp[n, share * j : share * j + share, :] = turned[share * piece : share * piece + share, :]


def attn_backward(narrow_ref, sides, cot, wq, vec, hmask, hot, dvec2, dhid, stat0, stat1, x_in, qkv_in, prob_in, grad_mixed_in, grad_stream_in,
                  input_grad, dwq, misc,
                  dbias, dvec, dtable, flat, ig32, stage, dp, gs, idx, lim_r, lim_c, count):
    step = pl.program_id(0)
    wins = cot.shape[0] // WTOK
    width = cot.shape[1]
    groups = width // 128

    @pl.when(step == 0)
    def _():
        count[0] = list_windows(sides, narrow_ref[0], wins, idx.shape[0], idx, lim_r, lim_c)
        spread(cot, stage, ig32)
        dp[...] = jnp.zeros_like(dp)
        for ref in (dwq, dbias, dvec, dtable):
            ref[...] = jnp.zeros_like(ref)

    @pl.when(step * CW < count[0])
    def _():
        first = step * CW
        for i in range(CW):
            rows = slice(WTOK * i, WTOK * i + KR)
            for g in range(groups):
                q = qkv_in[0, i, :, 128 * g : 128 * g + 128]
                k = qkv_in[0, i, :KR, width + 128 * g : width + 128 * g + 128]
                v = qkv_in[0, i, :KR, 2 * width + 128 * g : 2 * width + 128 * g + 128]
                do = grad_mixed_in[0, i, :, 128 * g : 128 * g + 128]
                q_bd = jnp.concatenate([q] * HG, 0) * hmask[...]
                do_bd = jnp.concatenate([do] * HG, 0) * hmask[...]
                prob = prob_in[0, i, g]
                gp = nt(v, do_bd)
                ds = prob * (gp - jnp.sum(gp * prob, 0, keepdims=True))
                dtable[g] += ds
                raw = (ds * 32 ** (-0.5)).astype(bf16)
                hm = hmask[...].astype(f32)
                o = tn(raw, k) * hm
                dq = o[:SLOT] + o[SLOT : 2 * SLOT] + o[2 * SLOT : 3 * SLOT] + o[3 * SLOT :]
                dp[rows, 128 * g : 128 * g + 128] = dq[:KR]
                dp[rows, width + 128 * g : width + 128 * g + 128] = nn(raw, q_bd)
                dp[rows, 2 * width + 128 * g : 2 * width + 128 * g + 128] = nn(prob.astype(bf16), do_bd)
        dproj = dp[:CR, :].astype(bf16)
        x = x_in[0].astype(f32)
        xhat, inverse = norm_stats(x)
        low = (xhat * vec[0:1] + vec[1:2]).astype(bf16)
        for j in range(3):
            cols = slice(width * j, width * j + width)
            dwq[j] += tn(low, dproj[:, cols])
        dbias[0] += fold_rows(dproj[:, :width].astype(f32))
        dbias[1] += fold_rows(dproj[:, 2 * width :].astype(f32))
        grad_normed = nt(dproj, wq[:, : 3 * width])
        dvec[0] += fold_rows(grad_normed * xhat)
        dvec[1] += fold_rows(grad_normed)
        gs[:CR, :] = grad_stream_in[0] + norm_grad(grad_normed, xhat, inverse, vec[0:1])
        for i in range(CW):
            @pl.when(first + i < count[0])
            def _():
                ig32[idx[first + i], :WTOK, :] = gs[WTOK * i : WTOK * i + WTOK, :]

    @pl.when(step == pl.num_programs(0) - 1)
    def _():
        gather_back(ig32, stage, input_grad)
        rows = [dvec[0], dvec[1], dbias[0], dbias[1], dvec2[3], dvec2[0], dvec2[1], dvec2[2]]
        for i, part in enumerate(rows):
            misc[i : i + 1, :] = jnp.sum(part, 0, keepdims=True)
        hid = jnp.sum(dhid[...], 0, keepdims=True)
        for i in range(hid.shape[1] // width):
            misc[8 + i : 9 + i, :] = hid[:, width * i : width * i + width]
        lane = lax.broadcasted_iota(jnp.int32, (1, width), 1)
        line = jnp.zeros((1, width), f32)
        for i, part in enumerate((stat0[0], stat0[1], stat1[...])):
            line = jnp.where(lane == i, jnp.sum(part), line)
        misc[12:13, :] = jnp.where(lane == 3, jnp.sum(stat0[2]) / 128.0, line)
        misc[13:16, :] = jnp.zeros((3, width), f32)
        flat[...] = jnp.zeros_like(flat)
        for g in range(groups):
            for k in range(WTOK):
                line = dtable[g, k : k + 1, :]
                for h in range(HG):
                    flat[HG * g + h : HG * g + h + 1, SLOT * k : SLOT * k + SLOT] = line[:, SLOT * h : SLOT * h + SLOT]
        rest = flat[...]
        misc[16:32, :] = jnp.zeros((16, width), f32)
        total = jnp.zeros((16, 256), f32)
        for _ in range(3):
            part = rest.astype(bf16)
            total += nn(part, hot[...])
            rest = rest - part.astype(f32)
        misc[16:32, :256] = total


def whole(a):
    nd = len(a.shape)
    return pl.BlockSpec(a.shape, lambda *_: (0,) * nd)


def per_chunk(shape):
    nd = len(shape)
    return pl.BlockSpec((1,) + tuple(shape[1:]), lambda c, *_: (c,) + (0,) * (nd - 1))


def sds(shape, dt):
    return jax.ShapeDtypeStruct(shape, dt)


def call(body, scalars, wholes, chunked, out_wholes, out_chunked, order_out, scratch, steps, cost):
    in_specs = [whole(a) for a in wholes] + [per_chunk(a.shape) for a in chunked]
    outs = [sds(s, d) for _, s, d in order_out]
    out_specs = [whole(sds(s, d)) if kind == "w" else per_chunk(s) for kind, s, d in order_out]
    slots = steps * CW
    return pl.pallas_call(
        body,
        grid_spec=pltpu.PrefetchScalarGridSpec(
            num_scalar_prefetch=len(scalars),
            grid=(steps,),
            in_specs=in_specs,
            out_specs=out_specs,
            scratch_shapes=list(scratch) + [
                pltpu.SMEM((slots + 1,), jnp.int32),
                pltpu.SMEM((slots + 1,), f32),
                pltpu.SMEM((slots + 1,), f32),
                pltpu.SMEM((1,), jnp.int32),
            ],
        ),
        out_shape=outs,
        compiler_params=pltpu.CompilerParams(vmem_limit_bytes=60 * 1024 * 1024, dimension_semantics=("arbitrary",)),
        cost_estimate=pl.CostEstimate(flops=cost, bytes_accessed=20000000, transcendentals=0),
    )(*scalars, *wholes, *chunked)


def loop_rows(total, body):
    size = next(n for n in (96, 64, 48, 32, 16) if total % n == 0)
    lax.fori_loop(0, total // size, lambda i, c: (body(pl.multiple_of(i * size, size), size), c)[1], 0)


def reduce_all(wide_n, narrow_n, share, m_ref, q_ref, o_ref, s_ref, gm_out, gt_out, s_out,
               send0, recv0, accm, acct, zsend, zrecv, gm, gt, sbuf, srecv, szrecv, *rest):
    send_sem, recv_sem = rest[-2:]
    bufs = rest[:-2]
    me_w = lax.axis_index("wide")
    me_n = lax.axis_index("narrow")
    width = accm.shape[2]
    n_bits = wide_n.bit_length() - 1
    bit = [lax.rem(me_w // (1 << b), 2) for b in range(n_bits)]
    mate = [me_w + (1 - 2 * bit[b]) * (1 << b) for b in range(n_bits)]
    peer = [lax.rem(me_n + s, narrow_n) for s in range(1, narrow_n)]
    sems = [0]

    def copy(src, dst, dev):
        k = sems[0]
        sems[0] += 1
        return pltpu.make_async_remote_copy(src_ref=src, dst_ref=dst, send_sem=send_sem.at[k], recv_sem=recv_sem.at[k],
                                            device_id=dev, device_id_type=pl.DeviceIdType.MESH)

    def at_wide(b):
        return (mate[b], me_n)

    barrier = pltpu.get_barrier_semaphore()
    for b in range(n_bits):
        pl.semaphore_signal(barrier, inc=1, device_id=at_wide(b), device_id_type=pl.DeviceIdType.MESH)
    for n in peer:
        pl.semaphore_signal(barrier, inc=1, device_id=(me_w, n), device_id_type=pl.DeviceIdType.MESH)
    pl.semaphore_wait(barrier, n_bits + narrow_n - 1)

    hm, ht = accm.shape[1], acct.shape[1]

    def attn_rows(n, start, size):
        flat = n * share
        if flat < q_ref.shape[0]:
            return q_ref[pl.ds(flat + start, size), :]
        return o_ref[pl.ds(flat - q_ref.shape[0] + start, size), :]

    away_m, away_t = (1 - bit[0]) * hm, (1 - bit[0]) * ht
    keep_m, keep_t = bit[0] * hm, bit[0] * ht
    sbuf[0] = s_ref[...]
    first = [copy(sbuf.at[0], srecv.at[0], at_wide(0))]
    first[0].start()
    for n in range(narrow_n):
        def pack_m(i, size):
            send0[n, pl.ds(i, size), :] = m_ref[n, pl.ds(pl.multiple_of(away_m + i, 16), size), :]
        def pack_t(i, size):
            send0[n, pl.ds(hm + i, size), :] = attn_rows(n, pl.multiple_of(away_t + i, 16), size)
        loop_rows(hm, pack_m)
        loop_rows(ht, pack_t)
        c = copy(send0.at[n], recv0.at[n], at_wide(0))
        c.start()
        first.append(c)
    first[0].wait()
    sbuf[1] = sbuf[0] + srecv[0]
    for n in range(narrow_n):
        first[n + 1].wait()
        def add_m(i, size):
            accm[n, pl.ds(i, size), :] = m_ref[n, pl.ds(pl.multiple_of(keep_m + i, 16), size), :] + recv0[n, pl.ds(i, size), :]
        def add_t(i, size):
            acct[n, pl.ds(i, size), :] = attn_rows(n, pl.multiple_of(keep_t + i, 16), size) + recv0[n, pl.ds(hm + i, size), :]
        loop_rows(hm, add_m)
        loop_rows(ht, add_t)

    streams, plan = plan_streams(n_bits, hm, ht)
    place = {st: streams[st][0] for st in streams}
    steps = n_bits - 1
    at = 0
    trail = []
    for s in range(steps):
        copies = []
        c = copy(sbuf.at[1 + s], srecv.at[1 + s], at_wide(plan["A"][s]))
        c.start()
        copies.append((None, None, None, None, None, None, c))
        for st in streams:
            start, size0, acc_name, name = streams[st]
            acc = accm if acc_name == "m" else acct
            b = plan[name][s]
            rows = plan[st][s]
            halves = plan[st][s + 1] < rows
            size = plan[st][s + 1]
            send, recv = bufs[2 * at], bufs[2 * at + 1]
            at += 1
            here = place[st]
            if halves:
                out_at, in_at = here + (1 - bit[b]) * size, here + bit[b] * size
            else:
                out_at, in_at = here, here
            for n in range(narrow_n):
                def pack(i, k):
                    send[n, pl.ds(i, k), :] = acc[n, pl.ds(pl.multiple_of(out_at + i, 16), k), :].astype(bf16)
                loop_rows(size, pack)
            c = copy(send, recv, at_wide(b))
            c.start()
            copies.append((acc, send, recv, in_at, size, halves, c))
            trail.append((st, s, b, in_at, size, halves))
            place[st] = in_at
        for acc, send, recv, in_at, size, halves, c in copies:
            c.wait()
            if acc is None:
                sbuf[2 + s] = sbuf[1 + s] + srecv[1 + s]
                continue
            for n in range(narrow_n):
                def add(i, k):
                    here = pl.ds(pl.multiple_of(in_at + i, 16), k)
                    mine = acc[n, here, :] if halves else send[n, pl.ds(i, k), :].astype(f32)
                    acc[n, here, :] = mine + recv[n, pl.ds(i, k), :].astype(f32)
                loop_rows(size, add)

    base = {}
    total = 0
    for st in streams:
        base[st] = total
        total += plan[st][steps]
    copies = []
    for i, n in enumerate(peer):
        c = copy(sbuf.at[n_bits], szrecv.at[i], (me_w, n))
        c.start()
        copies.append(c)
    for i, n in enumerate(peer):
        for st in streams:
            acc = accm if streams[st][2] == "m" else acct
            def pack(r, k):
                zsend[i, pl.ds(base[st] + r, k), :] = acc[n, pl.ds(pl.multiple_of(place[st] + r, 16), k), :].astype(bf16)
            loop_rows(plan[st][steps], pack)
        c = copy(zsend.at[i], zrecv.at[i], (me_w, n))
        c.start()
        copies.append(c)
    for c in copies:
        c.wait()
    for st in streams:
        is_m = streams[st][2] == "m"
        acc = accm if is_m else acct
        top = (keep_m if is_m else keep_t) + place[st]
        def add(r, k):
            value = acc[me_n, pl.ds(pl.multiple_of(place[st] + r, 16), k), :]
            for i in range(narrow_n - 1):
                value = value + zrecv[i, pl.ds(base[st] + r, k), :].astype(f32)
            if is_m:
                gm[pl.ds(pl.multiple_of(top + r, 16), k), :] = value.astype(bf16)
            else:
                gt[me_n, pl.ds(pl.multiple_of(top + r, 16), k), :] = value.astype(bf16)
        loop_rows(plan[st][steps], add)

    copies = []
    for st in streams:
        if streams[st][2] == "t":
            where = pl.ds(pl.multiple_of(keep_t + place[st], 16), plan[st][steps])
            for n in peer:
                c = copy(gt.at[me_n, where, :], gt.at[me_n, where, :], (me_w, n))
                c.start()
                copies.append(c)
    szero = sbuf[n_bits]
    total_s = jnp.zeros_like(szero)
    for n in range(narrow_n):
        behind = lax.rem(me_n + narrow_n - n, narrow_n)
        value = szero
        for i in range(1, narrow_n):
            value = jnp.where(behind == i, szrecv[i - 1], value)
        total_s = total_s + value
    s_out[...] = total_s
    pending = copies
    for s in reversed(range(steps)):
        for c in pending:
            c.wait()
        pending = []
        for st, s2, b, in_at, size, halves in trail:
            if s2 != s or not halves:
                continue
            is_m = streams[st][2] == "m"
            where = pl.ds(pl.multiple_of((keep_m if is_m else keep_t) + in_at, 16), size)
            if is_m:
                c = copy(gm.at[where, :], gm.at[where, :], at_wide(b))
            else:
                c = copy(gt.at[:, where, :], gt.at[:, where, :], at_wide(b))
            c.start()
            pending.append(c)
    for c in pending:
        c.wait()
    wm, wt = pl.ds(pl.multiple_of(keep_m, 16), hm), pl.ds(pl.multiple_of(keep_t, 16), ht)
    last = [copy(gm.at[wm, :], gm.at[wm, :], at_wide(0)), copy(gt.at[:, wt, :], gt.at[:, wt, :], at_wide(0))]
    for c in last:
        c.start()
    for c in last:
        c.wait()
    gm_out[...] = gm[...]
    gt_out[...] = gt[...]


def plan_streams(n_bits, hm, ht):
    rest = list(range(1, n_bits))
    half = len(rest) // 2
    plan = {"A": rest, "B": rest[half:] + rest[:half]}
    cut_m, cut_t = hm // 2, ht * 2 // 3
    streams = {"mA": (0, cut_m, "m", "A"), "mB": (cut_m, hm - cut_m, "m", "B"),
               "tA": (0, cut_t, "t", "A"), "tB": (cut_t, ht - cut_t, "t", "B")}
    for st, (_, size, _, _) in streams.items():
        sizes = [size]
        for _ in rest:
            sizes.append(sizes[-1] // 2 if sizes[-1] % 32 == 0 else sizes[-1])
        plan[st] = sizes
    return streams, plan


def reduce_call(wide_n, narrow_n, dmlp, dq, do, misc):
    parts, twice, width = dmlp.shape
    share = twice // 2
    hm, ht = share, share // 2
    n_bits = wide_n.bit_length() - 1
    streams, plan = plan_streams(n_bits, hm, ht)
    scratch = [
        pltpu.VMEM((narrow_n, hm + ht, width), f32), pltpu.VMEM((narrow_n, hm + ht, width), f32),
        pltpu.VMEM((narrow_n, hm, width), f32), pltpu.VMEM((narrow_n, ht, width), f32)]
    last = sum(plan[st][-1] for st in streams)
    scratch += [pltpu.VMEM((narrow_n - 1, last, width), bf16)] * 2
    scratch += [pltpu.VMEM((twice, width), bf16), pltpu.VMEM((narrow_n, share, width), bf16)]
    scratch += [pltpu.VMEM((n_bits + 1,) + misc.shape, f32), pltpu.VMEM((n_bits,) + misc.shape, f32),
                pltpu.VMEM((narrow_n - 1,) + misc.shape, f32)]
    for s in range(n_bits - 1):
        for st in streams:
            scratch += [pltpu.VMEM((narrow_n, plan[st][s + 1], width), bf16)] * 2
    copies = 1 + narrow_n + (n_bits - 1) * 5 + 2 * (narrow_n - 1) + 2 * (narrow_n - 1) + (n_bits - 1) * 4 + 2
    scratch += [pltpu.SemaphoreType.DMA((copies,)), pltpu.SemaphoreType.DMA((copies,))]
    vmem = pl.BlockSpec(memory_space=pltpu.VMEM)
    return pl.pallas_call(
        functools.partial(reduce_all, wide_n, narrow_n, share),
        out_shape=[sds((twice, width), bf16), sds((narrow_n, share, width), bf16), sds(misc.shape, f32)],
        in_specs=[vmem] * 4, out_specs=[vmem] * 3, scratch_shapes=scratch,
        compiler_params=pltpu.CompilerParams(collective_id=0, has_side_effects=True, vmem_limit_bytes=60 * 1024 * 1024),
    )(dmlp, dq, do, misc)


def adam_kernel(narrow_ref, gt, gm, misc, aw, af, as_, mw, mf, ms, tw, tf, ts, vw, vf, vs, bw, bf, bs,
                rms, an, al, afn, asn, mn, ml, mfn, msn, tn_, tfn, tsn, vn, vfn, vsn, bn, bfn, bsn):
    def put(new, w, g, m, v, rate, decay, low=None):
        out = adam_step(w, g, m, v, rate, decay)
        for ref, value in zip(new, out):
            ref[...] = value.reshape(ref.shape)
        if low is not None:
            low[...] = out[0].astype(bf16).reshape(low.shape)

    put((an, afn, asn), aw[...], gt[0].astype(f32), af[...], as_[...], 0.02, 0.05, al)
    put((mn, mfn, msn), mw[0], gm[0].astype(f32), mf[0], ms[0], 0.02, 0.05, ml)

    @pl.when(pl.program_id(0) == 0)
    def _():
        put((vn, vfn, vsn), vw[...], misc[0:8, :], vf[...], vs[...], 0.3, 0.0)
        stats = misc[12:13, :]
        for i in range(3):
            ratio = jnp.sqrt(stats[:, i : i + 1] / (stats[:, 3:4] * misc.shape[1]))
            rms[i] = ratio[0, 0]
        n = narrow_ref[0]
        share = bw.shape[1]
        grad = jnp.zeros((1, share), f32)
        per = misc.shape[1] // share
        for i in range(4):
            for k in range(per):
                grad = jnp.where(n == per * i + k, misc[8 + i : 9 + i, share * k : share * k + share], grad)
        put((bn, bfn, bsn), bw[...], grad, bf[...], bs[...], 0.1, 0.0)
        turned = jnp.concatenate([misc[16:32, :256], jnp.zeros((112, 256), f32)], 0).T
        count, heads = tw.shape
        put((tn_, tfn, tsn), tw[...], turned[:count, :heads], tf[...], ts[...], 0.3, 0.0)


def adam_call(narrow, gt, gm, misc, attn, mlp, table, vec, bias):
    width = gm.shape[1]
    share = mlp[0].shape[1]
    gt = gt.reshape(4, width, width)
    quarter = share // 2
    gm = gm.reshape(4, quarter, width)
    mlp = [a.reshape(4, quarter, width) for a in mlp]
    bias = [a.reshape(1, -1) for a in bias]
    col = pl.BlockSpec((width, width), lambda j, *_: (0, j))
    lead = lambda r: pl.BlockSpec((1, r, width), lambda j, *_: (j, 0, 0))
    smalls = list(table) + list(vec) + list(bias)
    args = [gt, gm, misc] + list(attn) + mlp + smalls
    in_specs = [lead(width), lead(quarter), whole(misc)] + [col] * 3 + [lead(quarter)] * 3 + [whole(a) for a in smalls]
    three = lambda a: [sds(a.shape, f32)] * 3
    outs = [sds((3,), f32), sds(attn[0].shape, f32), sds(attn[0].shape, bf16)] + [sds(attn[0].shape, f32)] * 2
    outs += [sds(mlp[0].shape, f32), sds(mlp[0].shape, bf16)] + [sds(mlp[0].shape, f32)] * 2
    outs += three(table[0]) + three(vec[0]) + three(bias[0])
    out_specs = [pl.BlockSpec(memory_space=pltpu.SMEM)] + [col] * 4 + [lead(quarter)] * 4
    out_specs += [whole(a) for a in smalls]
    r = pl.pallas_call(
        adam_kernel,
        grid_spec=pltpu.PrefetchScalarGridSpec(num_scalar_prefetch=1, grid=(4,), in_specs=in_specs, out_specs=out_specs),
        out_shape=outs,
        compiler_params=pltpu.CompilerParams(vmem_limit_bytes=60 * 1024 * 1024),
    )(narrow, *args)
    full = (2, share, width)
    return [r[0], *r[1:5], *r[9:12], *r[12:15], *[a.reshape(full) for a in r[5:9]], *[a.reshape(-1) for a in r[15:18]]]


def bias_layout(rel_table):
    pos = np.arange(WTOK)
    row, col = pos // WIN, pos % WIN
    off = (row[:, None] - row[None, :] + WIN - 1) * (2 * WIN - 1) + col[:, None] - col[None, :] + WIN - 1
    full = np.full((KR, SLOT), -1, np.int32)
    full[:WTOK, :WTOK] = off.T
    return full


def expand_bias(rel_table):
    full = bias_layout(rel_table)
    heads = rel_table.shape[1]
    hot = (jnp.asarray(full)[:, :, None] == jnp.arange(rel_table.shape[0])).astype(f32)
    b = jnp.einsum("kqt,th->khq", hot, rel_table * LOG2E, precision=highest)
    b = b.reshape(KR, heads // HG, HG * SLOT).transpose(1, 0, 2)
    dead = (np.arange(KR) >= WTOK)[None, :, None]
    return jnp.where(dead, -1e30, b), hot


def block(tokens, grid_sizes, cotangent, attn_weight, rel_table, vectors, w1, w2, mlp_bias, narrow, parts):
    rows, width = tokens.shape
    wins = rows // WTOK
    heads = rel_table.shape[1]
    groups = heads // HG
    steps = -(-wins // CW)
    weight_low = attn_weight.astype(bf16)
    bias, hot = expand_bias(rel_table)
    rinfo = jnp.asarray(row_info())
    kinfo = jnp.asarray(key_info())
    hmask = jnp.asarray(head_mask(width // heads), bf16)
    slots32 = pltpu.VMEM((wins + 1, KR, width), f32)
    stage = pltpu.VMEM((IMG_W * WTOK, width), f32)
    scal = (narrow.reshape(1).astype(jnp.int32), grid_sizes)
    x, qkv, prob, mixed, stream, stat0 = call(
        attn_forward, scal, (tokens, weight_low, vectors, bias, rinfo, kinfo, hmask), (), None, None,
        [("c", (steps, CR, width), bf16), ("c", (steps, CW, SLOT, 3 * width), bf16),
         ("c", (steps, CW, groups, KR, HG * SLOT), f32), ("c", (steps, CR, width), bf16),
         ("c", (steps, CR, width), f32), ("w", (3, 8, width), f32)],
        [slots32, stage, pltpu.VMEM((CR + 16, width), f32),
         pltpu.VMEM((CR + 16, 3 * width), f32), pltpu.VMEM((CR + 16, width), f32)],
        steps, 8 * rows * width * width)
    outputs, grad_stream, grad_mixed, dmlp, dwo, dhid, dvec2, stat1 = call(
        mlp_both, scal, (tokens, cotangent, w1, w2, weight_low[:, 3 * width :], vectors, mlp_bias.reshape(1, -1), rinfo),
        (mixed, stream), None, None,
        [("w", (rows, width), bf16), ("c", (steps, CR, width), f32), ("c", (steps, CW, SLOT, width), bf16),
         ("w", (parts, 2 * w1.shape[0] // parts, width), f32), ("w", (width, width), f32),
         ("w", (8, w1.shape[0]), f32), ("w", (4, 8, width), f32), ("w", (8, width), f32)],
        [pltpu.VMEM((width, w1.shape[0]), f32), pltpu.VMEM((width, w1.shape[0]), f32), slots32, slots32, stage,
         pltpu.VMEM((CR + 16, width), f32), pltpu.VMEM((CR + 16, width), f32)],
        steps, 52 * rows * width * width)
    hot2 = np.zeros((KR * SLOT, 256), np.float32)
    lay = bias_layout(rel_table).reshape(-1)
    hot2[np.arange(KR * SLOT)[lay >= 0], lay[lay >= 0]] = 1.0
    input_grad, dwq, misc = call(
        attn_backward, scal, (cotangent, weight_low, vectors, hmask, jnp.asarray(hot2, bf16), dvec2, dhid, stat0, stat1),
        (x, qkv, prob, grad_mixed, grad_stream), None, None,
        [("w", (rows, width), f32), ("w", (3, width, width), f32), ("w", (32, width), f32)],
        [pltpu.VMEM((2, 8, width), f32), pltpu.VMEM((2, 8, width), f32), pltpu.VMEM((groups, KR, HG * SLOT), f32),
         pltpu.VMEM((16, KR * SLOT), f32),
         slots32, stage, pltpu.VMEM((CR + 16, 3 * width), f32), pltpu.VMEM((CR + 16, width), f32)],
        steps, 16 * rows * width * width)
    return outputs, input_grad, dmlp, dwq, dwo, misc


def adam_step(weight, gradient, first_old, second_old, rate_value, decay_value):
    first_new = beta_one * first_old + (1.0 - beta_one) * gradient
    second_new = beta_two * second_old + (1.0 - beta_two) * gradient * gradient
    fix_one = 1.0 - beta_one**STEP
    fix_two = 1.0 - beta_two**STEP
    update = rate_value * (first_new / fix_one) / (jnp.sqrt(second_new / fix_two) + adam_eps)
    return (weight - update - rate_value * decay_value * weight, first_new, second_new)


def shards(wide_n, narrow_n, tokens, grid_sizes, cotangent, attn_weight, attn_first, attn_second, rel_table, table_first,
           table_second, vectors, vector_first, vector_second, mlp_weight, mlp_first, mlp_second, mlp_bias, bias_first,
           bias_second):
    width = tokens.shape[1]
    hidden_low = lax.all_gather(mlp_weight.astype(bf16), "narrow", axis=1, tiled=True)
    hidden_bias = lax.all_gather(mlp_bias, "narrow", axis=0, tiled=True)
    narrow = lax.axis_index("narrow").reshape(1).astype(jnp.int32)
    outputs, input_grad, dmlp, dwq, dwo, misc = block(
        tokens, grid_sizes, cotangent, attn_weight, rel_table, vectors, hidden_low[0], hidden_low[1], hidden_bias,
        narrow, narrow_n)
    gm, gt, misc = reduce_call(wide_n, narrow_n, dmlp, dwq.reshape(3 * width, width), dwo, misc)
    new = adam_call(narrow, gt, gm, misc, (attn_weight, attn_first, attn_second), (mlp_weight, mlp_first, mlp_second),
                    (rel_table, table_first, table_second), (vectors, vector_first, vector_second),
                    (mlp_bias, bias_first, bias_second))
    return (outputs, input_grad, *new)


def solution(mesh):
    rows = P(("wide", "narrow"), None)
    split = P(None, "narrow", None)
    return jax.shard_map(
        functools.partial(shards, mesh.shape["wide"], mesh.shape["narrow"]), mesh=mesh,
        in_specs=(rows, P("wide"), rows) + (P(),) * 9 + (split,) * 3 + (P("narrow"),) * 3,
        out_specs=(rows, rows) + (P(),) * 11 + (split,) * 4 + (P("narrow"),) * 3,
        check_vma=False)
```

```python
import functools

import jax
import jax.numpy as jnp
import numpy as np
from jax import lax
from jax.sharding import PartitionSpec as P
from jax.experimental import pallas as pl
from jax.experimental.pallas import tpu as pltpu

WIN = 7
WTOK = 49
WPI = 16
IMG_W = 16
STEP = 5
CW = 16
CR = CW * WTOK
SLOT = 64
KR = 56
HG = 4
LOG2E = 1.4426950408889634

norm_eps = 1e-05
beta_one = 0.5
beta_two = 0.5
adam_eps = 1e-08
highest = lax.Precision.HIGHEST
f32 = jnp.float32
bf16 = jnp.bfloat16


def nn(a, b):
    return lax.dot_general(a, b, (((1,), (0,)), ((), ())), preferred_element_type=f32)


def nt(a, b):
    return lax.dot_general(a, b, (((1,), (1,)), ((), ())), preferred_element_type=f32)


def tn(a, b):
    return lax.dot_general(a, b, (((0,), (0,)), ((), ())), preferred_element_type=f32)


def row_info():
    r = np.arange(CR)
    win = r // WTOK
    p = r % WTOK
    info = np.stack([win, p // WIN, p % WIN]).astype(np.float32)
    info[1, win >= CW] = 1000.0
    return np.ascontiguousarray(np.broadcast_to(info[:, :, None], (3, CR, 128)))


def key_info():
    p = np.arange(KR)
    info = np.stack([p // WIN, p % WIN]).astype(np.float32)
    return np.ascontiguousarray(np.broadcast_to(info[:, :, None], (2, KR, 128)))


def head_mask(head_size):
    row = np.arange(HG * SLOT)
    lane = np.arange(HG * head_size)
    return (((row // SLOT)[:, None] == (lane // head_size)[None, :]) & ((row % SLOT) < WTOK)[:, None]).astype(np.float32)


def fold_rows(t):
    return jnp.sum(t.reshape(t.shape[0] // 8, 8, t.shape[1]), 0)


def rep(v, n):
    return jnp.concatenate([v] * n, 1)


def fill_sides(sides, info, side_s):
    win = info[0]
    value = jnp.zeros_like(win)
    for i in range(CW):
        value = jnp.where(win == float(i), sides[i].astype(f32), value)
    side_s[...] = value


def corner(narrow, step, steps):
    u = WPI - 1 - (narrow * steps + step)
    return (WIN * (u // 4)).astype(f32), (WIN * lax.rem(u, 4)).astype(f32)


def chunk_valid(info, side_s, top, left):
    side = side_s[...]
    return jnp.where((info[1] + top < side) & (info[2] + left < side), 1.0, 0.0)


def norm_stats(x):
    mean = jnp.mean(x, -1, keepdims=True)
    centred = x - mean
    inverse = lax.rsqrt(jnp.mean(centred * centred, -1, keepdims=True) + norm_eps)
    return centred * inverse, inverse


def norm_grad(g, xhat, inverse, gain):
    scaled = g * gain
    m1 = jnp.mean(scaled, -1, keepdims=True)
    m2 = jnp.mean(scaled * xhat, -1, keepdims=True)
    return inverse * (scaled - m1 - xhat * m2)


class Links:
    def __init__(self, wide_n, narrow_n, send_sem, recv_sem):
        self.w = lax.axis_index("wide")
        self.n = lax.axis_index("narrow")
        self.bits = wide_n.bit_length() - 1
        self.bit = [lax.rem(self.w // (1 << b), 2) for b in range(self.bits)]
        self.mate = [self.w + (1 - 2 * self.bit[b]) * (1 << b) for b in range(self.bits)]
        self.peer = [lax.rem(self.n + s, narrow_n) for s in range(1, narrow_n)]
        self.send_sem, self.recv_sem = send_sem, recv_sem
        self.used = 0

    def copy(self, src, dst, device):
        k = self.used
        self.used += 1
        return pltpu.make_async_remote_copy(
            src_ref=src, dst_ref=dst, send_sem=self.send_sem.at[k], recv_sem=self.recv_sem.at[k],
            device_id=device, device_id_type=pl.DeviceIdType.MESH)

    def along(self, b):
        return (self.mate[b], self.n)

    def over(self, n):
        return (self.w, n)

    def barrier(self):
        sem = pltpu.get_barrier_semaphore()
        for b in range(self.bits):
            pl.semaphore_signal(sem, inc=1, device_id=self.along(b), device_id_type=pl.DeviceIdType.MESH)
        for n in self.peer:
            pl.semaphore_signal(sem, inc=1, device_id=self.over(n), device_id_type=pl.DeviceIdType.MESH)
        pl.semaphore_wait(sem, self.bits + len(self.peer))


def gather_cuts(wide_n, rows):
    bits = list(range(min(3, wide_n.bit_length() - 1)))
    first = rows // 256 * 128
    return [(0, first, bits[1:] + bits[:1]), (first, rows - first, bits[1:][::-1] + bits[:1])]


def gather_plan(links, wide_n, own, tail_own, all_w, all_tail):
    narrow_n, rows, _ = all_w.shape
    streams = gather_cuts(wide_n, rows)
    stages = [[]]
    place, sizes = [], []
    for start, size, order in streams:
        piece = size >> len(order)
        off = 0
        for k, b in enumerate(order):
            off = off + links.bit[b] * (piece << k)
        place.append(start + off)
        sizes.append(piece)
    for n in links.peer:
        stages[0].append(links.copy(tail_own, all_tail.at[links.n], links.over(n)))
        for at, size in zip(place, sizes):
            here = pl.ds(pl.multiple_of(at, 16), size)
            stages[0].append(links.copy(own.at[here, :], all_w.at[links.n, here, :], links.over(n)))
    for k in range(len(streams[0][2])):
        stage = []
        for s, (start, size, order) in enumerate(streams):
            here = pl.ds(pl.multiple_of(place[s], 16), sizes[s])
            for n in links.peer:
                part = all_w.at[n, here, :]
                stage.append(links.copy(part, part, links.along(order[k])))
            place[s] = place[s] - links.bit[order[k]] * sizes[s]
            sizes[s] = sizes[s] * 2
        stages.append(stage)
    return stages


def run_stages(stages, step, steps):
    for k, stage in enumerate(stages):
        @pl.when(step == min(k, steps - 1))
        def _():
            if k:
                for c in stages[k - 1]:
                    c.wait()
            for c in stage:
                c.start()


def expand_table(table, hot, wide_t, flat, bias):
    count, heads = table.shape
    wide_t[...] = jnp.zeros_like(wide_t)
    wide_t[:count, :heads] = table[...] * LOG2E
    rest = wide_t[...].T[:16, :]
    total = jnp.zeros((16, hot.shape[0]), f32)
    for _ in range(3):
        part = rest.astype(bf16)
        total += nt(part, hot[...])
        rest = rest - part.astype(f32)
    flat[...] = total
    bias[...] = jnp.full(bias.shape, -1e30, f32)
    for g in range(heads // HG):
        for k in range(WTOK):
            for h in range(HG):
                bias[g, k : k + 1, SLOT * h : SLOT * h + SLOT] = flat[HG * g + h : HG * g + h + 1, SLOT * k : SLOT * k + SLOT]


def turn(t):
    t = jnp.concatenate([t[:, :128], t[:, 128:]], 0).T
    return jnp.concatenate([t[:SLOT], t[SLOT:]], 1)


def padded(t):
    return jnp.concatenate([t, jnp.zeros((SLOT - KR, t.shape[1]), f32)], 0)


def four(t, mask):
    return jnp.concatenate([t] * HG, 0) * mask


BATCH = 8


def attn_forward(wide_n, narrow_n, comm, narrow_ref, sides, tok, attn_w, mlp_w, mlp_b, vec, table, hot, rinfo, kinfo, hmask, hmask2,
                 qkv_s, prob_out, mixed_out, stream_out, stats, gw_out, tail_out,
                 wq, pj, mx, turn_s, bias, wide_t, flat, side_s, own, tail_own, gw, tails, *sems):
    step = pl.program_id(0)
    steps = pl.num_programs(0)
    static_steps = comm[1]
    width = tok.shape[1]
    groups = width // 128
    scale = 32 ** (-0.5)
    narrow = narrow_ref[0]
    share = mlp_w.shape[1]

    @pl.when(step == 0)
    def _():
        for j in range(2):
            own[share * j : share * j + share, :] = mlp_w[j].astype(bf16)
        tail_own[...] = jnp.zeros_like(tail_own)
        rest = mlp_b[...]
        for i in range(3):
            part = rest.astype(bf16).astype(f32)
            tail_own[i : i + 1, :share] = part
            rest = rest - part
        if comm[0]:
            gw[lax.axis_index("narrow")] = own[...]
            tails[lax.axis_index("narrow")] = tail_own[...]
        else:
            for n in range(narrow_n):
                gw[n] = own[...]
                tails[n] = tail_own[...]

    if comm[0]:
        links = Links(wide_n, narrow_n, *sems)

        @pl.when(step == 0)
        def _():
            links.barrier()

        stages = gather_plan(links, wide_n, own, tail_own, gw, tails)
        run_stages(stages, step, static_steps)

    @pl.when(step == 0)
    def _():
        wq[...] = attn_w[...].astype(bf16)
        fill_sides(sides, rinfo, side_s)
        expand_table(table, hot, wide_t, flat, bias)
        for ref in (pj, mx, stats):
            ref[...] = jnp.zeros_like(ref)

    top, left = corner(narrow, step, static_steps)
    x = tok[...].astype(f32)
    valid = chunk_valid(rinfo, side_s, top, left)
    keep = rep(valid, groups)
    xhat, _ = norm_stats(x)
    low = (xhat * vec[0:1] + vec[1:2]).astype(bf16)
    pj[:CR, :width] = nn(low, wq[:, :width]) + vec[2:3]
    pj[:CR, width : 2 * width] = nn(low, wq[:, width : 2 * width])
    pj[:CR, 2 * width :] = nn(low, wq[:, 2 * width : 3 * width]) + vec[3:4]
    for i in range(CW):
        qkv_s[i] = pj[WTOK * i : WTOK * i + SLOT, :].astype(bf16)

    def score(b, carry):
        for k in range(BATCH):
            i = b * BATCH + k
            for g in range(groups):
                q_bd = four(qkv_s[i, :, 128 * g : 128 * g + 128], hmask[...])
                prob_out[i, g] = nt(qkv_s[i, :KR, width + 128 * g : width + 128 * g + 128], q_bd)
        return carry

    def soft(b, carry):
        for k in range(BATCH):
            i = b * BATCH + k
            side = sides[i].astype(f32)
            fill = jnp.where((kinfo[0] < side - top) & (kinfo[1] < side - left), 0.0, -10000.0 * LOG2E)
            fill = rep(fill, 2)
            for g in range(groups):
                s = prob_out[i, g] * (scale * LOG2E) + bias[g] + fill
                e = jnp.exp2(s - jnp.max(s, 0, keepdims=True))
                prob = e * (1.0 / jnp.sum(e, 0, keepdims=True))
                prob_out[i, g] = prob
                turn_s[i, g] = turn(padded(prob).astype(bf16))
        return carry

    lax.fori_loop(0, CW // BATCH, score, 0)
    lax.fori_loop(0, CW // BATCH, soft, 0)
    for i in range(CW):
        for g in range(groups):
            v_bd = four(qkv_s[i, :, 2 * width + 128 * g : 2 * width + 128 * g + 128], hmask2[...])
            mx[WTOK * i : WTOK * i + SLOT, 128 * g : 128 * g + 128] = nn(turn_s[i, g], v_bd)
    mixed = mx[:CR, :].astype(bf16)
    mixed_out[...] = mixed
    branch = (nn(mixed, wq[:, 3 * width :]) + vec[4:5]) * keep
    stream_out[...] = x + branch
    stats[0] += fold_rows(x * x * keep)
    stats[1] += fold_rows(branch * branch)
    stats[2, :, :128] += fold_rows(valid)

    @pl.when(step == steps - 1)
    def _():
        if comm[0]:
            for c in stages[-1]:
                c.wait()
        gw_out[...] = gw[...]
        tail_out[...] = tails[...]


def feed_forward(tile, narrow_ref, sides, cot, mixed_in, stream_in, attn_w, gw, tails, vec, rinfo,
                 out_ref, grad_stream_out, gm_s, dmlp, dwo, dhid, dvec,
                 wo, w1, w2, hb, dw1, dw2, mx, side_s):
    step = pl.program_id(0)
    steps = pl.num_programs(0)
    width = cot.shape[1]
    groups = width // 128
    hidden = w1.shape[0]
    shards_n, twice, _ = gw.shape
    share = twice // 2

    @pl.when(step == 0)
    def _():
        wo[...] = attn_w[...].astype(bf16)
        for n in range(shards_n):
            w1[share * n : share * n + share, :] = gw[n, :share, :]
            w2[share * n : share * n + share, :] = gw[n, share:, :]
            three = tails[n]
            hb[:, share * n : share * n + share] = (three[0:1] + three[1:2] + three[2:3])[:, :share]
        fill_sides(sides, rinfo, side_s)
        for ref in (mx, dw1, dw2, dwo, dhid, dvec):
            ref[...] = jnp.zeros_like(ref)

    top, left = corner(narrow_ref[0], step, steps)
    keep = rep(chunk_valid(rinfo, side_s, top, left), groups)
    cotan = cot[...].astype(f32)
    stream = stream_in[...]
    xhat2, inverse2 = norm_stats(stream)
    second = (xhat2 * vec[5:6] + vec[6:7]).astype(bf16)
    kept_cot = cotan * keep
    grad_low = kept_cot.astype(bf16)
    second_t = jnp.concatenate([second.T, jnp.ones((16, CR), bf16)], 0)
    grad_t = grad_low.T
    mlp_out = jnp.zeros((CR, width), f32)
    grad_second = jnp.zeros((CR, width), f32)
    for t in range(hidden // tile):
        cols = slice(tile * t, tile * t + tile)
        pre = nt(second, w1[cols, :]) + hb[0:1, cols]
        square = pre * pre
        half = 0.5 * jnp.tanh(pre * (square * (0.7978845608028654 * 0.044715) + 0.7978845608028654)) + 0.5
        active = (pre * half).astype(bf16)
        slope = half + (pre * (half - half * half)) * (square * (6 * 0.7978845608028654 * 0.044715) + 2 * 0.7978845608028654)
        grad_pre = (nt(grad_low, w2[cols, :]) * slope).astype(bf16)
        mlp_out += nn(active, w2[cols, :])
        grad_second += nn(grad_pre, w1[cols, :])
        outer = nn(second_t, grad_pre)
        dw1[:, cols] += outer[:width]
        dhid[:, cols] += outer[width : width + 8]
        dw2[:, cols] += nn(grad_t, active)
    branch = (mlp_out + vec[7:8]) * keep
    out_ref[...] = (stream + branch).astype(bf16)
    dvec[4] += fold_rows(branch * branch)
    dvec[0] += fold_rows(grad_second * xhat2)
    dvec[1] += fold_rows(grad_second)
    dvec[2] += fold_rows(kept_cot)
    grad_stream = cotan + norm_grad(grad_second, xhat2, inverse2, vec[5:6])
    grad_stream_out[...] = grad_stream
    grad_attn = grad_stream * keep
    dvec[3] += fold_rows(grad_attn)
    grad_attn_low = grad_attn.astype(bf16)
    dwo[...] += nn(mixed_in[...].T, grad_attn_low)
    mx[:CR, :] = nt(grad_attn_low, wo[...])
    for i in range(CW):
        gm_s[i] = mx[WTOK * i : WTOK * i + SLOT, :].astype(bf16)

    @pl.when(step == steps - 1)
    def _():
        for j, ref in enumerate((dw1, dw2)):
            for t in range(hidden // width):
                turned = ref[:, width * t : width * t + width].T
                for k in range(width // share):
                    n = (width * t) // share + k
                    dmlp[n, share * j : share * j + share, :] = turned[share * k : share * k + share, :]


def scatter_sizes(wide_n, share):
    n_bits = wide_n.bit_length() - 1
    rest = list(range(1, n_bits))
    half = len(rest) // 2
    plan = {"A": rest, "B": rest[half:] + rest[:half]}
    cut = share // 2
    streams = {"A": (0, cut), "B": (cut, share - cut)}
    sizes = {}
    for st, (_, size) in streams.items():
        sizes[st] = [size]
        for _ in rest:
            sizes[st].append(sizes[st][-1] // 2 if sizes[st][-1] % 32 == 0 else sizes[st][-1])
    return plan, streams, sizes


def scatter_stages(links, wide_n, narrow_n, share, dmlp, mine_out, send0, recv0, acc, zsend, zrecv, bufs):
    plan, streams, sizes = scatter_sizes(wide_n, share)
    bit = links.bit
    keep0, away0 = bit[0] * share, (1 - bit[0]) * share
    stages = []

    def pack0():
        for n in range(narrow_n):
            def one(i, size):
                send0[n, pl.ds(i, size), :] = dmlp[n, pl.ds(pl.multiple_of(away0 + i, 16), size), :].astype(send0.dtype)
            loop_rows(share, one)

    def add0():
        for n in range(narrow_n):
            def one(i, size):
                acc[n, pl.ds(i, size), :] = (dmlp[n, pl.ds(pl.multiple_of(keep0 + i, 16), size), :]
                                             + recv0[n, pl.ds(i, size), :].astype(f32))
            loop_rows(share, one)

    stages.append((pack0, [links.copy(send0, recv0, links.along(0))], add0))
    place = {st: streams[st][0] for st in streams}
    trail = []
    for s in range(links.bits - 1):
        work = []
        for k, st in enumerate(streams):
            b = plan[st][s]
            size = sizes[st][s + 1]
            halves = size < sizes[st][s]
            send, recv = bufs[2 * (2 * s + k)], bufs[2 * (2 * s + k) + 1]
            here = place[st]
            out_at, in_at = (here + (1 - bit[b]) * size, here + bit[b] * size) if halves else (here, here)
            place[st] = in_at
            work.append((send, recv, out_at, in_at, size, halves, links.copy(send, recv, links.along(b))))
            trail.append((st, s, b, in_at, size, halves))

        def pack(work=work):
            for send, recv, out_at, in_at, size, halves, _ in work:
                for n in range(narrow_n):
                    def one(i, k):
                        send[n, pl.ds(i, k), :] = acc[n, pl.ds(pl.multiple_of(out_at + i, 16), k), :].astype(send.dtype)
                    loop_rows(size, one)

        def add(work=work):
            for send, recv, out_at, in_at, size, halves, _ in work:
                for n in range(narrow_n):
                    def one(i, k):
                        here = pl.ds(pl.multiple_of(in_at + i, 16), k)
                        mine = acc[n, here, :] if halves else send[n, pl.ds(i, k), :].astype(f32)
                        acc[n, here, :] = mine + recv[n, pl.ds(i, k), :].astype(f32)
                    loop_rows(size, one)

        stages.append((pack, [w[-1] for w in work], add))
    base, total = {}, 0
    for st in streams:
        base[st] = total
        total += sizes[st][-1]

    def packz():
        for i, n in enumerate(links.peer):
            for st in streams:
                def one(r, k):
                    zsend[i, pl.ds(base[st] + r, k), :] = acc[n, pl.ds(pl.multiple_of(place[st] + r, 16), k), :].astype(zsend.dtype)
                loop_rows(sizes[st][-1], one)

    def addz():
        for st in streams:
            def one(r, k):
                value = acc[links.n, pl.ds(pl.multiple_of(place[st] + r, 16), k), :]
                for i in range(narrow_n - 1):
                    value = value + zrecv[i, pl.ds(base[st] + r, k), :].astype(f32)
                mine_out[pl.ds(base[st] + r, k), :] = value.astype(bf16)
            loop_rows(sizes[st][-1], one)

    stages.append((packz, [links.copy(zsend.at[i], zrecv.at[i], links.over(n)) for i, n in enumerate(links.peer)], addz))
    return stages


def attn_backward(wide_n, narrow_n, comm, tok, qkv_s, prob_in, gm_s, grad_stream_in, attn_w, vec, hot, hmask, hmask2,
                  dmlp, dhid, dvec2, stats,
                  input_grad, dwq, misc, mine_out,
                  wq, pj, gp_s, low_s, turn_s, dext, dvec, dtable, flat, send0, recv0, acc, zsend, zrecv, *rest):
    step = pl.program_id(0)
    steps = pl.num_programs(0)
    static_steps = comm[1]
    width = tok.shape[1]
    groups = width // 128
    scale = 32 ** (-0.5)
    share = dmlp.shape[1] // 2

    if comm[0]:
        links = Links(wide_n, narrow_n, *rest[-2:])

        @pl.when(step == 0)
        def _():
            links.barrier()

        stages = scatter_stages(links, wide_n, narrow_n, share, dmlp, mine_out, send0, recv0, acc, zsend, zrecv, rest[:-2])
        for k, (pack, copies, add) in enumerate(stages):
            @pl.when(step == min(k, static_steps - 1))
            def _():
                if k:
                    for c in stages[k - 1][1]:
                        c.wait()
                    stages[k - 1][2]()
                pack()
                for c in copies:
                    c.start()

    @pl.when(step == 0)
    def _():
        wq[...] = attn_w[:, : 3 * width].astype(bf16)
        for ref in (dwq, dext, dvec, dtable):
            ref[...] = jnp.zeros_like(ref)

    def first(b, carry):
        for k in range(BATCH):
            i = b * BATCH + k
            for g in range(groups):
                do_bd = four(gm_s[i, :, 128 * g : 128 * g + 128], hmask[...])
                gp_s[i, g] = nt(qkv_s[i, :KR, 2 * width + 128 * g : 2 * width + 128 * g + 128], do_bd)
        return carry

    def second(b, carry):
        for g in range(groups):
            total = dtable[g]
            for k in range(BATCH):
                i = b * BATCH + k
                gp = gp_s[i, g]
                prob = prob_in[i, g]
                ds = prob * (gp - jnp.sum(gp * prob, 0, keepdims=True))
                total = total + ds
                raw = padded(ds * scale).astype(bf16)
                low_s[i, g] = raw
                turn_s[i, g] = turn(raw)
            dtable[g] = total
        return carry

    lax.fori_loop(0, CW // BATCH, first, 0)
    lax.fori_loop(0, CW // BATCH, second, 0)
    for i in range(CW):
        rows = slice(WTOK * i, WTOK * i + SLOT)
        for g in range(groups):
            q_bd = four(qkv_s[i, :, 128 * g : 128 * g + 128], hmask[...])
            k_bd = four(qkv_s[i, :, width + 128 * g : width + 128 * g + 128], hmask2[...])
            do_bd = four(gm_s[i, :, 128 * g : 128 * g + 128], hmask[...])
            pj[rows, 128 * g : 128 * g + 128] = nn(turn_s[i, g], k_bd)
            pj[rows, width + 128 * g : width + 128 * g + 128] = nn(low_s[i, g], q_bd)
            pj[rows, 2 * width + 128 * g : 2 * width + 128 * g + 128] = nn(padded(prob_in[i, g]).astype(bf16), do_bd)
    dproj = pj[:CR, :].astype(bf16)
    x = tok[...].astype(f32)
    xhat, inverse = norm_stats(x)
    low = (xhat * vec[0:1] + vec[1:2]).astype(bf16)
    low_t = jnp.concatenate([low.T, jnp.ones((16, CR), bf16)], 0)
    for j in range(3):
        outer = nn(low_t, dproj[:, width * j : width * j + width])
        dwq[j] += outer[:width]
        dext[j] += outer[width : width + 8]
    grad_normed = nt(dproj, wq[...])
    dvec[0] += fold_rows(grad_normed * xhat)
    dvec[1] += fold_rows(grad_normed)
    input_grad[...] = grad_stream_in[...] + norm_grad(grad_normed, xhat, inverse, vec[0:1])

    @pl.when(step == steps - 1)
    def _():
        rows = [dvec[0], dvec[1], None, None, dvec2[3], dvec2[0], dvec2[1], dvec2[2]]
        for i, part in enumerate(rows):
            if part is not None:
                misc[i : i + 1, :] = jnp.sum(part, 0, keepdims=True)
        misc[2:3, :] = dext[0, 0:1, :]
        misc[3:4, :] = dext[2, 0:1, :]
        for i in range(dhid.shape[1] // width):
            misc[8 + i : 9 + i, :] = dhid[0:1, width * i : width * i + width]
        lane = lax.broadcasted_iota(jnp.int32, (1, width), 1)
        line = jnp.zeros((1, width), f32)
        for i, part in enumerate((stats[0], stats[1], dvec2[4])):
            line = jnp.where(lane == i, jnp.sum(part), line)
        misc[12:13, :] = jnp.where(lane == 3, jnp.sum(stats[2]) / 128.0, line)
        misc[13:16, :] = jnp.zeros((3, width), f32)
        flat[...] = jnp.zeros_like(flat)
        for g in range(groups):
            for k in range(WTOK):
                line = dtable[g, k : k + 1, :]
                for h in range(HG):
                    flat[HG * g + h : HG * g + h + 1, SLOT * k : SLOT * k + SLOT] = line[:, SLOT * h : SLOT * h + SLOT]
        rest_f = flat[...]
        total = jnp.zeros((16, 256), f32)
        for _ in range(3):
            part = rest_f.astype(bf16)
            total += nn(part, hot[...])
            rest_f = rest_f - part.astype(f32)
        misc[16:32, :] = jnp.zeros((16, width), f32)
        misc[16:32, :256] = total
        if comm[0]:
            for c in stages[-1][1]:
                c.wait()
            stages[-1][2]()


def sds(shape, dt):
    return jax.ShapeDtypeStruct(shape, dt)


def whole(a):
    nd = len(a.shape)
    return pl.BlockSpec(a.shape, lambda *_: (0,) * nd, pipeline_mode=pl.Buffered(1))


def whole_out(a):
    nd = len(a.shape)
    return pl.BlockSpec(a.shape, lambda *_: (0,) * nd)


def by_step(a, steps):
    nd = len(a.shape)
    return pl.BlockSpec((a.shape[0] // steps,) + tuple(a.shape[1:]), lambda c: (c,) + (0,) * (nd - 1))


def run(body, steps, scalars, stepped, wholes, out_stepped, out_wholes, scratch, flops, collective_id=None):
    smem = pl.BlockSpec(memory_space=pltpu.SMEM)
    params = dict(vmem_limit_bytes=62 * 1024 * 1024)
    if collective_id is not None:
        params.update(collective_id=collective_id, has_side_effects=True)
    return pl.pallas_call(
        body, grid=(steps,),
        in_specs=[smem] * len(scalars) + [by_step(a, steps) for a in stepped] + wholes[1],
        out_specs=[by_step(a, steps) for a in out_stepped] + [whole_out(a) for a in out_wholes],
        out_shape=list(out_stepped) + list(out_wholes), scratch_shapes=scratch,
        compiler_params=pltpu.CompilerParams(**params),
        cost_estimate=pl.CostEstimate(flops=flops, bytes_accessed=20000000, transcendentals=0),
    )(*scalars, *stepped, *wholes[0])


def wholes_of(*arrays):
    return (arrays, [whole(a) for a in arrays])


def loop_rows(total, body):
    size = next(n for n in (96, 64, 48, 32, 16) if total % n == 0)
    lax.fori_loop(0, total // size, lambda i, c: (body(pl.multiple_of(i * size, size), size), c)[1], 0)


def reduce_all(wide_n, narrow_n, share, mine_ref, q_ref, o_ref, s_ref, gm_out, gt_out, s_out,
               send0, recv0, acct, zsend, zrecv, gm, gt, sbuf, srecv, szrecv, *rest):
    bufs = rest[:-2]
    links = Links(wide_n, narrow_n, *rest[-2:])
    bit, me_n, peer, n_bits = links.bit, links.n, links.peer, links.bits
    plan, m_streams, m_sizes = scatter_sizes(wide_n, share)
    links.barrier()
    ht = acct.shape[1]
    steps = n_bits - 1

    def attn_rows(n, start, size):
        flat = n * share
        if flat < q_ref.shape[0]:
            return q_ref[pl.ds(flat + start, size), :]
        return o_ref[pl.ds(flat - q_ref.shape[0] + start, size), :]

    m_trail = []
    m_place = {}
    for st, (start, _) in m_streams.items():
        here = start
        for s in range(steps):
            b = plan[st][s]
            size = m_sizes[st][s + 1]
            halves = size < m_sizes[st][s]
            here = here + bit[b] * size if halves else here
            m_trail.append((st, s, b, here, size, halves))
        m_place[st] = here
    base = 0
    for st in m_streams:
        size = m_sizes[st][-1]
        gm[pl.ds(pl.multiple_of(bit[0] * share + m_place[st], 16), size), :] = mine_ref[base : base + size, :]
        base += size
    m_back = []
    for s in reversed(range(steps)):
        stage = []
        for st, s2, b, at, size, halves in m_trail:
            if s2 == s and halves:
                part = gm.at[pl.ds(pl.multiple_of(bit[0] * share + at, 16), size), :]
                stage.append(links.copy(part, part, links.along(b)))
        m_back.append(stage)
    part = gm.at[pl.ds(pl.multiple_of(bit[0] * share, 16), share), :]
    m_back.append([links.copy(part, part, links.along(0))])
    m_back.append([])

    def back(k):
        if 0 < k <= len(m_back) - 1:
            for c in m_back[k - 1]:
                c.wait()
        if k < len(m_back):
            for c in m_back[k]:
                c.start()

    away_t, keep_t = (1 - bit[0]) * ht, bit[0] * ht
    sbuf[0] = s_ref[...]
    copies = [links.copy(sbuf.at[0], srecv.at[0], links.along(0))]
    copies[0].start()
    for n in range(narrow_n):
        def pack_t(i, size):
            send0[n, pl.ds(i, size), :] = attn_rows(n, pl.multiple_of(away_t + i, 16), size)
        loop_rows(ht, pack_t)
        c = links.copy(send0.at[n], recv0.at[n], links.along(0))
        c.start()
        copies.append(c)
    back(0)
    copies[0].wait()
    sbuf[1] = sbuf[0] + srecv[0]
    for n in range(narrow_n):
        copies[n + 1].wait()
        def add_t(i, size):
            acct[n, pl.ds(i, size), :] = attn_rows(n, pl.multiple_of(keep_t + i, 16), size) + recv0[n, pl.ds(i, size), :]
        loop_rows(ht, add_t)

    streams, sizes = t_streams(wide_n, ht)
    place = {st: streams[st][0] for st in streams}
    trail = []
    for s in range(steps):
        work = []
        small = links.copy(sbuf.at[1 + s], srecv.at[1 + s], links.along(plan["A"][s]))
        small.start()
        for k, st in enumerate(streams):
            b = plan[st][s]
            size = sizes[st][s + 1]
            halves = size < sizes[st][s]
            send, recv = bufs[2 * (2 * s + k)], bufs[2 * (2 * s + k) + 1]
            here = place[st]
            out_at, in_at = (here + (1 - bit[b]) * size, here + bit[b] * size) if halves else (here, here)
            for n in range(narrow_n):
                def pack(i, k2):
                    send[n, pl.ds(i, k2), :] = acct[n, pl.ds(pl.multiple_of(out_at + i, 16), k2), :].astype(send.dtype)
                loop_rows(size, pack)
            c = links.copy(send, recv, links.along(b))
            c.start()
            work.append((send, recv, in_at, size, halves, c))
            trail.append((st, s, b, in_at, size, halves))
            place[st] = in_at
        back(1 + s)
        small.wait()
        sbuf[2 + s] = sbuf[1 + s] + srecv[1 + s]
        for send, recv, in_at, size, halves, c in work:
            c.wait()
            for n in range(narrow_n):
                def add(i, k2):
                    here = pl.ds(pl.multiple_of(in_at + i, 16), k2)
                    mine = acct[n, here, :] if halves else send[n, pl.ds(i, k2), :].astype(f32)
                    acct[n, here, :] = mine + recv[n, pl.ds(i, k2), :].astype(f32)
                loop_rows(size, add)

    z_base, total = {}, 0
    for st in streams:
        z_base[st] = total
        total += sizes[st][-1]
    copies = []
    for i, n in enumerate(peer):
        c = links.copy(sbuf.at[n_bits], szrecv.at[i], links.over(n))
        c.start()
        copies.append(c)
    for i, n in enumerate(peer):
        for st in streams:
            def pack(r, k):
                zsend[i, pl.ds(z_base[st] + r, k), :] = acct[n, pl.ds(pl.multiple_of(place[st] + r, 16), k), :].astype(bf16)
            loop_rows(sizes[st][-1], pack)
        c = links.copy(zsend.at[i], zrecv.at[i], links.over(n))
        c.start()
        copies.append(c)
    for k in range(1 + steps, len(m_back)):
        back(k)
    for c in copies:
        c.wait()
    for st in streams:
        top = keep_t + place[st]
        def add(r, k):
            value = acct[me_n, pl.ds(pl.multiple_of(place[st] + r, 16), k), :]
            for i in range(narrow_n - 1):
                value = value + zrecv[i, pl.ds(z_base[st] + r, k), :].astype(f32)
            gt[me_n, pl.ds(pl.multiple_of(top + r, 16), k), :] = value.astype(bf16)
        loop_rows(sizes[st][-1], add)

    pending = []
    for st in streams:
        where = pl.ds(pl.multiple_of(keep_t + place[st], 16), sizes[st][-1])
        for n in peer:
            part = gt.at[me_n, where, :]
            c = links.copy(part, part, links.over(n))
            c.start()
            pending.append(c)
    zero = sbuf[n_bits]
    total_s = jnp.zeros_like(zero)
    for n in range(narrow_n):
        behind = lax.rem(me_n + narrow_n - n, narrow_n)
        value = zero
        for i in range(1, narrow_n):
            value = jnp.where(behind == i, szrecv[i - 1], value)
        total_s = total_s + value
    s_out[...] = total_s
    gm_out[...] = gm[...]
    for s in reversed(range(steps)):
        for c in pending:
            c.wait()
        pending = []
        for st, s2, b, at, size, halves in trail:
            if s2 == s and halves:
                part = gt.at[:, pl.ds(pl.multiple_of(keep_t + at, 16), size), :]
                c = links.copy(part, part, links.along(b))
                c.start()
                pending.append(c)
    for c in pending:
        c.wait()
    part = gt.at[:, pl.ds(pl.multiple_of(keep_t, 16), ht), :]
    c = links.copy(part, part, links.along(0))
    c.start()
    c.wait()
    gt_out[...] = gt[...]


def t_streams(wide_n, ht):
    rest = range(1, wide_n.bit_length() - 1)
    cut = ht * 2 // 3
    streams = {"A": (0, cut), "B": (cut, ht - cut)}
    sizes = {}
    for st, (_, size) in streams.items():
        sizes[st] = [size]
        for _ in rest:
            sizes[st].append(sizes[st][-1] // 2 if sizes[st][-1] % 32 == 0 else sizes[st][-1])
    return streams, sizes


def reduce_call(wide_n, narrow_n, share, mine, dq, do, misc):
    width = mine.shape[1]
    ht = share // 2
    n_bits = wide_n.bit_length() - 1
    streams, sizes = t_streams(wide_n, ht)
    last = sum(sizes[st][-1] for st in streams)
    scratch = [
        pltpu.VMEM((narrow_n, ht, width), f32), pltpu.VMEM((narrow_n, ht, width), f32), pltpu.VMEM((narrow_n, ht, width), f32),
        pltpu.VMEM((narrow_n - 1, last, width), bf16), pltpu.VMEM((narrow_n - 1, last, width), bf16),
        pltpu.VMEM((2 * share, width), bf16), pltpu.VMEM((narrow_n, share, width), bf16),
        pltpu.VMEM((n_bits + 1,) + misc.shape, f32), pltpu.VMEM((n_bits,) + misc.shape, f32),
        pltpu.VMEM((narrow_n - 1,) + misc.shape, f32)]
    for s in range(n_bits - 1):
        for st in streams:
            scratch += [pltpu.VMEM((narrow_n, sizes[st][s + 1], width), bf16)] * 2
    copies = 2 + narrow_n + 7 * n_bits + 4 * narrow_n
    scratch += [pltpu.SemaphoreType.DMA((copies,)), pltpu.SemaphoreType.DMA((copies,))]
    vmem = pl.BlockSpec(memory_space=pltpu.VMEM)
    return pl.pallas_call(
        functools.partial(reduce_all, wide_n, narrow_n, share),
        out_shape=[sds((2 * share, width), bf16), sds((narrow_n, share, width), bf16), sds(misc.shape, f32)],
        in_specs=[vmem] * 4, out_specs=[vmem] * 3, scratch_shapes=scratch,
        compiler_params=pltpu.CompilerParams(collective_id=0, has_side_effects=True, vmem_limit_bytes=60 * 1024 * 1024),
    )(mine, dq, do, misc)


def adam_kernel(narrow_ref, gt, gm, misc, aw, af, as_, mw, mf, ms, tw, tf, ts, vw, vf, vs, bw, bf, bs,
                rms, an, al, afn, asn, mn, ml, mfn, msn, tn_, tfn, tsn, vn, vfn, vsn, bn, bfn, bsn):
    def put(new, w, g, m, v, rate, decay, low=None):
        out = adam_step(w, g, m, v, rate, decay)
        for ref, value in zip(new, out):
            ref[...] = value.reshape(ref.shape)
        if low is not None:
            low[...] = out[0].astype(bf16).reshape(low.shape)

    put((an, afn, asn), aw[...], gt[0].astype(f32), af[...], as_[...], 0.02, 0.05, al)
    put((mn, mfn, msn), mw[0], gm[0].astype(f32), mf[0], ms[0], 0.02, 0.05, ml)

    @pl.when(pl.program_id(0) == 0)
    def _():
        put((vn, vfn, vsn), vw[...], misc[0:8, :], vf[...], vs[...], 0.3, 0.0)
        stats = misc[12:13, :]
        for i in range(3):
            ratio = jnp.sqrt(stats[:, i : i + 1] / (stats[:, 3:4] * misc.shape[1]))
            rms[i] = ratio[0, 0]
        n = narrow_ref[0]
        share = bw.shape[1]
        grad = jnp.zeros((1, share), f32)
        per = misc.shape[1] // share
        for i in range(4):
            for k in range(per):
                grad = jnp.where(n == per * i + k, misc[8 + i : 9 + i, share * k : share * k + share], grad)
        put((bn, bfn, bsn), bw[...], grad, bf[...], bs[...], 0.1, 0.0)
        turned = jnp.concatenate([misc[16:32, :256], jnp.zeros((112, 256), f32)], 0).T
        count, heads = tw.shape
        put((tn_, tfn, tsn), tw[...], turned[:count, :heads], tf[...], ts[...], 0.3, 0.0)


def adam_call(narrow, gt, gm, misc, attn, mlp, table, vec, bias):
    width = gm.shape[1]
    share = mlp[0].shape[1]
    gt = gt.reshape(4, width, width)
    quarter = share // 2
    gm = gm.reshape(4, quarter, width)
    mlp = [a.reshape(4, quarter, width) for a in mlp]
    bias = [a.reshape(1, -1) for a in bias]
    col = pl.BlockSpec((width, width), lambda j, *_: (0, j))
    lead = lambda r: pl.BlockSpec((1, r, width), lambda j, *_: (j, 0, 0))
    smalls = list(table) + list(vec) + list(bias)
    args = [gt, gm, misc] + list(attn) + mlp + smalls
    in_specs = [lead(width), lead(quarter), whole(misc)] + [col] * 3 + [lead(quarter)] * 3 + [whole(a) for a in smalls]
    three = lambda a: [sds(a.shape, f32)] * 3
    outs = [sds((3,), f32), sds(attn[0].shape, f32), sds(attn[0].shape, bf16)] + [sds(attn[0].shape, f32)] * 2
    outs += [sds(mlp[0].shape, f32), sds(mlp[0].shape, bf16)] + [sds(mlp[0].shape, f32)] * 2
    outs += three(table[0]) + three(vec[0]) + three(bias[0])
    out_specs = [pl.BlockSpec(memory_space=pltpu.SMEM)] + [col] * 4 + [lead(quarter)] * 4
    out_specs += [whole_out(a) for a in smalls]
    r = pl.pallas_call(
        adam_kernel,
        grid_spec=pltpu.PrefetchScalarGridSpec(num_scalar_prefetch=1, grid=(4,), in_specs=in_specs, out_specs=out_specs),
        out_shape=outs,
        compiler_params=pltpu.CompilerParams(vmem_limit_bytes=60 * 1024 * 1024),
    )(narrow, *args)
    full = (2, share, width)
    return [r[0], *r[1:5], *r[9:12], *r[12:15], *[a.reshape(full) for a in r[5:9]], *[a.reshape(-1) for a in r[15:18]]]


def bias_layout(rel_table):
    pos = np.arange(WTOK)
    row, col = pos // WIN, pos % WIN
    off = (row[:, None] - row[None, :] + WIN - 1) * (2 * WIN - 1) + col[:, None] - col[None, :] + WIN - 1
    full = np.full((KR, SLOT), -1, np.int32)
    full[:WTOK, :WTOK] = off.T
    return full


def block(tokens, grid_sizes, cotangent, attn_weight, rel_table, vectors, mlp_weight, mlp_bias, narrow, wide_n, narrow_n, linked=True):
    rows, width = tokens.shape
    wins = rows // WTOK
    steps = wins // CW
    heads = rel_table.shape[1]
    groups = heads // HG
    share = mlp_weight.shape[1]
    hidden = share * narrow_n
    n_bits = wide_n.bit_length() - 1
    comm = (linked, steps)
    unit = rows * width * width
    hot = np.zeros((KR * SLOT, 256), np.float32)
    lay = bias_layout(rel_table).reshape(-1)
    hot[np.arange(KR * SLOT)[lay >= 0], lay[lay >= 0]] = 1.0
    hot = jnp.asarray(hot, bf16)
    mask = head_mask(width // heads)
    mask2 = mask.reshape(HG, SLOT, -1)[np.array([0, 2, 1, 3])].reshape(mask.shape)
    mask, mask2 = jnp.asarray(mask, bf16), jnp.asarray(mask2, bf16)
    rinfo, kinfo = jnp.asarray(row_info()), jnp.asarray(key_info())
    scal = (narrow, grid_sizes)
    pad = CR + 16
    copies = 3 * (narrow_n - 1) + 3 * 2 * (narrow_n - 1) + 4
    sem = [pltpu.SemaphoreType.DMA((copies,)), pltpu.SemaphoreType.DMA((copies,))] if linked else []
    sides = pltpu.VMEM((CR, 128), f32)
    table_s = pltpu.VMEM((groups, KR, HG * SLOT), f32)
    flat = pltpu.VMEM((16, KR * SLOT), f32)
    turned = pltpu.VMEM((CW, groups, SLOT, HG * SLOT), bf16)
    qkv, prob, mixed, stream, stats, gw, tails = run(
        functools.partial(attn_forward, wide_n, narrow_n, comm), steps, scal, (tokens,),
        wholes_of(attn_weight, mlp_weight, mlp_bias.reshape(1, -1), vectors, rel_table, hot, rinfo, kinfo, mask, mask2),
        [sds((wins, SLOT, 3 * width), bf16), sds((wins, groups, KR, HG * SLOT), f32), sds((rows, width), bf16), sds((rows, width), f32)],
        [sds((3, 8, width), f32), sds((narrow_n, 2 * share, width), bf16), sds((narrow_n, 8, width), f32)],
        [pltpu.VMEM((width, 4 * width), bf16), pltpu.VMEM((pad, 3 * width), f32), pltpu.VMEM((pad, width), f32), turned,
         table_s, pltpu.VMEM((256, 128), f32), flat, sides,
         pltpu.VMEM((2 * share, width), bf16), pltpu.VMEM((8, width), f32),
         pltpu.VMEM((narrow_n, 2 * share, width), bf16), pltpu.VMEM((narrow_n, 8, width), f32)] + sem,
        12 * unit, 1 if linked else None)
    out_proj = pl.BlockSpec((width, width), lambda *_: (0, 3), pipeline_mode=pl.Buffered(1))
    fixed = (attn_weight, gw, tails, vectors, rinfo)
    outputs, grad_stream, gm, dmlp, dwo, dhid, dvec2 = run(
        functools.partial(feed_forward, TILE), steps, scal, (cotangent, mixed, stream),
        (fixed, [out_proj] + [whole(a) for a in fixed[1:]]),
        [sds((rows, width), bf16), sds((rows, width), f32), sds((wins, SLOT, width), bf16)],
        [sds((narrow_n, 2 * share, width), f32), sds((width, width), f32), sds((8, hidden), f32), sds((5, 8, width), f32)],
        [pltpu.VMEM((width, width), bf16), pltpu.VMEM((hidden, width), bf16), pltpu.VMEM((hidden, width), bf16),
         pltpu.VMEM((1, hidden), f32), pltpu.VMEM((width, hidden), f32), pltpu.VMEM((width, hidden), f32),
         pltpu.VMEM((pad, width), f32), sides],
        52 * unit)
    _, streams, sizes = scatter_sizes(wide_n, share)
    last = sum(sizes[st][-1] for st in streams)
    bufs = []
    for s in range(n_bits - 1):
        for st in streams:
            bufs += [pltpu.VMEM((narrow_n, sizes[st][s + 1], width), bf16)] * 2
    copies = 1 + 2 * n_bits + narrow_n
    sem = [pltpu.SemaphoreType.DMA((copies,)), pltpu.SemaphoreType.DMA((copies,))] if linked else []
    input_grad, dwq, misc, mine = run(
        functools.partial(attn_backward, wide_n, narrow_n, comm), steps, (), (tokens, qkv, prob, gm, grad_stream),
        wholes_of(attn_weight, vectors, hot, mask, mask2, dmlp, dhid, dvec2, stats),
        [sds((rows, width), f32)],
        [sds((3, width, width), f32), sds((32, width), f32), sds((last, width), bf16)],
        [pltpu.VMEM((width, 3 * width), bf16), pltpu.VMEM((pad, 3 * width), f32),
         pltpu.VMEM((CW, groups, KR, HG * SLOT), f32), turned, turned, pltpu.VMEM((3, 8, width), f32),
         pltpu.VMEM((2, 8, width), f32), table_s, flat,
         pltpu.VMEM((narrow_n, share, width), bf16), pltpu.VMEM((narrow_n, share, width), bf16),
         pltpu.VMEM((narrow_n, share, width), f32), pltpu.VMEM((narrow_n - 1, last, width), bf16),
         pltpu.VMEM((narrow_n - 1, last, width), bf16)] + bufs + sem,
        20 * unit, 2 if linked else None)
    return outputs, input_grad, dmlp, dwq, dwo, misc, mine


TILE = 768


def adam_step(weight, gradient, first_old, second_old, rate_value, decay_value):
    first_new = beta_one * first_old + (1.0 - beta_one) * gradient
    second_new = beta_two * second_old + (1.0 - beta_two) * gradient * gradient
    fix_one = 1.0 - beta_one**STEP
    fix_two = 1.0 - beta_two**STEP
    update = rate_value * (first_new / fix_one) / (jnp.sqrt(second_new / fix_two) + adam_eps)
    return (weight - update - rate_value * decay_value * weight, first_new, second_new)


def shards(wide_n, narrow_n, tokens, grid_sizes, cotangent, attn_weight, attn_first, attn_second, rel_table, table_first,
           table_second, vectors, vector_first, vector_second, mlp_weight, mlp_first, mlp_second, mlp_bias, bias_first,
           bias_second):
    width = tokens.shape[1]
    narrow = lax.axis_index("narrow").reshape(1).astype(jnp.int32)
    outputs, input_grad, _, dwq, dwo, misc, mine = block(
        tokens, grid_sizes, cotangent, attn_weight, rel_table, vectors, mlp_weight, mlp_bias, narrow, wide_n, narrow_n)
    gm, gt, misc = reduce_call(wide_n, narrow_n, mlp_weight.shape[1], mine, dwq.reshape(3 * width, width), dwo, misc)
    new = adam_call(narrow, gt, gm, misc, (attn_weight, attn_first, attn_second), (mlp_weight, mlp_first, mlp_second),
                    (rel_table, table_first, table_second), (vectors, vector_first, vector_second),
                    (mlp_bias, bias_first, bias_second))
    return (outputs, input_grad, *new)


def solution(mesh):
    rows = P(("wide", "narrow"), None)
    split = P(None, "narrow", None)
    return jax.shard_map(
        functools.partial(shards, mesh.shape["wide"], mesh.shape["narrow"]), mesh=mesh,
        in_specs=(rows, P("wide"), rows) + (P(),) * 9 + (split,) * 3 + (P("narrow"),) * 3,
        out_specs=(rows, rows) + (P(),) * 11 + (split,) * 4 + (P("narrow"),) * 3,
        check_vma=False)
```

```python
import functools

import jax
import jax.numpy as jnp
import numpy as np
from jax import lax
from jax.sharding import PartitionSpec as P
from jax.experimental import pallas as pl
from jax.experimental.pallas import tpu as pltpu

WIN = 7
WTOK = 49
WPI = 16
IMG_W = 16
STEP = 5
CW = 16
CR = CW * WTOK
SLOT = 64
KR = 56
HG = 4
LOG2E = 1.4426950408889634

norm_eps = 1e-05
beta_one = 0.5
beta_two = 0.5
adam_eps = 1e-08
highest = lax.Precision.HIGHEST
f32 = jnp.float32
bf16 = jnp.bfloat16


def nn(a, b):
    return lax.dot_general(a, b, (((1,), (0,)), ((), ())), preferred_element_type=f32)


def nt(a, b):
    return lax.dot_general(a, b, (((1,), (1,)), ((), ())), preferred_element_type=f32)


def tn(a, b):
    return lax.dot_general(a, b, (((0,), (0,)), ((), ())), preferred_element_type=f32)


def row_info():
    r = np.arange(CR)
    win = r // WTOK
    p = r % WTOK
    info = np.stack([win, p // WIN, p % WIN]).astype(np.float32)
    info[1, win >= CW] = 1000.0
    return np.ascontiguousarray(np.broadcast_to(info[:, :, None], (3, CR, 128)))


def key_info():
    p = np.arange(KR)
    info = np.stack([p // WIN, p % WIN]).astype(np.float32)
    return np.ascontiguousarray(np.broadcast_to(info[:, :, None], (2, KR, 128)))


def head_mask(head_size):
    row = np.arange(HG * SLOT)
    lane = np.arange(HG * head_size)
    return (((row // SLOT)[:, None] == (lane // head_size)[None, :]) & ((row % SLOT) < WTOK)[:, None]).astype(np.float32)


def fold_rows(t):
    return jnp.sum(t.reshape(t.shape[0] // 8, 8, t.shape[1]), 0)


def rep(v, n):
    return jnp.concatenate([v] * n, 1)


def fill_sides(sides, info, side_s):
    win = info[0]
    value = jnp.zeros_like(win)
    for i in range(CW):
        value = jnp.where(win == float(i), sides[i].astype(f32), value)
    side_s[...] = value


def corner(narrow, step, steps):
    u = WPI - 1 - (narrow * steps + step)
    return (WIN * (u // 4)).astype(f32), (WIN * lax.rem(u, 4)).astype(f32)


def chunk_valid(info, side_s, top, left):
    side = side_s[...]
    return jnp.where((info[1] + top < side) & (info[2] + left < side), 1.0, 0.0)


def norm_stats(x):
    mean = jnp.mean(x, -1, keepdims=True)
    centred = x - mean
    inverse = lax.rsqrt(jnp.mean(centred * centred, -1, keepdims=True) + norm_eps)
    return centred * inverse, inverse


def norm_grad(g, xhat, inverse, gain):
    scaled = g * gain
    m1 = jnp.mean(scaled, -1, keepdims=True)
    m2 = jnp.mean(scaled * xhat, -1, keepdims=True)
    return inverse * (scaled - m1 - xhat * m2)


class Links:
    def __init__(self, wide_n, narrow_n, send_sem, recv_sem):
        self.w = lax.axis_index("wide")
        self.n = lax.axis_index("narrow")
        self.bits = wide_n.bit_length() - 1
        self.bit = [lax.rem(self.w // (1 << b), 2) for b in range(self.bits)]
        self.mate = [self.w + (1 - 2 * self.bit[b]) * (1 << b) for b in range(self.bits)]
        self.peer = [lax.rem(self.n + s, narrow_n) for s in range(1, narrow_n)]
        self.send_sem, self.recv_sem = send_sem, recv_sem
        self.used = 0
        self.all = []

    def copy(self, src, dst, device):
        k = self.used
        self.used += 1
        c = pltpu.make_async_remote_copy(
            src_ref=src, dst_ref=dst, send_sem=self.send_sem.at[k], recv_sem=self.recv_sem.at[k],
            device_id=device, device_id_type=pl.DeviceIdType.MESH)
        self.all.append(c)
        return c

    def along(self, b):
        return (self.mate[b], self.n)

    def over(self, n):
        return (self.w, n)

    def barrier(self):
        sem = pltpu.get_barrier_semaphore()
        for b in range(self.bits):
            pl.semaphore_signal(sem, inc=1, device_id=self.along(b), device_id_type=pl.DeviceIdType.MESH)
        for n in self.peer:
            pl.semaphore_signal(sem, inc=1, device_id=self.over(n), device_id_type=pl.DeviceIdType.MESH)
        pl.semaphore_wait(sem, self.bits + len(self.peer))


def gather_cuts(wide_n, rows):
    bits = list(range(min(3, wide_n.bit_length() - 1)))
    first = rows // 256 * 128
    return [(0, first, bits[1:] + bits[:1]), (first, rows - first, bits[1:][::-1] + bits[:1])]


def gather_plan(links, wide_n, own, tail_own, all_w, all_tail):
    narrow_n, rows, _ = all_w.shape
    streams = gather_cuts(wide_n, rows)
    stages = [[]]
    place, sizes = [], []
    for start, size, order in streams:
        piece = size >> len(order)
        off = 0
        for k, b in enumerate(order):
            off = off + links.bit[b] * (piece << k)
        place.append(start + off)
        sizes.append(piece)
    for n in links.peer:
        stages[0].append(links.copy(tail_own, all_tail.at[links.n], links.over(n)))
        for at, size in zip(place, sizes):
            here = pl.ds(pl.multiple_of(at, 16), size)
            stages[0].append(links.copy(own.at[here, :], all_w.at[links.n, here, :], links.over(n)))
    for k in range(len(streams[0][2])):
        stage = []
        for s, (start, size, order) in enumerate(streams):
            here = pl.ds(pl.multiple_of(place[s], 16), sizes[s])
            for n in links.peer:
                part = all_w.at[n, here, :]
                stage.append(links.copy(part, part, links.along(order[k])))
            place[s] = place[s] - links.bit[order[k]] * sizes[s]
            sizes[s] = sizes[s] * 2
        stages.append(stage)
    return stages


def run_stages(stages, step, steps):
    for k, stage in enumerate(stages):
        @pl.when(step == min(k, steps - 1))
        def _():
            if k:
                for c in stages[k - 1]:
                    c.wait()
            for c in stage:
                c.start()


def expand_table(table, hot, wide_t, flat, bias):
    heads, count = table.shape
    wide_t[...] = jnp.zeros_like(wide_t)
    wide_t[:heads, :count] = table[...] * LOG2E
    rest = wide_t[...]
    total = jnp.zeros((16, hot.shape[0]), f32)
    for _ in range(3):
        part = rest.astype(bf16)
        total += nt(part, hot[...])
        rest = rest - part.astype(f32)
    flat[...] = total
    bias[...] = jnp.full(bias.shape, -1e30, f32)
    for g in range(heads // HG):
        for k in range(WTOK):
            for h in range(HG):
                bias[g, k : k + 1, SLOT * h : SLOT * h + SLOT] = flat[HG * g + h : HG * g + h + 1, SLOT * k : SLOT * k + SLOT]


def turn(t):
    t = jnp.concatenate([t[:, :128], t[:, 128:]], 0).T
    return jnp.concatenate([t[:SLOT], t[SLOT:]], 1)


def padded(t):
    return jnp.concatenate([t, jnp.zeros((SLOT - KR, t.shape[1]), f32)], 0)


def four(t, mask):
    return jnp.concatenate([t] * HG, 0) * mask


BATCH = 16


def attn_forward(wide_n, narrow_n, comm, narrow_ref, sides, tok, attn_w, mlp_w, mlp_b, vec, table, hot, rinfo, kinfo, hmask, hmask2,
                 qkv_s, prob_out, mixed_out, stream_out, stats, gw_out, tail_out,
                 wq, pj, mx, turn_s, bias, wide_t, flat, side_s, own, tail_own, gw, tails, *sems):
    step = pl.program_id(0)
    steps = pl.num_programs(0)
    static_steps = comm[1]
    width = tok.shape[1]
    groups = width // 128
    scale = 32 ** (-0.5)
    narrow = narrow_ref[0]
    share = mlp_w.shape[1]

    @pl.when(step == 0)
    def _():
        for j in range(2):
            own[share * j : share * j + share, :] = mlp_w[j].astype(bf16)
        tail_own[...] = jnp.zeros_like(tail_own)
        rest = mlp_b[...].reshape(1, share)
        for i in range(3):
            part = rest.astype(bf16).astype(f32)
            tail_own[i : i + 1, :share] = part
            rest = rest - part
        if comm[0]:
            gw[lax.axis_index("narrow")] = own[...]
            tails[lax.axis_index("narrow")] = tail_own[...]
        else:
            for n in range(narrow_n):
                gw[n] = own[...]
                tails[n] = tail_own[...]

    if comm[0]:
        links = Links(wide_n, narrow_n, *sems)

        @pl.when(step == 0)
        def _():
            links.barrier()

        stages = gather_plan(links, wide_n, own, tail_own, gw, tails)
        run_stages(stages, step, static_steps)

    @pl.when(step == 0)
    def _():
        wq[...] = attn_w[...].astype(bf16)
        fill_sides(sides, rinfo, side_s)
        expand_table(table, hot, wide_t, flat, bias)
        for ref in (pj, mx, stats):
            ref[...] = jnp.zeros_like(ref)

    top, left = corner(narrow, step, static_steps)
    x = tok[...].astype(f32)
    valid = chunk_valid(rinfo, side_s, top, left)
    keep = rep(valid, groups)
    xhat, _ = norm_stats(x)
    low = (xhat * vec[0:1] + vec[1:2]).astype(bf16)
    pj[:CR, :width] = nn(low, wq[:, :width]) + vec[2:3]
    pj[:CR, width : 2 * width] = nn(low, wq[:, width : 2 * width])
    pj[:CR, 2 * width :] = nn(low, wq[:, 2 * width : 3 * width]) + vec[3:4]
    for i in range(CW):
        qkv_s[i] = pj[WTOK * i : WTOK * i + SLOT, :].astype(bf16)

    def score(b, carry):
        for k in range(BATCH):
            i = b * BATCH + k
            for g in range(groups):
                q_bd = four(qkv_s[i, :, 128 * g : 128 * g + 128], hmask[...])
                prob_out[i, g] = nt(qkv_s[i, :KR, width + 128 * g : width + 128 * g + 128], q_bd)
        return carry

    def soft(b, carry):
        for k in range(BATCH):
            i = b * BATCH + k
            side = sides[i].astype(f32)
            fill = jnp.where((kinfo[0] < side - top) & (kinfo[1] < side - left), 0.0, -10000.0 * LOG2E)
            fill = rep(fill, 2)
            for g in range(groups):
                s = prob_out[i, g] * (scale * LOG2E) + bias[g] + fill
                e = jnp.exp2(s - jnp.max(s, 0, keepdims=True))
                prob = e * (1.0 / jnp.sum(e, 0, keepdims=True))
                prob_out[i, g] = prob
                turn_s[i, g] = turn(padded(prob).astype(bf16))
        return carry

    lax.fori_loop(0, CW // BATCH, score, 0)
    lax.fori_loop(0, CW // BATCH, soft, 0)
    for i in range(CW):
        for g in range(groups):
            v_bd = four(qkv_s[i, :, 2 * width + 128 * g : 2 * width + 128 * g + 128], hmask2[...])
            mx[WTOK * i : WTOK * i + SLOT, 128 * g : 128 * g + 128] = nn(turn_s[i, g], v_bd)
    mixed = mx[:CR, :].astype(bf16)
    mixed_out[...] = mixed
    branch = (nn(mixed, wq[:, 3 * width :]) + vec[4:5]) * keep
    stream_out[...] = x + branch
    stats[0] += fold_rows(x * x * keep)
    stats[1] += fold_rows(branch * branch)
    stats[2, :, :128] += fold_rows(valid)

    @pl.when(step == steps - 1)
    def _():
        if comm[0]:
            for c in stages[-1]:
                c.wait()
        gw_out[...] = gw[...]
        tail_out[...] = tails[...]


def feed_forward(tile, narrow_ref, sides, cot, mixed_in, stream_in, attn_w, gw, tails, vec, rinfo,
                 out_ref, grad_stream_out, gm_s, dmlp, dwo, dhid, dvec,
                 wo, w1, w2, hb, dw1, dw2, mx, side_s):
    step = pl.program_id(0)
    steps = pl.num_programs(0)
    width = cot.shape[1]
    groups = width // 128
    hidden = w1.shape[0]
    shards_n, twice, _ = gw.shape
    share = twice // 2

    @pl.when(step == 0)
    def _():
        wo[...] = attn_w[...].astype(bf16)
        for n in range(shards_n):
            w1[share * n : share * n + share, :] = gw[n, :share, :]
            w2[share * n : share * n + share, :] = gw[n, share:, :]
            three = tails[n]
            hb[:, share * n : share * n + share] = (three[0:1] + three[1:2] + three[2:3])[:, :share]
        fill_sides(sides, rinfo, side_s)
        for ref in (mx, dw1, dw2, dwo, dhid, dvec):
            ref[...] = jnp.zeros_like(ref)

    top, left = corner(narrow_ref[0], step, steps)
    keep = rep(chunk_valid(rinfo, side_s, top, left), groups)
    cotan = cot[...].astype(f32)
    stream = stream_in[...]
    xhat2, inverse2 = norm_stats(stream)
    second = (xhat2 * vec[5:6] + vec[6:7]).astype(bf16)
    kept_cot = cotan * keep
    grad_low = kept_cot.astype(bf16)
    second_t = jnp.concatenate([second.T, jnp.ones((16, CR), bf16)], 0)
    grad_t = grad_low.T
    mlp_out = jnp.zeros((CR, width), f32)
    grad_second = jnp.zeros((CR, width), f32)
    for t in range(hidden // tile):
        cols = slice(tile * t, tile * t + tile)
        pre = nt(second, w1[cols, :]) + hb[0:1, cols]
        square = pre * pre
        half = 0.5 * jnp.tanh(pre * (square * (0.7978845608028654 * 0.044715) + 0.7978845608028654)) + 0.5
        active = (pre * half).astype(bf16)
        slope = half + (pre * (half - half * half)) * (square * (6 * 0.7978845608028654 * 0.044715) + 2 * 0.7978845608028654)
        grad_pre = (nt(grad_low, w2[cols, :]) * slope).astype(bf16)
        mlp_out += nn(active, w2[cols, :])
        grad_second += nn(grad_pre, w1[cols, :])
        outer = nn(second_t, grad_pre)
        dw1[:, cols] += outer[:width]
        dhid[:, cols] += outer[width : width + 8]
        dw2[:, cols] += nn(grad_t, active)
    branch = (mlp_out + vec[7:8]) * keep
    out_ref[...] = (stream + branch).astype(bf16)
    dvec[4] += fold_rows(branch * branch)
    dvec[0] += fold_rows(grad_second * xhat2)
    dvec[1] += fold_rows(grad_second)
    dvec[2] += fold_rows(kept_cot)
    grad_stream = cotan + norm_grad(grad_second, xhat2, inverse2, vec[5:6])
    grad_stream_out[...] = grad_stream
    grad_attn = grad_stream * keep
    dvec[3] += fold_rows(grad_attn)
    grad_attn_low = grad_attn.astype(bf16)
    dwo[...] += nn(mixed_in[...].T, grad_attn_low)
    mx[:CR, :] = nt(grad_attn_low, wo[...])
    for i in range(CW):
        gm_s[i] = mx[WTOK * i : WTOK * i + SLOT, :].astype(bf16)

    @pl.when(step == steps - 1)
    def _():
        for j, ref in enumerate((dw1, dw2)):
            for t in range(hidden // width):
                turned = ref[:, width * t : width * t + width].T
                for k in range(width // share):
                    n = (width * t) // share + k
                    dmlp[n, share * j : share * j + share, :] = turned[share * k : share * k + share, :]


def scatter_sizes(wide_n, share):
    n_bits = wide_n.bit_length() - 1
    rest = list(range(1, n_bits))
    half = len(rest) // 2
    plan = {"A": rest, "B": rest[half:] + rest[:half]}
    cut = share // 2
    streams = {"A": (0, cut), "B": (cut, share - cut)}
    sizes = {}
    for st, (_, size) in streams.items():
        sizes[st] = [size]
        for _ in rest:
            sizes[st].append(sizes[st][-1] // 2 if sizes[st][-1] % 32 == 0 else sizes[st][-1])
    return plan, streams, sizes


def scatter_stages(links, wide_n, narrow_n, share, dmlp, mine_out, send0, recv0, acc, zsend, zrecv, bufs):
    plan, streams, sizes = scatter_sizes(wide_n, share)
    bit = links.bit
    keep0, away0 = bit[0] * share, (1 - bit[0]) * share
    stages = []

    def pack0():
        for n in range(narrow_n):
            def one(i, size):
                send0[n, pl.ds(i, size), :] = dmlp[n, pl.ds(pl.multiple_of(away0 + i, 16), size), :].astype(send0.dtype)
            loop_rows(share, one)

    def add0():
        for n in range(narrow_n):
            def one(i, size):
                acc[n, pl.ds(i, size), :] = (dmlp[n, pl.ds(pl.multiple_of(keep0 + i, 16), size), :]
                                             + recv0[n, pl.ds(i, size), :].astype(f32))
            loop_rows(share, one)

    stages.append((pack0, [links.copy(send0, recv0, links.along(0))], add0))
    place = {st: streams[st][0] for st in streams}
    trail = []
    for s in range(links.bits - 1):
        work = []
        for k, st in enumerate(streams):
            b = plan[st][s]
            size = sizes[st][s + 1]
            halves = size < sizes[st][s]
            send, recv = bufs[2 * (2 * s + k)], bufs[2 * (2 * s + k) + 1]
            here = place[st]
            out_at, in_at = (here + (1 - bit[b]) * size, here + bit[b] * size) if halves else (here, here)
            place[st] = in_at
            work.append((send, recv, out_at, in_at, size, halves, links.copy(send, recv, links.along(b))))
            trail.append((st, s, b, in_at, size, halves))

        def pack(work=work):
            for send, recv, out_at, in_at, size, halves, _ in work:
                for n in range(narrow_n):
                    def one(i, k):
                        send[n, pl.ds(i, k), :] = acc[n, pl.ds(pl.multiple_of(out_at + i, 16), k), :].astype(send.dtype)
                    loop_rows(size, one)

        def add(work=work):
            for send, recv, out_at, in_at, size, halves, _ in work:
                for n in range(narrow_n):
                    def one(i, k):
                        here = pl.ds(pl.multiple_of(in_at + i, 16), k)
                        mine = acc[n, here, :] if halves else send[n, pl.ds(i, k), :].astype(f32)
                        acc[n, here, :] = mine + recv[n, pl.ds(i, k), :].astype(f32)
                    loop_rows(size, one)

        stages.append((pack, [w[-1] for w in work], add))
    base, total = {}, 0
    for st in streams:
        base[st] = total
        total += sizes[st][-1]

    def packz():
        for i, n in enumerate(links.peer):
            for st in streams:
                def one(r, k):
                    zsend[i, pl.ds(base[st] + r, k), :] = acc[n, pl.ds(pl.multiple_of(place[st] + r, 16), k), :].astype(zsend.dtype)
                loop_rows(sizes[st][-1], one)

    def addz():
        for st in streams:
            def one(r, k):
                value = acc[links.n, pl.ds(pl.multiple_of(place[st] + r, 16), k), :]
                for i in range(narrow_n - 1):
                    value = value + zrecv[i, pl.ds(base[st] + r, k), :].astype(f32)
                mine_out[pl.ds(base[st] + r, k), :] = value.astype(bf16)
            loop_rows(sizes[st][-1], one)

    stages.append((packz, [links.copy(zsend.at[i], zrecv.at[i], links.over(n)) for i, n in enumerate(links.peer)], addz))
    return stages


def attn_backward(wide_n, narrow_n, comm, tok, qkv_s, prob_in, gm_s, grad_stream_in, attn_w, vec, hot, hmask, hmask2,
                  dmlp, dhid, dvec2, stats,
                  input_grad, dwq, misc, mine_out,
                  wq, pj, gp_s, low_s, turn_s, dext, dvec, dtable, flat, send0, recv0, acc, zsend, zrecv, *rest):
    step = pl.program_id(0)
    steps = pl.num_programs(0)
    static_steps = comm[1]
    width = tok.shape[1]
    groups = width // 128
    scale = 32 ** (-0.5)
    share = dmlp.shape[1] // 2

    if comm[0]:
        links = Links(wide_n, narrow_n, *rest[-2:])

        @pl.when(step == 0)
        def _():
            links.barrier()

        stages = scatter_stages(links, wide_n, narrow_n, share, dmlp, mine_out, send0, recv0, acc, zsend, zrecv, rest[:-2])
        for k, (pack, copies, add) in enumerate(stages):
            @pl.when(step == min(k, static_steps - 1))
            def _():
                if k:
                    for c in stages[k - 1][1]:
                        c.wait()
                    stages[k - 1][2]()
                pack()
                for c in copies:
                    c.start()

    @pl.when(step == 0)
    def _():
        wq[...] = attn_w[:, : 3 * width].astype(bf16)
        for ref in (dwq, dext, dvec, dtable):
            ref[...] = jnp.zeros_like(ref)

    def first(b, carry):
        for k in range(BATCH):
            i = b * BATCH + k
            for g in range(groups):
                do_bd = four(gm_s[i, :, 128 * g : 128 * g + 128], hmask[...])
                gp_s[i, g] = nt(qkv_s[i, :KR, 2 * width + 128 * g : 2 * width + 128 * g + 128], do_bd)
        return carry

    def second(b, carry):
        for g in range(groups):
            total = dtable[g]
            for k in range(BATCH):
                i = b * BATCH + k
                gp = gp_s[i, g]
                prob = prob_in[i, g]
                ds = prob * (gp - jnp.sum(gp * prob, 0, keepdims=True))
                total = total + ds
                raw = padded(ds * scale).astype(bf16)
                low_s[i, g] = raw
                turn_s[i, g] = turn(raw)
            dtable[g] = total
        return carry

    lax.fori_loop(0, CW // BATCH, first, 0)
    lax.fori_loop(0, CW // BATCH, second, 0)
    for i in range(CW):
        rows = slice(WTOK * i, WTOK * i + SLOT)
        for g in range(groups):
            q_bd = four(qkv_s[i, :, 128 * g : 128 * g + 128], hmask[...])
            k_bd = four(qkv_s[i, :, width + 128 * g : width + 128 * g + 128], hmask2[...])
            do_bd = four(gm_s[i, :, 128 * g : 128 * g + 128], hmask[...])
            pj[rows, 128 * g : 128 * g + 128] = nn(turn_s[i, g], k_bd)
            pj[rows, width + 128 * g : width + 128 * g + 128] = nn(low_s[i, g], q_bd)
            pj[rows, 2 * width + 128 * g : 2 * width + 128 * g + 128] = nn(padded(prob_in[i, g]).astype(bf16), do_bd)
    dproj = pj[:CR, :].astype(bf16)
    x = tok[...].astype(f32)
    xhat, inverse = norm_stats(x)
    low = (xhat * vec[0:1] + vec[1:2]).astype(bf16)
    low_t = jnp.concatenate([low.T, jnp.ones((16, CR), bf16)], 0)
    for j in range(3):
        outer = nn(low_t, dproj[:, width * j : width * j + width])
        dwq[j] += outer[:width]
        dext[j] += outer[width : width + 8]
    grad_normed = nt(dproj, wq[...])
    dvec[0] += fold_rows(grad_normed * xhat)
    dvec[1] += fold_rows(grad_normed)
    input_grad[...] = grad_stream_in[...] + norm_grad(grad_normed, xhat, inverse, vec[0:1])

    @pl.when(step == steps - 1)
    def _():
        rows = [dvec[0], dvec[1], None, None, dvec2[3], dvec2[0], dvec2[1], dvec2[2]]
        for i, part in enumerate(rows):
            if part is not None:
                misc[i : i + 1, :] = jnp.sum(part, 0, keepdims=True)
        misc[2:3, :] = dext[0, 0:1, :]
        misc[3:4, :] = dext[2, 0:1, :]
        for i in range(dhid.shape[1] // width):
            misc[8 + i : 9 + i, :] = dhid[0:1, width * i : width * i + width]
        lane = lax.broadcasted_iota(jnp.int32, (1, width), 1)
        line = jnp.zeros((1, width), f32)
        for i, part in enumerate((stats[0], stats[1], dvec2[4])):
            line = jnp.where(lane == i, jnp.sum(part), line)
        misc[12:13, :] = jnp.where(lane == 3, jnp.sum(stats[2]) / 128.0, line)
        misc[13:16, :] = jnp.zeros((3, width), f32)
        flat[...] = jnp.zeros_like(flat)
        for g in range(groups):
            for k in range(WTOK):
                line = dtable[g, k : k + 1, :]
                for h in range(HG):
                    flat[HG * g + h : HG * g + h + 1, SLOT * k : SLOT * k + SLOT] = line[:, SLOT * h : SLOT * h + SLOT]
        rest_f = flat[...]
        total = jnp.zeros((16, 256), f32)
        for _ in range(3):
            part = rest_f.astype(bf16)
            total += nn(part, hot[...])
            rest_f = rest_f - part.astype(f32)
        misc[16:32, :] = jnp.zeros((16, width), f32)
        misc[16:32, :256] = total
        if comm[0]:
            for c in stages[-1][1]:
                c.wait()
            stages[-1][2]()


def sds(shape, dt):
    return jax.ShapeDtypeStruct(shape, dt)


def whole(a):
    nd = len(a.shape)
    return pl.BlockSpec(a.shape, lambda *_: (0,) * nd, pipeline_mode=pl.Buffered(1))


def whole_out(a):
    nd = len(a.shape)
    return pl.BlockSpec(a.shape, lambda *_: (0,) * nd)


def by_step(a, steps):
    nd = len(a.shape)
    return pl.BlockSpec((a.shape[0] // steps,) + tuple(a.shape[1:]), lambda c: (c,) + (0,) * (nd - 1))


def run(body, steps, scalars, stepped, wholes, out_stepped, out_wholes, scratch, flops, collective_id=None):
    smem = pl.BlockSpec(memory_space=pltpu.SMEM)
    params = dict(vmem_limit_bytes=62 * 1024 * 1024)
    if collective_id is not None:
        params.update(collective_id=collective_id, has_side_effects=True)
    return pl.pallas_call(
        body, grid=(steps,),
        in_specs=[smem] * len(scalars) + [by_step(a, steps) for a in stepped] + wholes[1],
        out_specs=[by_step(a, steps) for a in out_stepped] + [whole_out(a) for a in out_wholes],
        out_shape=list(out_stepped) + list(out_wholes), scratch_shapes=scratch,
        compiler_params=pltpu.CompilerParams(**params),
        cost_estimate=pl.CostEstimate(flops=flops, bytes_accessed=20000000, transcendentals=0),
    )(*scalars, *stepped, *wholes[0])


def wholes_of(*arrays):
    return (arrays, [whole(a) for a in arrays])


def loop_rows(total, body):
    size = next(n for n in (96, 64, 48, 32, 16) if total % n == 0)
    lax.fori_loop(0, total // size, lambda i, c: (body(pl.multiple_of(i * size, size), size), c)[1], 0)


def reduce_all(wide_n, narrow_n, share, mine_ref, q_ref, o_ref, s_ref, gm_out, gt_out, s_out,
               recv0, acct, zsend, zrecv, gm, gt, sbuf, srecv, szrecv, *rest):
    bufs = rest[:-2]
    links = Links(wide_n, narrow_n, *rest[-2:])
    bit, me_n, peer, n_bits = links.bit, links.n, links.peer, links.bits
    plan, m_streams, m_sizes = scatter_sizes(wide_n, share)
    links.barrier()
    ht = acct.shape[1]
    steps = n_bits - 1

    def attn_rows(n, start, size):
        flat = n * share
        if flat < q_ref.shape[0]:
            return q_ref[pl.ds(flat + start, size), :]
        return o_ref[pl.ds(flat - q_ref.shape[0] + start, size), :]

    m_trail = []
    m_place = {}
    for st, (start, _) in m_streams.items():
        here = start
        for s in range(steps):
            b = plan[st][s]
            size = m_sizes[st][s + 1]
            halves = size < m_sizes[st][s]
            here = here + bit[b] * size if halves else here
            m_trail.append((st, s, b, here, size, halves))
        m_place[st] = here
    base = 0
    for st in m_streams:
        size = m_sizes[st][-1]
        gm[pl.ds(pl.multiple_of(bit[0] * share + m_place[st], 16), size), :] = mine_ref[base : base + size, :]
        base += size
    m_back = []
    for s in reversed(range(steps)):
        stage = []
        for st, s2, b, at, size, halves in m_trail:
            if s2 == s and halves:
                part = gm.at[pl.ds(pl.multiple_of(bit[0] * share + at, 16), size), :]
                stage.append(links.copy(part, part, links.along(b)))
        m_back.append(stage)
    part = gm.at[pl.ds(pl.multiple_of(bit[0] * share, 16), share), :]
    m_back.append([links.copy(part, part, links.along(0))])
    m_back.append([])

    def back(k):
        if 0 < k <= len(m_back) - 1:
            for c in m_back[k - 1]:
                c.wait_recv()
        if k < len(m_back):
            for c in m_back[k]:
                c.start()

    away_t, keep_t = (1 - bit[0]) * ht, bit[0] * ht
    sbuf[0] = s_ref[...]
    copies = [links.copy(sbuf.at[0], srecv.at[0], links.along(0))]
    copies[0].start()
    for n in range(narrow_n):
        flat = n * share
        src, off = (q_ref, flat) if flat < q_ref.shape[0] else (o_ref, flat - q_ref.shape[0])
        c = links.copy(src.at[pl.ds(pl.multiple_of(off + away_t, 16), ht), :], recv0.at[n], links.along(0))
        c.start()
        copies.append(c)
    back(0)
    copies[0].wait_recv()
    sbuf[1] = sbuf[0] + srecv[0]
    for n in range(narrow_n):
        copies[n + 1].wait_recv()
        def add_t(i, size):
            acct[n, pl.ds(i, size), :] = attn_rows(n, pl.multiple_of(keep_t + i, 16), size) + recv0[n, pl.ds(i, size), :]
        loop_rows(ht, add_t)

    streams, sizes = t_streams(wide_n, ht)
    place = {st: streams[st][0] for st in streams}
    trail = []
    for s in range(steps):
        work = []
        small = links.copy(sbuf.at[1 + s], srecv.at[1 + s], links.along(plan["A"][s]))
        small.start()
        for k, st in enumerate(streams):
            b = plan[st][s]
            size = sizes[st][s + 1]
            halves = size < sizes[st][s]
            send, recv = bufs[2 * (2 * s + k)], bufs[2 * (2 * s + k) + 1]
            here = place[st]
            out_at, in_at = (here + (1 - bit[b]) * size, here + bit[b] * size) if halves else (here, here)
            for n in range(narrow_n):
                def pack(i, k2):
                    send[n, pl.ds(i, k2), :] = acct[n, pl.ds(pl.multiple_of(out_at + i, 16), k2), :].astype(send.dtype)
                loop_rows(size, pack)
            c = links.copy(send, recv, links.along(b))
            c.start()
            work.append((send, recv, in_at, size, halves, c))
            trail.append((st, s, b, in_at, size, halves))
            place[st] = in_at
        back(1 + s)
        small.wait_recv()
        sbuf[2 + s] = sbuf[1 + s] + srecv[1 + s]
        for send, recv, in_at, size, halves, c in work:
            c.wait_recv()
            for n in range(narrow_n):
                def add(i, k2):
                    here = pl.ds(pl.multiple_of(in_at + i, 16), k2)
                    mine = acct[n, here, :] if halves else send[n, pl.ds(i, k2), :].astype(f32)
                    acct[n, here, :] = mine + recv[n, pl.ds(i, k2), :].astype(f32)
                loop_rows(size, add)

    z_base, total = {}, 0
    for st in streams:
        z_base[st] = total
        total += sizes[st][-1]
    copies = []
    for i, n in enumerate(peer):
        c = links.copy(sbuf.at[n_bits], szrecv.at[i], links.over(n))
        c.start()
        copies.append(c)
    for i, n in enumerate(peer):
        for st in streams:
            def pack(r, k):
                zsend[i, pl.ds(z_base[st] + r, k), :] = acct[n, pl.ds(pl.multiple_of(place[st] + r, 16), k), :].astype(bf16)
            loop_rows(sizes[st][-1], pack)
        c = links.copy(zsend.at[i], zrecv.at[i], links.over(n))
        c.start()
        copies.append(c)
    for k in range(1 + steps, len(m_back)):
        back(k)
    for c in copies:
        c.wait_recv()
    for st in streams:
        top = keep_t + place[st]
        def add(r, k):
            value = acct[me_n, pl.ds(pl.multiple_of(place[st] + r, 16), k), :]
            for i in range(narrow_n - 1):
                value = value + zrecv[i, pl.ds(z_base[st] + r, k), :].astype(f32)
            gt[me_n, pl.ds(pl.multiple_of(top + r, 16), k), :] = value.astype(bf16)
        loop_rows(sizes[st][-1], add)

    pending = []
    for st in streams:
        where = pl.ds(pl.multiple_of(keep_t + place[st], 16), sizes[st][-1])
        for n in peer:
            part = gt.at[me_n, where, :]
            c = links.copy(part, part, links.over(n))
            c.start()
            pending.append(c)
    zero = sbuf[n_bits]
    total_s = jnp.zeros_like(zero)
    for n in range(narrow_n):
        behind = lax.rem(me_n + narrow_n - n, narrow_n)
        value = zero
        for i in range(1, narrow_n):
            value = jnp.where(behind == i, szrecv[i - 1], value)
        total_s = total_s + value
    s_out[...] = total_s
    gm_out[...] = gm[...]
    for s in reversed(range(steps)):
        for c in pending:
            c.wait_recv()
        pending = []
        for st, s2, b, at, size, halves in trail:
            if s2 == s and halves:
                part = gt.at[:, pl.ds(pl.multiple_of(keep_t + at, 16), size), :]
                c = links.copy(part, part, links.along(b))
                c.start()
                pending.append(c)
    for c in pending:
        c.wait_recv()
    part = gt.at[:, pl.ds(pl.multiple_of(keep_t, 16), ht), :]
    c = links.copy(part, part, links.along(0))
    c.start()
    c.wait_recv()
    gt_out[...] = gt[...]
    for c in links.all:
        c.wait_send()


def t_streams(wide_n, ht):
    rest = range(1, wide_n.bit_length() - 1)
    cut = ht * 2 // 3
    streams = {"A": (0, cut), "B": (cut, ht - cut)}
    sizes = {}
    for st, (_, size) in streams.items():
        sizes[st] = [size]
        for _ in rest:
            sizes[st].append(sizes[st][-1] // 2 if sizes[st][-1] % 32 == 0 else sizes[st][-1])
    return streams, sizes


def reduce_call(wide_n, narrow_n, share, mine, dq, do, misc):
    width = mine.shape[1]
    ht = share // 2
    n_bits = wide_n.bit_length() - 1
    streams, sizes = t_streams(wide_n, ht)
    last = sum(sizes[st][-1] for st in streams)
    scratch = [
        pltpu.VMEM((narrow_n, ht, width), f32), pltpu.VMEM((narrow_n, ht, width), f32),
        pltpu.VMEM((narrow_n - 1, last, width), bf16), pltpu.VMEM((narrow_n - 1, last, width), bf16),
        pltpu.VMEM((2 * share, width), bf16), pltpu.VMEM((narrow_n, share, width), bf16),
        pltpu.VMEM((n_bits + 1,) + misc.shape, f32), pltpu.VMEM((n_bits,) + misc.shape, f32),
        pltpu.VMEM((narrow_n - 1,) + misc.shape, f32)]
    for s in range(n_bits - 1):
        for st in streams:
            scratch += [pltpu.VMEM((narrow_n, sizes[st][s + 1], width), bf16)] * 2
    copies = 2 + narrow_n + 7 * n_bits + 4 * narrow_n
    scratch += [pltpu.SemaphoreType.DMA((copies,)), pltpu.SemaphoreType.DMA((copies,))]
    vmem = pl.BlockSpec(memory_space=pltpu.VMEM)
    return pl.pallas_call(
        functools.partial(reduce_all, wide_n, narrow_n, share),
        out_shape=[sds((2 * share, width), bf16), sds((narrow_n, share, width), bf16), sds(misc.shape, f32)],
        in_specs=[vmem] * 4, out_specs=[vmem] * 3, scratch_shapes=scratch,
        compiler_params=pltpu.CompilerParams(collective_id=0, has_side_effects=True, vmem_limit_bytes=60 * 1024 * 1024),
    )(mine, dq, do, misc)


def adam_kernel(narrow_ref, gt, gm, misc, aw, af, as_, mw, mf, ms, tw, tf, ts, vw, vf, vs, bw, bf, bs,
                rms, an, al, afn, asn, mn, ml, mfn, msn, tn_, tfn, tsn, vn, vfn, vsn, bn, bfn, bsn):
    def put(new, w, g, m, v, rate, decay, low=None):
        out = adam_step(w, g, m, v, rate, decay)
        for ref, value in zip(new, out):
            ref[...] = value.reshape(ref.shape)
        if low is not None:
            low[...] = out[0].astype(bf16).reshape(low.shape)

    put((an, afn, asn), aw[...], jnp.concatenate([gt[j].astype(f32) for j in range(4)], 1), af[...], as_[...], 0.02, 0.05, al)
    put((mn, mfn, msn), mw[0], gm[0].astype(f32), mf[0], ms[0], 0.02, 0.05, ml)

    @pl.when(pl.program_id(0) == 0)
    def _():
        put((vn, vfn, vsn), vw[...], misc[0:8, :], vf[...], vs[...], 0.3, 0.0)
        stats = misc[12:13, :]
        for i in range(3):
            ratio = jnp.sqrt(stats[:, i : i + 1] / (stats[:, 3:4] * misc.shape[1]))
            rms[i] = ratio[0, 0]
        n = narrow_ref[0]
        share = bw.shape[0]
        grad = jnp.zeros((1, share), f32)
        per = misc.shape[1] // share
        for i in range(4):
            for k in range(per):
                grad = jnp.where(n == per * i + k, misc[8 + i : 9 + i, share * k : share * k + share], grad)
        put((bn, bfn, bsn), bw[...], grad.reshape(share), bf[...], bs[...], 0.1, 0.0)
        heads, count = tw.shape
        put((tn_, tfn, tsn), tw[...], misc[16 : 16 + heads, :count], tf[...], ts[...], 0.3, 0.0)


def adam_call(narrow, gt, gm, misc, attn, mlp, table, vec, bias):
    width = gm.shape[1]
    share = mlp[0].shape[1]
    gt = gt.reshape(4, width, width)
    cuts = 8
    quarter = 2 * share // cuts
    rows = width // cuts
    gm = gm.reshape(cuts, quarter, width)
    mlp = [a.reshape(cuts, quarter, width) for a in mlp]
    line = pl.BlockSpec((rows, attn[0].shape[1]), lambda j, *_: (j, 0))
    lead = pl.BlockSpec((1, quarter, width), lambda j, *_: (j, 0, 0))
    split = pl.BlockSpec((4, rows, width), lambda j, *_: (0, j, 0))
    smalls = list(table) + list(vec) + list(bias)
    args = [gt, gm, misc] + list(attn) + mlp + smalls
    in_specs = [split, lead, whole(misc)] + [line] * 3 + [lead] * 3 + [whole(a) for a in smalls]
    three = lambda a: [sds(a.shape, f32)] * 3
    outs = [sds((3,), f32), sds(attn[0].shape, f32), sds(attn[0].shape, bf16)] + [sds(attn[0].shape, f32)] * 2
    outs += [sds(mlp[0].shape, f32), sds(mlp[0].shape, bf16)] + [sds(mlp[0].shape, f32)] * 2
    outs += three(table[0]) + three(vec[0]) + three(bias[0])
    out_specs = [pl.BlockSpec(memory_space=pltpu.SMEM)] + [line] * 4 + [lead] * 4
    out_specs += [whole_out(a) for a in smalls]
    r = pl.pallas_call(
        adam_kernel,
        grid_spec=pltpu.PrefetchScalarGridSpec(num_scalar_prefetch=1, grid=(cuts,), in_specs=in_specs, out_specs=out_specs),
        out_shape=outs,
        compiler_params=pltpu.CompilerParams(vmem_limit_bytes=60 * 1024 * 1024),
    )(narrow, *args)
    full = (2, share, width)
    return [r[0], *r[1:5], *[a.T for a in r[9:12]], *r[12:15], *[a.reshape(full) for a in r[5:9]], *r[15:18]]


def bias_layout(rel_table):
    pos = np.arange(WTOK)
    row, col = pos // WIN, pos % WIN
    off = (row[:, None] - row[None, :] + WIN - 1) * (2 * WIN - 1) + col[:, None] - col[None, :] + WIN - 1
    full = np.full((KR, SLOT), -1, np.int32)
    full[:WTOK, :WTOK] = off.T
    return full


def block(tokens, grid_sizes, cotangent, attn_weight, rel_table, vectors, mlp_weight, mlp_bias, narrow, wide_n, narrow_n, linked=True):
    rows, width = tokens.shape
    wins = rows // WTOK
    steps = wins // CW
    heads = rel_table.shape[0]
    groups = heads // HG
    share = mlp_weight.shape[1]
    hidden = share * narrow_n
    n_bits = wide_n.bit_length() - 1
    comm = (linked, steps)
    unit = rows * width * width
    hot = np.zeros((KR * SLOT, 256), np.float32)
    lay = bias_layout(rel_table).reshape(-1)
    hot[np.arange(KR * SLOT)[lay >= 0], lay[lay >= 0]] = 1.0
    hot = jnp.asarray(hot, bf16)
    mask = head_mask(width // heads)
    mask2 = mask.reshape(HG, SLOT, -1)[np.array([0, 2, 1, 3])].reshape(mask.shape)
    mask, mask2 = jnp.asarray(mask, bf16), jnp.asarray(mask2, bf16)
    rinfo, kinfo = jnp.asarray(row_info()), jnp.asarray(key_info())
    scal = (narrow, grid_sizes)
    pad = CR + 16
    copies = 3 * (narrow_n - 1) + 3 * 2 * (narrow_n - 1) + 4
    sem = [pltpu.SemaphoreType.DMA((copies,)), pltpu.SemaphoreType.DMA((copies,))] if linked else []
    sides = pltpu.VMEM((CR, 128), f32)
    table_s = pltpu.VMEM((groups, KR, HG * SLOT), f32)
    flat = pltpu.VMEM((16, KR * SLOT), f32)
    turned = pltpu.VMEM((CW, groups, SLOT, HG * SLOT), bf16)
    qkv, prob, mixed, stream, stats, gw, tails = run(
        functools.partial(attn_forward, wide_n, narrow_n, comm), steps, scal, (tokens,),
        wholes_of(attn_weight, mlp_weight, mlp_bias, vectors, rel_table, hot, rinfo, kinfo, mask, mask2),
        [sds((wins, SLOT, 3 * width), bf16), sds((wins, groups, KR, HG * SLOT), f32), sds((rows, width), bf16), sds((rows, width), f32)],
        [sds((3, 8, width), f32), sds((narrow_n, 2 * share, width), bf16), sds((narrow_n, 8, width), f32)],
        [pltpu.VMEM((width, 4 * width), bf16), pltpu.VMEM((pad, 3 * width), f32), pltpu.VMEM((pad, width), f32), turned,
         table_s, pltpu.VMEM((16, 256), f32), flat, sides,
         pltpu.VMEM((2 * share, width), bf16), pltpu.VMEM((8, width), f32),
         pltpu.VMEM((narrow_n, 2 * share, width), bf16), pltpu.VMEM((narrow_n, 8, width), f32)] + sem,
        12 * unit, 1 if linked else None)
    out_proj = pl.BlockSpec((width, width), lambda *_: (0, 3), pipeline_mode=pl.Buffered(1))
    fixed = (attn_weight, gw, tails, vectors, rinfo)
    outputs, grad_stream, gm, dmlp, dwo, dhid, dvec2 = run(
        functools.partial(feed_forward, TILE), steps, scal, (cotangent, mixed, stream),
        (fixed, [out_proj] + [whole(a) for a in fixed[1:]]),
        [sds((rows, width), bf16), sds((rows, width), f32), sds((wins, SLOT, width), bf16)],
        [sds((narrow_n, 2 * share, width), f32), sds((width, width), f32), sds((8, hidden), f32), sds((5, 8, width), f32)],
        [pltpu.VMEM((width, width), bf16), pltpu.VMEM((hidden, width), bf16), pltpu.VMEM((hidden, width), bf16),
         pltpu.VMEM((1, hidden), f32), pltpu.VMEM((width, hidden), f32), pltpu.VMEM((width, hidden), f32),
         pltpu.VMEM((pad, width), f32), sides],
        52 * unit)
    _, streams, sizes = scatter_sizes(wide_n, share)
    last = sum(sizes[st][-1] for st in streams)
    bufs = []
    for s in range(n_bits - 1):
        for st in streams:
            bufs += [pltpu.VMEM((narrow_n, sizes[st][s + 1], width), bf16)] * 2
    copies = 1 + 2 * n_bits + narrow_n
    sem = [pltpu.SemaphoreType.DMA((copies,)), pltpu.SemaphoreType.DMA((copies,))] if linked else []
    input_grad, dwq, misc, mine = run(
        functools.partial(attn_backward, wide_n, narrow_n, comm), steps, (), (tokens, qkv, prob, gm, grad_stream),
        wholes_of(attn_weight, vectors, hot, mask, mask2, dmlp, dhid, dvec2, stats),
        [sds((rows, width), f32)],
        [sds((3, width, width), f32), sds((32, width), f32), sds((last, width), bf16)],
        [pltpu.VMEM((width, 3 * width), bf16), pltpu.VMEM((pad, 3 * width), f32),
         pltpu.VMEM((CW, groups, KR, HG * SLOT), f32), turned, turned, pltpu.VMEM((3, 8, width), f32),
         pltpu.VMEM((2, 8, width), f32), table_s, flat,
         pltpu.VMEM((narrow_n, share, width), bf16), pltpu.VMEM((narrow_n, share, width), bf16),
         pltpu.VMEM((narrow_n, share, width), f32), pltpu.VMEM((narrow_n - 1, last, width), bf16),
         pltpu.VMEM((narrow_n - 1, last, width), bf16)] + bufs + sem,
        20 * unit, 2 if linked else None)
    return outputs, input_grad, dmlp, dwq, dwo, misc, mine


TILE = 768


def adam_step(weight, gradient, first_old, second_old, rate_value, decay_value):
    first_new = beta_one * first_old + (1.0 - beta_one) * gradient
    second_new = beta_two * second_old + (1.0 - beta_two) * gradient * gradient
    fix_one = 1.0 - beta_one**STEP
    fix_two = 1.0 - beta_two**STEP
    update = rate_value * (first_new / fix_one) / (jnp.sqrt(second_new / fix_two) + adam_eps)
    return (weight - update - rate_value * decay_value * weight, first_new, second_new)


def shards(wide_n, narrow_n, tokens, grid_sizes, cotangent, attn_weight, attn_first, attn_second, rel_table, table_first,
           table_second, vectors, vector_first, vector_second, mlp_weight, mlp_first, mlp_second, mlp_bias, bias_first,
           bias_second):
    width = tokens.shape[1]
    narrow = lax.axis_index("narrow").reshape(1).astype(jnp.int32)
    outputs, input_grad, _, dwq, dwo, misc, mine = block(
        tokens, grid_sizes, cotangent, attn_weight, rel_table.T, vectors, mlp_weight, mlp_bias, narrow, wide_n, narrow_n)
    gm, gt, misc = reduce_call(wide_n, narrow_n, mlp_weight.shape[1], mine, dwq.reshape(3 * width, width), dwo, misc)
    new = adam_call(narrow, gt, gm, misc, (attn_weight, attn_first, attn_second), (mlp_weight, mlp_first, mlp_second),
                    (rel_table.T, table_first.T, table_second.T), (vectors, vector_first, vector_second),
                    (mlp_bias, bias_first, bias_second))
    return (outputs, input_grad, *new)


def solution(mesh):
    rows = P(("wide", "narrow"), None)
    split = P(None, "narrow", None)
    return jax.shard_map(
        functools.partial(shards, mesh.shape["wide"], mesh.shape["narrow"]), mesh=mesh,
        in_specs=(rows, P("wide"), rows) + (P(),) * 9 + (split,) * 3 + (P("narrow"),) * 3,
        out_specs=(rows, rows) + (P(),) * 11 + (split,) * 4 + (P("narrow"),) * 3,
        check_vma=False)
```

```python
import functools

import jax
import jax.numpy as jnp
import numpy as np
from jax import lax
from jax.sharding import PartitionSpec as P
from jax.experimental import pallas as pl
from jax.experimental.pallas import tpu as pltpu

WIN = 7
WTOK = 49
WPI = 16
IMG_W = 16
STEP = 5
CW = 16
CR = CW * WTOK
SLOT = 64
KR = 56
HG = 4
LOG2E = 1.4426950408889634

norm_eps = 1e-05
beta_one = 0.5
beta_two = 0.5
adam_eps = 1e-08
highest = lax.Precision.HIGHEST
f32 = jnp.float32
bf16 = jnp.bfloat16


def nn(a, b):
    return lax.dot_general(a, b, (((1,), (0,)), ((), ())), preferred_element_type=f32)


def nt(a, b):
    return lax.dot_general(a, b, (((1,), (1,)), ((), ())), preferred_element_type=f32)


def tn(a, b):
    return lax.dot_general(a, b, (((0,), (0,)), ((), ())), preferred_element_type=f32)


def row_info():
    r = np.arange(CR)
    win = r // WTOK
    p = r % WTOK
    info = np.stack([win, p // WIN, p % WIN]).astype(np.float32)
    info[1, win >= CW] = 1000.0
    return np.ascontiguousarray(np.broadcast_to(info[:, :, None], (3, CR, 128)))


def key_info():
    p = np.arange(KR)
    info = np.stack([p // WIN, p % WIN]).astype(np.float32)
    return np.ascontiguousarray(np.broadcast_to(info[:, :, None], (2, KR, 128)))


def head_mask(head_size):
    row = np.arange(HG * SLOT)
    lane = np.arange(HG * head_size)
    return (((row // SLOT)[:, None] == (lane // head_size)[None, :]) & ((row % SLOT) < WTOK)[:, None]).astype(np.float32)


def fold_rows(t):
    return jnp.sum(t.reshape(t.shape[0] // 8, 8, t.shape[1]), 0)


def rep(v, n):
    return jnp.concatenate([v] * n, 1)


def fill_sides(sides, info, side_s):
    win = info[0]
    value = jnp.zeros_like(win)
    for i in range(CW):
        value = jnp.where(win == float(i), sides[i].astype(f32), value)
    side_s[...] = value


def corner(narrow, step, steps):
    u = WPI - 1 - (narrow * steps + step)
    return (WIN * (u // 4)).astype(f32), (WIN * lax.rem(u, 4)).astype(f32)


def chunk_valid(info, side_s, top, left):
    side = side_s[...]
    return jnp.where((info[1] + top < side) & (info[2] + left < side), 1.0, 0.0)


def norm_stats(x):
    mean = jnp.mean(x, -1, keepdims=True)
    centred = x - mean
    inverse = lax.rsqrt(jnp.mean(centred * centred, -1, keepdims=True) + norm_eps)
    return centred * inverse, inverse


def norm_grad(g, xhat, inverse, gain):
    scaled = g * gain
    m1 = jnp.mean(scaled, -1, keepdims=True)
    m2 = jnp.mean(scaled * xhat, -1, keepdims=True)
    return inverse * (scaled - m1 - xhat * m2)


class Links:
    def __init__(self, wide_n, narrow_n, send_sem, recv_sem):
        self.w = lax.axis_index("wide")
        self.n = lax.axis_index("narrow")
        self.bits = wide_n.bit_length() - 1
        self.bit = [lax.rem(self.w // (1 << b), 2) for b in range(self.bits)]
        self.mate = [self.w + (1 - 2 * self.bit[b]) * (1 << b) for b in range(self.bits)]
        self.peer = [lax.rem(self.n + s, narrow_n) for s in range(1, narrow_n)]
        self.send_sem, self.recv_sem = send_sem, recv_sem
        self.used = 0
        self.all = []

    def copy(self, src, dst, device):
        k = self.used
        self.used += 1
        c = pltpu.make_async_remote_copy(
            src_ref=src, dst_ref=dst, send_sem=self.send_sem.at[k], recv_sem=self.recv_sem.at[k],
            device_id=device, device_id_type=pl.DeviceIdType.MESH)
        self.all.append(c)
        return c

    def along(self, b):
        return (self.mate[b], self.n)

    def over(self, n):
        return (self.w, n)

    def barrier(self):
        sem = pltpu.get_barrier_semaphore()
        for b in range(self.bits):
            pl.semaphore_signal(sem, inc=1, device_id=self.along(b), device_id_type=pl.DeviceIdType.MESH)
        for n in self.peer:
            pl.semaphore_signal(sem, inc=1, device_id=self.over(n), device_id_type=pl.DeviceIdType.MESH)
        pl.semaphore_wait(sem, self.bits + len(self.peer))


def gather_cuts(wide_n, rows):
    bits = list(range(min(3, wide_n.bit_length() - 1)))
    first = rows // 256 * 128
    return [(0, first, bits[1:] + bits[:1]), (first, rows - first, bits[1:][::-1] + bits[:1])]


def gather_plan(links, wide_n, own, tail_own, all_w, all_tail):
    narrow_n, rows, _ = all_w.shape
    streams = gather_cuts(wide_n, rows)
    stages = [[]]
    place, sizes = [], []
    for start, size, order in streams:
        piece = size >> len(order)
        off = 0
        for k, b in enumerate(order):
            off = off + links.bit[b] * (piece << k)
        place.append(start + off)
        sizes.append(piece)
    for n in links.peer:
        stages[0].append(links.copy(tail_own, all_tail.at[links.n], links.over(n)))
        for at, size in zip(place, sizes):
            here = pl.ds(pl.multiple_of(at, 16), size)
            stages[0].append(links.copy(own.at[here, :], all_w.at[links.n, here, :], links.over(n)))
    for k in range(len(streams[0][2])):
        stage = []
        for s, (start, size, order) in enumerate(streams):
            here = pl.ds(pl.multiple_of(place[s], 16), sizes[s])
            for n in links.peer:
                part = all_w.at[n, here, :]
                stage.append(links.copy(part, part, links.along(order[k])))
            place[s] = place[s] - links.bit[order[k]] * sizes[s]
            sizes[s] = sizes[s] * 2
        stages.append(stage)
    return stages


def run_stages(stages, step, steps):
    for k, stage in enumerate(stages):
        @pl.when(step == min(k, steps - 1))
        def _():
            if k:
                for c in stages[k - 1]:
                    c.wait()
            for c in stage:
                c.start()


def expand_table(table, hot, wide_t, flat, bias):
    heads, count = table.shape
    wide_t[...] = jnp.zeros_like(wide_t)
    wide_t[:heads, :count] = table[...] * LOG2E
    rest = wide_t[...]
    total = jnp.zeros((16, hot.shape[0]), f32)
    for _ in range(3):
        part = rest.astype(bf16)
        total += nt(part, hot[...])
        rest = rest - part.astype(f32)
    flat[...] = total
    bias[...] = jnp.full(bias.shape, -1e30, f32)
    for g in range(heads // HG):
        for k in range(WTOK):
            for h in range(HG):
                bias[g, k : k + 1, SLOT * h : SLOT * h + SLOT] = flat[HG * g + h : HG * g + h + 1, SLOT * k : SLOT * k + SLOT]


def turn(t):
    t = jnp.concatenate([t[:, :128], t[:, 128:]], 0).T
    return jnp.concatenate([t[:SLOT], t[SLOT:]], 1)


def padded(t):
    return jnp.concatenate([t, jnp.zeros((SLOT - KR, t.shape[1]), f32)], 0)


def four(t, mask):
    return jnp.concatenate([t] * HG, 0) * mask


BATCH = 16


def attn_forward(wide_n, narrow_n, comm, narrow_ref, sides, tok, attn_w, mlp_w, mlp_b, vec, table, hot, rinfo, kinfo, hmask, hmask2,
                 qkv_s, prob_out, mixed_out, stream_out, stats, gw_out, tail_out,
                 wq, pj, mx, turn_s, bias, wide_t, flat, side_s, own, tail_own, gw, tails, *sems):
    step = pl.program_id(0)
    steps = pl.num_programs(0)
    static_steps = comm[1]
    width = tok.shape[1]
    groups = width // 128
    scale = 32 ** (-0.5)
    narrow = narrow_ref[0]
    share = mlp_w.shape[1]

    @pl.when(step == 0)
    def _():
        for j in range(2):
            own[share * j : share * j + share, :] = mlp_w[j].astype(bf16)
        tail_own[...] = jnp.zeros_like(tail_own)
        rest = mlp_b[...].reshape(1, share)
        for i in range(3):
            part = rest.astype(bf16).astype(f32)
            tail_own[i : i + 1, :share] = part
            rest = rest - part
        if comm[0]:
            gw[lax.axis_index("narrow")] = own[...]
            tails[lax.axis_index("narrow")] = tail_own[...]
        else:
            for n in range(narrow_n):
                gw[n] = own[...]
                tails[n] = tail_own[...]

    if comm[0]:
        links = Links(wide_n, narrow_n, *sems)

        @pl.when(step == 0)
        def _():
            links.barrier()

        stages = gather_plan(links, wide_n, own, tail_own, gw, tails)
        run_stages(stages, step, static_steps)

    @pl.when(step == 0)
    def _():
        wq[...] = attn_w[...].astype(bf16)
        fill_sides(sides, rinfo, side_s)
        expand_table(table, hot, wide_t, flat, bias)
        for ref in (pj, mx, stats):
            ref[...] = jnp.zeros_like(ref)

    top, left = corner(narrow, step, static_steps)
    x = tok[...].astype(f32)
    valid = chunk_valid(rinfo, side_s, top, left)
    keep = rep(valid, groups)
    xhat, _ = norm_stats(x)
    low = (xhat * vec[0:1] + vec[1:2]).astype(bf16)
    pj[:CR, :width] = nn(low, wq[:, :width]) + vec[2:3]
    pj[:CR, width : 2 * width] = nn(low, wq[:, width : 2 * width])
    pj[:CR, 2 * width :] = nn(low, wq[:, 2 * width : 3 * width]) + vec[3:4]
    for i in range(CW):
        qkv_s[i] = pj[WTOK * i : WTOK * i + SLOT, :].astype(bf16)

    def score(b, carry):
        for k in range(BATCH):
            i = b * BATCH + k
            for g in range(groups):
                q_bd = four(qkv_s[i, :, 128 * g : 128 * g + 128], hmask[...])
                prob_out[i, g] = nt(qkv_s[i, :KR, width + 128 * g : width + 128 * g + 128], q_bd)
        return carry

    def soft(b, carry):
        for k in range(BATCH):
            i = b * BATCH + k
            side = sides[i].astype(f32)
            fill = jnp.where((kinfo[0] < side - top) & (kinfo[1] < side - left), 0.0, -10000.0 * LOG2E)
            fill = rep(fill, 2)
            for g in range(groups):
                s = prob_out[i, g] * (scale * LOG2E) + bias[g] + fill
                e = jnp.exp2(s - jnp.max(s, 0, keepdims=True))
                prob = e * (1.0 / jnp.sum(e, 0, keepdims=True))
                prob_out[i, g] = prob
                turn_s[i, g] = turn(padded(prob).astype(bf16))
        return carry

    lax.fori_loop(0, CW // BATCH, score, 0)
    lax.fori_loop(0, CW // BATCH, soft, 0)
    for i in range(CW):
        for g in range(groups):
            v_bd = four(qkv_s[i, :, 2 * width + 128 * g : 2 * width + 128 * g + 128], hmask2[...])
            mx[WTOK * i : WTOK * i + SLOT, 128 * g : 128 * g + 128] = nn(turn_s[i, g], v_bd)
    mixed = mx[:CR, :].astype(bf16)
    mixed_out[...] = mixed
    branch = (nn(mixed, wq[:, 3 * width :]) + vec[4:5]) * keep
    stream_out[...] = x + branch
    stats[0] += fold_rows(x * x * keep)
    stats[1] += fold_rows(branch * branch)
    stats[2, :, :128] += fold_rows(valid)

    @pl.when(step == steps - 1)
    def _():
        if comm[0]:
            for c in stages[-1]:
                c.wait()
        gw_out[...] = gw[...]
        tail_out[...] = tails[...]


def feed_forward(tile, narrow_ref, sides, cot, mixed_in, stream_in, attn_w, gw, tails, vec, rinfo,
                 out_ref, grad_stream_out, gm_s, dmlp, dwo, dhid, dvec,
                 wo, w1, w2, hb, dw1, dw2, mx, side_s):
    step = pl.program_id(0)
    steps = pl.num_programs(0)
    width = cot.shape[1]
    groups = width // 128
    hidden = w1.shape[0]
    shards_n, twice, _ = gw.shape
    share = twice // 2

    @pl.when(step == 0)
    def _():
        wo[...] = attn_w[...].astype(bf16)
        for n in range(shards_n):
            w1[share * n : share * n + share, :] = gw[n, :share, :]
            w2[share * n : share * n + share, :] = gw[n, share:, :]
            three = tails[n]
            hb[:, share * n : share * n + share] = (three[0:1] + three[1:2] + three[2:3])[:, :share]
        fill_sides(sides, rinfo, side_s)
        for ref in (mx, dw1, dw2, dwo, dhid, dvec):
            ref[...] = jnp.zeros_like(ref)

    top, left = corner(narrow_ref[0], step, steps)
    keep = rep(chunk_valid(rinfo, side_s, top, left), groups)
    cotan = cot[...].astype(f32)
    stream = stream_in[...]
    xhat2, inverse2 = norm_stats(stream)
    second = (xhat2 * vec[5:6] + vec[6:7]).astype(bf16)
    kept_cot = cotan * keep
    grad_low = kept_cot.astype(bf16)
    second_t = jnp.concatenate([second.T, jnp.ones((16, CR), bf16)], 0)
    grad_t = grad_low.T
    mlp_out = jnp.zeros((CR, width), f32)
    grad_second = jnp.zeros((CR, width), f32)
    for t in range(hidden // tile):
        cols = slice(tile * t, tile * t + tile)
        pre = nt(second, w1[cols, :]) + hb[0:1, cols]
        square = pre * pre
        half = 0.5 * jnp.tanh(pre * (square * (0.7978845608028654 * 0.044715) + 0.7978845608028654)) + 0.5
        active = (pre * half).astype(bf16)
        slope = half + (pre * (half - half * half)) * (square * (6 * 0.7978845608028654 * 0.044715) + 2 * 0.7978845608028654)
        grad_pre = (nt(grad_low, w2[cols, :]) * slope).astype(bf16)
        mlp_out += nn(active, w2[cols, :])
        grad_second += nn(grad_pre, w1[cols, :])
        outer = nn(second_t, grad_pre)
        dw1[:, cols] += outer[:width]
        dhid[:, cols] += outer[width : width + 8]
        dw2[:, cols] += nn(grad_t, active)
    branch = (mlp_out + vec[7:8]) * keep
    out_ref[...] = (stream + branch).astype(bf16)
    dvec[4] += fold_rows(branch * branch)
    dvec[0] += fold_rows(grad_second * xhat2)
    dvec[1] += fold_rows(grad_second)
    dvec[2] += fold_rows(kept_cot)
    grad_stream = cotan + norm_grad(grad_second, xhat2, inverse2, vec[5:6])
    grad_stream_out[...] = grad_stream
    grad_attn = grad_stream * keep
    dvec[3] += fold_rows(grad_attn)
    grad_attn_low = grad_attn.astype(bf16)
    dwo[...] += nn(mixed_in[...].T, grad_attn_low)
    mx[:CR, :] = nt(grad_attn_low, wo[...])
    for i in range(CW):
        gm_s[i] = mx[WTOK * i : WTOK * i + SLOT, :].astype(bf16)

    @pl.when(step == steps - 1)
    def _():
        for j, ref in enumerate((dw1, dw2)):
            for t in range(hidden // width):
                turned = ref[:, width * t : width * t + width].T
                for k in range(width // share):
                    n = (width * t) // share + k
                    dmlp[n, share * j : share * j + share, :] = turned[share * k : share * k + share, :]


def scatter_sizes(wide_n, share):
    n_bits = wide_n.bit_length() - 1
    rest = list(range(1, n_bits))
    half = len(rest) // 2
    plan = {"A": rest, "B": rest[half:] + rest[:half]}
    cut = share // 2
    streams = {"A": (0, cut), "B": (cut, share - cut)}
    sizes = {}
    for st, (_, size) in streams.items():
        sizes[st] = [size]
        for _ in rest:
            sizes[st].append(sizes[st][-1] // 2 if sizes[st][-1] % 32 == 0 else sizes[st][-1])
    return plan, streams, sizes


def scatter_stages(links, wide_n, narrow_n, share, dmlp, mine_out, send0, recv0, acc, zsend, zrecv, bufs):
    plan, streams, sizes = scatter_sizes(wide_n, share)
    bit = links.bit
    keep0, away0 = bit[0] * share, (1 - bit[0]) * share
    stages = []

    def pack0():
        for n in range(narrow_n):
            def one(i, size):
                send0[n, pl.ds(i, size), :] = dmlp[n, pl.ds(pl.multiple_of(away0 + i, 16), size), :].astype(send0.dtype)
            loop_rows(share, one)

    def add0():
        for n in range(narrow_n):
            def one(i, size):
                acc[n, pl.ds(i, size), :] = (dmlp[n, pl.ds(pl.multiple_of(keep0 + i, 16), size), :]
                                             + recv0[n, pl.ds(i, size), :].astype(f32))
            loop_rows(share, one)

    stages.append((pack0, [links.copy(send0, recv0, links.along(0))], add0))
    place = {st: streams[st][0] for st in streams}
    trail = []
    for s in range(links.bits - 1):
        work = []
        for k, st in enumerate(streams):
            b = plan[st][s]
            size = sizes[st][s + 1]
            halves = size < sizes[st][s]
            send, recv = bufs[2 * (2 * s + k)], bufs[2 * (2 * s + k) + 1]
            here = place[st]
            out_at, in_at = (here + (1 - bit[b]) * size, here + bit[b] * size) if halves else (here, here)
            place[st] = in_at
            work.append((send, recv, out_at, in_at, size, halves, links.copy(send, recv, links.along(b))))
            trail.append((st, s, b, in_at, size, halves))

        def pack(work=work):
            for send, recv, out_at, in_at, size, halves, _ in work:
                for n in range(narrow_n):
                    def one(i, k):
                        send[n, pl.ds(i, k), :] = acc[n, pl.ds(pl.multiple_of(out_at + i, 16), k), :].astype(send.dtype)
                    loop_rows(size, one)

        def add(work=work):
            for send, recv, out_at, in_at, size, halves, _ in work:
                for n in range(narrow_n):
                    def one(i, k):
                        here = pl.ds(pl.multiple_of(in_at + i, 16), k)
                        mine = acc[n, here, :] if halves else send[n, pl.ds(i, k), :].astype(f32)
                        acc[n, here, :] = mine + recv[n, pl.ds(i, k), :].astype(f32)
                    loop_rows(size, one)

        stages.append((pack, [w[-1] for w in work], add))
    base, total = {}, 0
    for st in streams:
        base[st] = total
        total += sizes[st][-1]

    def packz():
        for i, n in enumerate(links.peer):
            for st in streams:
                def one(r, k):
                    zsend[i, pl.ds(base[st] + r, k), :] = acc[n, pl.ds(pl.multiple_of(place[st] + r, 16), k), :].astype(zsend.dtype)
                loop_rows(sizes[st][-1], one)

    def addz():
        for st in streams:
            def one(r, k):
                value = acc[links.n, pl.ds(pl.multiple_of(place[st] + r, 16), k), :]
                for i in range(narrow_n - 1):
                    value = value + zrecv[i, pl.ds(base[st] + r, k), :].astype(f32)
                mine_out[pl.ds(base[st] + r, k), :] = value.astype(bf16)
            loop_rows(sizes[st][-1], one)

    stages.append((packz, [links.copy(zsend.at[i], zrecv.at[i], links.over(n)) for i, n in enumerate(links.peer)], addz))
    return stages


def attn_backward(wide_n, narrow_n, comm, tok, qkv_s, prob_in, gm_s, vec, hot, hmask, hmask2,
                  dmlp, dhid, dvec2, stats,
                  dproj_out, dwq, misc, mine_out,
                  pj, gp_s, low_s, turn_s, dext, dtable, flat, send0, recv0, acc, zsend, zrecv, *rest):
    step = pl.program_id(0)
    steps = pl.num_programs(0)
    static_steps = comm[1]
    width = tok.shape[1]
    groups = width // 128
    scale = 32 ** (-0.5)
    share = dmlp.shape[1] // 2

    if comm[0]:
        links = Links(wide_n, narrow_n, *rest[-2:])

        @pl.when(step == 0)
        def _():
            links.barrier()

        stages = scatter_stages(links, wide_n, narrow_n, share, dmlp, mine_out, send0, recv0, acc, zsend, zrecv, rest[:-2])
        for k, (pack, copies, add) in enumerate(stages):
            @pl.when(step == min(k, static_steps - 1))
            def _():
                if k:
                    for c in stages[k - 1][1]:
                        c.wait()
                    stages[k - 1][2]()
                pack()
                for c in copies:
                    c.start()

    @pl.when(step == 0)
    def _():
        for ref in (dwq, dext, dtable):
            ref[...] = jnp.zeros_like(ref)

    def first(b, carry):
        for k in range(BATCH):
            i = b * BATCH + k
            for g in range(groups):
                do_bd = four(gm_s[i, :, 128 * g : 128 * g + 128], hmask[...])
                gp_s[i, g] = nt(qkv_s[i, :KR, 2 * width + 128 * g : 2 * width + 128 * g + 128], do_bd)
        return carry

    def second(b, carry):
        for g in range(groups):
            total = dtable[g]
            for k in range(BATCH):
                i = b * BATCH + k
                gp = gp_s[i, g]
                prob = prob_in[i, g]
                ds = prob * (gp - jnp.sum(gp * prob, 0, keepdims=True))
                total = total + ds
                raw = padded(ds * scale).astype(bf16)
                low_s[i, g] = raw
                turn_s[i, g] = turn(raw)
            dtable[g] = total
        return carry

    lax.fori_loop(0, CW // BATCH, first, 0)
    lax.fori_loop(0, CW // BATCH, second, 0)
    for i in range(CW):
        rows = slice(WTOK * i, WTOK * i + SLOT)
        for g in range(groups):
            q_bd = four(qkv_s[i, :, 128 * g : 128 * g + 128], hmask[...])
            k_bd = four(qkv_s[i, :, width + 128 * g : width + 128 * g + 128], hmask2[...])
            do_bd = four(gm_s[i, :, 128 * g : 128 * g + 128], hmask[...])
            pj[rows, 128 * g : 128 * g + 128] = nn(turn_s[i, g], k_bd)
            pj[rows, width + 128 * g : width + 128 * g + 128] = nn(low_s[i, g], q_bd)
            pj[rows, 2 * width + 128 * g : 2 * width + 128 * g + 128] = nn(padded(prob_in[i, g]).astype(bf16), do_bd)
    dproj = pj[:CR, :].astype(bf16)
    dproj_out[...] = dproj
    x = tok[...].astype(f32)
    xhat, _ = norm_stats(x)
    low = (xhat * vec[0:1] + vec[1:2]).astype(bf16)
    low_t = jnp.concatenate([low.T, jnp.ones((16, CR), bf16)], 0)
    for j in range(3):
        outer = nn(low_t, dproj[:, width * j : width * j + width])
        dwq[j] += outer[:width]
        dext[j] += outer[width : width + 8]

    @pl.when(step == steps - 1)
    def _():
        rows = [None, None, None, None, dvec2[3], dvec2[0], dvec2[1], dvec2[2]]
        for i, part in enumerate(rows):
            if part is not None:
                misc[i : i + 1, :] = jnp.sum(part, 0, keepdims=True)
        misc[0:2, :] = jnp.zeros((2, width), f32)
        misc[2:3, :] = dext[0, 0:1, :]
        misc[3:4, :] = dext[2, 0:1, :]
        for i in range(dhid.shape[1] // width):
            misc[8 + i : 9 + i, :] = dhid[0:1, width * i : width * i + width]
        lane = lax.broadcasted_iota(jnp.int32, (1, width), 1)
        line = jnp.zeros((1, width), f32)
        for i, part in enumerate((stats[0], stats[1], dvec2[4])):
            line = jnp.where(lane == i, jnp.sum(part), line)
        misc[12:13, :] = jnp.where(lane == 3, jnp.sum(stats[2]) / 128.0, line)
        misc[13:16, :] = jnp.zeros((3, width), f32)
        flat[...] = jnp.zeros_like(flat)
        for g in range(groups):
            for k in range(WTOK):
                line = dtable[g, k : k + 1, :]
                for h in range(HG):
                    flat[HG * g + h : HG * g + h + 1, SLOT * k : SLOT * k + SLOT] = line[:, SLOT * h : SLOT * h + SLOT]
        rest_f = flat[...]
        total = jnp.zeros((16, 256), f32)
        for _ in range(3):
            part = rest_f.astype(bf16)
            total += nn(part, hot[...])
            rest_f = rest_f - part.astype(f32)
        misc[16:32, :] = jnp.zeros((16, width), f32)
        misc[16:32, :256] = total
        if comm[0]:
            for c in stages[-1][1]:
                c.wait()
            stages[-1][2]()


def sds(shape, dt):
    return jax.ShapeDtypeStruct(shape, dt)


def whole(a):
    nd = len(a.shape)
    return pl.BlockSpec(a.shape, lambda *_: (0,) * nd, pipeline_mode=pl.Buffered(1))


def whole_out(a):
    nd = len(a.shape)
    return pl.BlockSpec(a.shape, lambda *_: (0,) * nd)


def by_step(a, steps):
    nd = len(a.shape)
    return pl.BlockSpec((a.shape[0] // steps,) + tuple(a.shape[1:]), lambda c, *_: (c,) + (0,) * (nd - 1))


def run(body, steps, scalars, stepped, wholes, out_stepped, out_wholes, scratch, flops, collective_id=None):
    smem = pl.BlockSpec(memory_space=pltpu.SMEM)
    params = dict(vmem_limit_bytes=62 * 1024 * 1024)
    if collective_id is not None:
        params.update(collective_id=collective_id, has_side_effects=True)
    return pl.pallas_call(
        body, grid=(steps,),
        in_specs=[smem] * len(scalars) + [by_step(a, steps) for a in stepped] + wholes[1],
        out_specs=[by_step(a, steps) for a in out_stepped] + [whole_out(a) for a in out_wholes],
        out_shape=list(out_stepped) + list(out_wholes), scratch_shapes=scratch,
        compiler_params=pltpu.CompilerParams(**params),
        cost_estimate=pl.CostEstimate(flops=flops, bytes_accessed=20000000, transcendentals=0),
    )(*scalars, *stepped, *wholes[0])


def wholes_of(*arrays):
    return (arrays, [whole(a) for a in arrays])


def loop_rows(total, body):
    size = next(n for n in (96, 64, 48, 32, 16) if total % n == 0)
    lax.fori_loop(0, total // size, lambda i, c: (body(pl.multiple_of(i * size, size), size), c)[1], 0)


def attn_chains(wide_n, half):
    rest = list(range(1, wide_n.bit_length() - 1))
    turned = rest[len(rest) // 2 :] + rest[: len(rest) // 2]
    chains, start = [], 0
    while start < half:
        sizes = [min(64, half - start)]
        for _ in rest:
            sizes.append(sizes[-1] // 2 if sizes[-1] % 32 == 0 else sizes[-1])
        chains.append((start, turned if len(chains) % 2 else rest, sizes))
        start += sizes[0]
    return chains


def reduce_all(wide_n, narrow_n, share, mine_ref, q_ref, o_ref, s_ref, vec, dproj, tok, attn_w, gm_out, gt_out, s_out, part_out,
               proj_s, tok_s, part_s, wide_w, wq, dvec, own_sem, recv0, acct, gm, gt, sbuf, srecv, szrecv, *rest):
    bufs = list(rest[:-2])
    links = Links(wide_n, narrow_n, *rest[-2:])
    bit, me_n, peer = links.bit, links.n, links.peer
    steps = links.bits - 1
    width = q_ref.shape[1]
    blocks = proj_s.shape[0]
    at_block = [pl.ds(CR * b, CR) for b in range(blocks)]
    from_hbm = [pltpu.make_async_copy(attn_w.at[:, pl.ds(0, 3 * width)], wide_w, own_sem.at[0])]
    for b in range(blocks):
        from_hbm.append(pltpu.make_async_copy(dproj.at[at_block[b], :], proj_s.at[b], own_sem.at[1 + 2 * b]))
        from_hbm.append(pltpu.make_async_copy(tok.at[at_block[b], :], tok_s.at[b], own_sem.at[2 + 2 * b]))
    to_hbm = [pltpu.make_async_copy(part_s.at[b], part_out.at[at_block[b], :], own_sem.at[1 + 2 * blocks + b]) for b in range(blocks)]
    for c in from_hbm:
        c.start()
    links.barrier()
    ht = acct.shape[1]
    away, keep = (1 - bit[0]) * ht, bit[0] * ht

    def rows_at(at, size):
        return pl.ds(pl.multiple_of(at, 16), size)

    def go(copies):
        for c in copies:
            c.start()

    def come(copies):
        for c in copies:
            c.wait_recv()

    def attn_chain(start, order, sizes):
        copies = []
        for n in range(narrow_n):
            flat = n * share
            src, off = (q_ref, flat) if flat < q_ref.shape[0] else (o_ref, flat - q_ref.shape[0])
            copies.append(links.copy(src.at[rows_at(off + away + start, sizes[0]), :],
                                     recv0.at[n, pl.ds(start, sizes[0]), :], links.along(0)))
        go(copies)
        yield
        come(copies)
        for n in range(narrow_n):
            flat = n * share
            src, off = (q_ref, flat) if flat < q_ref.shape[0] else (o_ref, flat - q_ref.shape[0])
            def add0(i, size):
                acct[n, pl.ds(start + i, size), :] = (src[rows_at(off + keep + start + i, size), :]
                                                      + recv0[n, pl.ds(start + i, size), :])
            loop_rows(sizes[0], add0)
        here = start
        trail = []
        for s in range(steps):
            b, size = order[s], sizes[s + 1]
            halves = size < sizes[s]
            send, recv = bufs.pop(0), bufs.pop(0)
            out_at, in_at = (here + (1 - bit[b]) * size, here + bit[b] * size) if halves else (here, here)
            for n in range(narrow_n):
                def pack(i, k):
                    send[n, pl.ds(i, k), :] = acct[n, rows_at(out_at + i, k), :].astype(bf16)
                loop_rows(size, pack)
            c = links.copy(send, recv, links.along(b))
            c.start()
            yield
            c.wait_recv()
            for n in range(narrow_n):
                def add(i, k):
                    own = acct[n, rows_at(in_at + i, k), :] if halves else send[n, pl.ds(i, k), :].astype(f32)
                    acct[n, rows_at(in_at + i, k), :] = own + recv[n, pl.ds(i, k), :].astype(f32)
                loop_rows(size, add)
            here = in_at
            trail.append((b, in_at, size, halves))
        size = sizes[-1]
        zsend, zrecv = bufs.pop(0), bufs.pop(0)
        copies = []
        for i, n in enumerate(peer):
            def pack(r, k):
                zsend[i, pl.ds(r, k), :] = acct[n, rows_at(here + r, k), :].astype(bf16)
            loop_rows(size, pack)
            copies.append(links.copy(zsend.at[i], zrecv.at[i], links.over(n)))
            copies[-1].start()
        yield
        come(copies)
        def add(r, k):
            value = acct[me_n, rows_at(here + r, k), :]
            for i in range(narrow_n - 1):
                value = value + zrecv[i, pl.ds(r, k), :].astype(f32)
            gt[me_n, rows_at(keep + here + r, k), :] = value.astype(bf16)
        loop_rows(size, add)
        part = gt.at[me_n, rows_at(keep + here, size), :]
        copies = [links.copy(part, part, links.over(n)) for n in peer]
        go(copies)
        yield
        come(copies)
        for b, at, size, halves in reversed(trail):
            if halves:
                part = gt.at[:, rows_at(keep + at, size), :]
                c = links.copy(part, part, links.along(b))
                c.start()
                yield
                c.wait_recv()
        part = gt.at[:, rows_at(keep + start, sizes[0]), :]
        c = links.copy(part, part, links.along(0))
        c.start()
        yield
        c.wait_recv()

    def small_chain():
        yield
        from_hbm[0].wait()
        wq[...] = wide_w[...].astype(bf16)
        dvec[...] = jnp.zeros_like(dvec)
        for b in range(blocks):
            from_hbm[1 + 2 * b].wait()
            from_hbm[2 + 2 * b].wait()
            xhat, inverse = norm_stats(tok_s[b].astype(f32))
            grad_normed = nt(proj_s[b], wq[...])
            dvec[0] += fold_rows(grad_normed * xhat)
            dvec[1] += fold_rows(grad_normed)
            part_s[b] = norm_grad(grad_normed, xhat, inverse, vec[0:1]).astype(bf16)
            to_hbm[b].start()
            yield
        sbuf[0] = s_ref[...]
        for i in range(2):
            sbuf[0, i : i + 1, :] = jnp.sum(dvec[i], 0, keepdims=True)
        for b in range(links.bits):
            c = links.copy(sbuf.at[b], srecv.at[b], links.along(b))
            c.start()
            yield
            c.wait_recv()
            sbuf[b + 1] = sbuf[b] + srecv[b]
        copies = [links.copy(sbuf.at[links.bits], szrecv.at[i], links.over(n)) for i, n in enumerate(peer)]
        go(copies)
        yield
        come(copies)
        own = sbuf[links.bits]
        total = jnp.zeros_like(own)
        for n in range(narrow_n):
            behind = lax.rem(me_n + narrow_n - n, narrow_n)
            value = own
            for i in range(1, narrow_n):
                value = jnp.where(behind == i, szrecv[i - 1], value)
            total = total + value
        s_out[...] = total

    def mlp_chain():
        plan, streams, sizes = scatter_sizes(wide_n, share)
        trail, base = [], 0
        for st, (here, _) in streams.items():
            for s in range(steps):
                b, size = plan[st][s], sizes[st][s + 1]
                halves = size < sizes[st][s]
                here = here + bit[b] * size if halves else here
                trail.append((s, b, here, size, halves))
            size = sizes[st][-1]
            gm[rows_at(bit[0] * share + here, size), :] = mine_ref[base : base + size, :]
            base += size
        yield
        yield
        for s in reversed(range(steps)):
            copies = []
            for s2, b, at, size, halves in trail:
                if s2 == s and halves:
                    part = gm.at[rows_at(bit[0] * share + at, size), :]
                    copies.append(links.copy(part, part, links.along(b)))
            go(copies)
            yield
            come(copies)
        part = gm.at[rows_at(bit[0] * share, share), :]
        c = links.copy(part, part, links.along(0))
        c.start()
        yield
        c.wait_recv()
        gm_out[...] = gm[...]

    going = [attn_chain(*c) for c in attn_chains(wide_n, ht)] + [mlp_chain(), small_chain()]
    while going:
        still = []
        for chain in going:
            try:
                next(chain)
                still.append(chain)
            except StopIteration:
                pass
        going = still
    gt_out[...] = gt[...]
    for c in links.all:
        c.wait_send()
    for c in to_hbm:
        c.wait()


def reduce_call(wide_n, narrow_n, share, mine, dq, do, misc, vec, dproj, tok, attn_w):
    width = mine.shape[1]
    rows = tok.shape[0]
    blocks = rows // CR
    ht = share // 2
    n_bits = wide_n.bit_length() - 1
    scratch = [
        pltpu.VMEM((blocks, CR, 3 * width), bf16), pltpu.VMEM((blocks, CR, width), bf16), pltpu.VMEM((blocks, CR, width), bf16),
        pltpu.VMEM((width, 3 * width), f32), pltpu.VMEM((width, 3 * width), bf16), pltpu.VMEM((2, 8, width), f32),
        pltpu.SemaphoreType.DMA((1 + 3 * blocks,)),
        pltpu.VMEM((narrow_n, ht, width), f32), pltpu.VMEM((narrow_n, ht, width), f32),
        pltpu.VMEM((2 * share, width), bf16), pltpu.VMEM((narrow_n, share, width), bf16),
        pltpu.VMEM((n_bits + 1,) + misc.shape, f32), pltpu.VMEM((n_bits,) + misc.shape, f32),
        pltpu.VMEM((narrow_n - 1,) + misc.shape, f32)]
    order = order_of_bufs(wide_n, narrow_n, ht)
    scratch += [pltpu.VMEM((lead, rows, width), bf16) for lead, rows in order for _ in range(2)]
    chains = len(attn_chains(wide_n, ht))
    copies = chains * (narrow_n + 2 * n_bits + 2 * narrow_n) + 4 * n_bits + narrow_n
    scratch += [pltpu.SemaphoreType.DMA((copies,)), pltpu.SemaphoreType.DMA((copies,))]
    vmem = pl.BlockSpec(memory_space=pltpu.VMEM)
    return pl.pallas_call(
        functools.partial(reduce_all, wide_n, narrow_n, share),
        out_shape=[sds((2 * share, width), bf16), sds((narrow_n, share, width), bf16), sds(misc.shape, f32),
                   sds((rows, width), bf16)],
        in_specs=[vmem] * 5 + [pl.BlockSpec(memory_space=pl.ANY)] * 3, out_specs=[vmem] * 3 + [pl.BlockSpec(memory_space=pl.ANY)], scratch_shapes=scratch,
        compiler_params=pltpu.CompilerParams(collective_id=0, has_side_effects=True, vmem_limit_bytes=60 * 1024 * 1024),
    )(mine, dq, do, misc, vec, dproj, tok, attn_w)


def order_of_bufs(wide_n, narrow_n, ht):
    chains = attn_chains(wide_n, ht)
    out = []
    for s in range(wide_n.bit_length() - 2):
        out += [(narrow_n, sizes[s + 1]) for _, _, sizes in chains]
    return out + [(narrow_n - 1, sizes[-1]) for _, _, sizes in chains]


def adam_kernel(narrow_ref, grad_stream, part, gt, gm, misc, aw, af, as_, mw, mf, ms, tw, tf, ts, vw, vf, vs, bw, bf, bs,
                input_grad, rms, an, al, afn, asn, mn, ml, mfn, msn, tn_, tfn, tsn, vn, vfn, vsn, bn, bfn, bsn):
    def put(new, w, g, m, v, rate, decay, low=None):
        out = adam_step(w, g, m, v, rate, decay)
        for ref, value in zip(new, out):
            ref[...] = value.reshape(ref.shape)
        if low is not None:
            low[...] = out[0].astype(bf16).reshape(low.shape)

    input_grad[...] = grad_stream[...] + part[...].astype(f32)
    put((an, afn, asn), aw[...], jnp.concatenate([gt[j].astype(f32) for j in range(4)], 1), af[...], as_[...], 0.02, 0.05, al)
    put((mn, mfn, msn), mw[0], gm[0].astype(f32), mf[0], ms[0], 0.02, 0.05, ml)

    @pl.when(pl.program_id(0) == 0)
    def _():
        put((vn, vfn, vsn), vw[...], misc[0:8, :], vf[...], vs[...], 0.3, 0.0)
        stats = misc[12:13, :]
        for i in range(3):
            ratio = jnp.sqrt(stats[:, i : i + 1] / (stats[:, 3:4] * misc.shape[1]))
            rms[i] = ratio[0, 0]
        n = narrow_ref[0]
        share = bw.shape[0]
        grad = jnp.zeros((1, share), f32)
        per = misc.shape[1] // share
        for i in range(4):
            for k in range(per):
                grad = jnp.where(n == per * i + k, misc[8 + i : 9 + i, share * k : share * k + share], grad)
        put((bn, bfn, bsn), bw[...], grad.reshape(share), bf[...], bs[...], 0.1, 0.0)
        heads, count = tw.shape
        put((tn_, tfn, tsn), tw[...], misc[16 : 16 + heads, :count], tf[...], ts[...], 0.3, 0.0)


def adam_call(narrow, grad_stream, part, gt, gm, misc, attn, mlp, table, vec, bias):
    width = gm.shape[1]
    share = mlp[0].shape[1]
    gt = gt.reshape(4, width, width)
    cuts = 4 if grad_stream.shape[0] % 64 == 0 else 2
    some = by_step(grad_stream, cuts)
    quarter = 2 * share // cuts
    rows = width // cuts
    gm = gm.reshape(cuts, quarter, width)
    mlp = [a.reshape(cuts, quarter, width) for a in mlp]
    line = pl.BlockSpec((rows, attn[0].shape[1]), lambda j, *_: (j, 0))
    lead = pl.BlockSpec((1, quarter, width), lambda j, *_: (j, 0, 0))
    split = pl.BlockSpec((4, rows, width), lambda j, *_: (0, j, 0))
    smalls = list(table) + list(vec) + list(bias)
    args = [grad_stream, part, gt, gm, misc] + list(attn) + mlp + smalls
    in_specs = [some, some, split, lead, whole(misc)] + [line] * 3 + [lead] * 3 + [whole(a) for a in smalls]
    three = lambda a: [sds(a.shape, f32)] * 3
    outs = [sds(grad_stream.shape, f32), sds((3,), f32), sds(attn[0].shape, f32), sds(attn[0].shape, bf16)] + [sds(attn[0].shape, f32)] * 2
    outs += [sds(mlp[0].shape, f32), sds(mlp[0].shape, bf16)] + [sds(mlp[0].shape, f32)] * 2
    outs += three(table[0]) + three(vec[0]) + three(bias[0])
    out_specs = [some, pl.BlockSpec(memory_space=pltpu.SMEM)] + [line] * 4 + [lead] * 4
    out_specs += [whole_out(a) for a in smalls]
    r = pl.pallas_call(
        adam_kernel,
        grid_spec=pltpu.PrefetchScalarGridSpec(num_scalar_prefetch=1, grid=(cuts,), in_specs=in_specs, out_specs=out_specs),
        out_shape=outs,
        compiler_params=pltpu.CompilerParams(vmem_limit_bytes=60 * 1024 * 1024),
    )(narrow, *args)
    full = (2, share, width)
    grad, r = r[0], r[1:]
    return [grad, r[0], *r[1:5], *[a.T for a in r[9:12]], *r[12:15], *[a.reshape(full) for a in r[5:9]], *r[15:18]]


def bias_layout(rel_table):
    pos = np.arange(WTOK)
    row, col = pos // WIN, pos % WIN
    off = (row[:, None] - row[None, :] + WIN - 1) * (2 * WIN - 1) + col[:, None] - col[None, :] + WIN - 1
    full = np.full((KR, SLOT), -1, np.int32)
    full[:WTOK, :WTOK] = off.T
    return full


def block(tokens, grid_sizes, cotangent, attn_weight, rel_table, vectors, mlp_weight, mlp_bias, narrow, wide_n, narrow_n, linked=True):
    rows, width = tokens.shape
    wins = rows // WTOK
    steps = wins // CW
    heads = rel_table.shape[0]
    groups = heads // HG
    share = mlp_weight.shape[1]
    hidden = share * narrow_n
    n_bits = wide_n.bit_length() - 1
    comm = (linked, steps)
    unit = rows * width * width
    hot = np.zeros((KR * SLOT, 256), np.float32)
    lay = bias_layout(rel_table).reshape(-1)
    hot[np.arange(KR * SLOT)[lay >= 0], lay[lay >= 0]] = 1.0
    hot = jnp.asarray(hot, bf16)
    mask = head_mask(width // heads)
    mask2 = mask.reshape(HG, SLOT, -1)[np.array([0, 2, 1, 3])].reshape(mask.shape)
    mask, mask2 = jnp.asarray(mask, bf16), jnp.asarray(mask2, bf16)
    rinfo, kinfo = jnp.asarray(row_info()), jnp.asarray(key_info())
    scal = (narrow, grid_sizes)
    pad = CR + 16
    copies = 3 * (narrow_n - 1) + 3 * 2 * (narrow_n - 1) + 4
    sem = [pltpu.SemaphoreType.DMA((copies,)), pltpu.SemaphoreType.DMA((copies,))] if linked else []
    sides = pltpu.VMEM((CR, 128), f32)
    table_s = pltpu.VMEM((groups, KR, HG * SLOT), f32)
    flat = pltpu.VMEM((16, KR * SLOT), f32)
    turned = pltpu.VMEM((CW, groups, SLOT, HG * SLOT), bf16)
    qkv, prob, mixed, stream, stats, gw, tails = run(
        functools.partial(attn_forward, wide_n, narrow_n, comm), steps, scal, (tokens,),
        wholes_of(attn_weight, mlp_weight, mlp_bias, vectors, rel_table, hot, rinfo, kinfo, mask, mask2),
        [sds((wins, SLOT, 3 * width), bf16), sds((wins, groups, KR, HG * SLOT), f32), sds((rows, width), bf16), sds((rows, width), f32)],
        [sds((3, 8, width), f32), sds((narrow_n, 2 * share, width), bf16), sds((narrow_n, 8, width), f32)],
        [pltpu.VMEM((width, 4 * width), bf16), pltpu.VMEM((pad, 3 * width), f32), pltpu.VMEM((pad, width), f32), turned,
         table_s, pltpu.VMEM((16, 256), f32), flat, sides,
         pltpu.VMEM((2 * share, width), bf16), pltpu.VMEM((8, width), f32),
         pltpu.VMEM((narrow_n, 2 * share, width), bf16), pltpu.VMEM((narrow_n, 8, width), f32)] + sem,
        12 * unit, 1 if linked else None)
    out_proj = pl.BlockSpec((width, width), lambda *_: (0, 3), pipeline_mode=pl.Buffered(1))
    fixed = (attn_weight, gw, tails, vectors, rinfo)
    outputs, grad_stream, gm, dmlp, dwo, dhid, dvec2 = run(
        functools.partial(feed_forward, TILE), steps, scal, (cotangent, mixed, stream),
        (fixed, [out_proj] + [whole(a) for a in fixed[1:]]),
        [sds((rows, width), bf16), sds((rows, width), f32), sds((wins, SLOT, width), bf16)],
        [sds((narrow_n, 2 * share, width), f32), sds((width, width), f32), sds((8, hidden), f32), sds((5, 8, width), f32)],
        [pltpu.VMEM((width, width), bf16), pltpu.VMEM((hidden, width), bf16), pltpu.VMEM((hidden, width), bf16),
         pltpu.VMEM((1, hidden), f32), pltpu.VMEM((width, hidden), f32), pltpu.VMEM((width, hidden), f32),
         pltpu.VMEM((pad, width), f32), sides],
        52 * unit)
    _, streams, sizes = scatter_sizes(wide_n, share)
    last = sum(sizes[st][-1] for st in streams)
    bufs = []
    for s in range(n_bits - 1):
        for st in streams:
            bufs += [pltpu.VMEM((narrow_n, sizes[st][s + 1], width), bf16)] * 2
    copies = 1 + 2 * n_bits + narrow_n
    sem = [pltpu.SemaphoreType.DMA((copies,)), pltpu.SemaphoreType.DMA((copies,))] if linked else []
    dproj, dwq, misc, mine = run(
        functools.partial(attn_backward, wide_n, narrow_n, comm), steps, (), (tokens, qkv, prob, gm),
        wholes_of(vectors, hot, mask, mask2, dmlp, dhid, dvec2, stats),
        [sds((rows, 3 * width), bf16)],
        [sds((3, width, width), f32), sds((32, width), f32), sds((last, width), bf16)],
        [pltpu.VMEM((pad, 3 * width), f32),
         pltpu.VMEM((CW, groups, KR, HG * SLOT), f32), turned, turned, pltpu.VMEM((3, 8, width), f32), table_s, flat,
         pltpu.VMEM((narrow_n, share, width), bf16), pltpu.VMEM((narrow_n, share, width), bf16),
         pltpu.VMEM((narrow_n, share, width), f32), pltpu.VMEM((narrow_n - 1, last, width), bf16),
         pltpu.VMEM((narrow_n - 1, last, width), bf16)] + bufs + sem,
        20 * unit, 2 if linked else None)
    return outputs, grad_stream, dmlp, dwq, dwo, misc, mine, dproj


TILE = 768


def adam_step(weight, gradient, first_old, second_old, rate_value, decay_value):
    first_new = beta_one * first_old + (1.0 - beta_one) * gradient
    second_new = beta_two * second_old + (1.0 - beta_two) * gradient * gradient
    fix_one = 1.0 - beta_one**STEP
    fix_two = 1.0 - beta_two**STEP
    update = rate_value * (first_new / fix_one) / (jnp.sqrt(second_new / fix_two) + adam_eps)
    return (weight - update - rate_value * decay_value * weight, first_new, second_new)


def shards(wide_n, narrow_n, tokens, grid_sizes, cotangent, attn_weight, attn_first, attn_second, rel_table, table_first,
           table_second, vectors, vector_first, vector_second, mlp_weight, mlp_first, mlp_second, mlp_bias, bias_first,
           bias_second):
    width = tokens.shape[1]
    narrow = lax.axis_index("narrow").reshape(1).astype(jnp.int32)
    outputs, grad_stream, _, dwq, dwo, misc, mine, dproj = block(
        tokens, grid_sizes, cotangent, attn_weight, rel_table.T, vectors, mlp_weight, mlp_bias, narrow, wide_n, narrow_n)
    gm, gt, misc, part = reduce_call(wide_n, narrow_n, mlp_weight.shape[1], mine, dwq.reshape(3 * width, width), dwo, misc,
                                     vectors, dproj, tokens, attn_weight)
    new = adam_call(narrow, grad_stream, part, gt, gm, misc, (attn_weight, attn_first, attn_second), (mlp_weight, mlp_first, mlp_second),
                    (rel_table.T, table_first.T, table_second.T), (vectors, vector_first, vector_second),
                    (mlp_bias, bias_first, bias_second))
    return (outputs, *new)


def solution(mesh):
    rows = P(("wide", "narrow"), None)
    split = P(None, "narrow", None)
    return jax.shard_map(
        functools.partial(shards, mesh.shape["wide"], mesh.shape["narrow"]), mesh=mesh,
        in_specs=(rows, P("wide"), rows) + (P(),) * 9 + (split,) * 3 + (P("narrow"),) * 3,
        out_specs=(rows, rows) + (P(),) * 11 + (split,) * 4 + (P("narrow"),) * 3,
        check_vma=False)
```

```python
import functools

import jax
import jax.numpy as jnp
import numpy as np
from jax import lax
from jax.sharding import PartitionSpec as P
from jax.experimental import pallas as pl
from jax.experimental.pallas import tpu as pltpu

WIN = 7
WTOK = 49
WPI = 16
IMG_W = 16
STEP = 5
CW = 16
CR = CW * WTOK
EVEN = CR // 256 * 256
ODD = 128
SLOT = 64
KR = 56
HG = 4
LOG2E = 1.4426950408889634

norm_eps = 1e-05
beta_one = 0.5
beta_two = 0.5
adam_eps = 1e-08
highest = lax.Precision.HIGHEST
f32 = jnp.float32
bf16 = jnp.bfloat16


def nn(a, b):
    return lax.dot_general(a, b, (((1,), (0,)), ((), ())), preferred_element_type=f32)


def nt(a, b):
    return lax.dot_general(a, b, (((1,), (1,)), ((), ())), preferred_element_type=f32)


def tn(a, b):
    return lax.dot_general(a, b, (((0,), (0,)), ((), ())), preferred_element_type=f32)


def row_info():
    r = np.arange(CR)
    win = r // WTOK
    p = r % WTOK
    info = np.stack([win, p // WIN, p % WIN]).astype(np.float32)
    info[1, win >= CW] = 1000.0
    return np.ascontiguousarray(np.broadcast_to(info[:, :, None], (3, CR, 128)))


def key_info():
    p = np.arange(KR)
    info = np.stack([p // WIN, p % WIN]).astype(np.float32)
    return np.ascontiguousarray(np.broadcast_to(info[:, :, None], (2, KR, 128)))


def head_mask(head_size):
    row = np.arange(HG * SLOT)
    lane = np.arange(HG * head_size)
    return (((row // SLOT)[:, None] == (lane // head_size)[None, :]) & ((row % SLOT) < WTOK)[:, None]).astype(np.float32)


def fold_rows(t):
    return jnp.sum(t.reshape(t.shape[0] // 8, 8, t.shape[1]), 0)


def rep(v, n):
    return jnp.concatenate([v] * n, 1)


def fill_sides(sides, info, side_s):
    win = info[0]
    value = jnp.zeros_like(win)
    for i in range(CW):
        value = jnp.where(win == float(i), sides[i].astype(f32), value)
    side_s[...] = value


def corner(narrow, step, steps):
    u = WPI - 1 - (narrow * steps + step)
    return (WIN * (u // 4)).astype(f32), (WIN * lax.rem(u, 4)).astype(f32)


def chunk_valid(info, side_s, top, left):
    side = side_s[...]
    return jnp.where((info[1] + top < side) & (info[2] + left < side), 1.0, 0.0)


def norm_stats(x):
    mean = jnp.mean(x, -1, keepdims=True)
    centred = x - mean
    inverse = lax.rsqrt(jnp.mean(centred * centred, -1, keepdims=True) + norm_eps)
    return centred * inverse, inverse


def norm_grad(g, xhat, inverse, gain):
    scaled = g * gain
    m1 = jnp.mean(scaled, -1, keepdims=True)
    m2 = jnp.mean(scaled * xhat, -1, keepdims=True)
    return inverse * (scaled - m1 - xhat * m2)


class Links:
    def __init__(self, wide_n, narrow_n, send_sem, recv_sem):
        self.w = lax.axis_index("wide")
        self.n = lax.axis_index("narrow")
        self.bits = wide_n.bit_length() - 1
        self.bit = [lax.rem(self.w // (1 << b), 2) for b in range(self.bits)]
        self.mate = [self.w + (1 - 2 * self.bit[b]) * (1 << b) for b in range(self.bits)]
        self.peer = [lax.rem(self.n + s, narrow_n) for s in range(1, narrow_n)]
        self.send_sem, self.recv_sem = send_sem, recv_sem
        self.used = 0
        self.all = []

    def copy(self, src, dst, device):
        k = self.used
        self.used += 1
        c = pltpu.make_async_remote_copy(
            src_ref=src, dst_ref=dst, send_sem=self.send_sem.at[k], recv_sem=self.recv_sem.at[k],
            device_id=device, device_id_type=pl.DeviceIdType.MESH)
        self.all.append(c)
        return c

    def along(self, b):
        return (self.mate[b], self.n)

    def over(self, n):
        return (self.w, n)

    def barrier(self):
        sem = pltpu.get_barrier_semaphore()
        for b in range(self.bits):
            pl.semaphore_signal(sem, inc=1, device_id=self.along(b), device_id_type=pl.DeviceIdType.MESH)
        for n in self.peer:
            pl.semaphore_signal(sem, inc=1, device_id=self.over(n), device_id_type=pl.DeviceIdType.MESH)
        pl.semaphore_wait(sem, self.bits + len(self.peer))


def gather_cuts(wide_n, rows):
    bits = list(range(min(3, wide_n.bit_length() - 1)))
    first = rows // 256 * 128
    return [(0, first, bits[1:] + bits[:1]), (first, rows - first, bits[1:][::-1] + bits[:1])]


def gather_plan(links, wide_n, own, tail_own, all_w, all_tail):
    narrow_n, rows, _ = all_w.shape
    streams = gather_cuts(wide_n, rows)
    stages = [[]]
    place, sizes = [], []
    for start, size, order in streams:
        piece = size >> len(order)
        off = 0
        for k, b in enumerate(order):
            off = off + links.bit[b] * (piece << k)
        place.append(start + off)
        sizes.append(piece)
    for n in links.peer:
        stages[0].append(links.copy(tail_own, all_tail.at[links.n], links.over(n)))
        for at, size in zip(place, sizes):
            here = pl.ds(pl.multiple_of(at, 16), size)
            stages[0].append(links.copy(own.at[here, :], all_w.at[links.n, here, :], links.over(n)))
    for k in range(len(streams[0][2])):
        stage = []
        for s, (start, size, order) in enumerate(streams):
            here = pl.ds(pl.multiple_of(place[s], 16), sizes[s])
            for n in links.peer:
                part = all_w.at[n, here, :]
                stage.append(links.copy(part, part, links.along(order[k])))
            place[s] = place[s] - links.bit[order[k]] * sizes[s]
            sizes[s] = sizes[s] * 2
        stages.append(stage)
    return stages


def run_stages(stages, step, steps):
    for k, stage in enumerate(stages):
        @pl.when(step == min(k, steps - 1))
        def _():
            if k:
                for c in stages[k - 1]:
                    c.wait()
            for c in stage:
                c.start()


def expand_table(table, hot, wide_t, flat, bias):
    heads, count = table.shape
    wide_t[...] = jnp.zeros_like(wide_t)
    wide_t[:heads, :count] = table[...] * LOG2E
    rest = wide_t[...]
    total = jnp.zeros((16, hot.shape[0]), f32)
    for _ in range(3):
        part = rest.astype(bf16)
        total += nt(part, hot[...])
        rest = rest - part.astype(f32)
    flat[...] = total
    bias[...] = jnp.full(bias.shape, -1e30, f32)
    for g in range(heads // HG):
        for k in range(WTOK):
            for h in range(HG):
                bias[g, k : k + 1, SLOT * h : SLOT * h + SLOT] = flat[HG * g + h : HG * g + h + 1, SLOT * k : SLOT * k + SLOT]


def turn(t):
    t = jnp.concatenate([t[:, :128], t[:, 128:]], 0).T
    return jnp.concatenate([t[:SLOT], t[SLOT:]], 1)


def padded(t):
    return jnp.concatenate([t, jnp.zeros((SLOT - KR, t.shape[1]), f32)], 0)


def four(t, mask):
    return jnp.concatenate([t] * HG, 0) * mask


BATCH = 16


def attn_forward(wide_n, narrow_n, comm, narrow_ref, sides, tok, attn_w, mlp_w, mlp_b, vec, table, hot, rinfo, kinfo, hmask, hmask2,
                 qkv_s, prob_out, mixed_out, stream_out, stats, gw_out, tail_out,
                 wq, pj, mx, turn_s, bias, wide_t, flat, side_s, own, tail_own, gw, tails, wide_w, hot_s, load_sem, *sems):
    step = pl.program_id(0)
    steps = pl.num_programs(0)
    static_steps = comm[1]
    width = tok.shape[1]
    groups = width // 128
    scale = 32 ** (-0.5)
    narrow = narrow_ref[0]
    share = mlp_w.shape[1]

    loads = [pltpu.make_async_copy(attn_w, wide_w, load_sem.at[0]), pltpu.make_async_copy(hot, hot_s, load_sem.at[1])]

    @pl.when(step == 0)
    def _():
        for c in loads:
            c.start()
        for j in range(2):
            own[share * j : share * j + share, :] = mlp_w[j].astype(bf16)
        tail_own[...] = jnp.zeros_like(tail_own)
        rest = mlp_b[...].reshape(1, share)
        for i in range(3):
            part = rest.astype(bf16).astype(f32)
            tail_own[i : i + 1, :share] = part
            rest = rest - part
        if comm[0]:
            gw[lax.axis_index("narrow")] = own[...]
            tails[lax.axis_index("narrow")] = tail_own[...]
        else:
            for n in range(narrow_n):
                gw[n] = own[...]
                tails[n] = tail_own[...]

    if comm[0]:
        links = Links(wide_n, narrow_n, *sems)

        @pl.when(step == 0)
        def _():
            links.barrier()

        stages = gather_plan(links, wide_n, own, tail_own, gw, tails)
        run_stages(stages, step, static_steps)

    @pl.when(step == 0)
    def _():
        fill_sides(sides, rinfo, side_s)
        for c in loads:
            c.wait()
        wq[...] = wide_w[...].astype(bf16)
        expand_table(table, hot_s, wide_t, flat, bias)
        for ref in (pj, mx, stats):
            ref[...] = jnp.zeros_like(ref)

    top, left = corner(narrow, step, static_steps)
    x = tok[...].astype(f32)
    valid = chunk_valid(rinfo, side_s, top, left)
    keep = rep(valid, groups)
    xhat, _ = norm_stats(x)
    low = (xhat * vec[0:1] + vec[1:2]).astype(bf16)
    pj[:CR, :width] = nn(low, wq[:, :width]) + vec[2:3]
    pj[:CR, width : 2 * width] = nn(low, wq[:, width : 2 * width])
    pj[:CR, 2 * width :] = nn(low, wq[:, 2 * width : 3 * width]) + vec[3:4]
    for i in range(CW):
        qkv_s[i] = pj[WTOK * i : WTOK * i + SLOT, :].astype(bf16)

    def score(b, carry):
        for k in range(BATCH):
            i = b * BATCH + k
            for g in range(groups):
                q_bd = four(qkv_s[i, :, 128 * g : 128 * g + 128], hmask[...])
                prob_out[i, g] = nt(qkv_s[i, :KR, width + 128 * g : width + 128 * g + 128], q_bd)
        return carry

    def soft(b, carry):
        for k in range(BATCH):
            i = b * BATCH + k
            side = sides[i].astype(f32)
            fill = jnp.where((kinfo[0] < side - top) & (kinfo[1] < side - left), 0.0, -10000.0 * LOG2E)
            fill = rep(fill, 2)
            for g in range(groups):
                s = prob_out[i, g] * (scale * LOG2E) + bias[g] + fill
                e = jnp.exp2(s - jnp.max(s, 0, keepdims=True))
                prob = e * (1.0 / jnp.sum(e, 0, keepdims=True))
                prob_out[i, g] = prob
                turn_s[i, g] = turn(padded(prob).astype(bf16))
        return carry

    lax.fori_loop(0, CW // BATCH, score, 0)
    lax.fori_loop(0, CW // BATCH, soft, 0)
    for i in range(CW):
        for g in range(groups):
            v_bd = four(qkv_s[i, :, 2 * width + 128 * g : 2 * width + 128 * g + 128], hmask2[...])
            mx[WTOK * i : WTOK * i + SLOT, 128 * g : 128 * g + 128] = nn(turn_s[i, g], v_bd)
    mixed = mx[:CR, :].astype(bf16)
    mixed_out[...] = mixed
    branch = (nn(mixed, wq[:, 3 * width :]) + vec[4:5]) * keep
    stream_out[...] = x + branch
    stats[0] += fold_rows(x * x * keep)
    stats[1] += fold_rows(branch * branch)
    stats[2, :, :128] += fold_rows(valid)

    @pl.when(step == steps - 1)
    def _():
        if comm[0]:
            for c in stages[-1]:
                c.wait()
        gw_out[...] = gw[...]
        tail_out[...] = tails[...]


def feed_forward(tile, narrow_ref, sides, cot, mixed_in, stream_in, attn_w, gw, tails, vec, rinfo,
                 out_ref, grad_stream_out, gm_s, dmlp, dwo, dhid, dvec,
                 wo, w1, w2, hb, dw1, dw2, mx, side_s, second_r, grad_r, pre_r, active_r, load_sem):
    step = pl.program_id(0)
    steps = pl.num_programs(0)
    width = cot.shape[1]
    groups = width // 128
    hidden = w1.shape[0]
    shards_n, twice, _ = gw.shape
    share = twice // 2
    loads = []
    for n in range(shards_n):
        for j, ref in enumerate((w1, w2)):
            loads.append(pltpu.make_async_copy(gw.at[n, pl.ds(share * j, share), :], ref.at[pl.ds(share * n, share), :],
                                               load_sem.at[2 * n + j]))

    @pl.when(step == 0)
    def _():
        for c in loads:
            c.start()
        wo[...] = attn_w[...].astype(bf16)
        for n in range(shards_n):
            three = tails[n]
            hb[:, share * n : share * n + share] = (three[0:1] + three[1:2] + three[2:3])[:, :share]
        fill_sides(sides, rinfo, side_s)
        for ref in (mx, dw1, dw2, dwo, dhid, dvec, second_r, grad_r, pre_r, active_r):
            ref[...] = jnp.zeros_like(ref)

    top, left = corner(narrow_ref[0], step, steps)
    keep = rep(chunk_valid(rinfo, side_s, top, left), groups)
    cotan = cot[...].astype(f32)
    stream = stream_in[...]
    xhat2, inverse2 = norm_stats(stream)
    second = (xhat2 * vec[5:6] + vec[6:7]).astype(bf16)
    kept_cot = cotan * keep
    grad_low = kept_cot.astype(bf16)
    second_t = jnp.concatenate([second[:EVEN].T, jnp.ones((16, EVEN), bf16)], 0)
    grad_t = grad_low[:EVEN].T
    odd = pl.ds(pl.multiple_of(step * (CR - EVEN), CR - EVEN), CR - EVEN)
    second_r[odd, :] = second[EVEN:]
    grad_r[odd, :] = grad_low[EVEN:]

    @pl.when(step == 0)
    def _():
        for c in loads:
            c.wait()

    mlp_out = jnp.zeros((CR, width), f32)
    grad_second = jnp.zeros((CR, width), f32)
    for t in range(hidden // tile):
        cols = slice(tile * t, tile * t + tile)
        pre = nt(second, w1[cols, :]) + hb[0:1, cols]
        square = pre * pre
        half = 0.5 * jnp.tanh(pre * (square * (0.7978845608028654 * 0.044715) + 0.7978845608028654)) + 0.5
        active = (pre * half).astype(bf16)
        slope = half + (pre * (half - half * half)) * (square * (6 * 0.7978845608028654 * 0.044715) + 2 * 0.7978845608028654)
        grad_pre = (nt(grad_low, w2[cols, :]) * slope).astype(bf16)
        mlp_out += nn(active, w2[cols, :])
        grad_second += nn(grad_pre, w1[cols, :])
        pre_r[odd, cols] = grad_pre[EVEN:]
        active_r[odd, cols] = active[EVEN:]
        outer = nn(second_t, grad_pre[:EVEN])
        dw1[:, cols] += outer[:width]
        dhid[:, cols] += outer[width : width + 8]
        dw2[:, cols] += nn(grad_t, active[:EVEN])
    branch = (mlp_out + vec[7:8]) * keep
    out_ref[...] = (stream + branch).astype(bf16)
    dvec[4] += fold_rows(branch * branch)
    dvec[0] += fold_rows(grad_second * xhat2)
    dvec[1] += fold_rows(grad_second)
    dvec[2] += fold_rows(kept_cot)
    grad_stream = cotan + norm_grad(grad_second, xhat2, inverse2, vec[5:6])
    grad_stream_out[...] = grad_stream
    grad_attn = grad_stream * keep
    dvec[3] += fold_rows(grad_attn)
    grad_attn_low = grad_attn.astype(bf16)
    dwo[...] += nn(mixed_in[...].T, grad_attn_low)
    mx[:CR, :] = nt(grad_attn_low, wo[...])
    for i in range(CW):
        gm_s[i] = mx[WTOK * i : WTOK * i + SLOT, :].astype(bf16)

    @pl.when(step == steps - 1)
    def _():
        rest_t = jnp.concatenate([second_r[...].T, jnp.ones((16, second_r.shape[0]), bf16)], 0)
        rest_g = grad_r[...].T
        for t in range(hidden // width):
            cols = slice(width * t, width * t + width)
            outer = nn(rest_t, pre_r[:, cols])
            dw1[:, cols] += outer[:width]
            dhid[:, cols] += outer[width : width + 8]
            dw2[:, cols] += nn(rest_g, active_r[:, cols])
        for j, ref in enumerate((dw1, dw2)):
            for t in range(hidden // width):
                turned = ref[:, width * t : width * t + width].T
                for k in range(width // share):
                    n = (width * t) // share + k
                    dmlp[n, share * j : share * j + share, :] = turned[share * k : share * k + share, :]


def scatter_sizes(wide_n, share):
    n_bits = wide_n.bit_length() - 1
    rest = list(range(1, n_bits))
    half = len(rest) // 2
    plan = {"A": rest, "B": rest[half:] + rest[:half]}
    cut = share // 2
    streams = {"A": (0, cut), "B": (cut, share - cut)}
    sizes = {}
    for st, (_, size) in streams.items():
        sizes[st] = [size]
        for _ in rest:
            sizes[st].append(sizes[st][-1] // 2 if sizes[st][-1] % 32 == 0 else sizes[st][-1])
    return plan, streams, sizes


def scatter_stages(links, wide_n, narrow_n, share, dmlp, mine_out, send0, recv0, acc, zsend, zrecv, bufs):
    plan, streams, sizes = scatter_sizes(wide_n, share)
    bit = links.bit
    keep0, away0 = bit[0] * share, (1 - bit[0]) * share
    stages = []

    def pack0():
        for n in range(narrow_n):
            def one(i, size):
                send0[n, pl.ds(i, size), :] = dmlp[n, pl.ds(pl.multiple_of(away0 + i, 16), size), :].astype(send0.dtype)
            loop_rows(share, one)

    def add0():
        for n in range(narrow_n):
            def one(i, size):
                acc[n, pl.ds(i, size), :] = (dmlp[n, pl.ds(pl.multiple_of(keep0 + i, 16), size), :]
                                             + recv0[n, pl.ds(i, size), :].astype(f32))
            loop_rows(share, one)

    stages.append((pack0, [links.copy(send0, recv0, links.along(0))], add0))
    place = {st: streams[st][0] for st in streams}
    trail = []
    for s in range(links.bits - 1):
        work = []
        for k, st in enumerate(streams):
            b = plan[st][s]
            size = sizes[st][s + 1]
            halves = size < sizes[st][s]
            send, recv = bufs[2 * (2 * s + k)], bufs[2 * (2 * s + k) + 1]
            here = place[st]
            out_at, in_at = (here + (1 - bit[b]) * size, here + bit[b] * size) if halves else (here, here)
            place[st] = in_at
            work.append((send, recv, out_at, in_at, size, halves, links.copy(send, recv, links.along(b))))
            trail.append((st, s, b, in_at, size, halves))

        def pack(work=work):
            for send, recv, out_at, in_at, size, halves, _ in work:
                for n in range(narrow_n):
                    def one(i, k):
                        send[n, pl.ds(i, k), :] = acc[n, pl.ds(pl.multiple_of(out_at + i, 16), k), :].astype(send.dtype)
                    loop_rows(size, one)

        def add(work=work):
            for send, recv, out_at, in_at, size, halves, _ in work:
                for n in range(narrow_n):
                    def one(i, k):
                        here = pl.ds(pl.multiple_of(in_at + i, 16), k)
                        mine = acc[n, here, :] if halves else send[n, pl.ds(i, k), :].astype(f32)
                        acc[n, here, :] = mine + recv[n, pl.ds(i, k), :].astype(f32)
                    loop_rows(size, one)

        stages.append((pack, [w[-1] for w in work], add))
    base, total = {}, 0
    for st in streams:
        base[st] = total
        total += sizes[st][-1]

    def packz():
        for i, n in enumerate(links.peer):
            for st in streams:
                def one(r, k):
                    zsend[i, pl.ds(base[st] + r, k), :] = acc[n, pl.ds(pl.multiple_of(place[st] + r, 16), k), :].astype(zsend.dtype)
                loop_rows(sizes[st][-1], one)

    def addz():
        for st in streams:
            def one(r, k):
                value = acc[links.n, pl.ds(pl.multiple_of(place[st] + r, 16), k), :]
                for i in range(narrow_n - 1):
                    value = value + zrecv[i, pl.ds(base[st] + r, k), :].astype(f32)
                mine_out[pl.ds(base[st] + r, k), :] = value.astype(bf16)
            loop_rows(sizes[st][-1], one)

    stages.append((packz, [links.copy(zsend.at[i], zrecv.at[i], links.over(n)) for i, n in enumerate(links.peer)], addz))
    return stages


def attn_backward(wide_n, narrow_n, comm, tok, qkv_s, prob_in, gm_s, vec, hot, hmask, hmask2,
                  dmlp, dhid, dvec2, stats,
                  dproj_out, dwq, misc, mine_out,
                  pj, gp_s, low_s, turn_s, dext, dtable, flat, low_r, proj_r, dmlp_s, load_sem, send0, recv0, acc, zsend, zrecv, *rest):
    step = pl.program_id(0)
    steps = pl.num_programs(0)
    static_steps = comm[1]
    width = tok.shape[1]
    groups = width // 128
    scale = 32 ** (-0.5)
    share = dmlp.shape[1] // 2
    load = pltpu.make_async_copy(dmlp, dmlp_s, load_sem.at[0])

    if comm[0]:
        links = Links(wide_n, narrow_n, *rest[-2:])

        @pl.when(step == 0)
        def _():
            links.barrier()

        @pl.when(step == 0)
        def _():
            load.start()

    @pl.when(step == 0)
    def _():
        for ref in (dwq, dext, dtable, low_r, proj_r):
            ref[...] = jnp.zeros_like(ref)

    def first(b, carry):
        for k in range(BATCH):
            i = b * BATCH + k
            for g in range(groups):
                do_bd = four(gm_s[i, :, 128 * g : 128 * g + 128], hmask[...])
                gp_s[i, g] = nt(qkv_s[i, :KR, 2 * width + 128 * g : 2 * width + 128 * g + 128], do_bd)
        return carry

    def second(b, carry):
        for g in range(groups):
            total = dtable[g]
            for k in range(BATCH):
                i = b * BATCH + k
                gp = gp_s[i, g]
                prob = prob_in[i, g]
                ds = prob * (gp - jnp.sum(gp * prob, 0, keepdims=True))
                total = total + ds
                raw = padded(ds * scale).astype(bf16)
                low_s[i, g] = raw
                turn_s[i, g] = turn(raw)
            dtable[g] = total
        return carry

    lax.fori_loop(0, CW // BATCH, first, 0)
    if comm[0]:
        stages = scatter_stages(links, wide_n, narrow_n, share, dmlp_s, mine_out, send0, recv0, acc, zsend, zrecv, rest[:-2])
        for k, (pack, copies, add) in enumerate(stages):
            @pl.when(step == min(k, static_steps - 1))
            def _():
                if not k:
                    load.wait()
                if k:
                    for c in stages[k - 1][1]:
                        c.wait()
                    stages[k - 1][2]()
                pack()
                for c in copies:
                    c.start()

    lax.fori_loop(0, CW // BATCH, second, 0)
    for i in range(CW):
        rows = slice(WTOK * i, WTOK * i + SLOT)
        for g in range(groups):
            q_bd = four(qkv_s[i, :, 128 * g : 128 * g + 128], hmask[...])
            k_bd = four(qkv_s[i, :, width + 128 * g : width + 128 * g + 128], hmask2[...])
            do_bd = four(gm_s[i, :, 128 * g : 128 * g + 128], hmask[...])
            pj[rows, 128 * g : 128 * g + 128] = nn(turn_s[i, g], k_bd)
            pj[rows, width + 128 * g : width + 128 * g + 128] = nn(low_s[i, g], q_bd)
            pj[rows, 2 * width + 128 * g : 2 * width + 128 * g + 128] = nn(padded(prob_in[i, g]).astype(bf16), do_bd)
    dproj = pj[:CR, :].astype(bf16)
    dproj_out[...] = dproj
    x = tok[...].astype(f32)
    xhat, _ = norm_stats(x)
    low = (xhat * vec[0:1] + vec[1:2]).astype(bf16)
    low_t = jnp.concatenate([low[:EVEN].T, jnp.ones((16, EVEN), bf16)], 0)
    odd = pl.ds(pl.multiple_of(step * (CR - EVEN), CR - EVEN), CR - EVEN)
    low_r[odd, :] = low[EVEN:]
    proj_r[odd, :] = dproj[EVEN:]
    for j in range(3):
        outer = nn(low_t, dproj[:EVEN, width * j : width * j + width])
        dwq[j] += outer[:width]
        dext[j] += outer[width : width + 8]

    @pl.when(step == steps - 1)
    def _():
        rest_t = jnp.concatenate([low_r[...].T, jnp.ones((16, low_r.shape[0]), bf16)], 0)
        for j in range(3):
            outer = nn(rest_t, proj_r[:, width * j : width * j + width])
            dwq[j] += outer[:width]
            dext[j] += outer[width : width + 8]
        rows = [None, None, None, None, dvec2[3], dvec2[0], dvec2[1], dvec2[2]]
        for i, part in enumerate(rows):
            if part is not None:
                misc[i : i + 1, :] = jnp.sum(part, 0, keepdims=True)
        misc[0:2, :] = jnp.zeros((2, width), f32)
        misc[2:3, :] = dext[0, 0:1, :]
        misc[3:4, :] = dext[2, 0:1, :]
        for i in range(dhid.shape[1] // width):
            misc[8 + i : 9 + i, :] = dhid[0:1, width * i : width * i + width]
        lane = lax.broadcasted_iota(jnp.int32, (1, width), 1)
        line = jnp.zeros((1, width), f32)
        for i, part in enumerate((stats[0], stats[1], dvec2[4])):
            line = jnp.where(lane == i, jnp.sum(part), line)
        misc[12:13, :] = jnp.where(lane == 3, jnp.sum(stats[2]) / 128.0, line)
        misc[13:16, :] = jnp.zeros((3, width), f32)
        flat[...] = jnp.zeros_like(flat)
        for g in range(groups):
            for k in range(WTOK):
                line = dtable[g, k : k + 1, :]
                for h in range(HG):
                    flat[HG * g + h : HG * g + h + 1, SLOT * k : SLOT * k + SLOT] = line[:, SLOT * h : SLOT * h + SLOT]
        rest_f = flat[...]
        total = jnp.zeros((16, 256), f32)
        for _ in range(3):
            part = rest_f.astype(bf16)
            total += nn(part, hot[...])
            rest_f = rest_f - part.astype(f32)
        misc[16:32, :] = jnp.zeros((16, width), f32)
        misc[16:32, :256] = total
        if comm[0]:
            for c in stages[-1][1]:
                c.wait()
            stages[-1][2]()


def sds(shape, dt):
    return jax.ShapeDtypeStruct(shape, dt)


def whole(a):
    nd = len(a.shape)
    return pl.BlockSpec(a.shape, lambda *_: (0,) * nd, pipeline_mode=pl.Buffered(1))


def whole_out(a):
    nd = len(a.shape)
    return pl.BlockSpec(a.shape, lambda *_: (0,) * nd)


def by_step(a, steps):
    nd = len(a.shape)
    return pl.BlockSpec((a.shape[0] // steps,) + tuple(a.shape[1:]), lambda c, *_: (c,) + (0,) * (nd - 1))


def run(body, steps, scalars, stepped, wholes, out_stepped, out_wholes, scratch, flops, collective_id=None):
    smem = pl.BlockSpec(memory_space=pltpu.SMEM)
    params = dict(vmem_limit_bytes=62 * 1024 * 1024)
    if collective_id is not None:
        params.update(collective_id=collective_id, has_side_effects=True)
    return pl.pallas_call(
        body, grid=(steps,),
        in_specs=[smem] * len(scalars) + [by_step(a, steps) for a in stepped] + wholes[1],
        out_specs=[by_step(a, steps) for a in out_stepped] + [whole_out(a) for a in out_wholes],
        out_shape=list(out_stepped) + list(out_wholes), scratch_shapes=scratch,
        compiler_params=pltpu.CompilerParams(**params),
        cost_estimate=pl.CostEstimate(flops=flops, bytes_accessed=20000000, transcendentals=0),
    )(*scalars, *stepped, *wholes[0])


def wholes_of(*arrays, far=()):
    return (arrays, [pl.BlockSpec(memory_space=pl.ANY) if i in far else whole(a) for i, a in enumerate(arrays)])


def loop_rows(total, body):
    size = next(n for n in (96, 64, 48, 32, 16) if total % n == 0)
    lax.fori_loop(0, total // size, lambda i, c: (body(pl.multiple_of(i * size, size), size), c)[1], 0)


def attn_chains(wide_n, half):
    rest = list(range(1, wide_n.bit_length() - 1))
    turned = rest[len(rest) // 2 :] + rest[: len(rest) // 2]
    chains, start = [], 0
    while start < half:
        sizes = [min(64, half - start)]
        for _ in rest:
            sizes.append(sizes[-1] // 2 if sizes[-1] % 32 == 0 else sizes[-1])
        chains.append((start, turned if len(chains) % 2 else rest, sizes))
        start += sizes[0]
    return chains


def reduce_all(wide_n, narrow_n, share, mine_ref, q_ref, o_ref, s_ref, vec, dproj, tok, attn_w, gm_out, gt_out, s_out, part_out,
               proj_s, tok_s, part_s, wide_w, wq, dvec, own_sem, recv0, acct, gm, gt, sbuf, srecv, szrecv, *rest):
    bufs = list(rest[:-2])
    links = Links(wide_n, narrow_n, *rest[-2:])
    bit, me_n, peer = links.bit, links.n, links.peer
    steps = links.bits - 1
    width = q_ref.shape[1]
    blocks = proj_s.shape[0]
    at_block = [pl.ds(CR * b, CR) for b in range(blocks)]
    from_hbm = [pltpu.make_async_copy(attn_w.at[:, pl.ds(0, 3 * width)], wide_w, own_sem.at[0])]
    for b in range(blocks):
        from_hbm.append(pltpu.make_async_copy(dproj.at[at_block[b], :], proj_s.at[b], own_sem.at[1 + 2 * b]))
        from_hbm.append(pltpu.make_async_copy(tok.at[at_block[b], :], tok_s.at[b], own_sem.at[2 + 2 * b]))
    to_hbm = [pltpu.make_async_copy(part_s.at[b], part_out.at[at_block[b], :], own_sem.at[1 + 2 * blocks + b]) for b in range(blocks)]
    for c in from_hbm:
        c.start()
    links.barrier()
    ht = acct.shape[1]
    away, keep = (1 - bit[0]) * ht, bit[0] * ht

    def rows_at(at, size):
        return pl.ds(pl.multiple_of(at, 16), size)

    def go(copies):
        for c in copies:
            c.start()

    def come(copies):
        for c in copies:
            c.wait_recv()

    def attn_chain(start, order, sizes):
        copies = []
        for n in range(narrow_n):
            flat = n * share
            src, off = (q_ref, flat) if flat < q_ref.shape[0] else (o_ref, flat - q_ref.shape[0])
            copies.append(links.copy(src.at[rows_at(off + away + start, sizes[0]), :],
                                     recv0.at[n, pl.ds(start, sizes[0]), :], links.along(0)))
        go(copies)
        yield
        come(copies)
        for n in range(narrow_n):
            flat = n * share
            src, off = (q_ref, flat) if flat < q_ref.shape[0] else (o_ref, flat - q_ref.shape[0])
            def add0(i, size):
                acct[n, pl.ds(start + i, size), :] = (src[rows_at(off + keep + start + i, size), :]
                                                      + recv0[n, pl.ds(start + i, size), :])
            loop_rows(sizes[0], add0)
        here = start
        trail = []
        for s in range(steps):
            b, size = order[s], sizes[s + 1]
            halves = size < sizes[s]
            send, recv = bufs.pop(0), bufs.pop(0)
            out_at, in_at = (here + (1 - bit[b]) * size, here + bit[b] * size) if halves else (here, here)
            for n in range(narrow_n):
                def pack(i, k):
                    send[n, pl.ds(i, k), :] = acct[n, rows_at(out_at + i, k), :].astype(bf16)
                loop_rows(size, pack)
            c = links.copy(send, recv, links.along(b))
            c.start()
            yield
            c.wait_recv()
            for n in range(narrow_n):
                def add(i, k):
                    own = acct[n, rows_at(in_at + i, k), :] if halves else send[n, pl.ds(i, k), :].astype(f32)
                    acct[n, rows_at(in_at + i, k), :] = own + recv[n, pl.ds(i, k), :].astype(f32)
                loop_rows(size, add)
            here = in_at
            trail.append((b, in_at, size, halves))
        size = sizes[-1]
        zsend, zrecv = bufs.pop(0), bufs.pop(0)
        copies = []
        for i, n in enumerate(peer):
            def pack(r, k):
                zsend[i, pl.ds(r, k), :] = acct[n, rows_at(here + r, k), :].astype(bf16)
            loop_rows(size, pack)
            copies.append(links.copy(zsend.at[i], zrecv.at[i], links.over(n)))
            copies[-1].start()
        yield
        come(copies)
        def add(r, k):
            value = acct[me_n, rows_at(here + r, k), :]
            for i in range(narrow_n - 1):
                value = value + zrecv[i, pl.ds(r, k), :].astype(f32)
            gt[me_n, rows_at(keep + here + r, k), :] = value.astype(bf16)
        loop_rows(size, add)
        part = gt.at[me_n, rows_at(keep + here, size), :]
        copies = [links.copy(part, part, links.over(n)) for n in peer]
        go(copies)
        yield
        come(copies)
        for b, at, size, halves in reversed(trail):
            if halves:
                part = gt.at[:, rows_at(keep + at, size), :]
                c = links.copy(part, part, links.along(b))
                c.start()
                yield
                c.wait_recv()
        part = gt.at[:, rows_at(keep + start, sizes[0]), :]
        c = links.copy(part, part, links.along(0))
        c.start()
        yield
        c.wait_recv()

    def small_chain():
        yield
        from_hbm[0].wait()
        wq[...] = wide_w[...].astype(bf16)
        dvec[...] = jnp.zeros_like(dvec)
        for b in range(blocks):
            from_hbm[1 + 2 * b].wait()
            from_hbm[2 + 2 * b].wait()
            xhat, inverse = norm_stats(tok_s[b].astype(f32))
            grad_normed = nt(proj_s[b], wq[...])
            dvec[0] += fold_rows(grad_normed * xhat)
            dvec[1] += fold_rows(grad_normed)
            part_s[b] = norm_grad(grad_normed, xhat, inverse, vec[0:1]).astype(bf16)
            to_hbm[b].start()
            yield
        sbuf[0] = s_ref[...]
        for i in range(2):
            sbuf[0, i : i + 1, :] = jnp.sum(dvec[i], 0, keepdims=True)
        for b in range(links.bits):
            c = links.copy(sbuf.at[b], srecv.at[b], links.along(b))
            c.start()
            yield
            c.wait_recv()
            sbuf[b + 1] = sbuf[b] + srecv[b]
        copies = [links.copy(sbuf.at[links.bits], szrecv.at[i], links.over(n)) for i, n in enumerate(peer)]
        go(copies)
        yield
        come(copies)
        own = sbuf[links.bits]
        total = jnp.zeros_like(own)
        for n in range(narrow_n):
            behind = lax.rem(me_n + narrow_n - n, narrow_n)
            value = own
            for i in range(1, narrow_n):
                value = jnp.where(behind == i, szrecv[i - 1], value)
            total = total + value
        s_out[...] = total

    def mlp_chain():
        plan, streams, sizes = scatter_sizes(wide_n, share)
        trail, base = [], 0
        for st, (here, _) in streams.items():
            for s in range(steps):
                b, size = plan[st][s], sizes[st][s + 1]
                halves = size < sizes[st][s]
                here = here + bit[b] * size if halves else here
                trail.append((s, b, here, size, halves))
            size = sizes[st][-1]
            gm[rows_at(bit[0] * share + here, size), :] = mine_ref[base : base + size, :]
            base += size
        yield
        yield
        for s in reversed(range(steps)):
            copies = []
            for s2, b, at, size, halves in trail:
                if s2 == s and halves:
                    part = gm.at[rows_at(bit[0] * share + at, size), :]
                    copies.append(links.copy(part, part, links.along(b)))
            go(copies)
            yield
            come(copies)
        part = gm.at[rows_at(bit[0] * share, share), :]
        c = links.copy(part, part, links.along(0))
        c.start()
        yield
        c.wait_recv()
        gm_out[...] = gm[...]

    going = [attn_chain(*c) for c in attn_chains(wide_n, ht)] + [mlp_chain(), small_chain()]
    while going:
        still = []
        for chain in going:
            try:
                next(chain)
                still.append(chain)
            except StopIteration:
                pass
        going = still
    gt_out[...] = gt[...]
    for c in links.all:
        c.wait_send()
    for c in to_hbm:
        c.wait()


def reduce_call(wide_n, narrow_n, share, mine, dq, do, misc, vec, dproj, tok, attn_w):
    width = mine.shape[1]
    rows = tok.shape[0]
    blocks = rows // CR
    ht = share // 2
    n_bits = wide_n.bit_length() - 1
    scratch = [
        pltpu.VMEM((blocks, CR, 3 * width), bf16), pltpu.VMEM((blocks, CR, width), bf16), pltpu.VMEM((blocks, CR, width), bf16),
        pltpu.VMEM((width, 3 * width), f32), pltpu.VMEM((width, 3 * width), bf16), pltpu.VMEM((2, 8, width), f32),
        pltpu.SemaphoreType.DMA((1 + 3 * blocks,)),
        pltpu.VMEM((narrow_n, ht, width), f32), pltpu.VMEM((narrow_n, ht, width), f32),
        pltpu.VMEM((2 * share, width), bf16), pltpu.VMEM((narrow_n, share, width), bf16),
        pltpu.VMEM((n_bits + 1,) + misc.shape, f32), pltpu.VMEM((n_bits,) + misc.shape, f32),
        pltpu.VMEM((narrow_n - 1,) + misc.shape, f32)]
    order = order_of_bufs(wide_n, narrow_n, ht)
    scratch += [pltpu.VMEM((lead, rows, width), bf16) for lead, rows in order for _ in range(2)]
    chains = len(attn_chains(wide_n, ht))
    copies = chains * (narrow_n + 2 * n_bits + 2 * narrow_n) + 4 * n_bits + narrow_n
    scratch += [pltpu.SemaphoreType.DMA((copies,)), pltpu.SemaphoreType.DMA((copies,))]
    vmem = pl.BlockSpec(memory_space=pltpu.VMEM)
    return pl.pallas_call(
        functools.partial(reduce_all, wide_n, narrow_n, share),
        out_shape=[sds((2 * share, width), bf16), sds((narrow_n, share, width), bf16), sds(misc.shape, f32),
                   sds((rows, width), bf16)],
        in_specs=[vmem] * 5 + [pl.BlockSpec(memory_space=pl.ANY)] * 3, out_specs=[vmem] * 3 + [pl.BlockSpec(memory_space=pl.ANY)], scratch_shapes=scratch,
        compiler_params=pltpu.CompilerParams(collective_id=0, has_side_effects=True, vmem_limit_bytes=60 * 1024 * 1024),
    )(mine, dq, do, misc, vec, dproj, tok, attn_w)


def order_of_bufs(wide_n, narrow_n, ht):
    chains = attn_chains(wide_n, ht)
    out = []
    for s in range(wide_n.bit_length() - 2):
        out += [(narrow_n, sizes[s + 1]) for _, _, sizes in chains]
    return out + [(narrow_n - 1, sizes[-1]) for _, _, sizes in chains]


def adam_kernel(narrow_ref, grad_stream, part, gt, gm, misc, aw, af, as_, mw, mf, ms, tw, tf, ts, vw, vf, vs, bw, bf, bs,
                input_grad, rms, an, al, afn, asn, mn, ml, mfn, msn, tn_, tfn, tsn, vn, vfn, vsn, bn, bfn, bsn):
    def put(new, w, g, m, v, rate, decay, low=None):
        out = adam_step(w, g, m, v, rate, decay)
        for ref, value in zip(new, out):
            ref[...] = value.reshape(ref.shape)
        if low is not None:
            low[...] = out[0].astype(bf16).reshape(low.shape)

    input_grad[...] = grad_stream[...] + part[...].astype(f32)
    put((an, afn, asn), aw[...], jnp.concatenate([gt[j].astype(f32) for j in range(4)], 1), af[...], as_[...], 0.02, 0.05, al)
    put((mn, mfn, msn), mw[0], gm[0].astype(f32), mf[0], ms[0], 0.02, 0.05, ml)

    @pl.when(pl.program_id(0) == 0)
    def _():
        put((vn, vfn, vsn), vw[...], misc[0:8, :], vf[...], vs[...], 0.3, 0.0)
        stats = misc[12:13, :]
        for i in range(3):
            ratio = jnp.sqrt(stats[:, i : i + 1] / (stats[:, 3:4] * misc.shape[1]))
            rms[i] = ratio[0, 0]
        n = narrow_ref[0]
        share = bw.shape[0]
        grad = jnp.zeros((1, share), f32)
        per = misc.shape[1] // share
        for i in range(4):
            for k in range(per):
                grad = jnp.where(n == per * i + k, misc[8 + i : 9 + i, share * k : share * k + share], grad)
        put((bn, bfn, bsn), bw[...], grad.reshape(share), bf[...], bs[...], 0.1, 0.0)
        heads, count = tw.shape
        put((tn_, tfn, tsn), tw[...], misc[16 : 16 + heads, :count], tf[...], ts[...], 0.3, 0.0)


def adam_call(narrow, grad_stream, part, gt, gm, misc, attn, mlp, table, vec, bias):
    width = gm.shape[1]
    share = mlp[0].shape[1]
    gt = gt.reshape(4, width, width)
    cuts = 4 if grad_stream.shape[0] % 64 == 0 else 2
    some = by_step(grad_stream, cuts)
    quarter = 2 * share // cuts
    rows = width // cuts
    gm = gm.reshape(cuts, quarter, width)
    mlp = [a.reshape(cuts, quarter, width) for a in mlp]
    line = pl.BlockSpec((rows, attn[0].shape[1]), lambda j, *_: (j, 0))
    lead = pl.BlockSpec((1, quarter, width), lambda j, *_: (j, 0, 0))
    split = pl.BlockSpec((4, rows, width), lambda j, *_: (0, j, 0))
    smalls = list(table) + list(vec) + list(bias)
    args = [grad_stream, part, gt, gm, misc] + list(attn) + mlp + smalls
    in_specs = [some, some, split, lead, whole(misc)] + [line] * 3 + [lead] * 3 + [whole(a) for a in smalls]
    three = lambda a: [sds(a.shape, f32)] * 3
    outs = [sds(grad_stream.shape, f32), sds((3,), f32), sds(attn[0].shape, f32), sds(attn[0].shape, bf16)] + [sds(attn[0].shape, f32)] * 2
    outs += [sds(mlp[0].shape, f32), sds(mlp[0].shape, bf16)] + [sds(mlp[0].shape, f32)] * 2
    outs += three(table[0]) + three(vec[0]) + three(bias[0])
    out_specs = [some, pl.BlockSpec(memory_space=pltpu.SMEM)] + [line] * 4 + [lead] * 4
    out_specs += [whole_out(a) for a in smalls]
    r = pl.pallas_call(
        adam_kernel,
        grid_spec=pltpu.PrefetchScalarGridSpec(num_scalar_prefetch=1, grid=(cuts,), in_specs=in_specs, out_specs=out_specs),
        out_shape=outs,
        compiler_params=pltpu.CompilerParams(vmem_limit_bytes=60 * 1024 * 1024),
    )(narrow, *args)
    full = (2, share, width)
    grad, r = r[0], r[1:]
    return [grad, r[0], *r[1:5], *[a.T for a in r[9:12]], *r[12:15], *[a.reshape(full) for a in r[5:9]], *r[15:18]]


def bias_layout(rel_table):
    pos = np.arange(WTOK)
    row, col = pos // WIN, pos % WIN
    off = (row[:, None] - row[None, :] + WIN - 1) * (2 * WIN - 1) + col[:, None] - col[None, :] + WIN - 1
    full = np.full((KR, SLOT), -1, np.int32)
    full[:WTOK, :WTOK] = off.T
    return full


def block(tokens, grid_sizes, cotangent, attn_weight, rel_table, vectors, mlp_weight, mlp_bias, narrow, wide_n, narrow_n, linked=True):
    rows, width = tokens.shape
    wins = rows // WTOK
    steps = wins // CW
    heads = rel_table.shape[0]
    groups = heads // HG
    share = mlp_weight.shape[1]
    hidden = share * narrow_n
    n_bits = wide_n.bit_length() - 1
    comm = (linked, steps)
    unit = rows * width * width
    hot = np.zeros((KR * SLOT, 256), np.float32)
    lay = bias_layout(rel_table).reshape(-1)
    hot[np.arange(KR * SLOT)[lay >= 0], lay[lay >= 0]] = 1.0
    hot = jnp.asarray(hot, bf16)
    mask = head_mask(width // heads)
    mask2 = mask.reshape(HG, SLOT, -1)[np.array([0, 2, 1, 3])].reshape(mask.shape)
    mask, mask2 = jnp.asarray(mask, bf16), jnp.asarray(mask2, bf16)
    rinfo, kinfo = jnp.asarray(row_info()), jnp.asarray(key_info())
    scal = (narrow, grid_sizes)
    pad = CR + 16
    copies = 3 * (narrow_n - 1) + 3 * 2 * (narrow_n - 1) + 4
    sem = [pltpu.SemaphoreType.DMA((copies,)), pltpu.SemaphoreType.DMA((copies,))] if linked else []
    sides = pltpu.VMEM((CR, 128), f32)
    table_s = pltpu.VMEM((groups, KR, HG * SLOT), f32)
    flat = pltpu.VMEM((16, KR * SLOT), f32)
    turned = pltpu.VMEM((CW, groups, SLOT, HG * SLOT), bf16)
    qkv, prob, mixed, stream, stats, gw, tails = run(
        functools.partial(attn_forward, wide_n, narrow_n, comm), steps, scal, (tokens,),
        wholes_of(attn_weight, mlp_weight, mlp_bias, vectors, rel_table, hot, rinfo, kinfo, mask, mask2, far=(0, 5)),
        [sds((wins, SLOT, 3 * width), bf16), sds((wins, groups, KR, HG * SLOT), f32), sds((rows, width), bf16), sds((rows, width), f32)],
        [sds((3, 8, width), f32), sds((narrow_n, 2 * share, width), bf16), sds((narrow_n, 8, width), f32)],
        [pltpu.VMEM((width, 4 * width), bf16), pltpu.VMEM((pad, 3 * width), f32), pltpu.VMEM((pad, width), f32), turned,
         table_s, pltpu.VMEM((16, 256), f32), flat, sides,
         pltpu.VMEM((2 * share, width), bf16), pltpu.VMEM((8, width), f32),
         pltpu.VMEM((narrow_n, 2 * share, width), bf16), pltpu.VMEM((narrow_n, 8, width), f32),
         pltpu.VMEM((width, 4 * width), f32), pltpu.VMEM(hot.shape, bf16), pltpu.SemaphoreType.DMA((2,))] + sem,
        12 * unit, 1 if linked else None)
    out_proj = pl.BlockSpec((width, width), lambda *_: (0, 3), pipeline_mode=pl.Buffered(1))
    fixed = (attn_weight, gw, tails, vectors, rinfo)
    outputs, grad_stream, gm, dmlp, dwo, dhid, dvec2 = run(
        functools.partial(feed_forward, TILE), steps, scal, (cotangent, mixed, stream),
        (fixed, [out_proj, pl.BlockSpec(memory_space=pl.ANY)] + [whole(a) for a in fixed[2:]]),
        [sds((rows, width), bf16), sds((rows, width), f32), sds((wins, SLOT, width), bf16)],
        [sds((narrow_n, 2 * share, width), f32), sds((width, width), f32), sds((8, hidden), f32), sds((5, 8, width), f32)],
        [pltpu.VMEM((width, width), bf16), pltpu.VMEM((hidden, width), bf16), pltpu.VMEM((hidden, width), bf16),
         pltpu.VMEM((1, hidden), f32), pltpu.VMEM((width, hidden), f32), pltpu.VMEM((width, hidden), f32),
         pltpu.VMEM((pad, width), f32), sides, pltpu.VMEM((ODD, width), bf16), pltpu.VMEM((ODD, width), bf16),
         pltpu.VMEM((ODD, hidden), bf16), pltpu.VMEM((ODD, hidden), bf16), pltpu.SemaphoreType.DMA((2 * narrow_n,))],
        52 * unit)
    _, streams, sizes = scatter_sizes(wide_n, share)
    last = sum(sizes[st][-1] for st in streams)
    bufs = []
    for s in range(n_bits - 1):
        for st in streams:
            bufs += [pltpu.VMEM((narrow_n, sizes[st][s + 1], width), bf16)] * 2
    copies = 1 + 2 * n_bits + narrow_n
    sem = [pltpu.SemaphoreType.DMA((copies,)), pltpu.SemaphoreType.DMA((copies,))] if linked else []
    dproj, dwq, misc, mine = run(
        functools.partial(attn_backward, wide_n, narrow_n, comm), steps, (), (tokens, qkv, prob, gm),
        wholes_of(vectors, hot, mask, mask2, dmlp, dhid, dvec2, stats, far=(4,)),
        [sds((rows, 3 * width), bf16)],
        [sds((3, width, width), f32), sds((32, width), f32), sds((last, width), bf16)],
        [pltpu.VMEM((pad, 3 * width), f32),
         pltpu.VMEM((CW, groups, KR, HG * SLOT), f32), turned, turned, pltpu.VMEM((3, 8, width), f32), table_s, flat,
         pltpu.VMEM((ODD, width), bf16), pltpu.VMEM((ODD, 3 * width), bf16), pltpu.VMEM(dmlp.shape, f32), pltpu.SemaphoreType.DMA((1,)),
         pltpu.VMEM((narrow_n, share, width), bf16), pltpu.VMEM((narrow_n, share, width), bf16),
         pltpu.VMEM((narrow_n, share, width), f32), pltpu.VMEM((narrow_n - 1, last, width), bf16),
         pltpu.VMEM((narrow_n - 1, last, width), bf16)] + bufs + sem,
        20 * unit, 2 if linked else None)
    return outputs, grad_stream, dmlp, dwq, dwo, misc, mine, dproj


TILE = 768


def adam_step(weight, gradient, first_old, second_old, rate_value, decay_value):
    first_new = beta_one * first_old + (1.0 - beta_one) * gradient
    second_new = beta_two * second_old + (1.0 - beta_two) * gradient * gradient
    fix_one = 1.0 - beta_one**STEP
    fix_two = 1.0 - beta_two**STEP
    update = rate_value * (first_new / fix_one) / (jnp.sqrt(second_new / fix_two) + adam_eps)
    return (weight - update - rate_value * decay_value * weight, first_new, second_new)


def shards(wide_n, narrow_n, tokens, grid_sizes, cotangent, attn_weight, attn_first, attn_second, rel_table, table_first,
           table_second, vectors, vector_first, vector_second, mlp_weight, mlp_first, mlp_second, mlp_bias, bias_first,
           bias_second):
    width = tokens.shape[1]
    narrow = lax.axis_index("narrow").reshape(1).astype(jnp.int32)
    outputs, grad_stream, _, dwq, dwo, misc, mine, dproj = block(
        tokens, grid_sizes, cotangent, attn_weight, rel_table.T, vectors, mlp_weight, mlp_bias, narrow, wide_n, narrow_n)
    gm, gt, misc, part = reduce_call(wide_n, narrow_n, mlp_weight.shape[1], mine, dwq.reshape(3 * width, width), dwo, misc,
                                     vectors, dproj, tokens, attn_weight)
    new = adam_call(narrow, grad_stream, part, gt, gm, misc, (attn_weight, attn_first, attn_second), (mlp_weight, mlp_first, mlp_second),
                    (rel_table.T, table_first.T, table_second.T), (vectors, vector_first, vector_second),
                    (mlp_bias, bias_first, bias_second))
    return (outputs, *new)


def solution(mesh):
    rows = P(("wide", "narrow"), None)
    split = P(None, "narrow", None)
    return jax.shard_map(
        functools.partial(shards, mesh.shape["wide"], mesh.shape["narrow"]), mesh=mesh,
        in_specs=(rows, P("wide"), rows) + (P(),) * 9 + (split,) * 3 + (P("narrow"),) * 3,
        out_specs=(rows, rows) + (P(),) * 11 + (split,) * 4 + (P("narrow"),) * 3,
        check_vma=False)
```

```python
import functools

import jax
import jax.numpy as jnp
import numpy as np
from jax import lax
from jax.sharding import PartitionSpec as P
from jax.experimental import pallas as pl
from jax.experimental.pallas import tpu as pltpu

WIN = 7
WTOK = 49
WPI = 16
IMG_W = 16
STEP = 5
CW = 16
CR = CW * WTOK
EVEN = CR // 256 * 256
ODD = 128
SLOT = 64
KR = 56
HG = 4
LOG2E = 1.4426950408889634

norm_eps = 1e-05
beta_one = 0.5
beta_two = 0.5
adam_eps = 1e-08
highest = lax.Precision.HIGHEST
f32 = jnp.float32
bf16 = jnp.bfloat16


def nn(a, b):
    return lax.dot_general(a, b, (((1,), (0,)), ((), ())), preferred_element_type=f32)


def nt(a, b):
    return lax.dot_general(a, b, (((1,), (1,)), ((), ())), preferred_element_type=f32)


def tn(a, b):
    return lax.dot_general(a, b, (((0,), (0,)), ((), ())), preferred_element_type=f32)


def row_info():
    r = np.arange(CR)
    win = r // WTOK
    p = r % WTOK
    info = np.stack([win, p // WIN, p % WIN]).astype(np.float32)
    info[1, win >= CW] = 1000.0
    return np.ascontiguousarray(np.broadcast_to(info[:, :, None], (3, CR, 128)))


def key_info():
    p = np.arange(KR)
    info = np.stack([p // WIN, p % WIN]).astype(np.float32)
    return np.ascontiguousarray(np.broadcast_to(info[:, :, None], (2, KR, 128)))


def head_mask(head_size):
    row = np.arange(HG * SLOT)
    lane = np.arange(HG * head_size)
    return (((row // SLOT)[:, None] == (lane // head_size)[None, :]) & ((row % SLOT) < WTOK)[:, None]).astype(np.float32)


def fold_rows(t):
    return jnp.sum(t.reshape(t.shape[0] // 8, 8, t.shape[1]), 0)


def rep(v, n):
    return jnp.concatenate([v] * n, 1)


def fill_sides(sides, info, side_s):
    win = info[0]
    value = jnp.zeros_like(win)
    for i in range(CW):
        value = jnp.where(win == float(i), sides[i].astype(f32), value)
    side_s[...] = value


def corner(narrow, step, steps):
    u = WPI - 1 - (narrow * steps + step)
    return (WIN * (u // 4)).astype(f32), (WIN * lax.rem(u, 4)).astype(f32)


def chunk_valid(info, side_s, top, left):
    side = side_s[...]
    return jnp.where((info[1] + top < side) & (info[2] + left < side), 1.0, 0.0)


def norm_stats(x):
    mean = jnp.mean(x, -1, keepdims=True)
    centred = x - mean
    inverse = lax.rsqrt(jnp.mean(centred * centred, -1, keepdims=True) + norm_eps)
    return centred * inverse, inverse


def norm_grad(g, xhat, inverse, gain):
    scaled = g * gain
    m1 = jnp.mean(scaled, -1, keepdims=True)
    m2 = jnp.mean(scaled * xhat, -1, keepdims=True)
    return inverse * (scaled - m1 - xhat * m2)


class Links:
    def __init__(self, wide_n, narrow_n, send_sem, recv_sem):
        self.w = lax.axis_index("wide")
        self.n = lax.axis_index("narrow")
        self.bits = wide_n.bit_length() - 1
        self.bit = [lax.rem(self.w // (1 << b), 2) for b in range(self.bits)]
        self.mate = [self.w + (1 - 2 * self.bit[b]) * (1 << b) for b in range(self.bits)]
        self.peer = [lax.rem(self.n + s, narrow_n) for s in range(1, narrow_n)]
        self.send_sem, self.recv_sem = send_sem, recv_sem
        self.used = 0
        self.all = []

    def copy(self, src, dst, device):
        k = self.used
        self.used += 1
        c = pltpu.make_async_remote_copy(
            src_ref=src, dst_ref=dst, send_sem=self.send_sem.at[k], recv_sem=self.recv_sem.at[k],
            device_id=device, device_id_type=pl.DeviceIdType.MESH)
        self.all.append(c)
        return c

    def along(self, b):
        return (self.mate[b], self.n)

    def over(self, n):
        return (self.w, n)

    def barrier(self):
        sem = pltpu.get_barrier_semaphore()
        for b in range(self.bits):
            pl.semaphore_signal(sem, inc=1, device_id=self.along(b), device_id_type=pl.DeviceIdType.MESH)
        for n in self.peer:
            pl.semaphore_signal(sem, inc=1, device_id=self.over(n), device_id_type=pl.DeviceIdType.MESH)
        pl.semaphore_wait(sem, self.bits + len(self.peer))


def gather_cuts(wide_n, rows):
    bits = list(range(min(3, wide_n.bit_length() - 1)))
    first = rows // 256 * 128
    return [(0, first, bits[1:] + bits[:1]), (first, rows - first, bits[1:][::-1] + bits[:1])]


def gather_plan(links, wide_n, own, tail_own, all_w, all_tail):
    narrow_n, rows, _ = all_w.shape
    streams = gather_cuts(wide_n, rows)
    stages = [[]]
    place, sizes = [], []
    for start, size, order in streams:
        piece = size >> len(order)
        off = 0
        for k, b in enumerate(order):
            off = off + links.bit[b] * (piece << k)
        place.append(start + off)
        sizes.append(piece)
    for n in links.peer:
        stages[0].append(links.copy(tail_own, all_tail.at[links.n], links.over(n)))
        for at, size in zip(place, sizes):
            here = pl.ds(pl.multiple_of(at, 16), size)
            stages[0].append(links.copy(own.at[here, :], all_w.at[links.n, here, :], links.over(n)))
    for k in range(len(streams[0][2])):
        stage = []
        for s, (start, size, order) in enumerate(streams):
            here = pl.ds(pl.multiple_of(place[s], 16), sizes[s])
            for n in links.peer:
                part = all_w.at[n, here, :]
                stage.append(links.copy(part, part, links.along(order[k])))
            place[s] = place[s] - links.bit[order[k]] * sizes[s]
            sizes[s] = sizes[s] * 2
        stages.append(stage)
    return stages


def run_stages(stages, step, steps):
    for k, stage in enumerate(stages):
        @pl.when(step == min(k, steps - 1))
        def _():
            if k:
                for c in stages[k - 1]:
                    c.wait()
            for c in stage:
                c.start()


def expand_table(table, hot, wide_t, flat, bias):
    heads, count = table.shape
    wide_t[...] = jnp.zeros_like(wide_t)
    wide_t[:heads, :count] = table[...] * LOG2E
    rest = wide_t[...]
    total = jnp.zeros((16, hot.shape[0]), f32)
    for _ in range(3):
        part = rest.astype(bf16)
        total += nt(part, hot[...])
        rest = rest - part.astype(f32)
    flat[...] = total
    bias[...] = jnp.full(bias.shape, -1e30, f32)
    for g in range(heads // HG):
        for k in range(WTOK):
            for h in range(HG):
                bias[g, k : k + 1, SLOT * h : SLOT * h + SLOT] = flat[HG * g + h : HG * g + h + 1, SLOT * k : SLOT * k + SLOT]


def turn(t):
    t = jnp.concatenate([t[:, :128], t[:, 128:]], 0).T
    return jnp.concatenate([t[:SLOT], t[SLOT:]], 1)


def padded(t):
    return jnp.concatenate([t, jnp.zeros((SLOT - KR, t.shape[1]), f32)], 0)


def four(t, mask):
    return jnp.concatenate([t] * HG, 0) * mask


BATCH = 16


def attn_forward(wide_n, narrow_n, comm, narrow_ref, sides, tok, attn_w, mlp_w, mlp_b, vec, table, hot, rinfo, kinfo, hmask, hmask2,
                 qkv_s, prob_out, mixed_out, stream_out, stats, gw_out, tail_out,
                 wq, pj, mx, turn_s, bias, wide_t, flat, side_s, own, tail_own, gw, tails, wide_w, hot_s, load_sem, *sems):
    step = pl.program_id(0)
    steps = pl.num_programs(0)
    static_steps = comm[1]
    width = tok.shape[1]
    groups = width // 128
    scale = 32 ** (-0.5)
    narrow = narrow_ref[0]
    share = mlp_w.shape[1]

    loads = [pltpu.make_async_copy(attn_w, wide_w, load_sem.at[0]), pltpu.make_async_copy(hot, hot_s, load_sem.at[1])]

    @pl.when(step == 0)
    def _():
        for c in loads:
            c.start()
        for j in range(2):
            own[share * j : share * j + share, :] = mlp_w[j].astype(bf16)
        tail_own[...] = jnp.zeros_like(tail_own)
        rest = mlp_b[...].reshape(1, share)
        for i in range(3):
            part = rest.astype(bf16).astype(f32)
            tail_own[i : i + 1, :share] = part
            rest = rest - part
        if comm[0]:
            gw[lax.axis_index("narrow")] = own[...]
            tails[lax.axis_index("narrow")] = tail_own[...]
        else:
            for n in range(narrow_n):
                gw[n] = own[...]
                tails[n] = tail_own[...]

    if comm[0]:
        links = Links(wide_n, narrow_n, *sems)

        @pl.when(step == 0)
        def _():
            links.barrier()

        stages = gather_plan(links, wide_n, own, tail_own, gw, tails)
        run_stages(stages, step, static_steps)

    @pl.when(step == 0)
    def _():
        fill_sides(sides, rinfo, side_s)
        for c in loads:
            c.wait()
        wq[...] = wide_w[...].astype(bf16)
        expand_table(table, hot_s, wide_t, flat, bias)
        for ref in (pj, mx, stats):
            ref[...] = jnp.zeros_like(ref)

    top, left = corner(narrow, step, static_steps)
    x = tok[...].astype(f32)
    valid = chunk_valid(rinfo, side_s, top, left)
    keep = rep(valid, groups)
    xhat, _ = norm_stats(x)
    low = (xhat * vec[0:1] + vec[1:2]).astype(bf16)
    pj[:CR, :width] = nn(low, wq[:, :width]) + vec[2:3]
    pj[:CR, width : 2 * width] = nn(low, wq[:, width : 2 * width])
    pj[:CR, 2 * width :] = nn(low, wq[:, 2 * width : 3 * width]) + vec[3:4]
    for i in range(CW):
        qkv_s[i] = pj[WTOK * i : WTOK * i + SLOT, :].astype(bf16)

    def score(b, carry):
        for k in range(BATCH):
            i = b * BATCH + k
            for g in range(groups):
                q_bd = four(qkv_s[i, :, 128 * g : 128 * g + 128], hmask[...])
                prob_out[i, g] = nt(qkv_s[i, :KR, width + 128 * g : width + 128 * g + 128], q_bd)
        return carry

    def soft(b, carry):
        for k in range(BATCH):
            i = b * BATCH + k
            side = sides[i].astype(f32)
            fill = jnp.where((kinfo[0] < side - top) & (kinfo[1] < side - left), 0.0, -10000.0 * LOG2E)
            fill = rep(fill, 2)
            for g in range(groups):
                s = prob_out[i, g] * (scale * LOG2E) + bias[g] + fill
                e = jnp.exp2(s - jnp.max(s, 0, keepdims=True))
                prob = e * (1.0 / jnp.sum(e, 0, keepdims=True))
                prob_out[i, g] = prob
                turn_s[i, g] = turn(padded(prob).astype(bf16))
        return carry

    lax.fori_loop(0, CW // BATCH, score, 0)
    lax.fori_loop(0, CW // BATCH, soft, 0)
    for i in range(CW):
        for g in range(groups):
            v_bd = four(qkv_s[i, :, 2 * width + 128 * g : 2 * width + 128 * g + 128], hmask2[...])
            mx[WTOK * i : WTOK * i + SLOT, 128 * g : 128 * g + 128] = nn(turn_s[i, g], v_bd)
    mixed = mx[:CR, :].astype(bf16)
    mixed_out[...] = mixed
    branch = (nn(mixed, wq[:, 3 * width :]) + vec[4:5]) * keep
    stream_out[...] = x + branch
    stats[0] += fold_rows(x * x * keep)
    stats[1] += fold_rows(branch * branch)
    stats[2, :, :128] += fold_rows(valid)

    @pl.when(step == steps - 1)
    def _():
        if comm[0]:
            for c in stages[-1]:
                c.wait()
        gw_out[...] = gw[...]
        tail_out[...] = tails[...]


def feed_forward(tile, narrow_ref, sides, cot, mixed_in, stream_in, attn_w, gw, tails, vec, rinfo,
                 out_ref, grad_stream_out, gm_s, dmlp, dwo, dhid, dvec,
                 wo, w1, w2, hb, dw1, dw2, mx, side_s, second_r, grad_r, pre_r, active_r, load_sem):
    step = pl.program_id(0)
    steps = pl.num_programs(0)
    width = cot.shape[1]
    groups = width // 128
    hidden = w1.shape[0]
    shards_n, twice, _ = gw.shape
    share = twice // 2
    loads = []
    for n in range(shards_n):
        for j, ref in enumerate((w1, w2)):
            loads.append(pltpu.make_async_copy(gw.at[n, pl.ds(share * j, share), :], ref.at[pl.ds(share * n, share), :],
                                               load_sem.at[2 * n + j]))

    @pl.when(step == 0)
    def _():
        for c in loads:
            c.start()
        wo[...] = attn_w[...].astype(bf16)
        for n in range(shards_n):
            three = tails[n]
            hb[:, share * n : share * n + share] = (three[0:1] + three[1:2] + three[2:3])[:, :share]
        fill_sides(sides, rinfo, side_s)
        for ref in (mx, dw1, dw2, dwo, dhid, dvec, second_r, grad_r, pre_r, active_r):
            ref[...] = jnp.zeros_like(ref)

    top, left = corner(narrow_ref[0], step, steps)
    keep = rep(chunk_valid(rinfo, side_s, top, left), groups)
    cotan = cot[...].astype(f32)
    stream = stream_in[...]
    xhat2, inverse2 = norm_stats(stream)
    second = (xhat2 * vec[5:6] + vec[6:7]).astype(bf16)
    kept_cot = cotan * keep
    grad_low = kept_cot.astype(bf16)
    second_t = jnp.concatenate([second[:EVEN].T, jnp.ones((16, EVEN), bf16)], 0)
    grad_t = grad_low[:EVEN].T
    odd = pl.ds(pl.multiple_of(step * (CR - EVEN), CR - EVEN), CR - EVEN)
    second_r[odd, :] = second[EVEN:]
    grad_r[odd, :] = grad_low[EVEN:]

    @pl.when(step == 0)
    def _():
        for c in loads:
            c.wait()

    mlp_out = jnp.zeros((CR, width), f32)
    grad_second = jnp.zeros((CR, width), f32)
    for t in range(hidden // tile):
        cols = slice(tile * t, tile * t + tile)
        pre = nt(second, w1[cols, :]) + hb[0:1, cols]
        square = pre * pre
        half = 0.5 * jnp.tanh(pre * (square * (0.7978845608028654 * 0.044715) + 0.7978845608028654)) + 0.5
        active = (pre * half).astype(bf16)
        slope = half + (pre * (half - half * half)) * (square * (6 * 0.7978845608028654 * 0.044715) + 2 * 0.7978845608028654)
        grad_pre = (nt(grad_low, w2[cols, :]) * slope).astype(bf16)
        mlp_out += nn(active, w2[cols, :])
        grad_second += nn(grad_pre, w1[cols, :])
        pre_r[odd, cols] = grad_pre[EVEN:]
        active_r[odd, cols] = active[EVEN:]
        outer = nn(second_t, grad_pre[:EVEN])
        dw1[:, cols] += outer[:width]
        dhid[:, cols] += outer[width : width + 8]
        dw2[:, cols] += nn(grad_t, active[:EVEN])
    branch = (mlp_out + vec[7:8]) * keep
    out_ref[...] = (stream + branch).astype(bf16)
    dvec[4] += fold_rows(branch * branch)
    dvec[0] += fold_rows(grad_second * xhat2)
    dvec[1] += fold_rows(grad_second)
    dvec[2] += fold_rows(kept_cot)
    grad_stream = cotan + norm_grad(grad_second, xhat2, inverse2, vec[5:6])
    grad_stream_out[...] = grad_stream
    grad_attn = grad_stream * keep
    dvec[3] += fold_rows(grad_attn)
    grad_attn_low = grad_attn.astype(bf16)
    dwo[...] += nn(mixed_in[...].T, grad_attn_low)
    mx[:CR, :] = nt(grad_attn_low, wo[...])
    for i in range(CW):
        gm_s[i] = mx[WTOK * i : WTOK * i + SLOT, :].astype(bf16)

    @pl.when(step == steps - 1)
    def _():
        rest_t = jnp.concatenate([second_r[...].T, jnp.ones((16, second_r.shape[0]), bf16)], 0)
        rest_g = grad_r[...].T
        for t in range(hidden // width):
            cols = slice(width * t, width * t + width)
            outer = nn(rest_t, pre_r[:, cols])
            dw1[:, cols] += outer[:width]
            dhid[:, cols] += outer[width : width + 8]
            dw2[:, cols] += nn(rest_g, active_r[:, cols])
        for j, ref in enumerate((dw1, dw2)):
            for t in range(hidden // width):
                turned = ref[:, width * t : width * t + width].T
                for k in range(width // share):
                    n = (width * t) // share + k
                    dmlp[n, share * j : share * j + share, :] = turned[share * k : share * k + share, :]


def scatter_sizes(wide_n, share):
    n_bits = wide_n.bit_length() - 1
    rest = list(range(1, n_bits))
    half = len(rest) // 2
    plan = {"A": rest, "B": rest[half:] + rest[:half]}
    cut = share // 2
    streams = {"A": (0, cut), "B": (cut, share - cut)}
    sizes = {}
    for st, (_, size) in streams.items():
        sizes[st] = [size]
        for _ in rest:
            sizes[st].append(sizes[st][-1] // 2 if sizes[st][-1] % 32 == 0 else sizes[st][-1])
    return plan, streams, sizes


def scatter_stages(links, wide_n, narrow_n, share, dmlp, mine_out, send0, recv0, acc, zsend, zrecv, bufs):
    plan, streams, sizes = scatter_sizes(wide_n, share)
    bit = links.bit
    keep0, away0 = bit[0] * share, (1 - bit[0]) * share
    stages = []

    def pack0():
        for n in range(narrow_n):
            def one(i, size):
                send0[n, pl.ds(i, size), :] = dmlp[n, pl.ds(pl.multiple_of(away0 + i, 16), size), :].astype(send0.dtype)
            loop_rows(share, one)

    def add0():
        for n in range(narrow_n):
            def one(i, size):
                acc[n, pl.ds(i, size), :] = (dmlp[n, pl.ds(pl.multiple_of(keep0 + i, 16), size), :]
                                             + recv0[n, pl.ds(i, size), :].astype(f32))
            loop_rows(share, one)

    stages.append((pack0, [links.copy(send0, recv0, links.along(0))], add0))
    place = {st: streams[st][0] for st in streams}
    trail = []
    for s in range(links.bits - 1):
        work = []
        for k, st in enumerate(streams):
            b = plan[st][s]
            size = sizes[st][s + 1]
            halves = size < sizes[st][s]
            send, recv = bufs[2 * (2 * s + k)], bufs[2 * (2 * s + k) + 1]
            here = place[st]
            out_at, in_at = (here + (1 - bit[b]) * size, here + bit[b] * size) if halves else (here, here)
            place[st] = in_at
            work.append((send, recv, out_at, in_at, size, halves, links.copy(send, recv, links.along(b))))
            trail.append((st, s, b, in_at, size, halves))

        def pack(work=work):
            for send, recv, out_at, in_at, size, halves, _ in work:
                for n in range(narrow_n):
                    def one(i, k):
                        send[n, pl.ds(i, k), :] = acc[n, pl.ds(pl.multiple_of(out_at + i, 16), k), :].astype(send.dtype)
                    loop_rows(size, one)

        def add(work=work):
            for send, recv, out_at, in_at, size, halves, _ in work:
                for n in range(narrow_n):
                    def one(i, k):
                        here = pl.ds(pl.multiple_of(in_at + i, 16), k)
                        mine = acc[n, here, :] if halves else send[n, pl.ds(i, k), :].astype(f32)
                        acc[n, here, :] = mine + recv[n, pl.ds(i, k), :].astype(f32)
                    loop_rows(size, one)

        stages.append((pack, [w[-1] for w in work], add))
    base, total = {}, 0
    for st in streams:
        base[st] = total
        total += sizes[st][-1]

    def packz():
        for i, n in enumerate(links.peer):
            for st in streams:
                def one(r, k):
                    zsend[i, pl.ds(base[st] + r, k), :] = acc[n, pl.ds(pl.multiple_of(place[st] + r, 16), k), :].astype(zsend.dtype)
                loop_rows(sizes[st][-1], one)

    def addz():
        for st in streams:
            def one(r, k):
                value = acc[links.n, pl.ds(pl.multiple_of(place[st] + r, 16), k), :]
                for i in range(narrow_n - 1):
                    value = value + zrecv[i, pl.ds(base[st] + r, k), :].astype(f32)
                mine_out[pl.ds(base[st] + r, k), :] = value.astype(bf16)
            loop_rows(sizes[st][-1], one)

    stages.append((packz, [links.copy(zsend.at[i], zrecv.at[i], links.over(n)) for i, n in enumerate(links.peer)], addz))
    return stages


def attn_backward(wide_n, narrow_n, comm, tok, qkv_s, prob_in, gm_s, vec, hot, hmask, hmask2,
                  dmlp, dhid, dvec2, stats,
                  dproj_out, dwq, misc, mine_out,
                  pj, gp_s, low_s, turn_s, dext, dtable, flat, low_r, proj_r, dmlp_s, load_sem, send0, recv0, acc, zsend, zrecv, *rest):
    step = pl.program_id(0)
    steps = pl.num_programs(0)
    static_steps = comm[1]
    width = tok.shape[1]
    groups = width // 128
    scale = 32 ** (-0.5)
    share = dmlp.shape[1] // 2
    load = pltpu.make_async_copy(dmlp, dmlp_s, load_sem.at[0])

    if comm[0]:
        links = Links(wide_n, narrow_n, *rest[-2:])

        @pl.when(step == 0)
        def _():
            links.barrier()

        @pl.when(step == 0)
        def _():
            load.start()

    @pl.when(step == 0)
    def _():
        for ref in (dwq, dext, dtable, low_r, proj_r):
            ref[...] = jnp.zeros_like(ref)

    def first(b, carry):
        for k in range(BATCH):
            i = b * BATCH + k
            for g in range(groups):
                do_bd = four(gm_s[i, :, 128 * g : 128 * g + 128], hmask[...])
                gp_s[i, g] = nt(qkv_s[i, :KR, 2 * width + 128 * g : 2 * width + 128 * g + 128], do_bd)
        return carry

    def second(b, carry):
        for g in range(groups):
            total = dtable[g]
            for k in range(BATCH):
                i = b * BATCH + k
                gp = gp_s[i, g]
                prob = prob_in[i, g]
                ds = prob * (gp - jnp.sum(gp * prob, 0, keepdims=True))
                total = total + ds
                raw = padded(ds * scale).astype(bf16)
                low_s[i, g] = raw
                turn_s[i, g] = turn(raw)
            dtable[g] = total
        return carry

    lax.fori_loop(0, CW // BATCH, first, 0)
    if comm[0]:
        stages = scatter_stages(links, wide_n, narrow_n, share, dmlp_s, mine_out, send0, recv0, acc, zsend, zrecv, rest[:-2])
        for k, (pack, copies, add) in enumerate(stages):
            @pl.when(step == min(k, static_steps - 1))
            def _():
                if not k:
                    load.wait()
                if k:
                    for c in stages[k - 1][1]:
                        c.wait()
                    stages[k - 1][2]()
                pack()
                for c in copies:
                    c.start()

    lax.fori_loop(0, CW // BATCH, second, 0)
    for i in range(CW):
        rows = slice(WTOK * i, WTOK * i + SLOT)
        for g in range(groups):
            q_bd = four(qkv_s[i, :, 128 * g : 128 * g + 128], hmask[...])
            k_bd = four(qkv_s[i, :, width + 128 * g : width + 128 * g + 128], hmask2[...])
            do_bd = four(gm_s[i, :, 128 * g : 128 * g + 128], hmask[...])
            pj[rows, 128 * g : 128 * g + 128] = nn(turn_s[i, g], k_bd)
            pj[rows, width + 128 * g : width + 128 * g + 128] = nn(low_s[i, g], q_bd)
            pj[rows, 2 * width + 128 * g : 2 * width + 128 * g + 128] = nn(padded(prob_in[i, g]).astype(bf16), do_bd)
    dproj = pj[:CR, :].astype(bf16)
    dproj_out[...] = dproj
    x = tok[...].astype(f32)
    xhat, _ = norm_stats(x)
    low = (xhat * vec[0:1] + vec[1:2]).astype(bf16)
    low_t = jnp.concatenate([low[:EVEN].T, jnp.ones((16, EVEN), bf16)], 0)
    odd = pl.ds(pl.multiple_of(step * (CR - EVEN), CR - EVEN), CR - EVEN)
    low_r[odd, :] = low[EVEN:]
    proj_r[odd, :] = dproj[EVEN:]
    for j in range(3):
        outer = nn(low_t, dproj[:EVEN, width * j : width * j + width])
        dwq[j] += outer[:width]
        dext[j] += outer[width : width + 8]

    @pl.when(step == steps - 1)
    def _():
        rest_t = jnp.concatenate([low_r[...].T, jnp.ones((16, low_r.shape[0]), bf16)], 0)
        for j in range(3):
            outer = nn(rest_t, proj_r[:, width * j : width * j + width])
            dwq[j] += outer[:width]
            dext[j] += outer[width : width + 8]
        rows = [None, None, None, None, dvec2[3], dvec2[0], dvec2[1], dvec2[2]]
        for i, part in enumerate(rows):
            if part is not None:
                misc[i : i + 1, :] = jnp.sum(part, 0, keepdims=True)
        misc[0:2, :] = jnp.zeros((2, width), f32)
        misc[2:3, :] = dext[0, 0:1, :]
        misc[3:4, :] = dext[2, 0:1, :]
        for i in range(dhid.shape[1] // width):
            misc[8 + i : 9 + i, :] = dhid[0:1, width * i : width * i + width]
        lane = lax.broadcasted_iota(jnp.int32, (1, width), 1)
        line = jnp.zeros((1, width), f32)
        for i, part in enumerate((stats[0], stats[1], dvec2[4])):
            line = jnp.where(lane == i, jnp.sum(part), line)
        misc[12:13, :] = jnp.where(lane == 3, jnp.sum(stats[2]) / 128.0, line)
        misc[13:16, :] = jnp.zeros((3, width), f32)
        flat[...] = jnp.zeros_like(flat)
        for g in range(groups):
            for k in range(WTOK):
                line = dtable[g, k : k + 1, :]
                for h in range(HG):
                    flat[HG * g + h : HG * g + h + 1, SLOT * k : SLOT * k + SLOT] = line[:, SLOT * h : SLOT * h + SLOT]
        rest_f = flat[...]
        total = jnp.zeros((16, 256), f32)
        for _ in range(3):
            part = rest_f.astype(bf16)
            total += nn(part, hot[...])
            rest_f = rest_f - part.astype(f32)
        misc[16:32, :] = jnp.zeros((16, width), f32)
        misc[16:32, :256] = total
        if comm[0]:
            for c in stages[-1][1]:
                c.wait()
            stages[-1][2]()


def sds(shape, dt):
    return jax.ShapeDtypeStruct(shape, dt)


def whole(a):
    nd = len(a.shape)
    return pl.BlockSpec(a.shape, lambda *_: (0,) * nd, pipeline_mode=pl.Buffered(1))


def whole_out(a):
    nd = len(a.shape)
    return pl.BlockSpec(a.shape, lambda *_: (0,) * nd)


def by_step(a, steps):
    nd = len(a.shape)
    return pl.BlockSpec((a.shape[0] // steps,) + tuple(a.shape[1:]), lambda c, *_: (c,) + (0,) * (nd - 1))


def run(body, steps, scalars, stepped, wholes, out_stepped, out_wholes, scratch, flops, collective_id=None):
    smem = pl.BlockSpec(memory_space=pltpu.SMEM)
    params = dict(vmem_limit_bytes=62 * 1024 * 1024)
    if collective_id is not None:
        params.update(collective_id=collective_id, has_side_effects=True)
    return pl.pallas_call(
        body, grid=(steps,),
        in_specs=[smem] * len(scalars) + [by_step(a, steps) for a in stepped] + wholes[1],
        out_specs=[by_step(a, steps) for a in out_stepped] + [whole_out(a) for a in out_wholes],
        out_shape=list(out_stepped) + list(out_wholes), scratch_shapes=scratch,
        compiler_params=pltpu.CompilerParams(**params),
        cost_estimate=pl.CostEstimate(flops=flops, bytes_accessed=20000000, transcendentals=0),
    )(*scalars, *stepped, *wholes[0])


def wholes_of(*arrays, far=()):
    return (arrays, [pl.BlockSpec(memory_space=pl.ANY) if i in far else whole(a) for i, a in enumerate(arrays)])


def loop_rows(total, body):
    size = next(n for n in (96, 64, 48, 32, 16) if total % n == 0)
    lax.fori_loop(0, total // size, lambda i, c: (body(pl.multiple_of(i * size, size), size), c)[1], 0)


def attn_chains(wide_n, half):
    rest = list(range(1, wide_n.bit_length() - 1))
    turned = rest[len(rest) // 2 :] + rest[: len(rest) // 2]
    chains, start = [], 0
    while start < half:
        sizes = [min(64, half - start)]
        for _ in rest:
            sizes.append(sizes[-1] // 2 if sizes[-1] % 32 == 0 else sizes[-1])
        chains.append((start, turned if len(chains) % 2 else rest, sizes))
        start += sizes[0]
    return chains


def reduce_all(wide_n, narrow_n, share, mine_ref, q_ref, o_ref, s_ref, vec, dproj, tok, attn_w, gm_out, gt_out, s_out, part_out,
               proj_s, tok_s, part_s, wide_w, wq, dvec, own_sem, recv0, acct, gm, gt, sbuf, srecv, szrecv, *rest):
    bufs = list(rest[:-2])
    links = Links(wide_n, narrow_n, *rest[-2:])
    bit, me_n, peer = links.bit, links.n, links.peer
    steps = links.bits - 1
    width = q_ref.shape[1]
    blocks = proj_s.shape[0]
    at_block = [pl.ds(CR * b, CR) for b in range(blocks)]
    from_hbm = [pltpu.make_async_copy(attn_w.at[:, pl.ds(0, 3 * width)], wide_w, own_sem.at[0])]
    for b in range(blocks):
        from_hbm.append(pltpu.make_async_copy(dproj.at[at_block[b], :], proj_s.at[b], own_sem.at[1 + 2 * b]))
        from_hbm.append(pltpu.make_async_copy(tok.at[at_block[b], :], tok_s.at[b], own_sem.at[2 + 2 * b]))
    to_hbm = [pltpu.make_async_copy(part_s.at[b], part_out.at[at_block[b], :], own_sem.at[1 + 2 * blocks + b]) for b in range(blocks)]
    for c in from_hbm:
        c.start()
    links.barrier()
    ht = acct.shape[1]
    away, keep = (1 - bit[0]) * ht, bit[0] * ht

    def rows_at(at, size):
        return pl.ds(pl.multiple_of(at, 16), size)

    def go(copies):
        for c in copies:
            c.start()

    def come(copies):
        for c in copies:
            c.wait_recv()

    def attn_chain(start, order, sizes):
        copies = []
        for n in range(narrow_n):
            flat = n * share
            src, off = (q_ref, flat) if flat < q_ref.shape[0] else (o_ref, flat - q_ref.shape[0])
            copies.append(links.copy(src.at[rows_at(off + away + start, sizes[0]), :],
                                     recv0.at[n, pl.ds(start, sizes[0]), :], links.along(0)))
        go(copies)
        yield
        come(copies)
        for n in range(narrow_n):
            flat = n * share
            src, off = (q_ref, flat) if flat < q_ref.shape[0] else (o_ref, flat - q_ref.shape[0])
            def add0(i, size):
                acct[n, pl.ds(start + i, size), :] = (src[rows_at(off + keep + start + i, size), :]
                                                      + recv0[n, pl.ds(start + i, size), :])
            loop_rows(sizes[0], add0)
        here = start
        trail = []
        for s in range(steps):
            b, size = order[s], sizes[s + 1]
            halves = size < sizes[s]
            send, recv = bufs.pop(0), bufs.pop(0)
            out_at, in_at = (here + (1 - bit[b]) * size, here + bit[b] * size) if halves else (here, here)
            for n in range(narrow_n):
                def pack(i, k):
                    send[n, pl.ds(i, k), :] = acct[n, rows_at(out_at + i, k), :].astype(bf16)
                loop_rows(size, pack)
            c = links.copy(send, recv, links.along(b))
            c.start()
            yield
            c.wait_recv()
            for n in range(narrow_n):
                def add(i, k):
                    own = acct[n, rows_at(in_at + i, k), :] if halves else send[n, pl.ds(i, k), :].astype(f32)
                    acct[n, rows_at(in_at + i, k), :] = own + recv[n, pl.ds(i, k), :].astype(f32)
                loop_rows(size, add)
            here = in_at
            trail.append((b, in_at, size, halves))
        size = sizes[-1]
        zsend, zrecv = bufs.pop(0), bufs.pop(0)
        copies = []
        for i, n in enumerate(peer):
            def pack(r, k):
                zsend[i, pl.ds(r, k), :] = acct[n, rows_at(here + r, k), :].astype(bf16)
            loop_rows(size, pack)
            copies.append(links.copy(zsend.at[i], zrecv.at[i], links.over(n)))
            copies[-1].start()
        yield
        come(copies)
        def add(r, k):
            value = acct[me_n, rows_at(here + r, k), :]
            for i in range(narrow_n - 1):
                value = value + zrecv[i, pl.ds(r, k), :].astype(f32)
            gt[me_n, rows_at(keep + here + r, k), :] = value.astype(bf16)
        loop_rows(size, add)
        part = gt.at[me_n, rows_at(keep + here, size), :]
        copies = [links.copy(part, part, links.over(n)) for n in peer]
        go(copies)
        yield
        come(copies)
        for b, at, size, halves in reversed(trail):
            if halves:
                part = gt.at[:, rows_at(keep + at, size), :]
                c = links.copy(part, part, links.along(b))
                c.start()
                yield
                c.wait_recv()
        part = gt.at[:, rows_at(keep + start, sizes[0]), :]
        c = links.copy(part, part, links.along(0))
        c.start()
        yield
        c.wait_recv()

    def small_chain():
        yield
        from_hbm[0].wait()
        wq[...] = wide_w[...].astype(bf16)
        dvec[...] = jnp.zeros_like(dvec)
        for b in range(blocks):
            from_hbm[1 + 2 * b].wait()
            from_hbm[2 + 2 * b].wait()
            xhat, inverse = norm_stats(tok_s[b].astype(f32))
            grad_normed = nt(proj_s[b], wq[...])
            dvec[0] += fold_rows(grad_normed * xhat)
            dvec[1] += fold_rows(grad_normed)
            part_s[b] = norm_grad(grad_normed, xhat, inverse, vec[0:1]).astype(bf16)
            to_hbm[b].start()
            if b % 2:
                yield
        sbuf[0] = s_ref[...]
        for i in range(2):
            sbuf[0, i : i + 1, :] = jnp.sum(dvec[i], 0, keepdims=True)
        for b in range(links.bits):
            c = links.copy(sbuf.at[b], srecv.at[b], links.along(b))
            c.start()
            yield
            c.wait_recv()
            sbuf[b + 1] = sbuf[b] + srecv[b]
        copies = [links.copy(sbuf.at[links.bits], szrecv.at[i], links.over(n)) for i, n in enumerate(peer)]
        go(copies)
        yield
        come(copies)
        own = sbuf[links.bits]
        total = jnp.zeros_like(own)
        for n in range(narrow_n):
            behind = lax.rem(me_n + narrow_n - n, narrow_n)
            value = own
            for i in range(1, narrow_n):
                value = jnp.where(behind == i, szrecv[i - 1], value)
            total = total + value
        s_out[...] = total

    def mlp_chain():
        plan, streams, sizes = scatter_sizes(wide_n, share)
        trail, base = [], 0
        for st, (here, _) in streams.items():
            for s in range(steps):
                b, size = plan[st][s], sizes[st][s + 1]
                halves = size < sizes[st][s]
                here = here + bit[b] * size if halves else here
                trail.append((s, b, here, size, halves))
            size = sizes[st][-1]
            gm[rows_at(bit[0] * share + here, size), :] = mine_ref[base : base + size, :]
            base += size
        yield
        yield
        for s in reversed(range(steps)):
            copies = []
            for s2, b, at, size, halves in trail:
                if s2 == s and halves:
                    part = gm.at[rows_at(bit[0] * share + at, size), :]
                    copies.append(links.copy(part, part, links.along(b)))
            go(copies)
            yield
            come(copies)
        part = gm.at[rows_at(bit[0] * share, share), :]
        c = links.copy(part, part, links.along(0))
        c.start()
        yield
        c.wait_recv()
        gm_out[...] = gm[...]

    going = [attn_chain(*c) for c in attn_chains(wide_n, ht)] + [mlp_chain(), small_chain()]
    while going:
        still = []
        for chain in going:
            try:
                next(chain)
                still.append(chain)
            except StopIteration:
                pass
        going = still
    gt_out[...] = gt[...]
    for c in links.all:
        c.wait_send()
    for c in to_hbm:
        c.wait()


def reduce_call(wide_n, narrow_n, share, mine, dq, do, misc, vec, dproj, tok, attn_w):
    width = mine.shape[1]
    rows = tok.shape[0]
    blocks = rows // CR
    ht = share // 2
    n_bits = wide_n.bit_length() - 1
    scratch = [
        pltpu.VMEM((blocks, CR, 3 * width), bf16), pltpu.VMEM((blocks, CR, width), bf16), pltpu.VMEM((blocks, CR, width), bf16),
        pltpu.VMEM((width, 3 * width), f32), pltpu.VMEM((width, 3 * width), bf16), pltpu.VMEM((2, 8, width), f32),
        pltpu.SemaphoreType.DMA((1 + 3 * blocks,)),
        pltpu.VMEM((narrow_n, ht, width), f32), pltpu.VMEM((narrow_n, ht, width), f32),
        pltpu.VMEM((2 * share, width), bf16), pltpu.VMEM((narrow_n, share, width), bf16),
        pltpu.VMEM((n_bits + 1,) + misc.shape, f32), pltpu.VMEM((n_bits,) + misc.shape, f32),
        pltpu.VMEM((narrow_n - 1,) + misc.shape, f32)]
    order = order_of_bufs(wide_n, narrow_n, ht)
    scratch += [pltpu.VMEM((lead, rows, width), bf16) for lead, rows in order for _ in range(2)]
    chains = len(attn_chains(wide_n, ht))
    copies = chains * (narrow_n + 2 * n_bits + 2 * narrow_n) + 4 * n_bits + narrow_n
    scratch += [pltpu.SemaphoreType.DMA((copies,)), pltpu.SemaphoreType.DMA((copies,))]
    vmem = pl.BlockSpec(memory_space=pltpu.VMEM)
    return pl.pallas_call(
        functools.partial(reduce_all, wide_n, narrow_n, share),
        out_shape=[sds((2 * share, width), bf16), sds((narrow_n, share, width), bf16), sds(misc.shape, f32),
                   sds((rows, width), bf16)],
        in_specs=[vmem] * 5 + [pl.BlockSpec(memory_space=pl.ANY)] * 3, out_specs=[vmem] * 3 + [pl.BlockSpec(memory_space=pl.ANY)], scratch_shapes=scratch,
        compiler_params=pltpu.CompilerParams(collective_id=0, has_side_effects=True, vmem_limit_bytes=60 * 1024 * 1024),
    )(mine, dq, do, misc, vec, dproj, tok, attn_w)


def order_of_bufs(wide_n, narrow_n, ht):
    chains = attn_chains(wide_n, ht)
    out = []
    for s in range(wide_n.bit_length() - 2):
        out += [(narrow_n, sizes[s + 1]) for _, _, sizes in chains]
    return out + [(narrow_n - 1, sizes[-1]) for _, _, sizes in chains]


def adam_kernel(narrow_ref, grad_stream, part, gt, gm, misc, aw, af, as_, mw, mf, ms, tw, tf, ts, vw, vf, vs, bw, bf, bs,
                input_grad, rms, an, al, afn, asn, mn, ml, mfn, msn, tn_, tfn, tsn, vn, vfn, vsn, bn, bfn, bsn):
    def put(new, w, g, m, v, rate, decay, low=None):
        out = adam_step(w, g, m, v, rate, decay)
        for ref, value in zip(new, out):
            ref[...] = value.reshape(ref.shape)
        if low is not None:
            low[...] = out[0].astype(bf16).reshape(low.shape)

    input_grad[...] = grad_stream[...] + part[...].astype(f32)
    put((an, afn, asn), aw[...], jnp.concatenate([gt[j].astype(f32) for j in range(4)], 1), af[...], as_[...], 0.02, 0.05, al)
    put((mn, mfn, msn), mw[0], gm[0].astype(f32), mf[0], ms[0], 0.02, 0.05, ml)

    @pl.when(pl.program_id(0) == 0)
    def _():
        put((vn, vfn, vsn), vw[...], misc[0:8, :], vf[...], vs[...], 0.3, 0.0)
        stats = misc[12:13, :]
        for i in range(3):
            ratio = jnp.sqrt(stats[:, i : i + 1] / (stats[:, 3:4] * misc.shape[1]))
            rms[i] = ratio[0, 0]
        n = narrow_ref[0]
        share = bw.shape[0]
        grad = jnp.zeros((1, share), f32)
        per = misc.shape[1] // share
        for i in range(4):
            for k in range(per):
                grad = jnp.where(n == per * i + k, misc[8 + i : 9 + i, share * k : share * k + share], grad)
        put((bn, bfn, bsn), bw[...], grad.reshape(share), bf[...], bs[...], 0.1, 0.0)
        heads, count = tw.shape
        put((tn_, tfn, tsn), tw[...], misc[16 : 16 + heads, :count], tf[...], ts[...], 0.3, 0.0)


def adam_call(narrow, grad_stream, part, gt, gm, misc, attn, mlp, table, vec, bias):
    width = gm.shape[1]
    share = mlp[0].shape[1]
    gt = gt.reshape(4, width, width)
    cuts = 4 if grad_stream.shape[0] % 64 == 0 else 2
    some = by_step(grad_stream, cuts)
    quarter = 2 * share // cuts
    rows = width // cuts
    gm = gm.reshape(cuts, quarter, width)
    mlp = [a.reshape(cuts, quarter, width) for a in mlp]
    line = pl.BlockSpec((rows, attn[0].shape[1]), lambda j, *_: (j, 0))
    lead = pl.BlockSpec((1, quarter, width), lambda j, *_: (j, 0, 0))
    split = pl.BlockSpec((4, rows, width), lambda j, *_: (0, j, 0))
    smalls = list(table) + list(vec) + list(bias)
    args = [grad_stream, part, gt, gm, misc] + list(attn) + mlp + smalls
    in_specs = [some, some, split, lead, whole(misc)] + [line] * 3 + [lead] * 3 + [whole(a) for a in smalls]
    three = lambda a: [sds(a.shape, f32)] * 3
    outs = [sds(grad_stream.shape, f32), sds((3,), f32), sds(attn[0].shape, f32), sds(attn[0].shape, bf16)] + [sds(attn[0].shape, f32)] * 2
    outs += [sds(mlp[0].shape, f32), sds(mlp[0].shape, bf16)] + [sds(mlp[0].shape, f32)] * 2
    outs += three(table[0]) + three(vec[0]) + three(bias[0])
    out_specs = [some, pl.BlockSpec(memory_space=pltpu.SMEM)] + [line] * 4 + [lead] * 4
    out_specs += [whole_out(a) for a in smalls]
    r = pl.pallas_call(
        adam_kernel,
        grid_spec=pltpu.PrefetchScalarGridSpec(num_scalar_prefetch=1, grid=(cuts,), in_specs=in_specs, out_specs=out_specs),
        out_shape=outs,
        compiler_params=pltpu.CompilerParams(vmem_limit_bytes=60 * 1024 * 1024),
    )(narrow, *args)
    full = (2, share, width)
    grad, r = r[0], r[1:]
    return [grad, r[0], *r[1:5], *[a.T for a in r[9:12]], *r[12:15], *[a.reshape(full) for a in r[5:9]], *r[15:18]]


def bias_layout(rel_table):
    pos = np.arange(WTOK)
    row, col = pos // WIN, pos % WIN
    off = (row[:, None] - row[None, :] + WIN - 1) * (2 * WIN - 1) + col[:, None] - col[None, :] + WIN - 1
    full = np.full((KR, SLOT), -1, np.int32)
    full[:WTOK, :WTOK] = off.T
    return full


def block(tokens, grid_sizes, cotangent, attn_weight, rel_table, vectors, mlp_weight, mlp_bias, narrow, wide_n, narrow_n, linked=True):
    rows, width = tokens.shape
    wins = rows // WTOK
    steps = wins // CW
    heads = rel_table.shape[0]
    groups = heads // HG
    share = mlp_weight.shape[1]
    hidden = share * narrow_n
    n_bits = wide_n.bit_length() - 1
    comm = (linked, steps)
    unit = rows * width * width
    hot = np.zeros((KR * SLOT, 256), np.float32)
    lay = bias_layout(rel_table).reshape(-1)
    hot[np.arange(KR * SLOT)[lay >= 0], lay[lay >= 0]] = 1.0
    hot = jnp.asarray(hot, bf16)
    mask = head_mask(width // heads)
    mask2 = mask.reshape(HG, SLOT, -1)[np.array([0, 2, 1, 3])].reshape(mask.shape)
    mask, mask2 = jnp.asarray(mask, bf16), jnp.asarray(mask2, bf16)
    rinfo, kinfo = jnp.asarray(row_info()), jnp.asarray(key_info())
    scal = (narrow, grid_sizes)
    pad = CR + 16
    copies = 3 * (narrow_n - 1) + 3 * 2 * (narrow_n - 1) + 4
    sem = [pltpu.SemaphoreType.DMA((copies,)), pltpu.SemaphoreType.DMA((copies,))] if linked else []
    sides = pltpu.VMEM((CR, 128), f32)
    table_s = pltpu.VMEM((groups, KR, HG * SLOT), f32)
    flat = pltpu.VMEM((16, KR * SLOT), f32)
    turned = pltpu.VMEM((CW, groups, SLOT, HG * SLOT), bf16)
    qkv, prob, mixed, stream, stats, gw, tails = run(
        functools.partial(attn_forward, wide_n, narrow_n, comm), steps, scal, (tokens,),
        wholes_of(attn_weight, mlp_weight, mlp_bias, vectors, rel_table, hot, rinfo, kinfo, mask, mask2, far=(0, 5)),
        [sds((wins, SLOT, 3 * width), bf16), sds((wins, groups, KR, HG * SLOT), f32), sds((rows, width), bf16), sds((rows, width), f32)],
        [sds((3, 8, width), f32), sds((narrow_n, 2 * share, width), bf16), sds((narrow_n, 8, width), f32)],
        [pltpu.VMEM((width, 4 * width), bf16), pltpu.VMEM((pad, 3 * width), f32), pltpu.VMEM((pad, width), f32), turned,
         table_s, pltpu.VMEM((16, 256), f32), flat, sides,
         pltpu.VMEM((2 * share, width), bf16), pltpu.VMEM((8, width), f32),
         pltpu.VMEM((narrow_n, 2 * share, width), bf16), pltpu.VMEM((narrow_n, 8, width), f32),
         pltpu.VMEM((width, 4 * width), f32), pltpu.VMEM(hot.shape, bf16), pltpu.SemaphoreType.DMA((2,))] + sem,
        12 * unit, 1 if linked else None)
    out_proj = pl.BlockSpec((width, width), lambda *_: (0, 3), pipeline_mode=pl.Buffered(1))
    fixed = (attn_weight, gw, tails, vectors, rinfo)
    outputs, grad_stream, gm, dmlp, dwo, dhid, dvec2 = run(
        functools.partial(feed_forward, TILE), steps, scal, (cotangent, mixed, stream),
        (fixed, [out_proj, pl.BlockSpec(memory_space=pl.ANY)] + [whole(a) for a in fixed[2:]]),
        [sds((rows, width), bf16), sds((rows, width), f32), sds((wins, SLOT, width), bf16)],
        [sds((narrow_n, 2 * share, width), f32), sds((width, width), f32), sds((8, hidden), f32), sds((5, 8, width), f32)],
        [pltpu.VMEM((width, width), bf16), pltpu.VMEM((hidden, width), bf16), pltpu.VMEM((hidden, width), bf16),
         pltpu.VMEM((1, hidden), f32), pltpu.VMEM((width, hidden), f32), pltpu.VMEM((width, hidden), f32),
         pltpu.VMEM((pad, width), f32), sides, pltpu.VMEM((ODD, width), bf16), pltpu.VMEM((ODD, width), bf16),
         pltpu.VMEM((ODD, hidden), bf16), pltpu.VMEM((ODD, hidden), bf16), pltpu.SemaphoreType.DMA((2 * narrow_n,))],
        52 * unit)
    _, streams, sizes = scatter_sizes(wide_n, share)
    last = sum(sizes[st][-1] for st in streams)
    bufs = []
    for s in range(n_bits - 1):
        for st in streams:
            bufs += [pltpu.VMEM((narrow_n, sizes[st][s + 1], width), bf16)] * 2
    copies = 1 + 2 * n_bits + narrow_n
    sem = [pltpu.SemaphoreType.DMA((copies,)), pltpu.SemaphoreType.DMA((copies,))] if linked else []
    dproj, dwq, misc, mine = run(
        functools.partial(attn_backward, wide_n, narrow_n, comm), steps, (), (tokens, qkv, prob, gm),
        wholes_of(vectors, hot, mask, mask2, dmlp, dhid, dvec2, stats, far=(4,)),
        [sds((rows, 3 * width), bf16)],
        [sds((3, width, width), f32), sds((32, width), f32), sds((last, width), bf16)],
        [pltpu.VMEM((pad, 3 * width), f32),
         pltpu.VMEM((CW, groups, KR, HG * SLOT), f32), turned, turned, pltpu.VMEM((3, 8, width), f32), table_s, flat,
         pltpu.VMEM((ODD, width), bf16), pltpu.VMEM((ODD, 3 * width), bf16), pltpu.VMEM(dmlp.shape, f32), pltpu.SemaphoreType.DMA((1,)),
         pltpu.VMEM((narrow_n, share, width), bf16), pltpu.VMEM((narrow_n, share, width), bf16),
         pltpu.VMEM((narrow_n, share, width), f32), pltpu.VMEM((narrow_n - 1, last, width), bf16),
         pltpu.VMEM((narrow_n - 1, last, width), bf16)] + bufs + sem,
        20 * unit, 2 if linked else None)
    return outputs, grad_stream, dmlp, dwq, dwo, misc, mine, dproj


TILE = 768


def adam_step(weight, gradient, first_old, second_old, rate_value, decay_value):
    first_new = beta_one * first_old + (1.0 - beta_one) * gradient
    second_new = beta_two * second_old + (1.0 - beta_two) * gradient * gradient
    fix_one = 1.0 - beta_one**STEP
    fix_two = 1.0 - beta_two**STEP
    update = rate_value * (first_new / fix_one) / (jnp.sqrt(second_new / fix_two) + adam_eps)
    return (weight - update - rate_value * decay_value * weight, first_new, second_new)


def shards(wide_n, narrow_n, tokens, grid_sizes, cotangent, attn_weight, attn_first, attn_second, rel_table, table_first,
           table_second, vectors, vector_first, vector_second, mlp_weight, mlp_first, mlp_second, mlp_bias, bias_first,
           bias_second):
    width = tokens.shape[1]
    narrow = lax.axis_index("narrow").reshape(1).astype(jnp.int32)
    outputs, grad_stream, _, dwq, dwo, misc, mine, dproj = block(
        tokens, grid_sizes, cotangent, attn_weight, rel_table.T, vectors, mlp_weight, mlp_bias, narrow, wide_n, narrow_n)
    gm, gt, misc, part = reduce_call(wide_n, narrow_n, mlp_weight.shape[1], mine, dwq.reshape(3 * width, width), dwo, misc,
                                     vectors, dproj, tokens, attn_weight)
    new = adam_call(narrow, grad_stream, part, gt, gm, misc, (attn_weight, attn_first, attn_second), (mlp_weight, mlp_first, mlp_second),
                    (rel_table.T, table_first.T, table_second.T), (vectors, vector_first, vector_second),
                    (mlp_bias, bias_first, bias_second))
    return (outputs, *new)


def solution(mesh):
    rows = P(("wide", "narrow"), None)
    split = P(None, "narrow", None)
    return jax.shard_map(
        functools.partial(shards, mesh.shape["wide"], mesh.shape["narrow"]), mesh=mesh,
        in_specs=(rows, P("wide"), rows) + (P(),) * 9 + (split,) * 3 + (P("narrow"),) * 3,
        out_specs=(rows, rows) + (P(),) * 11 + (split,) * 4 + (P("narrow"),) * 3,
        check_vma=False)
```

```python
import functools

import jax
import jax.numpy as jnp
import numpy as np
from jax import lax
from jax.sharding import PartitionSpec as P
from jax.experimental import pallas as pl
from jax.experimental.pallas import tpu as pltpu

WIN = 7
WTOK = 49
WPI = 16
IMG_W = 16
STEP = 5
CW = 16
CR = CW * WTOK
EVEN = CR // 256 * 256
ODD = 128
SLOT = 64
KR = 56
HG = 4
LOG2E = 1.4426950408889634

norm_eps = 1e-05
beta_one = 0.5
beta_two = 0.5
adam_eps = 1e-08
highest = lax.Precision.HIGHEST
f32 = jnp.float32
bf16 = jnp.bfloat16


def nn(a, b):
    return lax.dot_general(a, b, (((1,), (0,)), ((), ())), preferred_element_type=f32)


def nt(a, b):
    return lax.dot_general(a, b, (((1,), (1,)), ((), ())), preferred_element_type=f32)


def tn(a, b):
    return lax.dot_general(a, b, (((0,), (0,)), ((), ())), preferred_element_type=f32)


def row_info():
    r = np.arange(CR)
    win = r // WTOK
    p = r % WTOK
    info = np.stack([win, p // WIN, p % WIN]).astype(np.float32)
    info[1, win >= CW] = 1000.0
    return np.ascontiguousarray(np.broadcast_to(info[:, :, None], (3, CR, 128)))


def key_info():
    p = np.arange(KR)
    info = np.stack([p // WIN, p % WIN]).astype(np.float32)
    return np.ascontiguousarray(np.broadcast_to(info[:, :, None], (2, KR, 128)))


def head_mask(head_size):
    row = np.arange(HG * SLOT)
    lane = np.arange(HG * head_size)
    return (((row // SLOT)[:, None] == (lane // head_size)[None, :]) & ((row % SLOT) < WTOK)[:, None]).astype(np.float32)


def fold_rows(t):
    return jnp.sum(t.reshape(t.shape[0] // 8, 8, t.shape[1]), 0)


def rep(v, n):
    return jnp.concatenate([v] * n, 1)


def fill_sides(sides, info, side_s):
    win = info[0]
    value = jnp.zeros_like(win)
    for i in range(CW):
        value = jnp.where(win == float(i), sides[i].astype(f32), value)
    side_s[...] = value


def corner(narrow, step, steps):
    u = WPI - 1 - (narrow * steps + step)
    return (WIN * (u // 4)).astype(f32), (WIN * lax.rem(u, 4)).astype(f32)


def chunk_valid(info, side_s, top, left):
    side = side_s[...]
    return jnp.where((info[1] + top < side) & (info[2] + left < side), 1.0, 0.0)


def norm_stats(x):
    mean = jnp.mean(x, -1, keepdims=True)
    centred = x - mean
    inverse = lax.rsqrt(jnp.mean(centred * centred, -1, keepdims=True) + norm_eps)
    return centred * inverse, inverse


def norm_grad(g, xhat, inverse, gain):
    scaled = g * gain
    m1 = jnp.mean(scaled, -1, keepdims=True)
    m2 = jnp.mean(scaled * xhat, -1, keepdims=True)
    return inverse * (scaled - m1 - xhat * m2)


class Links:
    def __init__(self, wide_n, narrow_n, send_sem, recv_sem):
        self.w = lax.axis_index("wide")
        self.n = lax.axis_index("narrow")
        self.bits = wide_n.bit_length() - 1
        self.bit = [lax.rem(self.w // (1 << b), 2) for b in range(self.bits)]
        self.mate = [self.w + (1 - 2 * self.bit[b]) * (1 << b) for b in range(self.bits)]
        self.peer = [lax.rem(self.n + s, narrow_n) for s in range(1, narrow_n)]
        self.send_sem, self.recv_sem = send_sem, recv_sem
        self.used = 0
        self.all = []

    def copy(self, src, dst, device):
        k = self.used
        self.used += 1
        c = pltpu.make_async_remote_copy(
            src_ref=src, dst_ref=dst, send_sem=self.send_sem.at[k], recv_sem=self.recv_sem.at[k],
            device_id=device, device_id_type=pl.DeviceIdType.MESH)
        self.all.append(c)
        return c

    def along(self, b):
        return (self.mate[b], self.n)

    def over(self, n):
        return (self.w, n)

    def barrier(self):
        sem = pltpu.get_barrier_semaphore()
        for b in range(self.bits):
            pl.semaphore_signal(sem, inc=1, device_id=self.along(b), device_id_type=pl.DeviceIdType.MESH)
        for n in self.peer:
            pl.semaphore_signal(sem, inc=1, device_id=self.over(n), device_id_type=pl.DeviceIdType.MESH)
        pl.semaphore_wait(sem, self.bits + len(self.peer))


def gather_cuts(wide_n, rows):
    bits = list(range(min(3, wide_n.bit_length() - 1)))
    first = rows // 256 * 128
    return [(0, first, bits[1:] + bits[:1]), (first, rows - first, bits[1:][::-1] + bits[:1])]


def gather_plan(links, wide_n, own, tail_own, all_w, all_tail):
    narrow_n, rows, _ = all_w.shape
    streams = gather_cuts(wide_n, rows)
    stages = [[]]
    place, sizes = [], []
    for start, size, order in streams:
        piece = size >> len(order)
        off = 0
        for k, b in enumerate(order):
            off = off + links.bit[b] * (piece << k)
        place.append(start + off)
        sizes.append(piece)
    for n in links.peer:
        stages[0].append(links.copy(tail_own, all_tail.at[links.n], links.over(n)))
        for at, size in zip(place, sizes):
            here = pl.ds(pl.multiple_of(at, 16), size)
            stages[0].append(links.copy(own.at[here, :], all_w.at[links.n, here, :], links.over(n)))
    for k in range(len(streams[0][2])):
        stage = []
        for s, (start, size, order) in enumerate(streams):
            here = pl.ds(pl.multiple_of(place[s], 16), sizes[s])
            for n in links.peer:
                part = all_w.at[n, here, :]
                stage.append(links.copy(part, part, links.along(order[k])))
            place[s] = place[s] - links.bit[order[k]] * sizes[s]
            sizes[s] = sizes[s] * 2
        stages.append(stage)
    return stages


def run_stages(stages, step, steps):
    for k, stage in enumerate(stages):
        @pl.when(step == min(k, steps - 1))
        def _():
            if k:
                for c in stages[k - 1]:
                    c.wait()
            for c in stage:
                c.start()


def expand_table(table, hot, wide_t, flat, bias):
    heads, count = table.shape
    wide_t[...] = jnp.zeros_like(wide_t)
    wide_t[:heads, :count] = table[...] * LOG2E
    rest = wide_t[...]
    total = jnp.zeros((16, hot.shape[0]), f32)
    for _ in range(3):
        part = rest.astype(bf16)
        total += nt(part, hot[...])
        rest = rest - part.astype(f32)
    flat[...] = total
    bias[...] = jnp.full(bias.shape, -1e30, f32)
    for g in range(heads // HG):
        for k in range(WTOK):
            for h in range(HG):
                bias[g, k : k + 1, SLOT * h : SLOT * h + SLOT] = flat[HG * g + h : HG * g + h + 1, SLOT * k : SLOT * k + SLOT]


def turn(t):
    t = jnp.concatenate([t[:, :128], t[:, 128:]], 0).T
    return jnp.concatenate([t[:SLOT], t[SLOT:]], 1)


def padded(t):
    return jnp.concatenate([t, jnp.zeros((SLOT - KR, t.shape[1]), f32)], 0)


def four(t, mask):
    return jnp.concatenate([t] * HG, 0) * mask


BATCH = 16


def attn_forward(wide_n, narrow_n, comm, narrow_ref, sides, tok, attn_w, mlp_w, mlp_b, vec, table, hot, rinfo, kinfo, hmask, hmask2,
                 qkv_s, prob_out, mixed_out, stream_out, stats, gw_out, tail_out,
                 wq, pj, mx, turn_s, bias, wide_t, flat, side_s, own, tail_own, gw, tails, wide_w, hot_s, load_sem, *sems):
    step = pl.program_id(0)
    steps = pl.num_programs(0)
    static_steps = comm[1]
    width = tok.shape[1]
    groups = width // 128
    scale = 32 ** (-0.5)
    narrow = narrow_ref[0]
    share = mlp_w.shape[1]

    loads = [pltpu.make_async_copy(attn_w, wide_w, load_sem.at[0]), pltpu.make_async_copy(hot, hot_s, load_sem.at[1])]

    @pl.when(step == 0)
    def _():
        for c in loads:
            c.start()
        for j in range(2):
            own[share * j : share * j + share, :] = mlp_w[j].astype(bf16)
        tail_own[...] = jnp.zeros_like(tail_own)
        rest = mlp_b[...].reshape(1, share)
        for i in range(3):
            part = rest.astype(bf16).astype(f32)
            tail_own[i : i + 1, :share] = part
            rest = rest - part
        if comm[0]:
            gw[lax.axis_index("narrow")] = own[...]
            tails[lax.axis_index("narrow")] = tail_own[...]
        else:
            for n in range(narrow_n):
                gw[n] = own[...]
                tails[n] = tail_own[...]

    if comm[0]:
        links = Links(wide_n, narrow_n, *sems)

        @pl.when(step == 0)
        def _():
            links.barrier()

        stages = gather_plan(links, wide_n, own, tail_own, gw, tails)
        run_stages(stages, step, static_steps)

    @pl.when(step == 0)
    def _():
        fill_sides(sides, rinfo, side_s)
        for c in loads:
            c.wait()
        wq[...] = wide_w[...].astype(bf16)
        expand_table(table, hot_s, wide_t, flat, bias)
        for ref in (pj, mx, stats):
            ref[...] = jnp.zeros_like(ref)

    top, left = corner(narrow, step, static_steps)
    x = tok[...].astype(f32)
    valid = chunk_valid(rinfo, side_s, top, left)
    keep = rep(valid, groups)
    xhat, _ = norm_stats(x)
    low = (xhat * vec[0:1] + vec[1:2]).astype(bf16)
    pj[:CR, :width] = nn(low, wq[:, :width]) + vec[2:3]
    pj[:CR, width : 2 * width] = nn(low, wq[:, width : 2 * width])
    pj[:CR, 2 * width :] = nn(low, wq[:, 2 * width : 3 * width]) + vec[3:4]
    for i in range(CW):
        qkv_s[i] = pj[WTOK * i : WTOK * i + SLOT, :].astype(bf16)

    def score(b, carry):
        for k in range(BATCH):
            i = b * BATCH + k
            for g in range(groups):
                q_bd = four(qkv_s[i, :, 128 * g : 128 * g + 128], hmask[...])
                prob_out[i, g] = nt(qkv_s[i, :KR, width + 128 * g : width + 128 * g + 128], q_bd)
        return carry

    def soft(b, carry):
        for k in range(BATCH):
            i = b * BATCH + k
            side = sides[i].astype(f32)
            fill = jnp.where((kinfo[0] < side - top) & (kinfo[1] < side - left), 0.0, -10000.0 * LOG2E)
            fill = rep(fill, 2)
            for g in range(groups):
                s = prob_out[i, g] * (scale * LOG2E) + bias[g] + fill
                e = jnp.exp2(s - jnp.max(s, 0, keepdims=True))
                prob = e * (1.0 / jnp.sum(e, 0, keepdims=True))
                prob_out[i, g] = prob
                turn_s[i, g] = turn(padded(prob).astype(bf16))
        return carry

    lax.fori_loop(0, CW // BATCH, score, 0)
    lax.fori_loop(0, CW // BATCH, soft, 0)
    for i in range(CW):
        for g in range(groups):
            v_bd = four(qkv_s[i, :, 2 * width + 128 * g : 2 * width + 128 * g + 128], hmask2[...])
            mx[WTOK * i : WTOK * i + SLOT, 128 * g : 128 * g + 128] = nn(turn_s[i, g], v_bd)
    mixed = mx[:CR, :].astype(bf16)
    mixed_out[...] = mixed
    branch = (nn(mixed, wq[:, 3 * width :]) + vec[4:5]) * keep
    stream_out[...] = x + branch
    stats[0] += fold_rows(x * x * keep)
    stats[1] += fold_rows(branch * branch)
    stats[2, :, :128] += fold_rows(valid)

    @pl.when(step == steps - 1)
    def _():
        if comm[0]:
            for c in stages[-1]:
                c.wait()
        gw_out[...] = gw[...]
        tail_out[...] = tails[...]


def feed_forward(tile, narrow_ref, sides, cot, mixed_in, stream_in, attn_w, gw, tails, vec, rinfo,
                 out_ref, grad_stream_out, gm_s, dmlp, dwo, dhid, dvec,
                 wo, w1, w2, hb, dw1, dw2, mx, side_s, second_r, grad_r, pre_r, active_r, load_sem):
    step = pl.program_id(0)
    steps = pl.num_programs(0)
    width = cot.shape[1]
    groups = width // 128
    hidden = w1.shape[0]
    shards_n, twice, _ = gw.shape
    share = twice // 2
    loads = []
    for n in range(shards_n):
        for j, ref in enumerate((w1, w2)):
            loads.append(pltpu.make_async_copy(gw.at[n, pl.ds(share * j, share), :], ref.at[pl.ds(share * n, share), :],
                                               load_sem.at[2 * n + j]))

    @pl.when(step == 0)
    def _():
        for c in loads:
            c.start()
        wo[...] = attn_w[...].astype(bf16)
        for n in range(shards_n):
            three = tails[n]
            hb[:, share * n : share * n + share] = (three[0:1] + three[1:2] + three[2:3])[:, :share]
        fill_sides(sides, rinfo, side_s)
        for ref in (mx, dw1, dw2, dwo, dhid, dvec, second_r, grad_r, pre_r, active_r):
            ref[...] = jnp.zeros_like(ref)

    top, left = corner(narrow_ref[0], step, steps)
    keep = rep(chunk_valid(rinfo, side_s, top, left), groups)
    cotan = cot[...].astype(f32)
    stream = stream_in[...]
    xhat2, inverse2 = norm_stats(stream)
    second = (xhat2 * vec[5:6] + vec[6:7]).astype(bf16)
    kept_cot = cotan * keep
    grad_low = kept_cot.astype(bf16)
    second_t = jnp.concatenate([second[:EVEN].T, jnp.ones((16, EVEN), bf16)], 0)
    grad_t = grad_low[:EVEN].T
    odd = pl.ds(pl.multiple_of(step * (CR - EVEN), CR - EVEN), CR - EVEN)
    second_r[odd, :] = second[EVEN:]
    grad_r[odd, :] = grad_low[EVEN:]

    @pl.when(step == 0)
    def _():
        for c in loads:
            c.wait()

    mlp_out = jnp.zeros((CR, width), f32)
    grad_second = jnp.zeros((CR, width), f32)
    for t in range(hidden // tile):
        cols = slice(tile * t, tile * t + tile)
        pre = nt(second, w1[cols, :]) + hb[0:1, cols]
        square = pre * pre
        half = 0.5 * jnp.tanh(pre * (square * (0.7978845608028654 * 0.044715) + 0.7978845608028654)) + 0.5
        active = (pre * half).astype(bf16)
        slope = half + (pre * (half - half * half)) * (square * (6 * 0.7978845608028654 * 0.044715) + 2 * 0.7978845608028654)
        grad_pre = (nt(grad_low, w2[cols, :]) * slope).astype(bf16)
        mlp_out += nn(active, w2[cols, :])
        grad_second += nn(grad_pre, w1[cols, :])
        pre_r[odd, cols] = grad_pre[EVEN:]
        active_r[odd, cols] = active[EVEN:]
        outer = nn(second_t, grad_pre[:EVEN])
        dw1[:, cols] += outer[:width]
        dhid[:, cols] += outer[width : width + 8]
        dw2[:, cols] += nn(grad_t, active[:EVEN])
    branch = (mlp_out + vec[7:8]) * keep
    out_ref[...] = (stream + branch).astype(bf16)
    dvec[4] += fold_rows(branch * branch)
    dvec[0] += fold_rows(grad_second * xhat2)
    dvec[1] += fold_rows(grad_second)
    dvec[2] += fold_rows(kept_cot)
    grad_stream = cotan + norm_grad(grad_second, xhat2, inverse2, vec[5:6])
    grad_stream_out[...] = grad_stream
    grad_attn = grad_stream * keep
    dvec[3] += fold_rows(grad_attn)
    grad_attn_low = grad_attn.astype(bf16)
    dwo[...] += nn(mixed_in[...].T, grad_attn_low)
    mx[:CR, :] = nt(grad_attn_low, wo[...])
    for i in range(CW):
        gm_s[i] = mx[WTOK * i : WTOK * i + SLOT, :].astype(bf16)

    @pl.when(step == steps - 1)
    def _():
        rest_t = jnp.concatenate([second_r[...].T, jnp.ones((16, second_r.shape[0]), bf16)], 0)
        rest_g = grad_r[...].T
        for t in range(hidden // width):
            cols = slice(width * t, width * t + width)
            outer = nn(rest_t, pre_r[:, cols])
            dw1[:, cols] += outer[:width]
            dhid[:, cols] += outer[width : width + 8]
            dw2[:, cols] += nn(rest_g, active_r[:, cols])
        for j, ref in enumerate((dw1, dw2)):
            for t in range(hidden // width):
                turned = ref[:, width * t : width * t + width].T
                for k in range(width // share):
                    n = (width * t) // share + k
                    dmlp[n, share * j : share * j + share, :] = turned[share * k : share * k + share, :]


def scatter_sizes(wide_n, share):
    n_bits = wide_n.bit_length() - 1
    rest = list(range(1, n_bits))
    half = len(rest) // 2
    plan = {"A": rest, "B": rest[half:] + rest[:half]}
    cut = share // 2
    streams = {"A": (0, cut), "B": (cut, share - cut)}
    sizes = {}
    for st, (_, size) in streams.items():
        sizes[st] = [size]
        for _ in rest:
            sizes[st].append(sizes[st][-1] // 2 if sizes[st][-1] % 32 == 0 else sizes[st][-1])
    return plan, streams, sizes


def scatter_stages(links, wide_n, narrow_n, share, dmlp, mine_out, send0, recv0, acc, zsend, zrecv, bufs):
    plan, streams, sizes = scatter_sizes(wide_n, share)
    bit = links.bit
    keep0, away0 = bit[0] * share, (1 - bit[0]) * share
    stages = []

    def pack0():
        for n in range(narrow_n):
            def one(i, size):
                send0[n, pl.ds(i, size), :] = dmlp[n, pl.ds(pl.multiple_of(away0 + i, 16), size), :].astype(send0.dtype)
            loop_rows(share, one)

    def add0():
        for n in range(narrow_n):
            def one(i, size):
                acc[n, pl.ds(i, size), :] = (dmlp[n, pl.ds(pl.multiple_of(keep0 + i, 16), size), :]
                                             + recv0[n, pl.ds(i, size), :].astype(f32))
            loop_rows(share, one)

    stages.append((pack0, [links.copy(send0, recv0, links.along(0))], add0))
    place = {st: streams[st][0] for st in streams}
    trail = []
    for s in range(links.bits - 1):
        work = []
        for k, st in enumerate(streams):
            b = plan[st][s]
            size = sizes[st][s + 1]
            halves = size < sizes[st][s]
            send, recv = bufs[2 * (2 * s + k)], bufs[2 * (2 * s + k) + 1]
            here = place[st]
            out_at, in_at = (here + (1 - bit[b]) * size, here + bit[b] * size) if halves else (here, here)
            place[st] = in_at
            work.append((send, recv, out_at, in_at, size, halves, links.copy(send, recv, links.along(b))))
            trail.append((st, s, b, in_at, size, halves))

        def pack(work=work):
            for send, recv, out_at, in_at, size, halves, _ in work:
                for n in range(narrow_n):
                    def one(i, k):
                        send[n, pl.ds(i, k), :] = acc[n, pl.ds(pl.multiple_of(out_at + i, 16), k), :].astype(send.dtype)
                    loop_rows(size, one)

        def add(work=work):
            for send, recv, out_at, in_at, size, halves, _ in work:
                for n in range(narrow_n):
                    def one(i, k):
                        here = pl.ds(pl.multiple_of(in_at + i, 16), k)
                        mine = acc[n, here, :] if halves else send[n, pl.ds(i, k), :].astype(f32)
                        acc[n, here, :] = mine + recv[n, pl.ds(i, k), :].astype(f32)
                    loop_rows(size, one)

        stages.append((pack, [w[-1] for w in work], add))
    base, total = {}, 0
    for st in streams:
        base[st] = total
        total += sizes[st][-1]

    def packz():
        for i, n in enumerate(links.peer):
            for st in streams:
                def one(r, k):
                    zsend[i, pl.ds(base[st] + r, k), :] = acc[n, pl.ds(pl.multiple_of(place[st] + r, 16), k), :].astype(zsend.dtype)
                loop_rows(sizes[st][-1], one)

    def addz():
        for st in streams:
            def one(r, k):
                value = acc[links.n, pl.ds(pl.multiple_of(place[st] + r, 16), k), :]
                for i in range(narrow_n - 1):
                    value = value + zrecv[i, pl.ds(base[st] + r, k), :].astype(f32)
                mine_out[pl.ds(base[st] + r, k), :] = value.astype(bf16)
            loop_rows(sizes[st][-1], one)

    stages.append((packz, [links.copy(zsend.at[i], zrecv.at[i], links.over(n)) for i, n in enumerate(links.peer)], addz))
    return stages


def attn_backward(wide_n, narrow_n, comm, tok, qkv_s, prob_in, gm_s, vec, hot, hmask, hmask2,
                  dmlp, dhid, dvec2, stats,
                  dproj_out, dwq, misc, mine_out,
                  pj, gp_s, low_s, turn_s, dext, dtable, flat, low_r, proj_r, dmlp_s, load_sem, send0, recv0, acc, zsend, zrecv, *rest):
    step = pl.program_id(0)
    steps = pl.num_programs(0)
    static_steps = comm[1]
    width = tok.shape[1]
    groups = width // 128
    scale = 32 ** (-0.5)
    share = dmlp.shape[1] // 2
    load = pltpu.make_async_copy(dmlp, dmlp_s, load_sem.at[0])

    if comm[0]:
        links = Links(wide_n, narrow_n, *rest[-2:])

        @pl.when(step == 0)
        def _():
            links.barrier()

        @pl.when(step == 0)
        def _():
            load.start()

    @pl.when(step == 0)
    def _():
        for ref in (dwq, dext, dtable, low_r, proj_r):
            ref[...] = jnp.zeros_like(ref)

    def first(b, carry):
        for k in range(BATCH):
            i = b * BATCH + k
            for g in range(groups):
                do_bd = four(gm_s[i, :, 128 * g : 128 * g + 128], hmask[...])
                gp_s[i, g] = nt(qkv_s[i, :KR, 2 * width + 128 * g : 2 * width + 128 * g + 128], do_bd)
        return carry

    def second(b, carry):
        for g in range(groups):
            total = dtable[g]
            for k in range(BATCH):
                i = b * BATCH + k
                gp = gp_s[i, g]
                prob = prob_in[i, g]
                ds = prob * (gp - jnp.sum(gp * prob, 0, keepdims=True))
                total = total + ds
                raw = padded(ds * scale).astype(bf16)
                low_s[i, g] = raw
                turn_s[i, g] = turn(raw)
            dtable[g] = total
        return carry

    lax.fori_loop(0, CW // BATCH, first, 0)
    if comm[0]:
        stages = scatter_stages(links, wide_n, narrow_n, share, dmlp_s, mine_out, send0, recv0, acc, zsend, zrecv, rest[:-2])
        for k, (pack, copies, add) in enumerate(stages):
            @pl.when(step == min(k, static_steps - 1))
            def _():
                if not k:
                    load.wait()
                if k:
                    for c in stages[k - 1][1]:
                        c.wait()
                    stages[k - 1][2]()
                pack()
                for c in copies:
                    c.start()

    lax.fori_loop(0, CW // BATCH, second, 0)
    for i in range(CW):
        rows = slice(WTOK * i, WTOK * i + SLOT)
        for g in range(groups):
            q_bd = four(qkv_s[i, :, 128 * g : 128 * g + 128], hmask[...])
            k_bd = four(qkv_s[i, :, width + 128 * g : width + 128 * g + 128], hmask2[...])
            do_bd = four(gm_s[i, :, 128 * g : 128 * g + 128], hmask[...])
            pj[rows, 128 * g : 128 * g + 128] = nn(turn_s[i, g], k_bd)
            pj[rows, width + 128 * g : width + 128 * g + 128] = nn(low_s[i, g], q_bd)
            pj[rows, 2 * width + 128 * g : 2 * width + 128 * g + 128] = nn(padded(prob_in[i, g]).astype(bf16), do_bd)
    dproj = pj[:CR, :].astype(bf16)
    dproj_out[...] = dproj
    x = tok[...].astype(f32)
    xhat, _ = norm_stats(x)
    low = (xhat * vec[0:1] + vec[1:2]).astype(bf16)
    low_t = jnp.concatenate([low[:EVEN].T, jnp.ones((16, EVEN), bf16)], 0)
    odd = pl.ds(pl.multiple_of(step * (CR - EVEN), CR - EVEN), CR - EVEN)
    low_r[odd, :] = low[EVEN:]
    proj_r[odd, :] = dproj[EVEN:]
    for j in range(3):
        outer = nn(low_t, dproj[:EVEN, width * j : width * j + width])
        dwq[j] += outer[:width]
        dext[j] += outer[width : width + 8]

    @pl.when(step == steps - 1)
    def _():
        rest_t = jnp.concatenate([low_r[...].T, jnp.ones((16, low_r.shape[0]), bf16)], 0)
        for j in range(3):
            outer = nn(rest_t, proj_r[:, width * j : width * j + width])
            dwq[j] += outer[:width]
            dext[j] += outer[width : width + 8]
        rows = [None, None, None, None, dvec2[3], dvec2[0], dvec2[1], dvec2[2]]
        for i, part in enumerate(rows):
            if part is not None:
                misc[i : i + 1, :] = jnp.sum(part, 0, keepdims=True)
        misc[0:2, :] = jnp.zeros((2, width), f32)
        misc[2:3, :] = dext[0, 0:1, :]
        misc[3:4, :] = dext[2, 0:1, :]
        for i in range(dhid.shape[1] // width):
            misc[8 + i : 9 + i, :] = dhid[0:1, width * i : width * i + width]
        lane = lax.broadcasted_iota(jnp.int32, (1, width), 1)
        line = jnp.zeros((1, width), f32)
        for i, part in enumerate((stats[0], stats[1], dvec2[4])):
            line = jnp.where(lane == i, jnp.sum(part), line)
        misc[12:13, :] = jnp.where(lane == 3, jnp.sum(stats[2]) / 128.0, line)
        misc[13:16, :] = jnp.zeros((3, width), f32)
        flat[...] = jnp.zeros_like(flat)
        for g in range(groups):
            for k in range(WTOK):
                line = dtable[g, k : k + 1, :]
                for h in range(HG):
                    flat[HG * g + h : HG * g + h + 1, SLOT * k : SLOT * k + SLOT] = line[:, SLOT * h : SLOT * h + SLOT]
        rest_f = flat[...]
        total = jnp.zeros((16, 256), f32)
        for _ in range(3):
            part = rest_f.astype(bf16)
            total += nn(part, hot[...])
            rest_f = rest_f - part.astype(f32)
        misc[16:32, :] = jnp.zeros((16, width), f32)
        misc[16:32, :256] = total
        if comm[0]:
            for c in stages[-1][1]:
                c.wait()
            stages[-1][2]()


def sds(shape, dt):
    return jax.ShapeDtypeStruct(shape, dt)


def whole(a):
    nd = len(a.shape)
    return pl.BlockSpec(a.shape, lambda *_: (0,) * nd, pipeline_mode=pl.Buffered(1))


def whole_out(a):
    nd = len(a.shape)
    return pl.BlockSpec(a.shape, lambda *_: (0,) * nd)


def by_step(a, steps):
    nd = len(a.shape)
    return pl.BlockSpec((a.shape[0] // steps,) + tuple(a.shape[1:]), lambda c, *_: (c,) + (0,) * (nd - 1))


def run(body, steps, scalars, stepped, wholes, out_stepped, out_wholes, scratch, flops, collective_id=None):
    smem = pl.BlockSpec(memory_space=pltpu.SMEM)
    params = dict(vmem_limit_bytes=62 * 1024 * 1024)
    if collective_id is not None:
        params.update(collective_id=collective_id, has_side_effects=True)
    return pl.pallas_call(
        body, grid=(steps,),
        in_specs=[smem] * len(scalars) + [by_step(a, steps) for a in stepped] + wholes[1],
        out_specs=[by_step(a, steps) for a in out_stepped] + [whole_out(a) for a in out_wholes],
        out_shape=list(out_stepped) + list(out_wholes), scratch_shapes=scratch,
        compiler_params=pltpu.CompilerParams(**params),
        cost_estimate=pl.CostEstimate(flops=flops, bytes_accessed=20000000, transcendentals=0),
    )(*scalars, *stepped, *wholes[0])


def wholes_of(*arrays, far=()):
    return (arrays, [pl.BlockSpec(memory_space=pl.ANY) if i in far else whole(a) for i, a in enumerate(arrays)])


def loop_rows(total, body):
    size = next(n for n in (96, 64, 48, 32, 16) if total % n == 0)
    lax.fori_loop(0, total // size, lambda i, c: (body(pl.multiple_of(i * size, size), size), c)[1], 0)


def attn_chains(wide_n, half):
    rest = list(range(1, wide_n.bit_length() - 1))
    turned = rest[len(rest) // 2 :] + rest[: len(rest) // 2]
    chains, start = [], 0
    while start < half:
        sizes = [min(64, half - start)]
        for _ in rest:
            sizes.append(sizes[-1] // 2 if sizes[-1] % 32 == 0 else sizes[-1])
        chains.append((start, turned if len(chains) % 2 else rest, sizes))
        start += sizes[0]
    return chains


def reduce_all(wide_n, narrow_n, share, mine_ref, q_ref, o_ref, s_ref, vec, dproj, tok, attn_w, gm_out, gt_out, s_out, part_out,
               proj_s, tok_s, part_s, wide_w, wq, dvec, own_sem, recv0, acct, gm, gt, sbuf, srecv, szrecv, *rest):
    bufs = list(rest[:-2])
    links = Links(wide_n, narrow_n, *rest[-2:])
    bit, me_n, peer = links.bit, links.n, links.peer
    steps = links.bits - 1
    width = q_ref.shape[1]
    blocks = proj_s.shape[0]
    at_block = [pl.ds(CR * b, CR) for b in range(blocks)]
    from_hbm = [pltpu.make_async_copy(attn_w.at[:, pl.ds(0, 3 * width)], wide_w, own_sem.at[0])]
    for b in range(blocks):
        from_hbm.append(pltpu.make_async_copy(dproj.at[at_block[b], :], proj_s.at[b], own_sem.at[1 + 2 * b]))
        from_hbm.append(pltpu.make_async_copy(tok.at[at_block[b], :], tok_s.at[b], own_sem.at[2 + 2 * b]))
    to_hbm = [pltpu.make_async_copy(part_s.at[b], part_out.at[at_block[b], :], own_sem.at[1 + 2 * blocks + b]) for b in range(blocks)]
    for c in from_hbm:
        c.start()
    links.barrier()
    ht = acct.shape[1]
    away, keep = (1 - bit[0]) * ht, bit[0] * ht

    def rows_at(at, size):
        return pl.ds(pl.multiple_of(at, 16), size)

    def go(copies):
        for c in copies:
            c.start()

    def come(copies):
        for c in copies:
            c.wait_recv()

    def attn_chain(start, order, sizes):
        copies = []
        for n in range(narrow_n):
            flat = n * share
            src, off = (q_ref, flat) if flat < q_ref.shape[0] else (o_ref, flat - q_ref.shape[0])
            copies.append(links.copy(src.at[rows_at(off + away + start, sizes[0]), :],
                                     recv0.at[n, pl.ds(start, sizes[0]), :], links.along(0)))
        go(copies)
        yield
        come(copies)
        for n in range(narrow_n):
            flat = n * share
            src, off = (q_ref, flat) if flat < q_ref.shape[0] else (o_ref, flat - q_ref.shape[0])
            def add0(i, size):
                acct[n, pl.ds(start + i, size), :] = (src[rows_at(off + keep + start + i, size), :]
                                                      + recv0[n, pl.ds(start + i, size), :])
            loop_rows(sizes[0], add0)
        here = start
        trail = []
        for s in range(steps):
            b, size = order[s], sizes[s + 1]
            halves = size < sizes[s]
            send, recv = bufs.pop(0), bufs.pop(0)
            out_at, in_at = (here + (1 - bit[b]) * size, here + bit[b] * size) if halves else (here, here)
            for n in range(narrow_n):
                def pack(i, k):
                    send[n, pl.ds(i, k), :] = acct[n, rows_at(out_at + i, k), :].astype(bf16)
                loop_rows(size, pack)
            c = links.copy(send, recv, links.along(b))
            c.start()
            yield
            c.wait_recv()
            for n in range(narrow_n):
                def add(i, k):
                    own = acct[n, rows_at(in_at + i, k), :] if halves else send[n, pl.ds(i, k), :].astype(f32)
                    acct[n, rows_at(in_at + i, k), :] = own + recv[n, pl.ds(i, k), :].astype(f32)
                loop_rows(size, add)
            here = in_at
            trail.append((b, in_at, size, halves))
        size = sizes[-1]
        zsend, zrecv = bufs.pop(0), bufs.pop(0)
        copies = []
        for i, n in enumerate(peer):
            def pack(r, k):
                zsend[i, pl.ds(r, k), :] = acct[n, rows_at(here + r, k), :].astype(bf16)
            loop_rows(size, pack)
            copies.append(links.copy(zsend.at[i], zrecv.at[i], links.over(n)))
            copies[-1].start()
        yield
        come(copies)
        def add(r, k):
            value = acct[me_n, rows_at(here + r, k), :]
            for i in range(narrow_n - 1):
                value = value + zrecv[i, pl.ds(r, k), :].astype(f32)
            gt[me_n, rows_at(keep + here + r, k), :] = value.astype(bf16)
        loop_rows(size, add)
        part = gt.at[me_n, rows_at(keep + here, size), :]
        copies = [links.copy(part, part, links.over(n)) for n in peer]
        go(copies)
        yield
        come(copies)
        for b, at, size, halves in reversed(trail):
            if halves:
                part = gt.at[:, rows_at(keep + at, size), :]
                c = links.copy(part, part, links.along(b))
                c.start()
                yield
                c.wait_recv()
        part = gt.at[:, rows_at(keep + start, sizes[0]), :]
        c = links.copy(part, part, links.along(0))
        c.start()
        yield
        c.wait_recv()

    def small_chain():
        yield
        from_hbm[0].wait()
        wq[...] = wide_w[...].astype(bf16)
        dvec[...] = jnp.zeros_like(dvec)
        for b in range(blocks):
            from_hbm[1 + 2 * b].wait()
            from_hbm[2 + 2 * b].wait()
            xhat, inverse = norm_stats(tok_s[b].astype(f32))
            grad_normed = nt(proj_s[b], wq[...])
            dvec[0] += fold_rows(grad_normed * xhat)
            dvec[1] += fold_rows(grad_normed)
            part_s[b] = norm_grad(grad_normed, xhat, inverse, vec[0:1]).astype(bf16)
            to_hbm[b].start()
            if b % 2:
                yield
        sbuf[0] = s_ref[...]
        for i in range(2):
            sbuf[0, i : i + 1, :] = jnp.sum(dvec[i], 0, keepdims=True)
        for b in range(links.bits):
            c = links.copy(sbuf.at[b], srecv.at[b], links.along(b))
            c.start()
            yield
            c.wait_recv()
            sbuf[b + 1] = sbuf[b] + srecv[b]
        copies = [links.copy(sbuf.at[links.bits], szrecv.at[i], links.over(n)) for i, n in enumerate(peer)]
        go(copies)
        yield
        come(copies)
        own = sbuf[links.bits]
        total = jnp.zeros_like(own)
        for n in range(narrow_n):
            behind = lax.rem(me_n + narrow_n - n, narrow_n)
            value = own
            for i in range(1, narrow_n):
                value = jnp.where(behind == i, szrecv[i - 1], value)
            total = total + value
        s_out[...] = total

    def mlp_chain():
        plan, streams, sizes = scatter_sizes(wide_n, share)
        trail, base = [], 0
        for st, (here, _) in streams.items():
            for s in range(steps):
                b, size = plan[st][s], sizes[st][s + 1]
                halves = size < sizes[st][s]
                here = here + bit[b] * size if halves else here
                trail.append((s, b, here, size, halves))
            size = sizes[st][-1]
            gm[rows_at(bit[0] * share + here, size), :] = mine_ref[base : base + size, :]
            base += size
        yield
        yield
        for s in reversed(range(steps)):
            copies = []
            for s2, b, at, size, halves in trail:
                if s2 == s and halves:
                    part = gm.at[rows_at(bit[0] * share + at, size), :]
                    copies.append(links.copy(part, part, links.along(b)))
            go(copies)
            yield
            come(copies)
        part = gm.at[rows_at(bit[0] * share, share), :]
        c = links.copy(part, part, links.along(0))
        c.start()
        yield
        c.wait_recv()
        gm_out[...] = gm[...]

    going = [attn_chain(*c) for c in attn_chains(wide_n, ht)] + [mlp_chain(), small_chain()]
    rounds = 0
    while going:
        still = []
        if rounds == 3:
            going = going[-1:] + going[:-1]
        rounds += 1
        for chain in going:
            try:
                next(chain)
                still.append(chain)
            except StopIteration:
                pass
        going = still
    gt_out[...] = gt[...]
    for c in links.all:
        c.wait_send()
    for c in to_hbm:
        c.wait()


def reduce_call(wide_n, narrow_n, share, mine, dq, do, misc, vec, dproj, tok, attn_w):
    width = mine.shape[1]
    rows = tok.shape[0]
    blocks = rows // CR
    ht = share // 2
    n_bits = wide_n.bit_length() - 1
    scratch = [
        pltpu.VMEM((blocks, CR, 3 * width), bf16), pltpu.VMEM((blocks, CR, width), bf16), pltpu.VMEM((blocks, CR, width), bf16),
        pltpu.VMEM((width, 3 * width), f32), pltpu.VMEM((width, 3 * width), bf16), pltpu.VMEM((2, 8, width), f32),
        pltpu.SemaphoreType.DMA((1 + 3 * blocks,)),
        pltpu.VMEM((narrow_n, ht, width), f32), pltpu.VMEM((narrow_n, ht, width), f32),
        pltpu.VMEM((2 * share, width), bf16), pltpu.VMEM((narrow_n, share, width), bf16),
        pltpu.VMEM((n_bits + 1,) + misc.shape, f32), pltpu.VMEM((n_bits,) + misc.shape, f32),
        pltpu.VMEM((narrow_n - 1,) + misc.shape, f32)]
    order = order_of_bufs(wide_n, narrow_n, ht)
    scratch += [pltpu.VMEM((lead, rows, width), bf16) for lead, rows in order for _ in range(2)]
    chains = len(attn_chains(wide_n, ht))
    copies = chains * (narrow_n + 2 * n_bits + 2 * narrow_n) + 4 * n_bits + narrow_n
    scratch += [pltpu.SemaphoreType.DMA((copies,)), pltpu.SemaphoreType.DMA((copies,))]
    vmem = pl.BlockSpec(memory_space=pltpu.VMEM)
    return pl.pallas_call(
        functools.partial(reduce_all, wide_n, narrow_n, share),
        out_shape=[sds((2 * share, width), bf16), sds((narrow_n, share, width), bf16), sds(misc.shape, f32),
                   sds((rows, width), bf16)],
        in_specs=[vmem] * 5 + [pl.BlockSpec(memory_space=pl.ANY)] * 3, out_specs=[vmem] * 3 + [pl.BlockSpec(memory_space=pl.ANY)], scratch_shapes=scratch,
        compiler_params=pltpu.CompilerParams(collective_id=0, has_side_effects=True, vmem_limit_bytes=60 * 1024 * 1024),
    )(mine, dq, do, misc, vec, dproj, tok, attn_w)


def order_of_bufs(wide_n, narrow_n, ht):
    chains = attn_chains(wide_n, ht)
    out = []
    for s in range(wide_n.bit_length() - 2):
        out += [(narrow_n, sizes[s + 1]) for _, _, sizes in chains]
    return out + [(narrow_n - 1, sizes[-1]) for _, _, sizes in chains]


def adam_kernel(narrow_ref, grad_stream, part, gt, gm, misc, aw, af, as_, mw, mf, ms, tw, tf, ts, vw, vf, vs, bw, bf, bs,
                input_grad, rms, an, al, afn, asn, mn, ml, mfn, msn, tn_, tfn, tsn, vn, vfn, vsn, bn, bfn, bsn):
    def put(new, w, g, m, v, rate, decay, low=None):
        out = adam_step(w, g, m, v, rate, decay)
        for ref, value in zip(new, out):
            ref[...] = value.reshape(ref.shape)
        if low is not None:
            low[...] = out[0].astype(bf16).reshape(low.shape)

    input_grad[...] = grad_stream[...] + part[...].astype(f32)
    put((an, afn, asn), aw[...], jnp.concatenate([gt[j].astype(f32) for j in range(4)], 1), af[...], as_[...], 0.02, 0.05, al)
    put((mn, mfn, msn), mw[0], gm[0].astype(f32), mf[0], ms[0], 0.02, 0.05, ml)

    @pl.when(pl.program_id(0) == 0)
    def _():
        put((vn, vfn, vsn), vw[...], misc[0:8, :], vf[...], vs[...], 0.3, 0.0)
        stats = misc[12:13, :]
        for i in range(3):
            ratio = jnp.sqrt(stats[:, i : i + 1] / (stats[:, 3:4] * misc.shape[1]))
            rms[i] = ratio[0, 0]
        n = narrow_ref[0]
        share = bw.shape[0]
        grad = jnp.zeros((1, share), f32)
        per = misc.shape[1] // share
        for i in range(4):
            for k in range(per):
                grad = jnp.where(n == per * i + k, misc[8 + i : 9 + i, share * k : share * k + share], grad)
        put((bn, bfn, bsn), bw[...], grad.reshape(share), bf[...], bs[...], 0.1, 0.0)
        heads, count = tw.shape
        put((tn_, tfn, tsn), tw[...], misc[16 : 16 + heads, :count], tf[...], ts[...], 0.3, 0.0)


def adam_call(narrow, grad_stream, part, gt, gm, misc, attn, mlp, table, vec, bias):
    width = gm.shape[1]
    share = mlp[0].shape[1]
    gt = gt.reshape(4, width, width)
    cuts = 4 if grad_stream.shape[0] % 64 == 0 else 2
    some = by_step(grad_stream, cuts)
    quarter = 2 * share // cuts
    rows = width // cuts
    gm = gm.reshape(cuts, quarter, width)
    mlp = [a.reshape(cuts, quarter, width) for a in mlp]
    line = pl.BlockSpec((rows, attn[0].shape[1]), lambda j, *_: (j, 0))
    lead = pl.BlockSpec((1, quarter, width), lambda j, *_: (j, 0, 0))
    split = pl.BlockSpec((4, rows, width), lambda j, *_: (0, j, 0))
    smalls = list(table) + list(vec) + list(bias)
    args = [grad_stream, part, gt, gm, misc] + list(attn) + mlp + smalls
    in_specs = [some, some, split, lead, whole(misc)] + [line] * 3 + [lead] * 3 + [whole(a) for a in smalls]
    three = lambda a: [sds(a.shape, f32)] * 3
    outs = [sds(grad_stream.shape, f32), sds((3,), f32), sds(attn[0].shape, f32), sds(attn[0].shape, bf16)] + [sds(attn[0].shape, f32)] * 2
    outs += [sds(mlp[0].shape, f32), sds(mlp[0].shape, bf16)] + [sds(mlp[0].shape, f32)] * 2
    outs += three(table[0]) + three(vec[0]) + three(bias[0])
    out_specs = [some, pl.BlockSpec(memory_space=pltpu.SMEM)] + [line] * 4 + [lead] * 4
    out_specs += [whole_out(a) for a in smalls]
    r = pl.pallas_call(
        adam_kernel,
        grid_spec=pltpu.PrefetchScalarGridSpec(num_scalar_prefetch=1, grid=(cuts,), in_specs=in_specs, out_specs=out_specs),
        out_shape=outs,
        compiler_params=pltpu.CompilerParams(vmem_limit_bytes=60 * 1024 * 1024),
    )(narrow, *args)
    full = (2, share, width)
    grad, r = r[0], r[1:]
    return [grad, r[0], *r[1:5], *[a.T for a in r[9:12]], *r[12:15], *[a.reshape(full) for a in r[5:9]], *r[15:18]]


def bias_layout(rel_table):
    pos = np.arange(WTOK)
    row, col = pos // WIN, pos % WIN
    off = (row[:, None] - row[None, :] + WIN - 1) * (2 * WIN - 1) + col[:, None] - col[None, :] + WIN - 1
    full = np.full((KR, SLOT), -1, np.int32)
    full[:WTOK, :WTOK] = off.T
    return full


def block(tokens, grid_sizes, cotangent, attn_weight, rel_table, vectors, mlp_weight, mlp_bias, narrow, wide_n, narrow_n, linked=True):
    rows, width = tokens.shape
    wins = rows // WTOK
    steps = wins // CW
    heads = rel_table.shape[0]
    groups = heads // HG
    share = mlp_weight.shape[1]
    hidden = share * narrow_n
    n_bits = wide_n.bit_length() - 1
    comm = (linked, steps)
    unit = rows * width * width
    hot = np.zeros((KR * SLOT, 256), np.float32)
    lay = bias_layout(rel_table).reshape(-1)
    hot[np.arange(KR * SLOT)[lay >= 0], lay[lay >= 0]] = 1.0
    hot = jnp.asarray(hot, bf16)
    mask = head_mask(width // heads)
    mask2 = mask.reshape(HG, SLOT, -1)[np.array([0, 2, 1, 3])].reshape(mask.shape)
    mask, mask2 = jnp.asarray(mask, bf16), jnp.asarray(mask2, bf16)
    rinfo, kinfo = jnp.asarray(row_info()), jnp.asarray(key_info())
    scal = (narrow, grid_sizes)
    pad = CR + 16
    copies = 3 * (narrow_n - 1) + 3 * 2 * (narrow_n - 1) + 4
    sem = [pltpu.SemaphoreType.DMA((copies,)), pltpu.SemaphoreType.DMA((copies,))] if linked else []
    sides = pltpu.VMEM((CR, 128), f32)
    table_s = pltpu.VMEM((groups, KR, HG * SLOT), f32)
    flat = pltpu.VMEM((16, KR * SLOT), f32)
    turned = pltpu.VMEM((CW, groups, SLOT, HG * SLOT), bf16)
    qkv, prob, mixed, stream, stats, gw, tails = run(
        functools.partial(attn_forward, wide_n, narrow_n, comm), steps, scal, (tokens,),
        wholes_of(attn_weight, mlp_weight, mlp_bias, vectors, rel_table, hot, rinfo, kinfo, mask, mask2, far=(0, 5)),
        [sds((wins, SLOT, 3 * width), bf16), sds((wins, groups, KR, HG * SLOT), f32), sds((rows, width), bf16), sds((rows, width), f32)],
        [sds((3, 8, width), f32), sds((narrow_n, 2 * share, width), bf16), sds((narrow_n, 8, width), f32)],
        [pltpu.VMEM((width, 4 * width), bf16), pltpu.VMEM((pad, 3 * width), f32), pltpu.VMEM((pad, width), f32), turned,
         table_s, pltpu.VMEM((16, 256), f32), flat, sides,
         pltpu.VMEM((2 * share, width), bf16), pltpu.VMEM((8, width), f32),
         pltpu.VMEM((narrow_n, 2 * share, width), bf16), pltpu.VMEM((narrow_n, 8, width), f32),
         pltpu.VMEM((width, 4 * width), f32), pltpu.VMEM(hot.shape, bf16), pltpu.SemaphoreType.DMA((2,))] + sem,
        12 * unit, 1 if linked else None)
    out_proj = pl.BlockSpec((width, width), lambda *_: (0, 3), pipeline_mode=pl.Buffered(1))
    fixed = (attn_weight, gw, tails, vectors, rinfo)
    outputs, grad_stream, gm, dmlp, dwo, dhid, dvec2 = run(
        functools.partial(feed_forward, TILE), steps, scal, (cotangent, mixed, stream),
        (fixed, [out_proj, pl.BlockSpec(memory_space=pl.ANY)] + [whole(a) for a in fixed[2:]]),
        [sds((rows, width), bf16), sds((rows, width), f32), sds((wins, SLOT, width), bf16)],
        [sds((narrow_n, 2 * share, width), f32), sds((width, width), f32), sds((8, hidden), f32), sds((5, 8, width), f32)],
        [pltpu.VMEM((width, width), bf16), pltpu.VMEM((hidden, width), bf16), pltpu.VMEM((hidden, width), bf16),
         pltpu.VMEM((1, hidden), f32), pltpu.VMEM((width, hidden), f32), pltpu.VMEM((width, hidden), f32),
         pltpu.VMEM((pad, width), f32), sides, pltpu.VMEM((ODD, width), bf16), pltpu.VMEM((ODD, width), bf16),
         pltpu.VMEM((ODD, hidden), bf16), pltpu.VMEM((ODD, hidden), bf16), pltpu.SemaphoreType.DMA((2 * narrow_n,))],
        52 * unit)
    _, streams, sizes = scatter_sizes(wide_n, share)
    last = sum(sizes[st][-1] for st in streams)
    bufs = []
    for s in range(n_bits - 1):
        for st in streams:
            bufs += [pltpu.VMEM((narrow_n, sizes[st][s + 1], width), bf16)] * 2
    copies = 1 + 2 * n_bits + narrow_n
    sem = [pltpu.SemaphoreType.DMA((copies,)), pltpu.SemaphoreType.DMA((copies,))] if linked else []
    dproj, dwq, misc, mine = run(
        functools.partial(attn_backward, wide_n, narrow_n, comm), steps, (), (tokens, qkv, prob, gm),
        wholes_of(vectors, hot, mask, mask2, dmlp, dhid, dvec2, stats, far=(4,)),
        [sds((rows, 3 * width), bf16)],
        [sds((3, width, width), f32), sds((32, width), f32), sds((last, width), bf16)],
        [pltpu.VMEM((pad, 3 * width), f32),
         pltpu.VMEM((CW, groups, KR, HG * SLOT), f32), turned, turned, pltpu.VMEM((3, 8, width), f32), table_s, flat,
         pltpu.VMEM((ODD, width), bf16), pltpu.VMEM((ODD, 3 * width), bf16), pltpu.VMEM(dmlp.shape, f32), pltpu.SemaphoreType.DMA((1,)),
         pltpu.VMEM((narrow_n, share, width), bf16), pltpu.VMEM((narrow_n, share, width), bf16),
         pltpu.VMEM((narrow_n, share, width), f32), pltpu.VMEM((narrow_n - 1, last, width), bf16),
         pltpu.VMEM((narrow_n - 1, last, width), bf16)] + bufs + sem,
        20 * unit, 2 if linked else None)
    return outputs, grad_stream, dmlp, dwq, dwo, misc, mine, dproj


TILE = 768


def adam_step(weight, gradient, first_old, second_old, rate_value, decay_value):
    first_new = beta_one * first_old + (1.0 - beta_one) * gradient
    second_new = beta_two * second_old + (1.0 - beta_two) * gradient * gradient
    fix_one = 1.0 - beta_one**STEP
    fix_two = 1.0 - beta_two**STEP
    update = rate_value * (first_new / fix_one) / (jnp.sqrt(second_new / fix_two) + adam_eps)
    return (weight - update - rate_value * decay_value * weight, first_new, second_new)


def shards(wide_n, narrow_n, tokens, grid_sizes, cotangent, attn_weight, attn_first, attn_second, rel_table, table_first,
           table_second, vectors, vector_first, vector_second, mlp_weight, mlp_first, mlp_second, mlp_bias, bias_first,
           bias_second):
    width = tokens.shape[1]
    narrow = lax.axis_index("narrow").reshape(1).astype(jnp.int32)
    outputs, grad_stream, _, dwq, dwo, misc, mine, dproj = block(
        tokens, grid_sizes, cotangent, attn_weight, rel_table.T, vectors, mlp_weight, mlp_bias, narrow, wide_n, narrow_n)
    gm, gt, misc, part = reduce_call(wide_n, narrow_n, mlp_weight.shape[1], mine, dwq.reshape(3 * width, width), dwo, misc,
                                     vectors, dproj, tokens, attn_weight)
    new = adam_call(narrow, grad_stream, part, gt, gm, misc, (attn_weight, attn_first, attn_second), (mlp_weight, mlp_first, mlp_second),
                    (rel_table.T, table_first.T, table_second.T), (vectors, vector_first, vector_second),
                    (mlp_bias, bias_first, bias_second))
    return (outputs, *new)


def solution(mesh):
    rows = P(("wide", "narrow"), None)
    split = P(None, "narrow", None)
    return jax.shard_map(
        functools.partial(shards, mesh.shape["wide"], mesh.shape["narrow"]), mesh=mesh,
        in_specs=(rows, P("wide"), rows) + (P(),) * 9 + (split,) * 3 + (P("narrow"),) * 3,
        out_specs=(rows, rows) + (P(),) * 11 + (split,) * 4 + (P("narrow"),) * 3,
        check_vma=False)
```

```python
import functools

import jax
import jax.numpy as jnp
import numpy as np
from jax import lax
from jax.sharding import PartitionSpec as P
from jax.experimental import pallas as pl
from jax.experimental.pallas import tpu as pltpu

WIN = 7
WTOK = 49
WPI = 16
IMG_W = 16
STEP = 5
CW = 16
CR = CW * WTOK
EVEN = CR // 256 * 256
ODD = 128
SLOT = 64
KR = 56
HG = 4
LOG2E = 1.4426950408889634

norm_eps = 1e-05
beta_one = 0.5
beta_two = 0.5
adam_eps = 1e-08
highest = lax.Precision.HIGHEST
f32 = jnp.float32
bf16 = jnp.bfloat16


def nn(a, b):
    return lax.dot_general(a, b, (((1,), (0,)), ((), ())), preferred_element_type=f32)


def nt(a, b):
    return lax.dot_general(a, b, (((1,), (1,)), ((), ())), preferred_element_type=f32)


def tn(a, b):
    return lax.dot_general(a, b, (((0,), (0,)), ((), ())), preferred_element_type=f32)


def row_info():
    r = np.arange(CR)
    win = r // WTOK
    p = r % WTOK
    info = np.stack([win, p // WIN, p % WIN]).astype(np.float32)
    info[1, win >= CW] = 1000.0
    return np.ascontiguousarray(np.broadcast_to(info[:, :, None], (3, CR, 128)))


def key_info():
    p = np.arange(KR)
    info = np.stack([p // WIN, p % WIN]).astype(np.float32)
    return np.ascontiguousarray(np.broadcast_to(info[:, :, None], (2, KR, 128)))


def head_mask(head_size):
    row = np.arange(HG * SLOT)
    lane = np.arange(HG * head_size)
    return (((row // SLOT)[:, None] == (lane // head_size)[None, :]) & ((row % SLOT) < WTOK)[:, None]).astype(np.float32)


def fold_rows(t):
    return jnp.sum(t.reshape(t.shape[0] // 8, 8, t.shape[1]), 0)


def rep(v, n):
    return jnp.concatenate([v] * n, 1)


def fill_sides(sides, info, side_s):
    win = info[0]
    value = jnp.zeros_like(win)
    for i in range(CW):
        value = jnp.where(win == float(i), sides[i].astype(f32), value)
    side_s[...] = value


def corner(narrow, step, steps):
    u = WPI - 1 - (narrow * steps + step)
    return (WIN * (u // 4)).astype(f32), (WIN * lax.rem(u, 4)).astype(f32)


def chunk_valid(info, side_s, top, left):
    side = side_s[...]
    return jnp.where((info[1] + top < side) & (info[2] + left < side), 1.0, 0.0)


def norm_stats(x):
    mean = jnp.mean(x, -1, keepdims=True)
    centred = x - mean
    inverse = lax.rsqrt(jnp.mean(centred * centred, -1, keepdims=True) + norm_eps)
    return centred * inverse, inverse


def norm_grad(g, xhat, inverse, gain):
    scaled = g * gain
    m1 = jnp.mean(scaled, -1, keepdims=True)
    m2 = jnp.mean(scaled * xhat, -1, keepdims=True)
    return inverse * (scaled - m1 - xhat * m2)


class Links:
    def __init__(self, wide_n, narrow_n, send_sem, recv_sem):
        self.w = lax.axis_index("wide")
        self.n = lax.axis_index("narrow")
        self.bits = wide_n.bit_length() - 1
        self.bit = [lax.rem(self.w // (1 << b), 2) for b in range(self.bits)]
        self.mate = [self.w + (1 - 2 * self.bit[b]) * (1 << b) for b in range(self.bits)]
        self.peer = [lax.rem(self.n + s, narrow_n) for s in range(1, narrow_n)]
        self.send_sem, self.recv_sem = send_sem, recv_sem
        self.used = 0
        self.all = []

    def copy(self, src, dst, device):
        k = self.used
        self.used += 1
        c = pltpu.make_async_remote_copy(
            src_ref=src, dst_ref=dst, send_sem=self.send_sem.at[k], recv_sem=self.recv_sem.at[k],
            device_id=device, device_id_type=pl.DeviceIdType.MESH)
        self.all.append(c)
        return c

    def along(self, b):
        return (self.mate[b], self.n)

    def over(self, n):
        return (self.w, n)

    def barrier(self):
        sem = pltpu.get_barrier_semaphore()
        for b in range(self.bits):
            pl.semaphore_signal(sem, inc=1, device_id=self.along(b), device_id_type=pl.DeviceIdType.MESH)
        for n in self.peer:
            pl.semaphore_signal(sem, inc=1, device_id=self.over(n), device_id_type=pl.DeviceIdType.MESH)
        pl.semaphore_wait(sem, self.bits + len(self.peer))


def gather_cuts(wide_n, rows):
    bits = list(range(min(3, wide_n.bit_length() - 1)))
    first = rows // 256 * 128
    return [(0, first, bits[1:] + bits[:1]), (first, rows - first, bits[1:][::-1] + bits[:1])]


def gather_plan(links, wide_n, own, tail_own, all_w, all_tail):
    narrow_n, rows, _ = all_w.shape
    streams = gather_cuts(wide_n, rows)
    stages = [[]]
    place, sizes = [], []
    for start, size, order in streams:
        piece = size >> len(order)
        off = 0
        for k, b in enumerate(order):
            off = off + links.bit[b] * (piece << k)
        place.append(start + off)
        sizes.append(piece)
    for n in links.peer:
        stages[0].append(links.copy(tail_own, all_tail.at[links.n], links.over(n)))
        for at, size in zip(place, sizes):
            here = pl.ds(pl.multiple_of(at, 16), size)
            stages[0].append(links.copy(own.at[here, :], all_w.at[links.n, here, :], links.over(n)))
    for k in range(len(streams[0][2])):
        stage = []
        for s, (start, size, order) in enumerate(streams):
            here = pl.ds(pl.multiple_of(place[s], 16), sizes[s])
            for n in links.peer:
                part = all_w.at[n, here, :]
                stage.append(links.copy(part, part, links.along(order[k])))
            place[s] = place[s] - links.bit[order[k]] * sizes[s]
            sizes[s] = sizes[s] * 2
        stages.append(stage)
    return stages


def run_stages(stages, step, steps):
    for k, stage in enumerate(stages):
        @pl.when(step == min(k, steps - 1))
        def _():
            if k:
                for c in stages[k - 1]:
                    c.wait()
            for c in stage:
                c.start()


def expand_table(table, hot, wide_t, flat, bias):
    heads, count = table.shape
    wide_t[...] = jnp.zeros_like(wide_t)
    wide_t[:heads, :count] = table[...] * LOG2E
    rest = wide_t[...]
    total = jnp.zeros((16, hot.shape[0]), f32)
    for _ in range(3):
        part = rest.astype(bf16)
        total += nt(part, hot[...])
        rest = rest - part.astype(f32)
    flat[...] = total
    bias[...] = jnp.full(bias.shape, -1e30, f32)
    for g in range(heads // HG):
        for k in range(WTOK):
            for h in range(HG):
                bias[g, k : k + 1, SLOT * h : SLOT * h + SLOT] = flat[HG * g + h : HG * g + h + 1, SLOT * k : SLOT * k + SLOT]


def turn(t):
    t = jnp.concatenate([t[:, :128], t[:, 128:]], 0).T
    return jnp.concatenate([t[:SLOT], t[SLOT:]], 1)


def padded(t):
    return jnp.concatenate([t, jnp.zeros((SLOT - KR, t.shape[1]), f32)], 0)


def four(t, mask):
    return jnp.concatenate([t] * HG, 0) * mask


BATCH = 16


def attn_forward(wide_n, narrow_n, comm, narrow_ref, sides, tok, attn_w, mlp_w, mlp_b, vec, table, hot, rinfo, kinfo, hmask, hmask2,
                 qkv_s, prob_out, mixed_out, stream_out, stats, gw_out, tail_out,
                 wq, pj, mx, turn_s, bias, wide_t, flat, side_s, own, tail_own, gw, tails, wide_w, hot_s, load_sem, *sems):
    step = pl.program_id(0)
    steps = pl.num_programs(0)
    static_steps = comm[1]
    width = tok.shape[1]
    groups = width // 128
    scale = 32 ** (-0.5)
    narrow = narrow_ref[0]
    share = mlp_w.shape[1]

    loads = [pltpu.make_async_copy(attn_w, wide_w, load_sem.at[0]), pltpu.make_async_copy(hot, hot_s, load_sem.at[1])]

    @pl.when(step == 0)
    def _():
        for c in loads:
            c.start()
        for j in range(2):
            own[share * j : share * j + share, :] = mlp_w[j].astype(bf16)
        tail_own[...] = jnp.zeros_like(tail_own)
        rest = mlp_b[...].reshape(1, share)
        for i in range(3):
            part = rest.astype(bf16).astype(f32)
            tail_own[i : i + 1, :share] = part
            rest = rest - part
        if comm[0]:
            gw[lax.axis_index("narrow")] = own[...]
            tails[lax.axis_index("narrow")] = tail_own[...]
        else:
            for n in range(narrow_n):
                gw[n] = own[...]
                tails[n] = tail_own[...]

    if comm[0]:
        links = Links(wide_n, narrow_n, *sems)

        @pl.when(step == 0)
        def _():
            links.barrier()

        stages = gather_plan(links, wide_n, own, tail_own, gw, tails)
        run_stages(stages, step, static_steps)

    @pl.when(step == 0)
    def _():
        fill_sides(sides, rinfo, side_s)
        for c in loads:
            c.wait()
        wq[...] = wide_w[...].astype(bf16)
        expand_table(table, hot_s, wide_t, flat, bias)
        for ref in (pj, mx, stats):
            ref[...] = jnp.zeros_like(ref)

    top, left = corner(narrow, step, static_steps)
    x = tok[...].astype(f32)
    valid = chunk_valid(rinfo, side_s, top, left)
    keep = rep(valid, groups)
    xhat, _ = norm_stats(x)
    low = (xhat * vec[0:1] + vec[1:2]).astype(bf16)
    pj[:CR, :width] = nn(low, wq[:, :width]) + vec[2:3]
    pj[:CR, width : 2 * width] = nn(low, wq[:, width : 2 * width])
    pj[:CR, 2 * width :] = nn(low, wq[:, 2 * width : 3 * width]) + vec[3:4]
    for i in range(CW):
        qkv_s[i] = pj[WTOK * i : WTOK * i + SLOT, :].astype(bf16)

    def score(b, carry):
        for k in range(BATCH):
            i = b * BATCH + k
            for g in range(groups):
                q_bd = four(qkv_s[i, :, 128 * g : 128 * g + 128], hmask[...])
                prob_out[i, g] = nt(qkv_s[i, :KR, width + 128 * g : width + 128 * g + 128], q_bd)
        return carry

    def soft(b, carry):
        for k in range(BATCH):
            i = b * BATCH + k
            side = sides[i].astype(f32)
            fill = jnp.where((kinfo[0] < side - top) & (kinfo[1] < side - left), 0.0, -10000.0 * LOG2E)
            fill = rep(fill, 2)
            for g in range(groups):
                s = prob_out[i, g] * (scale * LOG2E) + bias[g] + fill
                e = jnp.exp2(s - jnp.max(s, 0, keepdims=True))
                prob = e * (1.0 / jnp.sum(e, 0, keepdims=True))
                prob_out[i, g] = prob
                turn_s[i, g] = turn(padded(prob).astype(bf16))
        return carry

    lax.fori_loop(0, CW // BATCH, score, 0)
    lax.fori_loop(0, CW // BATCH, soft, 0)
    for i in range(CW):
        for g in range(groups):
            v_bd = four(qkv_s[i, :, 2 * width + 128 * g : 2 * width + 128 * g + 128], hmask2[...])
            mx[WTOK * i : WTOK * i + SLOT, 128 * g : 128 * g + 128] = nn(turn_s[i, g], v_bd)
    mixed = mx[:CR, :].astype(bf16)
    mixed_out[...] = mixed
    branch = (nn(mixed, wq[:, 3 * width :]) + vec[4:5]) * keep
    stream_out[...] = x + branch
    stats[0] += fold_rows(x * x * keep)
    stats[1] += fold_rows(branch * branch)
    stats[2, :, :128] += fold_rows(valid)

    @pl.when(step == steps - 1)
    def _():
        if comm[0]:
            for c in stages[-1]:
                c.wait()
        gw_out[...] = gw[...]
        tail_out[...] = tails[...]


def feed_forward(tile, narrow_ref, sides, cot, mixed_in, stream_in, attn_w, gw, tails, vec, rinfo,
                 out_ref, grad_stream_out, gm_s, dmlp, dwo, dhid, dvec,
                 wo, w1, w2, hb, dw1, dw2, mx, side_s, second_r, grad_r, pre_r, active_r, load_sem):
    step = pl.program_id(0)
    steps = pl.num_programs(0)
    width = cot.shape[1]
    groups = width // 128
    hidden = w1.shape[0]
    shards_n, twice, _ = gw.shape
    share = twice // 2
    loads = []
    for n in range(shards_n):
        for j, ref in enumerate((w1, w2)):
            loads.append(pltpu.make_async_copy(gw.at[n, pl.ds(share * j, share), :], ref.at[pl.ds(share * n, share), :],
                                               load_sem.at[2 * n + j]))

    @pl.when(step == 0)
    def _():
        for c in loads:
            c.start()
        wo[...] = attn_w[...].astype(bf16)
        for n in range(shards_n):
            three = tails[n]
            hb[:, share * n : share * n + share] = (three[0:1] + three[1:2] + three[2:3])[:, :share]
        fill_sides(sides, rinfo, side_s)
        for ref in (mx, dw1, dw2, dwo, dhid, dvec, second_r, grad_r, pre_r, active_r):
            ref[...] = jnp.zeros_like(ref)

    top, left = corner(narrow_ref[0], step, steps)
    keep = rep(chunk_valid(rinfo, side_s, top, left), groups)
    cotan = cot[...].astype(f32)
    stream = stream_in[...]
    xhat2, inverse2 = norm_stats(stream)
    second = (xhat2 * vec[5:6] + vec[6:7]).astype(bf16)
    kept_cot = cotan * keep
    grad_low = kept_cot.astype(bf16)
    second_t = jnp.concatenate([second[:EVEN].T, jnp.ones((16, EVEN), bf16)], 0)
    grad_t = grad_low[:EVEN].T
    odd = pl.ds(pl.multiple_of(step * (CR - EVEN), CR - EVEN), CR - EVEN)
    second_r[odd, :] = second[EVEN:]
    grad_r[odd, :] = grad_low[EVEN:]

    @pl.when(step == 0)
    def _():
        for c in loads:
            c.wait()

    mlp_out = jnp.zeros((CR, width), f32)
    grad_second = jnp.zeros((CR, width), f32)
    for t in range(hidden // tile):
        cols = slice(tile * t, tile * t + tile)
        pre = nt(second, w1[cols, :]) + hb[0:1, cols]
        square = pre * pre
        half = 0.5 * jnp.tanh(pre * (square * (0.7978845608028654 * 0.044715) + 0.7978845608028654)) + 0.5
        active = (pre * half).astype(bf16)
        slope = half + (pre * (half - half * half)) * (square * (6 * 0.7978845608028654 * 0.044715) + 2 * 0.7978845608028654)
        grad_pre = (nt(grad_low, w2[cols, :]) * slope).astype(bf16)
        mlp_out += nn(active, w2[cols, :])
        grad_second += nn(grad_pre, w1[cols, :])
        pre_r[odd, cols] = grad_pre[EVEN:]
        active_r[odd, cols] = active[EVEN:]
        outer = nn(second_t, grad_pre[:EVEN])
        dw1[:, cols] += outer[:width]
        dhid[:, cols] += outer[width : width + 8]
        dw2[:, cols] += nn(grad_t, active[:EVEN])
    branch = (mlp_out + vec[7:8]) * keep
    out_ref[...] = (stream + branch).astype(bf16)
    dvec[4] += fold_rows(branch * branch)
    dvec[0] += fold_rows(grad_second * xhat2)
    dvec[1] += fold_rows(grad_second)
    dvec[2] += fold_rows(kept_cot)
    grad_stream = cotan + norm_grad(grad_second, xhat2, inverse2, vec[5:6])
    grad_stream_out[...] = grad_stream
    grad_attn = grad_stream * keep
    dvec[3] += fold_rows(grad_attn)
    grad_attn_low = grad_attn.astype(bf16)
    dwo[...] += nn(mixed_in[...].T, grad_attn_low)
    mx[:CR, :] = nt(grad_attn_low, wo[...])
    for i in range(CW):
        gm_s[i] = mx[WTOK * i : WTOK * i + SLOT, :].astype(bf16)

    @pl.when(step == steps - 1)
    def _():
        rest_t = jnp.concatenate([second_r[...].T, jnp.ones((16, second_r.shape[0]), bf16)], 0)
        rest_g = grad_r[...].T
        for t in range(hidden // width):
            cols = slice(width * t, width * t + width)
            outer = nn(rest_t, pre_r[:, cols])
            dw1[:, cols] += outer[:width]
            dhid[:, cols] += outer[width : width + 8]
            dw2[:, cols] += nn(rest_g, active_r[:, cols])
        for j, ref in enumerate((dw1, dw2)):
            for t in range(hidden // width):
                turned = ref[:, width * t : width * t + width].T
                for k in range(width // share):
                    n = (width * t) // share + k
                    dmlp[n, share * j : share * j + share, :] = turned[share * k : share * k + share, :]


def scatter_sizes(wide_n, share):
    n_bits = wide_n.bit_length() - 1
    rest = list(range(1, n_bits))
    half = len(rest) // 2
    plan = {"A": rest, "B": rest[half:] + rest[:half]}
    cut = share // 2
    streams = {"A": (0, cut), "B": (cut, share - cut)}
    sizes = {}
    for st, (_, size) in streams.items():
        sizes[st] = [size]
        for _ in rest:
            sizes[st].append(sizes[st][-1] // 2 if sizes[st][-1] % 32 == 0 else sizes[st][-1])
    return plan, streams, sizes


def scatter_stages(links, wide_n, narrow_n, share, dmlp, mine_out, send0, recv0, acc, zsend, zrecv, bufs):
    plan, streams, sizes = scatter_sizes(wide_n, share)
    bit = links.bit
    keep0, away0 = bit[0] * share, (1 - bit[0]) * share
    stages = []

    def pack0():
        for n in range(narrow_n):
            def one(i, size):
                send0[n, pl.ds(i, size), :] = dmlp[n, pl.ds(pl.multiple_of(away0 + i, 16), size), :].astype(send0.dtype)
            loop_rows(share, one)

    def add0():
        for n in range(narrow_n):
            def one(i, size):
                acc[n, pl.ds(i, size), :] = (dmlp[n, pl.ds(pl.multiple_of(keep0 + i, 16), size), :]
                                             + recv0[n, pl.ds(i, size), :].astype(f32))
            loop_rows(share, one)

    stages.append((pack0, [links.copy(send0, recv0, links.along(0))], add0))
    place = {st: streams[st][0] for st in streams}
    trail = []
    for s in range(links.bits - 1):
        work = []
        for k, st in enumerate(streams):
            b = plan[st][s]
            size = sizes[st][s + 1]
            halves = size < sizes[st][s]
            send, recv = bufs[2 * (2 * s + k)], bufs[2 * (2 * s + k) + 1]
            here = place[st]
            out_at, in_at = (here + (1 - bit[b]) * size, here + bit[b] * size) if halves else (here, here)
            place[st] = in_at
            work.append((send, recv, out_at, in_at, size, halves, links.copy(send, recv, links.along(b))))
            trail.append((st, s, b, in_at, size, halves))

        def pack(work=work):
            for send, recv, out_at, in_at, size, halves, _ in work:
                for n in range(narrow_n):
                    def one(i, k):
                        send[n, pl.ds(i, k), :] = acc[n, pl.ds(pl.multiple_of(out_at + i, 16), k), :].astype(send.dtype)
                    loop_rows(size, one)

        def add(work=work):
            for send, recv, out_at, in_at, size, halves, _ in work:
                for n in range(narrow_n):
                    def one(i, k):
                        here = pl.ds(pl.multiple_of(in_at + i, 16), k)
                        mine = acc[n, here, :] if halves else send[n, pl.ds(i, k), :].astype(f32)
                        acc[n, here, :] = mine + recv[n, pl.ds(i, k), :].astype(f32)
                    loop_rows(size, one)

        stages.append((pack, [w[-1] for w in work], add))
    base, total = {}, 0
    for st in streams:
        base[st] = total
        total += sizes[st][-1]

    def packz():
        for i, n in enumerate(links.peer):
            for st in streams:
                def one(r, k):
                    zsend[i, pl.ds(base[st] + r, k), :] = acc[n, pl.ds(pl.multiple_of(place[st] + r, 16), k), :].astype(zsend.dtype)
                loop_rows(sizes[st][-1], one)

    def addz():
        for st in streams:
            def one(r, k):
                value = acc[links.n, pl.ds(pl.multiple_of(place[st] + r, 16), k), :]
                for i in range(narrow_n - 1):
                    value = value + zrecv[i, pl.ds(base[st] + r, k), :].astype(f32)
                mine_out[pl.ds(base[st] + r, k), :] = value.astype(bf16)
            loop_rows(sizes[st][-1], one)

    stages.append((packz, [links.copy(zsend.at[i], zrecv.at[i], links.over(n)) for i, n in enumerate(links.peer)], addz))
    return stages


def attn_backward(wide_n, narrow_n, comm, tok, qkv_s, prob_in, gm_s, vec, hot, hmask, hmask2,
                  dmlp, dhid, dvec2, stats,
                  dproj_out, dwq, misc, mine_out,
                  pj, gp_s, low_s, turn_s, dext, dtable, flat, low_r, proj_r, dmlp_s, load_sem, send0, recv0, acc, zsend, zrecv, *rest):
    step = pl.program_id(0)
    steps = pl.num_programs(0)
    static_steps = comm[1]
    width = tok.shape[1]
    groups = width // 128
    scale = 32 ** (-0.5)
    share = dmlp.shape[1] // 2
    load = pltpu.make_async_copy(dmlp, dmlp_s, load_sem.at[0])

    if comm[0]:
        links = Links(wide_n, narrow_n, *rest[-2:])

        @pl.when(step == 0)
        def _():
            links.barrier()

        @pl.when(step == 0)
        def _():
            load.start()

    @pl.when(step == 0)
    def _():
        for ref in (dwq, dext, dtable, low_r, proj_r):
            ref[...] = jnp.zeros_like(ref)

    def first(b, carry):
        for k in range(BATCH):
            i = b * BATCH + k
            for g in range(groups):
                do_bd = four(gm_s[i, :, 128 * g : 128 * g + 128], hmask[...])
                gp_s[i, g] = nt(qkv_s[i, :KR, 2 * width + 128 * g : 2 * width + 128 * g + 128], do_bd)
        return carry

    def second(b, carry):
        for g in range(groups):
            total = dtable[g]
            for k in range(BATCH):
                i = b * BATCH + k
                gp = gp_s[i, g]
                prob = prob_in[i, g]
                ds = prob * (gp - jnp.sum(gp * prob, 0, keepdims=True))
                total = total + ds
                raw = padded(ds * scale).astype(bf16)
                low_s[i, g] = raw
                turn_s[i, g] = turn(raw)
            dtable[g] = total
        return carry

    lax.fori_loop(0, CW // BATCH, first, 0)
    if comm[0]:
        stages = scatter_stages(links, wide_n, narrow_n, share, dmlp_s, mine_out, send0, recv0, acc, zsend, zrecv, rest[:-2])
        for k, (pack, copies, add) in enumerate(stages):
            @pl.when(step == min(k, static_steps - 1))
            def _():
                if not k:
                    load.wait()
                if k:
                    for c in stages[k - 1][1]:
                        c.wait()
                    stages[k - 1][2]()
                pack()
                for c in copies:
                    c.start()

    lax.fori_loop(0, CW // BATCH, second, 0)
    for i in range(CW):
        rows = slice(WTOK * i, WTOK * i + SLOT)
        for g in range(groups):
            q_bd = four(qkv_s[i, :, 128 * g : 128 * g + 128], hmask[...])
            k_bd = four(qkv_s[i, :, width + 128 * g : width + 128 * g + 128], hmask2[...])
            do_bd = four(gm_s[i, :, 128 * g : 128 * g + 128], hmask[...])
            pj[rows, 128 * g : 128 * g + 128] = nn(turn_s[i, g], k_bd)
            pj[rows, width + 128 * g : width + 128 * g + 128] = nn(low_s[i, g], q_bd)
            pj[rows, 2 * width + 128 * g : 2 * width + 128 * g + 128] = nn(padded(prob_in[i, g]).astype(bf16), do_bd)
    dproj = pj[:CR, :].astype(bf16)
    dproj_out[...] = dproj
    x = tok[...].astype(f32)
    xhat, _ = norm_stats(x)
    low = (xhat * vec[0:1] + vec[1:2]).astype(bf16)
    low_t = jnp.concatenate([low[:EVEN].T, jnp.ones((16, EVEN), bf16)], 0)
    odd = pl.ds(pl.multiple_of(step * (CR - EVEN), CR - EVEN), CR - EVEN)
    low_r[odd, :] = low[EVEN:]
    proj_r[odd, :] = dproj[EVEN:]
    for j in range(3):
        outer = nn(low_t, dproj[:EVEN, width * j : width * j + width])
        dwq[j] += outer[:width]
        dext[j] += outer[width : width + 8]

    @pl.when(step == steps - 1)
    def _():
        rest_t = jnp.concatenate([low_r[...].T, jnp.ones((16, low_r.shape[0]), bf16)], 0)
        for j in range(3):
            outer = nn(rest_t, proj_r[:, width * j : width * j + width])
            dwq[j] += outer[:width]
            dext[j] += outer[width : width + 8]
        rows = [None, None, None, None, dvec2[3], dvec2[0], dvec2[1], dvec2[2]]
        for i, part in enumerate(rows):
            if part is not None:
                misc[i : i + 1, :] = jnp.sum(part, 0, keepdims=True)
        misc[0:2, :] = jnp.zeros((2, width), f32)
        misc[2:3, :] = dext[0, 0:1, :]
        misc[3:4, :] = dext[2, 0:1, :]
        for i in range(dhid.shape[1] // width):
            misc[8 + i : 9 + i, :] = dhid[0:1, width * i : width * i + width]
        lane = lax.broadcasted_iota(jnp.int32, (1, width), 1)
        line = jnp.zeros((1, width), f32)
        for i, part in enumerate((stats[0], stats[1], dvec2[4])):
            line = jnp.where(lane == i, jnp.sum(part), line)
        misc[12:13, :] = jnp.where(lane == 3, jnp.sum(stats[2]) / 128.0, line)
        misc[13:16, :] = jnp.zeros((3, width), f32)
        flat[...] = jnp.zeros_like(flat)
        for g in range(groups):
            for k in range(WTOK):
                line = dtable[g, k : k + 1, :]
                for h in range(HG):
                    flat[HG * g + h : HG * g + h + 1, SLOT * k : SLOT * k + SLOT] = line[:, SLOT * h : SLOT * h + SLOT]
        rest_f = flat[...]
        total = jnp.zeros((16, 256), f32)
        for _ in range(3):
            part = rest_f.astype(bf16)
            total += nn(part, hot[...])
            rest_f = rest_f - part.astype(f32)
        misc[16:32, :] = jnp.zeros((16, width), f32)
        misc[16:32, :256] = total
        if comm[0]:
            for c in stages[-1][1]:
                c.wait()
            stages[-1][2]()


def sds(shape, dt):
    return jax.ShapeDtypeStruct(shape, dt)


def whole(a):
    nd = len(a.shape)
    return pl.BlockSpec(a.shape, lambda *_: (0,) * nd, pipeline_mode=pl.Buffered(1))


def whole_out(a):
    nd = len(a.shape)
    return pl.BlockSpec(a.shape, lambda *_: (0,) * nd)


def by_step(a, steps):
    nd = len(a.shape)
    return pl.BlockSpec((a.shape[0] // steps,) + tuple(a.shape[1:]), lambda c, *_: (c,) + (0,) * (nd - 1))


def run(body, steps, scalars, stepped, wholes, out_stepped, out_wholes, scratch, flops, collective_id=None):
    smem = pl.BlockSpec(memory_space=pltpu.SMEM)
    params = dict(vmem_limit_bytes=62 * 1024 * 1024)
    if collective_id is not None:
        params.update(collective_id=collective_id, has_side_effects=True)
    return pl.pallas_call(
        body, grid=(steps,),
        in_specs=[smem] * len(scalars) + [by_step(a, steps) for a in stepped] + wholes[1],
        out_specs=[by_step(a, steps) for a in out_stepped] + [whole_out(a) for a in out_wholes],
        out_shape=list(out_stepped) + list(out_wholes), scratch_shapes=scratch,
        compiler_params=pltpu.CompilerParams(**params),
        cost_estimate=pl.CostEstimate(flops=flops, bytes_accessed=20000000, transcendentals=0),
    )(*scalars, *stepped, *wholes[0])


def wholes_of(*arrays, far=()):
    return (arrays, [pl.BlockSpec(memory_space=pl.ANY) if i in far else whole(a) for i, a in enumerate(arrays)])


def loop_rows(total, body):
    size = next(n for n in (96, 64, 48, 32, 16) if total % n == 0)
    lax.fori_loop(0, total // size, lambda i, c: (body(pl.multiple_of(i * size, size), size), c)[1], 0)


def attn_chains(wide_n, half):
    rest = list(range(1, wide_n.bit_length() - 1))
    turned = rest[len(rest) // 2 :] + rest[: len(rest) // 2]
    chains, start = [], 0
    while start < half:
        sizes = [min(64, half - start)]
        for _ in rest:
            sizes.append(sizes[-1] // 2 if sizes[-1] % 32 == 0 else sizes[-1])
        chains.append((start, turned if len(chains) % 2 else rest, sizes))
        start += sizes[0]
    return chains


def reduce_all(wide_n, narrow_n, share, mine_ref, q_ref, o_ref, s_ref, vec, dproj, tok, attn_w, gm_out, gt_out, s_out, part_out,
               proj_s, tok_s, part_s, wide_w, wq, dvec, own_sem, recv0, acct, gm, gt, sbuf, srecv, szrecv, *rest):
    bufs = list(rest[:-2])
    links = Links(wide_n, narrow_n, *rest[-2:])
    bit, me_n, peer = links.bit, links.n, links.peer
    steps = links.bits - 1
    width = q_ref.shape[1]
    blocks = proj_s.shape[0]
    at_block = [pl.ds(CR * b, CR) for b in range(blocks)]
    from_hbm = [pltpu.make_async_copy(attn_w.at[:, pl.ds(0, 3 * width)], wide_w, own_sem.at[0])]
    for b in range(blocks):
        from_hbm.append(pltpu.make_async_copy(dproj.at[at_block[b], :], proj_s.at[b], own_sem.at[1 + 2 * b]))
        from_hbm.append(pltpu.make_async_copy(tok.at[at_block[b], :], tok_s.at[b], own_sem.at[2 + 2 * b]))
    to_hbm = [pltpu.make_async_copy(part_s.at[b], part_out.at[at_block[b], :], own_sem.at[1 + 2 * blocks + b]) for b in range(blocks)]
    for c in from_hbm:
        c.start()
    links.barrier()
    ht = acct.shape[1]
    away, keep = (1 - bit[0]) * ht, bit[0] * ht

    def rows_at(at, size):
        return pl.ds(pl.multiple_of(at, 16), size)

    def go(copies):
        for c in copies:
            c.start()

    def come(copies):
        for c in copies:
            c.wait_recv()

    def attn_chain(start, order, sizes):
        copies = []
        for n in range(narrow_n):
            flat = n * share
            src, off = (q_ref, flat) if flat < q_ref.shape[0] else (o_ref, flat - q_ref.shape[0])
            copies.append(links.copy(src.at[rows_at(off + away + start, sizes[0]), :],
                                     recv0.at[n, pl.ds(start, sizes[0]), :], links.along(0)))
        go(copies)
        yield
        come(copies)
        for n in range(narrow_n):
            flat = n * share
            src, off = (q_ref, flat) if flat < q_ref.shape[0] else (o_ref, flat - q_ref.shape[0])
            def add0(i, size):
                acct[n, pl.ds(start + i, size), :] = (src[rows_at(off + keep + start + i, size), :]
                                                      + recv0[n, pl.ds(start + i, size), :])
            loop_rows(sizes[0], add0)
        here = start
        trail = []
        for s in range(steps):
            b, size = order[s], sizes[s + 1]
            halves = size < sizes[s]
            send, recv = bufs.pop(0), bufs.pop(0)
            out_at, in_at = (here + (1 - bit[b]) * size, here + bit[b] * size) if halves else (here, here)
            for n in range(narrow_n):
                def pack(i, k):
                    send[n, pl.ds(i, k), :] = acct[n, rows_at(out_at + i, k), :].astype(bf16)
                loop_rows(size, pack)
            c = links.copy(send, recv, links.along(b))
            c.start()
            yield
            c.wait_recv()
            for n in range(narrow_n):
                def add(i, k):
                    own = acct[n, rows_at(in_at + i, k), :] if halves else send[n, pl.ds(i, k), :].astype(f32)
                    acct[n, rows_at(in_at + i, k), :] = own + recv[n, pl.ds(i, k), :].astype(f32)
                loop_rows(size, add)
            here = in_at
            trail.append((b, in_at, size, halves))
        size = sizes[-1]
        zsend, zrecv = bufs.pop(0), bufs.pop(0)
        copies = []
        for i, n in enumerate(peer):
            def pack(r, k):
                zsend[i, pl.ds(r, k), :] = acct[n, rows_at(here + r, k), :].astype(bf16)
            loop_rows(size, pack)
            copies.append(links.copy(zsend.at[i], zrecv.at[i], links.over(n)))
            copies[-1].start()
        yield
        come(copies)
        def add(r, k):
            value = acct[me_n, rows_at(here + r, k), :]
            for i in range(narrow_n - 1):
                value = value + zrecv[i, pl.ds(r, k), :].astype(f32)
            gt[me_n, rows_at(keep + here + r, k), :] = value.astype(bf16)
        loop_rows(size, add)
        part = gt.at[me_n, rows_at(keep + here, size), :]
        copies = [links.copy(part, part, links.over(n)) for n in peer]
        go(copies)
        yield
        come(copies)
        for b, at, size, halves in reversed(trail):
            if halves:
                part = gt.at[:, rows_at(keep + at, size), :]
                c = links.copy(part, part, links.along(b))
                c.start()
                yield
                c.wait_recv()
        part = gt.at[:, rows_at(keep + start, sizes[0]), :]
        c = links.copy(part, part, links.along(0))
        c.start()
        yield
        c.wait_recv()

    def small_chain():
        yield
        from_hbm[0].wait()
        wq[...] = wide_w[...].astype(bf16)
        dvec[...] = jnp.zeros_like(dvec)
        for b in range(blocks):
            from_hbm[1 + 2 * b].wait()
            from_hbm[2 + 2 * b].wait()
            xhat, inverse = norm_stats(tok_s[b].astype(f32))
            grad_normed = nt(proj_s[b], wq[...])
            dvec[0] += fold_rows(grad_normed * xhat)
            dvec[1] += fold_rows(grad_normed)
            part_s[b] = norm_grad(grad_normed, xhat, inverse, vec[0:1]).astype(bf16)
            to_hbm[b].start()
            if b % 2 and b + 1 < blocks:
                yield
        sbuf[0] = s_ref[...]
        for i in range(2):
            sbuf[0, i : i + 1, :] = jnp.sum(dvec[i], 0, keepdims=True)
        for b in range(links.bits):
            c = links.copy(sbuf.at[b], srecv.at[b], links.along(b))
            c.start()
            yield
            c.wait_recv()
            sbuf[b + 1] = sbuf[b] + srecv[b]
        copies = [links.copy(sbuf.at[links.bits], szrecv.at[i], links.over(n)) for i, n in enumerate(peer)]
        go(copies)
        yield
        come(copies)
        own = sbuf[links.bits]
        total = jnp.zeros_like(own)
        for n in range(narrow_n):
            behind = lax.rem(me_n + narrow_n - n, narrow_n)
            value = own
            for i in range(1, narrow_n):
                value = jnp.where(behind == i, szrecv[i - 1], value)
            total = total + value
        s_out[...] = total

    def mlp_chain():
        plan, streams, sizes = scatter_sizes(wide_n, share)
        trail, base = [], 0
        for st, (here, _) in streams.items():
            for s in range(steps):
                b, size = plan[st][s], sizes[st][s + 1]
                halves = size < sizes[st][s]
                here = here + bit[b] * size if halves else here
                trail.append((s, b, here, size, halves))
            size = sizes[st][-1]
            gm[rows_at(bit[0] * share + here, size), :] = mine_ref[base : base + size, :]
            base += size
        yield
        yield
        for s in reversed(range(steps)):
            copies = []
            for s2, b, at, size, halves in trail:
                if s2 == s and halves:
                    part = gm.at[rows_at(bit[0] * share + at, size), :]
                    copies.append(links.copy(part, part, links.along(b)))
            go(copies)
            yield
            come(copies)
        part = gm.at[rows_at(bit[0] * share, share), :]
        c = links.copy(part, part, links.along(0))
        c.start()
        yield
        c.wait_recv()
        gm_out[...] = gm[...]

    going = [attn_chain(*c) for c in attn_chains(wide_n, ht)] + [mlp_chain(), small_chain()]
    rounds = 0
    while going:
        still = []
        if rounds == 3:
            going = going[-1:] + going[:-1]
        rounds += 1
        for chain in going:
            try:
                next(chain)
                still.append(chain)
            except StopIteration:
                pass
        going = still
    gt_out[...] = gt[...]
    for c in links.all:
        c.wait_send()
    for c in to_hbm:
        c.wait()


def reduce_call(wide_n, narrow_n, share, mine, dq, do, misc, vec, dproj, tok, attn_w):
    width = mine.shape[1]
    rows = tok.shape[0]
    blocks = rows // CR
    ht = share // 2
    n_bits = wide_n.bit_length() - 1
    scratch = [
        pltpu.VMEM((blocks, CR, 3 * width), bf16), pltpu.VMEM((blocks, CR, width), bf16), pltpu.VMEM((blocks, CR, width), bf16),
        pltpu.VMEM((width, 3 * width), f32), pltpu.VMEM((width, 3 * width), bf16), pltpu.VMEM((2, 8, width), f32),
        pltpu.SemaphoreType.DMA((1 + 3 * blocks,)),
        pltpu.VMEM((narrow_n, ht, width), f32), pltpu.VMEM((narrow_n, ht, width), f32),
        pltpu.VMEM((2 * share, width), bf16), pltpu.VMEM((narrow_n, share, width), bf16),
        pltpu.VMEM((n_bits + 1,) + misc.shape, f32), pltpu.VMEM((n_bits,) + misc.shape, f32),
        pltpu.VMEM((narrow_n - 1,) + misc.shape, f32)]
    order = order_of_bufs(wide_n, narrow_n, ht)
    scratch += [pltpu.VMEM((lead, rows, width), bf16) for lead, rows in order for _ in range(2)]
    chains = len(attn_chains(wide_n, ht))
    copies = chains * (narrow_n + 2 * n_bits + 2 * narrow_n) + 4 * n_bits + narrow_n
    scratch += [pltpu.SemaphoreType.DMA((copies,)), pltpu.SemaphoreType.DMA((copies,))]
    vmem = pl.BlockSpec(memory_space=pltpu.VMEM)
    return pl.pallas_call(
        functools.partial(reduce_all, wide_n, narrow_n, share),
        out_shape=[sds((2 * share, width), bf16), sds((narrow_n, share, width), bf16), sds(misc.shape, f32),
                   sds((rows, width), bf16)],
        in_specs=[vmem] * 5 + [pl.BlockSpec(memory_space=pl.ANY)] * 3, out_specs=[vmem] * 3 + [pl.BlockSpec(memory_space=pl.ANY)], scratch_shapes=scratch,
        compiler_params=pltpu.CompilerParams(collective_id=0, has_side_effects=True, vmem_limit_bytes=60 * 1024 * 1024),
    )(mine, dq, do, misc, vec, dproj, tok, attn_w)


def order_of_bufs(wide_n, narrow_n, ht):
    chains = attn_chains(wide_n, ht)
    out = []
    for s in range(wide_n.bit_length() - 2):
        out += [(narrow_n, sizes[s + 1]) for _, _, sizes in chains]
    return out + [(narrow_n - 1, sizes[-1]) for _, _, sizes in chains]


def adam_kernel(narrow_ref, grad_stream, part, gt, gm, misc, aw, af, as_, mw, mf, ms, tw, tf, ts, vw, vf, vs, bw, bf, bs,
                input_grad, rms, an, al, afn, asn, mn, ml, mfn, msn, tn_, tfn, tsn, vn, vfn, vsn, bn, bfn, bsn):
    def put(new, w, g, m, v, rate, decay, low=None):
        out = adam_step(w, g, m, v, rate, decay)
        for ref, value in zip(new, out):
            ref[...] = value.reshape(ref.shape)
        if low is not None:
            low[...] = out[0].astype(bf16).reshape(low.shape)

    input_grad[...] = grad_stream[...] + part[...].astype(f32)
    put((an, afn, asn), aw[...], jnp.concatenate([gt[j].astype(f32) for j in range(4)], 1), af[...], as_[...], 0.02, 0.05, al)
    put((mn, mfn, msn), mw[0], gm[0].astype(f32), mf[0], ms[0], 0.02, 0.05, ml)

    @pl.when(pl.program_id(0) == 0)
    def _():
        put((vn, vfn, vsn), vw[...], misc[0:8, :], vf[...], vs[...], 0.3, 0.0)
        stats = misc[12:13, :]
        for i in range(3):
            ratio = jnp.sqrt(stats[:, i : i + 1] / (stats[:, 3:4] * misc.shape[1]))
            rms[i] = ratio[0, 0]
        n = narrow_ref[0]
        share = bw.shape[0]
        grad = jnp.zeros((1, share), f32)
        per = misc.shape[1] // share
        for i in range(4):
            for k in range(per):
                grad = jnp.where(n == per * i + k, misc[8 + i : 9 + i, share * k : share * k + share], grad)
        put((bn, bfn, bsn), bw[...], grad.reshape(share), bf[...], bs[...], 0.1, 0.0)
        heads, count = tw.shape
        put((tn_, tfn, tsn), tw[...], misc[16 : 16 + heads, :count], tf[...], ts[...], 0.3, 0.0)


def adam_call(narrow, grad_stream, part, gt, gm, misc, attn, mlp, table, vec, bias):
    width = gm.shape[1]
    share = mlp[0].shape[1]
    gt = gt.reshape(4, width, width)
    cuts = 4 if grad_stream.shape[0] % 64 == 0 else 2
    some = by_step(grad_stream, cuts)
    quarter = 2 * share // cuts
    rows = width // cuts
    gm = gm.reshape(cuts, quarter, width)
    mlp = [a.reshape(cuts, quarter, width) for a in mlp]
    line = pl.BlockSpec((rows, attn[0].shape[1]), lambda j, *_: (j, 0))
    lead = pl.BlockSpec((1, quarter, width), lambda j, *_: (j, 0, 0))
    split = pl.BlockSpec((4, rows, width), lambda j, *_: (0, j, 0))
    smalls = list(table) + list(vec) + list(bias)
    args = [grad_stream, part, gt, gm, misc] + list(attn) + mlp + smalls
    in_specs = [some, some, split, lead, whole(misc)] + [line] * 3 + [lead] * 3 + [whole(a) for a in smalls]
    three = lambda a: [sds(a.shape, f32)] * 3
    outs = [sds(grad_stream.shape, f32), sds((3,), f32), sds(attn[0].shape, f32), sds(attn[0].shape, bf16)] + [sds(attn[0].shape, f32)] * 2
    outs += [sds(mlp[0].shape, f32), sds(mlp[0].shape, bf16)] + [sds(mlp[0].shape, f32)] * 2
    outs += three(table[0]) + three(vec[0]) + three(bias[0])
    out_specs = [some, pl.BlockSpec(memory_space=pltpu.SMEM)] + [line] * 4 + [lead] * 4
    out_specs += [whole_out(a) for a in smalls]
    r = pl.pallas_call(
        adam_kernel,
        grid_spec=pltpu.PrefetchScalarGridSpec(num_scalar_prefetch=1, grid=(cuts,), in_specs=in_specs, out_specs=out_specs),
        out_shape=outs,
        compiler_params=pltpu.CompilerParams(vmem_limit_bytes=60 * 1024 * 1024),
    )(narrow, *args)
    full = (2, share, width)
    grad, r = r[0], r[1:]
    return [grad, r[0], *r[1:5], *[a.T for a in r[9:12]], *r[12:15], *[a.reshape(full) for a in r[5:9]], *r[15:18]]


def bias_layout(rel_table):
    pos = np.arange(WTOK)
    row, col = pos // WIN, pos % WIN
    off = (row[:, None] - row[None, :] + WIN - 1) * (2 * WIN - 1) + col[:, None] - col[None, :] + WIN - 1
    full = np.full((KR, SLOT), -1, np.int32)
    full[:WTOK, :WTOK] = off.T
    return full


def block(tokens, grid_sizes, cotangent, attn_weight, rel_table, vectors, mlp_weight, mlp_bias, narrow, wide_n, narrow_n, linked=True):
    rows, width = tokens.shape
    wins = rows // WTOK
    steps = wins // CW
    heads = rel_table.shape[0]
    groups = heads // HG
    share = mlp_weight.shape[1]
    hidden = share * narrow_n
    n_bits = wide_n.bit_length() - 1
    comm = (linked, steps)
    unit = rows * width * width
    hot = np.zeros((KR * SLOT, 256), np.float32)
    lay = bias_layout(rel_table).reshape(-1)
    hot[np.arange(KR * SLOT)[lay >= 0], lay[lay >= 0]] = 1.0
    hot = jnp.asarray(hot, bf16)
    mask = head_mask(width // heads)
    mask2 = mask.reshape(HG, SLOT, -1)[np.array([0, 2, 1, 3])].reshape(mask.shape)
    mask, mask2 = jnp.asarray(mask, bf16), jnp.asarray(mask2, bf16)
    rinfo, kinfo = jnp.asarray(row_info()), jnp.asarray(key_info())
    scal = (narrow, grid_sizes)
    pad = CR + 16
    copies = 3 * (narrow_n - 1) + 3 * 2 * (narrow_n - 1) + 4
    sem = [pltpu.SemaphoreType.DMA((copies,)), pltpu.SemaphoreType.DMA((copies,))] if linked else []
    sides = pltpu.VMEM((CR, 128), f32)
    table_s = pltpu.VMEM((groups, KR, HG * SLOT), f32)
    flat = pltpu.VMEM((16, KR * SLOT), f32)
    turned = pltpu.VMEM((CW, groups, SLOT, HG * SLOT), bf16)
    qkv, prob, mixed, stream, stats, gw, tails = run(
        functools.partial(attn_forward, wide_n, narrow_n, comm), steps, scal, (tokens,),
        wholes_of(attn_weight, mlp_weight, mlp_bias, vectors, rel_table, hot, rinfo, kinfo, mask, mask2, far=(0, 5)),
        [sds((wins, SLOT, 3 * width), bf16), sds((wins, groups, KR, HG * SLOT), f32), sds((rows, width), bf16), sds((rows, width), f32)],
        [sds((3, 8, width), f32), sds((narrow_n, 2 * share, width), bf16), sds((narrow_n, 8, width), f32)],
        [pltpu.VMEM((width, 4 * width), bf16), pltpu.VMEM((pad, 3 * width), f32), pltpu.VMEM((pad, width), f32), turned,
         table_s, pltpu.VMEM((16, 256), f32), flat, sides,
         pltpu.VMEM((2 * share, width), bf16), pltpu.VMEM((8, width), f32),
         pltpu.VMEM((narrow_n, 2 * share, width), bf16), pltpu.VMEM((narrow_n, 8, width), f32),
         pltpu.VMEM((width, 4 * width), f32), pltpu.VMEM(hot.shape, bf16), pltpu.SemaphoreType.DMA((2,))] + sem,
        12 * unit, 1 if linked else None)
    out_proj = pl.BlockSpec((width, width), lambda *_: (0, 3), pipeline_mode=pl.Buffered(1))
    fixed = (attn_weight, gw, tails, vectors, rinfo)
    outputs, grad_stream, gm, dmlp, dwo, dhid, dvec2 = run(
        functools.partial(feed_forward, TILE), steps, scal, (cotangent, mixed, stream),
        (fixed, [out_proj, pl.BlockSpec(memory_space=pl.ANY)] + [whole(a) for a in fixed[2:]]),
        [sds((rows, width), bf16), sds((rows, width), f32), sds((wins, SLOT, width), bf16)],
        [sds((narrow_n, 2 * share, width), f32), sds((width, width), f32), sds((8, hidden), f32), sds((5, 8, width), f32)],
        [pltpu.VMEM((width, width), bf16), pltpu.VMEM((hidden, width), bf16), pltpu.VMEM((hidden, width), bf16),
         pltpu.VMEM((1, hidden), f32), pltpu.VMEM((width, hidden), f32), pltpu.VMEM((width, hidden), f32),
         pltpu.VMEM((pad, width), f32), sides, pltpu.VMEM((ODD, width), bf16), pltpu.VMEM((ODD, width), bf16),
         pltpu.VMEM((ODD, hidden), bf16), pltpu.VMEM((ODD, hidden), bf16), pltpu.SemaphoreType.DMA((2 * narrow_n,))],
        52 * unit)
    _, streams, sizes = scatter_sizes(wide_n, share)
    last = sum(sizes[st][-1] for st in streams)
    bufs = []
    for s in range(n_bits - 1):
        for st in streams:
            bufs += [pltpu.VMEM((narrow_n, sizes[st][s + 1], width), bf16)] * 2
    copies = 1 + 2 * n_bits + narrow_n
    sem = [pltpu.SemaphoreType.DMA((copies,)), pltpu.SemaphoreType.DMA((copies,))] if linked else []
    dproj, dwq, misc, mine = run(
        functools.partial(attn_backward, wide_n, narrow_n, comm), steps, (), (tokens, qkv, prob, gm),
        wholes_of(vectors, hot, mask, mask2, dmlp, dhid, dvec2, stats, far=(4,)),
        [sds((rows, 3 * width), bf16)],
        [sds((3, width, width), f32), sds((32, width), f32), sds((last, width), bf16)],
        [pltpu.VMEM((pad, 3 * width), f32),
         pltpu.VMEM((CW, groups, KR, HG * SLOT), f32), turned, turned, pltpu.VMEM((3, 8, width), f32), table_s, flat,
         pltpu.VMEM((ODD, width), bf16), pltpu.VMEM((ODD, 3 * width), bf16), pltpu.VMEM(dmlp.shape, f32), pltpu.SemaphoreType.DMA((1,)),
         pltpu.VMEM((narrow_n, share, width), bf16), pltpu.VMEM((narrow_n, share, width), bf16),
         pltpu.VMEM((narrow_n, share, width), f32), pltpu.VMEM((narrow_n - 1, last, width), bf16),
         pltpu.VMEM((narrow_n - 1, last, width), bf16)] + bufs + sem,
        20 * unit, 2 if linked else None)
    return outputs, grad_stream, dmlp, dwq, dwo, misc, mine, dproj


TILE = 768


def adam_step(weight, gradient, first_old, second_old, rate_value, decay_value):
    first_new = beta_one * first_old + (1.0 - beta_one) * gradient
    second_new = beta_two * second_old + (1.0 - beta_two) * gradient * gradient
    fix_one = 1.0 - beta_one**STEP
    fix_two = 1.0 - beta_two**STEP
    update = rate_value * (first_new / fix_one) / (jnp.sqrt(second_new / fix_two) + adam_eps)
    return (weight - update - rate_value * decay_value * weight, first_new, second_new)


def shards(wide_n, narrow_n, tokens, grid_sizes, cotangent, attn_weight, attn_first, attn_second, rel_table, table_first,
           table_second, vectors, vector_first, vector_second, mlp_weight, mlp_first, mlp_second, mlp_bias, bias_first,
           bias_second):
    width = tokens.shape[1]
    narrow = lax.axis_index("narrow").reshape(1).astype(jnp.int32)
    outputs, grad_stream, _, dwq, dwo, misc, mine, dproj = block(
        tokens, grid_sizes, cotangent, attn_weight, rel_table.T, vectors, mlp_weight, mlp_bias, narrow, wide_n, narrow_n)
    gm, gt, misc, part = reduce_call(wide_n, narrow_n, mlp_weight.shape[1], mine, dwq.reshape(3 * width, width), dwo, misc,
                                     vectors, dproj, tokens, attn_weight)
    new = adam_call(narrow, grad_stream, part, gt, gm, misc, (attn_weight, attn_first, attn_second), (mlp_weight, mlp_first, mlp_second),
                    (rel_table.T, table_first.T, table_second.T), (vectors, vector_first, vector_second),
                    (mlp_bias, bias_first, bias_second))
    return (outputs, *new)


def solution(mesh):
    rows = P(("wide", "narrow"), None)
    split = P(None, "narrow", None)
    return jax.shard_map(
        functools.partial(shards, mesh.shape["wide"], mesh.shape["narrow"]), mesh=mesh,
        in_specs=(rows, P("wide"), rows) + (P(),) * 9 + (split,) * 3 + (P("narrow"),) * 3,
        out_specs=(rows, rows) + (P(),) * 11 + (split,) * 4 + (P("narrow"),) * 3,
        check_vma=False)
```
